32 devices in a mesh: copies: 2 (over y), tile: 4 (over z), sub: 4 (over x, core), lev: 1.
Axes of the slice: x: 2, y: 2, z: 4, core: 2. Of those that a mesh axis runs over, the one named last changes fastest.
Arguments:
- water_heat_state: float32 [4, 512, 512], P('lev', ('copies', 'tile'), 'sub'), parts along dimension 1, may hold values from -6 to 6
- diffusion_coefficient: float32 [256, 512], P('tile', 'sub'), may hold values from 0.004 to 0.03
- upper_current_vector: float32 [2, 512, 512], P(None, ('copies', 'tile'), 'sub'), parts along dimension 1, may hold values from -4 to 4
- remap_blocks: int32 [16, 4], P(('tile', 'sub', 'lev')), may hold values from 0 to 15, as said below
- remap_rows: bfloat16 [16, 4, 128, 64], P(('tile', 'sub', 'lev')), may hold values from -0.75 to 0.75
- remap_cols: bfloat16 [16, 4, 128, 128], P(('tile', 'sub', 'lev')), may hold values from -0.5 to 0.5
- neighbors: int32 [1, 16, 4], P(None, ('tile', 'sub', 'lev')), may hold values from -1 to 15, as said below
- thickness: float32 [1, 32, 5, 16384], P(None, ('copies', 'tile', 'sub', 'lev')), parts along dimension 1, may hold values from 0.5 to 6
- concentration: float32 [1, 32, 5, 16384], P(None, ('copies', 'tile', 'sub', 'lev')), parts along dimension 1, may hold values from 0.18 to 0.2
- ice_velocity: float32 [1, 32, 2, 16384], P(None, ('copies', 'tile', 'sub', 'lev')), parts along dimension 1, may hold values from -3 to 3
- wind_stress: float32 [1, 32, 2, 16384], P(None, ('copies', 'tile', 'sub', 'lev')), parts along dimension 1, may hold values from -6 to 6
Outputs:
- updated_heat_state: float32 [4, 512, 512], P('lev', ('copies', 'tile'), 'sub'), parts along dimension 1
- current_out: float32 [2, 512, 512], P(None, ('copies', 'tile'), 'sub'), parts along dimension 1
- velocity_out: float32 [1, 32, 2, 16384], P(None, ('copies', 'tile', 'sub', 'lev')), parts along dimension 1
The draws below stay inside these ranges and needn't reach their ends.
There are 2 independent parts, one for each index of `copies`. The reference program is written for one: setup_inputs(seed, part) draws one part's arguments, and reference() takes and returns one part's arrays. A program takes and returns all parts, laid end to end along the dimension named above; an argument that names none is the same for every part. Nothing has to cross between parts.
Inputs may be any that keep to these rules, and one draw needn't show every extreme that they name: `remap_blocks`: every ice block is named by exactly four pairs over all devices. The block n lives on device n mod 16; the pairs of device e name only blocks living on devices with the same position along `tile` as e (e // 4); the pairs of one device name at most 1 block living on any one device, and this is reached. `neighbors`: -1 marks a coast. Links are mutual: if b is the north (east) neighbour of a, then a is the south (west) neighbour of b. For each direction, the blocks of one device have their neighbours on distinct devices.
All inputs are finite; a program needn't handle non-finite values.
Results may differ from the reference program's by a relative error of at most 0.0044.
Values may be sent and summed in bfloat16 or wider, within the bound.
No kernel may reach another device: no remote copies, remote signals or barrier semaphores. Data moves between devices by JAX's collectives and lax.ppermute only.
A program may use at most 64 MiB of HBM per device.

```python
import math
import jax
import jax.numpy as jnp
from jax import lax

TX = 64
TY = 128
BS = 128
CAT = 5
BLK_DEV = 1
SUBCYCLES = 4
GROUP = 4
DEVP = 16
PAIRS_DEV = 4
NB = 16
NX = 256
NY = 512
SEA_STRATA = 4
N_TILE = 4
N_SUB = 4
N_LEV = 1


def draw_remap_blocks(key, part):
    key = jax.random.fold_in(key, 11)
    shuffled = jax.random.permutation(key, GROUP)
    shuffled = (shuffled - shuffled[0] + GROUP // 2) % GROUP
    pair_index = jnp.arange(PAIRS_DEV)
    offsets = shuffled[pair_index % GROUP]
    sources = jnp.arange(DEVP)[:, None]
    tile_base = sources // GROUP * GROUP
    members = sources % GROUP
    owners = tile_base + (members - offsets[None, :]) % GROUP
    return ((pair_index // 4)[None, :] * DEVP + owners).astype(jnp.int32)


def draw_neighbors(key, part):
    key = jax.random.fold_in(key, 23)
    key_list = jax.random.split(key, 8)
    east_slot = jax.random.permutation(key_list[0], BLK_DEV)
    north_slot = jax.random.permutation(key_list[1], BLK_DEV)
    east_perm = jax.random.permutation(key_list[2], DEVP)
    north_perm = jax.random.permutation(key_list[3], DEVP)
    east_offset = jax.random.permutation(key_list[6], DEVP)[:BLK_DEV]
    north_offset = jax.random.permutation(key_list[7], DEVP)[:BLK_DEV]
    east_open = jax.random.randint(key_list[4], (BLK_DEV, DEVP), 0, 8) > 0
    north_open = jax.random.randint(key_list[5], (BLK_DEV, DEVP), 0, 8) > 0
    places = jnp.arange(DEVP)[None, :]
    east_place = (east_perm[None, :] + east_offset[:, None]) % DEVP
    north_place = (north_perm[None, :] + north_offset[:, None]) % DEVP
    east_index = east_slot[:, None] * DEVP + east_place
    north_index = north_slot[:, None] * DEVP + north_place
    east_back = jnp.argsort(east_slot)
    north_back = jnp.argsort(north_slot)
    east_inverse = jnp.argsort(east_perm)
    north_inverse = jnp.argsort(north_perm)
    west_place = east_inverse[(places - east_offset[east_back][:, None]) % DEVP]
    south_place = north_inverse[(places - north_offset[north_back][:, None]) % DEVP]
    west_index = east_back[:, None] * DEVP + west_place
    south_index = north_back[:, None] * DEVP + south_place
    west_open = east_open[east_back[:, None], west_place]
    south_open = north_open[north_back[:, None], south_place]
    stacked = jnp.stack([jnp.where(north_open, north_index, -1), jnp.where(south_open, south_index, -1), jnp.where(east_open, east_index, -1), jnp.where(west_open, west_index, -1)], axis=-1)
    return stacked.astype(jnp.int32)


def block_scale(own_key, extent, cuts, low, largest):
    def one(position, parts):
        draws = jax.random.uniform(jax.random.fold_in(jax.random.fold_in(own_key, 6), position), (parts,), jnp.float32, low / len(cuts), largest / len(cuts))
        return jnp.repeat(jnp.exp(draws), extent[position] // parts).reshape((-1,) + (1,) * (len(extent) - position - 1))

    level = one(*cuts[0])
    for cut in cuts[1:]:
        level = level * one(*cut)
    return level


def scatter_about(rng, extent, deviation, most, cuts=(), dtype=jnp.bfloat16):
    level = block_scale(rng, extent, cuts, -0.22, 0.18) if cuts else 1.0
    values = jax.random.normal(rng, extent, jnp.float32) * deviation * level
    return jnp.minimum(jnp.maximum(values, -most), most).astype(dtype)


def setup_inputs(seed: int = 0, part: int = 0) -> dict:
    splits = jax.random.split(jax.random.key(seed), 12)
    own_keys = jax.random.split(jax.random.fold_in(splits[11], part), 12)
    return {
        "water_heat_state": scatter_about(own_keys[0], (SEA_STRATA, NX, NY), 1.0, 6.0, ((1, 4), (2, 4)), jnp.float32),
        "diffusion_coefficient": jnp.clip(jnp.exp(math.log(0.03) - 2.014903 * jax.random.uniform(splits[1], (NX, NY), jnp.float32) ** block_scale(splits[1], (NX, NY), ((0, 4), (1, 4)), -0.2, 0.2)), 0.004, 0.03),
        "upper_current_vector": scatter_about(own_keys[2], (2, NX, NY), 0.5, 4.0, ((1, 4), (2, 4)), jnp.float32),
        "remap_blocks": draw_remap_blocks(jax.random.fold_in(splits[11], 71), part),
        "remap_rows": scatter_about(splits[4], (DEVP, PAIRS_DEV, BS, TX), TX ** -0.5, 0.75, ((0, 16),)),
        "remap_cols": scatter_about(splits[5], (DEVP, PAIRS_DEV, BS, TY), TY ** -0.5, 0.5, ((0, 16),)),
        "neighbors": draw_neighbors(jax.random.fold_in(splits[11], 71), part),
        "thickness": jnp.clip(jnp.exp(math.log(6.0) - 2.4849066 * jax.random.uniform(own_keys[7], (BLK_DEV, DEVP, CAT, BS * BS), jnp.float32) ** block_scale(own_keys[7], (BLK_DEV, DEVP, CAT, BS * BS), ((1, 16),), -0.2, 0.2)), 0.5, 6.0),
        "concentration": jnp.clip(0.18 + 0.019999996 * jax.random.uniform(own_keys[8], (BLK_DEV, DEVP, CAT, BS * BS), jnp.float32) ** block_scale(own_keys[8], (BLK_DEV, DEVP, CAT, BS * BS), ((1, 16),), -0.2, 0.2), 0.18, 0.2),
        "ice_velocity": jnp.clip(jax.random.uniform(own_keys[9], (BLK_DEV, DEVP, 2, BS * BS), jnp.float32, -3.0, 3.0) * block_scale(own_keys[9], (BLK_DEV, DEVP, 2, BS * BS), ((1, 16),), -0.4, 0.0), -3.0, 3.0),
        "wind_stress": scatter_about(own_keys[10], (BLK_DEV, DEVP, 2, BS * BS), 1.0, 6.0, ((1, 16),), jnp.float32),
    }


STRENGTH_DECAY = 5.0
VISCOUS_STEP = 0.24
SUBCYCLE_STEP = 0.5
CORIOLIS_TURN = 0.1
BASE_MASS = 0.5
HEAT_RATE = 0.2
THIN_ICE = 0.1
THERMAL_DIFFUSE = 0.5
STRESS_MIXING = 0.5
OPPOSITE = (1, 0, 3, 2)


def second_derivative(padded):
    return (padded[..., 2:, 1:-1] + padded[..., :-2, 1:-1] + padded[..., 1:-1, 2:]
            + padded[..., 1:-1, :-2] - 4.0 * padded[..., 1:-1, 1:-1])


def block_edges(velocity):
    return jnp.stack([velocity[:, :, -1, :], velocity[:, :, 0, :], velocity[:, :, :, -1], velocity[:, :, :, 0]], axis=1)


def with_halo(velocity, rim_halos):
    padded = jnp.pad(velocity, ((0, 0), (0, 0), (1, 1), (1, 1)))
    padded = padded.at[:, :, -1, 1:-1].set(rim_halos[:, 0])
    padded = padded.at[:, :, 0, 1:-1].set(rim_halos[:, 1])
    padded = padded.at[:, :, 1:-1, -1].set(rim_halos[:, 2])
    padded = padded.at[:, :, 1:-1, 0].set(rim_halos[:, 3])
    return padded


def ice_coefficients(thickness, concentration):
    total_cover = jnp.sum(concentration, axis=1)
    volume = jnp.sum(concentration * thickness, axis=1)
    ice_mass = volume + BASE_MASS
    strength = volume * jnp.exp(-STRENGTH_DECAY * (1.0 - total_cover))
    conduct = jnp.sum(concentration / (thickness + THIN_ICE), axis=1)
    return VISCOUS_STEP * strength / ice_mass, SUBCYCLE_STEP / ice_mass, total_cover, conduct


def subcycle(velocity, rim_halos, viscous, step_mass, drag_rate, wind_force, current_ice):
    spread = second_derivative(with_halo(velocity, rim_halos))
    pushed = velocity + viscous[:, None] * spread + step_mass[:, None] * (wind_force + drag_rate[:, None] * current_ice)
    turned = jnp.stack([pushed[:, 0] + CORIOLIS_TURN * velocity[:, 1],
                        pushed[:, 1] - CORIOLIS_TURN * velocity[:, 0]], axis=1)
    return turned / (1.0 + step_mass * drag_rate)[:, None]


def ice_fluxes(velocity, conduct, drag_rate, forcing):
    heat_flux = -HEAT_RATE * conduct * forcing[:, 0]
    stress = drag_rate[:, None] * (velocity - forcing[:, 1:])
    return jnp.concatenate([heat_flux[:, None], stress], axis=1)


def reference(water_heat_state, diffusion_coefficient, upper_current_vector, remap_blocks, remap_rows, remap_cols, neighbors,
              thickness, concentration, ice_velocity, wind_stress):
    bordered_heat_state = jnp.pad(water_heat_state, ((0, 0), (2, 2), (2, 2)))
    diffused_warmth = water_heat_state - diffusion_coefficient * second_derivative(second_derivative(bordered_heat_state))
    topmost_warmth = jnp.sum(diffused_warmth, axis=0) / SEA_STRATA
    topmost_slab = jnp.concatenate([topmost_warmth[None], upper_current_vector], axis=0).astype(jnp.bfloat16)
    surface_tiles = topmost_slab.reshape(3, N_TILE, TX, N_SUB, TY).transpose(1, 3, 0, 2, 4).reshape(N_TILE * N_SUB, 3, TX, TY)
    source_tiles = jnp.repeat(surface_tiles, N_LEV, axis=0)

    def forward_pairs(pair_items):
        row_weights, col_weights, tile_fields = pair_items
        partial_rows = jnp.einsum('mbx,fxy->mfby', row_weights.astype(jnp.float32),
                                  tile_fields.astype(jnp.float32)).astype(jnp.bfloat16)
        return jnp.einsum('mfby,mcy->mfbc', partial_rows.astype(jnp.float32),
                          col_weights.astype(jnp.float32)).astype(jnp.bfloat16)

    pieces = lax.map(forward_pairs, (remap_rows, remap_cols, source_tiles))
    forcing = jnp.zeros((NB, 3, BS, BS), jnp.float32).at[remap_blocks.reshape(-1)].add(
        pieces.reshape(-1, 3, BS, BS).astype(jnp.float32))

    thick_blocks = thickness.reshape(NB, CAT, BS, BS)
    cover_blocks = concentration.reshape(NB, CAT, BS, BS)
    velocity = ice_velocity.reshape(NB, 2, BS, BS)
    wind_force = wind_stress.reshape(NB, 2, BS, BS)
    neighbor_ids = neighbors.reshape(NB, 4)
    linked = neighbor_ids >= 0
    safe_ids = jnp.where(linked, neighbor_ids, 0)
    mask_edges = linked.astype(jnp.float32)[:, :, None, None]
    opposite = jnp.array(OPPOSITE, jnp.int32)[None, :]
    viscous, step_mass, drag_rate, conduct = ice_coefficients(thick_blocks, cover_blocks)
    current_ice = forcing[:, 1:]
    for subcycle_index in range(SUBCYCLES):
        rim_edges = block_edges(velocity)
        rim_halos = rim_edges[safe_ids, opposite] * mask_edges
        velocity = subcycle(velocity, rim_halos, viscous, step_mass, drag_rate, wind_force, current_ice)
    fluxes = ice_fluxes(velocity, conduct, drag_rate, forcing).astype(jnp.bfloat16)
    returned = fluxes[remap_blocks]

    def backward_pairs(pair_items):
        row_weights, col_weights, block_flux_terms = pair_items
        partial_cols = jnp.einsum('mbx,mfbc->mfxc', row_weights.astype(jnp.float32),
                                  block_flux_terms.astype(jnp.float32)).astype(jnp.bfloat16)
        return jnp.einsum('mfxc,mcy->fxy', partial_cols.astype(jnp.float32), col_weights.astype(jnp.float32))

    exchange_parts = lax.map(backward_pairs, (remap_rows, remap_cols, returned))
    tile_terms = jnp.sum(exchange_parts.reshape(N_TILE * N_SUB, N_LEV, 3, TX, TY), axis=1)
    mesh_factors = tile_terms.reshape(N_TILE, N_SUB, 3, TX, TY).transpose(2, 0, 3, 1, 4).reshape(3, NX, NY)
    updated_heat_state = diffused_warmth + THERMAL_DIFFUSE * mesh_factors[0]
    current_out = upper_current_vector + STRESS_MIXING * mesh_factors[1:]
    return updated_heat_state, current_out, velocity.reshape(BLK_DEV, DEVP, 2, BS * BS)
```

```python
import jax
import jax.numpy as jnp
from jax import lax
from jax.sharding import PartitionSpec as P

SUBCYCLES = 4


STRENGTH_DECAY = 5.0
VISCOUS_STEP = 0.24
SUBCYCLE_STEP = 0.5
CORIOLIS_TURN = 0.1
BASE_MASS = 0.5
HEAT_RATE = 0.2
THIN_ICE = 0.1
THERMAL_DIFFUSE = 0.5
STRESS_MIXING = 0.5
OPPOSITE = (1, 0, 3, 2)


def extended(value, sides, width):
    for axis, dim in sides:
        size, length = (lax.axis_size(axis), value.shape[dim])
        up = [(i, (i + 1) % size) for i in range(size - 1)]
        down = [(j, i) for i, j in up]
        last = lax.slice_in_dim(value, length - width, length, axis=dim)
        leading = lax.slice_in_dim(value, 0, width, axis=dim)
        before = lax.ppermute(last, axis, up)
        after = lax.ppermute(leading, axis, down)
        value = jnp.concatenate([before, value, after], axis=dim)
    return value


def second_derivative(padded):
    return (
        padded[..., 2:, 1:-1]
        + padded[..., :-2, 1:-1]
        + padded[..., 1:-1, 2:]
        + padded[..., 1:-1, :-2]
        - 4.0 * padded[..., 1:-1, 1:-1]
    )


def block_edges(velocity):
    return jnp.stack(
        [velocity[:, :, -1, :], velocity[:, :, 0, :], velocity[:, :, :, -1], velocity[:, :, :, 0]],
        axis=1,
    )


def with_halo(velocity, rim_halos):
    padded = jnp.pad(velocity, ((0, 0), (0, 0), (1, 1), (1, 1)))
    padded = padded.at[:, :, -1, 1:-1].set(rim_halos[:, 0])
    padded = padded.at[:, :, 0, 1:-1].set(rim_halos[:, 1])
    padded = padded.at[:, :, 1:-1, -1].set(rim_halos[:, 2])
    padded = padded.at[:, :, 1:-1, 0].set(rim_halos[:, 3])
    return padded


def ice_coefficients(thickness, concentration):
    total_cover = jnp.sum(concentration, axis=1)
    volume = jnp.sum(concentration * thickness, axis=1)
    ice_mass = volume + BASE_MASS
    strength = volume * jnp.exp(-STRENGTH_DECAY * (1.0 - total_cover))
    conduct = jnp.sum(concentration / (thickness + THIN_ICE), axis=1)
    return (VISCOUS_STEP * strength / ice_mass, SUBCYCLE_STEP / ice_mass, total_cover, conduct)


def subcycle(velocity, rim_halos, viscous, step_mass, drag_rate, wind_force, current_ice):
    spread = second_derivative(with_halo(velocity, rim_halos))
    pushed = (
        velocity
        + viscous[:, None] * spread
        + step_mass[:, None] * (wind_force + drag_rate[:, None] * current_ice)
    )
    turned = jnp.stack(
        [
            pushed[:, 0] + CORIOLIS_TURN * velocity[:, 1],
            pushed[:, 1] - CORIOLIS_TURN * velocity[:, 0],
        ],
        axis=1,
    )
    return turned / (1.0 + step_mass * drag_rate)[:, None]


def ice_fluxes(velocity, conduct, drag_rate, forcing):
    heat_flux = -HEAT_RATE * conduct * forcing[:, 0]
    stress = drag_rate[:, None] * (velocity - forcing[:, 1:])
    return jnp.concatenate([heat_flux[:, None], stress], axis=1)


def shards(
    water_heat_state,
    diffusion_coefficient,
    upper_current_vector,
    remap_blocks,
    remap_rows,
    remap_cols,
    neighbors,
    thickness,
    concentration,
    ice_velocity,
    wind_stress,
):
    tile_count = lax.axis_size("tile")
    group_count = lax.axis_size("sub") * lax.axis_size("lev")
    device_count = tile_count * group_count
    vertical_total = water_heat_state.shape[0] * lax.axis_size("lev")
    bordered_heat_state = extended(water_heat_state, (("tile", 1), ("sub", 2)), 2)
    diffused_warmth = water_heat_state - diffusion_coefficient * second_derivative(
        second_derivative(bordered_heat_state)
    )
    topmost_warmth = lax.psum(jnp.sum(diffused_warmth, axis=0), "lev") / vertical_total
    topmost_slab = jnp.concatenate([topmost_warmth[None], upper_current_vector], axis=0).astype(
        jnp.bfloat16
    )
    row_weights = remap_rows[0]
    col_weights = remap_cols[0]
    target_blocks = remap_blocks[0]
    pair_count = target_blocks.shape[0]
    block_side = row_weights.shape[1]
    item_width = 3 * block_side * block_side
    capacity = (pair_count + group_count - 1) // group_count
    partial_rows = jnp.einsum(
        "mbx,fxy->mfby", row_weights, topmost_slab, preferred_element_type=jnp.float32
    ).astype(jnp.bfloat16)
    pieces = (
        jnp.einsum("mfby,mcy->mfbc", partial_rows, col_weights, preferred_element_type=jnp.float32)
        .astype(jnp.bfloat16)
        .reshape(pair_count, item_width)
    )
    owner_member = target_blocks % device_count % group_count
    owner_slot = target_blocks // device_count
    pair_order = jnp.arange(pair_count)
    slot_rank = jnp.sum(
        (owner_member[None, :] == owner_member[:, None])
        & (pair_order[None, :] < pair_order[:, None]),
        axis=1,
    )
    outgoing = (
        jnp.zeros((group_count, capacity, item_width), jnp.bfloat16)
        .at[owner_member, slot_rank]
        .set(pieces)
    )
    labels = (
        jnp.full((group_count, capacity), -1, jnp.int32).at[owner_member, slot_rank].set(owner_slot)
    )
    incoming, in_labels = (
        lax.all_to_all(outgoing, ("sub", "lev"), split_axis=0, concat_axis=0, tiled=True),
        lax.all_to_all(labels, ("sub", "lev"), split_axis=0, concat_axis=0, tiled=True),
    )
    incoming = incoming.reshape(group_count * capacity, item_width)
    block_count = thickness.shape[0]
    selector = (in_labels.reshape(1, -1) == jnp.arange(block_count)[:, None]).astype(jnp.bfloat16)
    forcing = jnp.dot(selector, incoming, preferred_element_type=jnp.float32).reshape(
        block_count, 3, block_side, block_side
    )
    category_count = thickness.shape[2]
    thick_blocks = thickness[:, 0].reshape(block_count, category_count, block_side, block_side)
    cover_blocks = concentration[:, 0].reshape(block_count, category_count, block_side, block_side)
    velocity = ice_velocity[:, 0].reshape(block_count, 2, block_side, block_side)
    wind_force = wind_stress[:, 0].reshape(block_count, 2, block_side, block_side)
    neighbor_ids = neighbors[:, 0, :]
    linked = neighbor_ids >= 0
    mask_edges = linked.astype(jnp.float32)[:, :, None, None]
    opposite = jnp.array(OPPOSITE, jnp.int32)[None, :]
    source_dev = jnp.where(linked, neighbor_ids % device_count, 0)
    source_slot = jnp.where(linked, neighbor_ids // device_count, 0)
    viscous, step_mass, drag_rate, conduct = ice_coefficients(thick_blocks, cover_blocks)
    current_ice = forcing[:, 1:]
    for subcycle_index in range(SUBCYCLES):
        rim_edges = block_edges(velocity)
        sent_rims = rim_edges.reshape(1, block_count, 8 * block_side)
        everything = lax.all_to_all(
            jnp.broadcast_to(sent_rims, (device_count, block_count, 8 * block_side)),
            ("tile", "sub", "lev"),
            split_axis=0,
            concat_axis=0,
            tiled=True,
        )
        rim_halos = everything.reshape(device_count * block_count * 4, 2, block_side)[
            (source_dev * block_count + source_slot) * 4 + opposite
        ]
        velocity = subcycle(
            velocity, rim_halos * mask_edges, viscous, step_mass, drag_rate, wind_force, current_ice
        )
    fluxes = (
        ice_fluxes(velocity, conduct, drag_rate, forcing)
        .astype(jnp.bfloat16)
        .reshape(block_count, item_width)
    )
    replies = jnp.dot(selector.T, fluxes, preferred_element_type=jnp.float32).astype(jnp.bfloat16)
    returned = lax.all_to_all(
        replies.reshape(group_count, capacity, item_width),
        ("sub", "lev"),
        split_axis=0,
        concat_axis=0,
        tiled=True,
    )
    answers = returned.reshape(group_count * capacity, item_width)[
        owner_member * capacity + slot_rank
    ]
    answers = answers.reshape(pair_count, 3, block_side, block_side)
    partial_cols = jnp.einsum(
        "mbx,mfbc->mfxc", row_weights, answers, preferred_element_type=jnp.float32
    ).astype(jnp.bfloat16)
    exchange_parts = jnp.einsum(
        "mfxc,mcy->fxy", partial_cols, col_weights, preferred_element_type=jnp.float32
    )
    exchange_parts = lax.psum(exchange_parts, "lev")
    updated_heat_state = diffused_warmth + THERMAL_DIFFUSE * exchange_parts[0]
    current_out = upper_current_vector + STRESS_MIXING * exchange_parts[1:]
    return (
        updated_heat_state,
        current_out,
        velocity.reshape(block_count, 1, 2, block_side * block_side),
    )


def solution(mesh):
    return jax.shard_map(
        shards,
        mesh=mesh,
        in_specs=(
            P("lev", ("copies", "tile"), "sub"),
            P("tile", "sub"),
            P(None, ("copies", "tile"), "sub"),
            P(("tile", "sub", "lev"), None),
            P(("tile", "sub", "lev"), None, None, None),
            P(("tile", "sub", "lev"), None, None, None),
            P(None, ("tile", "sub", "lev"), None),
            P(None, ("copies", "tile", "sub", "lev"), None, None),
            P(None, ("copies", "tile", "sub", "lev"), None, None),
            P(None, ("copies", "tile", "sub", "lev"), None, None),
            P(None, ("copies", "tile", "sub", "lev"), None, None),
        ),
        out_specs=(
            P("lev", ("copies", "tile"), "sub"),
            P(None, ("copies", "tile"), "sub"),
            P(None, ("copies", "tile", "sub", "lev"), None, None),
        ),
        check_vma=False,
    )
```

```python
import functools

import jax
import jax.numpy as jnp
from jax import lax
from jax.experimental import pallas as pl
from jax.experimental.pallas import tpu as pltpu
from jax.sharding import PartitionSpec as P

SUBCYCLES = 4
STRENGTH_DECAY = 5.0
VISCOUS_STEP = 0.24
SUBCYCLE_STEP = 0.5
CORIOLIS_TURN = 0.1
BASE_MASS = 0.5
HEAT_RATE = 0.2
THIN_ICE = 0.1
THERMAL_DIFFUSE = 0.5
STRESS_MIXING = 0.5

OPPOSITE = (1, 0, 3, 2)
LATERAL = ((2, 3), (2, 3), (0, 1), (0, 1))
DEPTH = SUBCYCLES
TILE_ROWS = 16
F32 = jnp.float32
BF16 = jnp.bfloat16
VMEM_LIMIT = 16 * 1024 * 1024


def call(kernel, outs, args, scratch=(), smem=(), flops=1_000_000):
    specs = [
        pl.BlockSpec(memory_space=pltpu.SMEM if i in smem else pltpu.VMEM) for i in range(len(args))
    ]
    size = sum(a.size * a.dtype.itemsize for a in args)
    return pl.pallas_call(
        kernel,
        out_shape=outs,
        in_specs=specs,
        out_specs=jax.tree.map(lambda _: pl.BlockSpec(memory_space=pltpu.VMEM), outs),
        scratch_shapes=list(scratch),
        compiler_params=pltpu.CompilerParams(vmem_limit_bytes=VMEM_LIMIT),
        cost_estimate=pl.CostEstimate(flops=flops, bytes_accessed=size, transcendentals=0),
    )(*args)


def iota(shape, axis):
    return lax.broadcasted_iota(jnp.int32, shape, axis)


def roll(x, shift, axis):
    return pltpu.roll(x, shift % x.shape[axis], axis)


def flag(condition):
    return jnp.where(condition, 1.0, 0.0).astype(F32)


def forward_kernel(group, blocks, rows, cols, currents, *outs):
    side = rows.shape[1]
    depth = cols.shape[1]
    devices = group[0]
    members = group[1]
    me = group[2]()
    fields = [currents[c].astype(BF16) for c in range(2)]
    pairs = rows.shape[0]
    for k, out in enumerate(outs):
        partner = me ^ k
        pair = jnp.int32(0)
        found = jnp.int32(0)
        for m in range(pairs):
            owner = lax.rem(lax.rem(blocks[0, m], devices), members)
            pair = jnp.where(owner == partner, m, pair)
            found = jnp.where(owner == partner, 1, found)
        if pairs == members:
            out[0:side] = rows[pair]
            out[side : side + depth] = cols[pair]
        else:
            out[0:side] = jnp.where(found > 0, rows[pair].astype(F32), 0.0).astype(BF16)
            out[side : side + depth] = jnp.where(found > 0, cols[pair].astype(F32), 0.0).astype(BF16)
        for c in range(2):
            out[side + depth + c * side : side + depth + (c + 1) * side] = fields[c]


def put_side_rims(store, planes, at):
    size = planes[0].shape[0]
    lane = iota((size, size), 1)
    mixed = jnp.zeros((size, size), F32)
    for i, plane in enumerate(planes):
        turned = roll(plane, DEPTH + 2 * DEPTH * i, 1)
        mixed = jnp.where(lane // (2 * DEPTH) == i, turned, mixed)
    across = mixed.T
    for i, plane in enumerate(planes):
        for k in range(DEPTH):
            base = i * DEPTH + k
            store[at(0) + base : at(0) + base + 1] = plane[size - 1 - k : size - k]
            store[at(1) + base : at(1) + base + 1] = plane[k : k + 1]
            east = 2 * DEPTH * i + DEPTH - 1 - k
            west = 2 * DEPTH * i + DEPTH + k
            store[at(2) + base : at(2) + base + 1] = across[east : east + 1]
            store[at(3) + base : at(3) + base + 1] = across[west : west + 1]


def rims_kernel(
    where_am_i, links, thick, conc, ice, water, out, viscous_o, gain_o, mass_o, drag_o, conduct_o,
    speed_o, store,
):
    tile_count, sub_count, lev_count, place = where_am_i
    my_tile, my_sub, my_lev = place()
    size = thick.shape[1]
    cover = jnp.zeros((size, size), F32)
    volume = jnp.zeros((size, size), F32)
    conduct = jnp.zeros((size, size), F32)
    for c in range(thick.shape[0]):
        h, a = thick[c], conc[c]
        cover = cover + a
        volume = volume + a * h
        conduct = conduct + a / (h + THIN_ICE)
    mass = volume + BASE_MASS
    viscous = VISCOUS_STEP * (volume * jnp.exp(-STRENGTH_DECAY * (1.0 - cover))) / mass
    step_mass = SUBCYCLE_STEP / mass
    gain = 1.0 / (1.0 + step_mass * cover)
    speed_x = ice[pl.ds(0, size, stride=2), :]
    speed_y = ice[pl.ds(1, size, stride=2), :]
    viscous_o[...] = viscous
    gain_o[...] = gain
    mass_o[...] = step_mass
    drag_o[...] = cover
    conduct_o[...] = -HEAT_RATE * conduct
    speed_o[0] = speed_x
    speed_o[1] = speed_y
    side_rows = 4 * 4 * DEPTH
    put_side_rims(store, [speed_x, speed_y, viscous, gain], lambda side: side * 4 * DEPTH)
    rim_rows = store[0:side_rows].astype(BF16)
    for d in range(out.shape[0]):
        out[d, 0:side_rows] = rim_rows
    levels, rows, width = water.shape
    lane = iota((rows, width), 1)
    mixed = jnp.zeros((rows, width), F32)
    for l in range(levels):
        mixed = jnp.where(lane // 4 == l, roll(water[l], 2 + 4 * l, 1), mixed)
    across = jnp.concatenate([mixed, jnp.zeros((width - rows, width), F32)], axis=0).T
    row_lane = iota((1, width), 1)
    names = jnp.zeros((1, width), F32)
    for q in range(4):
        high = links[0, 0, q] >> 7
        low = links[0, 0, q] & 127
        names = jnp.where(row_lane == q, high.astype(F32), names)
        names = jnp.where(row_lane == 4 + q, low.astype(F32), names)
    spare = out.shape[1] - side_rows
    blank = jnp.concatenate(
        [jnp.zeros((2 * levels, width), F32), names, jnp.zeros((spare - 2 * levels - 1, width), F32)]
    )
    empty = blank.astype(BF16)
    for d in range(out.shape[0]):
        out[d, side_rows:] = empty
    tail = blank[2 * levels :]
    for dt in (-1, 0, 1):
        for ds in (-1, 0, 1):
            if dt == 0 and ds == 0:
                continue
            strip = []
            for l in range(levels):
                for j in range(2):
                    r = rows - 1 - j if dt > 0 else j
                    if ds == 0:
                        strip.append(water[l, r : r + 1])
                    elif dt == 0:
                        at = 4 * l + (1 - j if ds > 0 else 2 + j)
                        strip.append(across[at : at + 1])
                    else:
                        line = water[l, r : r + 1]
                        strip.append(roll(line, 1, 1) if ds > 0 else line)
            message = jnp.concatenate(strip + [tail], axis=0).astype(BF16)
            to_tile, to_sub = my_tile + dt, my_sub + ds
            inside = (to_tile >= 0) & (to_tile < tile_count) & (to_sub >= 0) & (to_sub < sub_count)

            @pl.when(inside)
            def _():
                out[(to_tile * sub_count + to_sub) * lev_count + my_lev, side_rows:] = message


def remap_forward(chunks, field_rows, side, depth):
    total = None
    for chunk, fields in zip(chunks, field_rows):
        down = chunk[0:side]
        right = chunk[side : side + depth]
        wide = jnp.concatenate(fields, axis=1) if len(fields) > 1 else fields[0]
        part = lax.dot_general(down, wide, (((0,), (0,)), ((), ())), preferred_element_type=F32)
        part = part.astype(BF16)
        width = fields[0].shape[1]
        if len(fields) > 1:
            part = jnp.concatenate(
                [part[:, c * width : (c + 1) * width] for c in range(len(fields))], axis=0
            )
        piece = lax.dot_general(part, right, (((1,), (1,)), ((), ())), preferred_element_type=F32)
        piece = piece.astype(BF16).astype(F32)
        total = piece if total is None else total + piece
    return total


def forcing_kernel(group, side, mass, drag, wind, *refs):
    chunks = refs[:group]
    out, current_o, push_o, store = refs[group:]
    size = mass.shape[0]
    depth = chunks[0].shape[0] - 3 * side
    fields = [
        [c[side + depth : 2 * side + depth], c[2 * side + depth : 3 * side + depth]] for c in chunks
    ]
    total = remap_forward(chunks, fields, side, depth)
    pushes = []
    for c in range(2):
        current = total[c * size : (c + 1) * size]
        current_o[c] = current
        force = wind[pl.ds(c, size, stride=2), :]
        push = mass[...] * (force + drag[...] * current)
        push_o[c] = push
        pushes.append(push)
    put_side_rims(store, pushes, lambda q: q * 2 * DEPTH)
    message = store[...].astype(BF16)
    for d in range(out.shape[0]):
        out[d] = message


def ocean_kernel(where_am_i, strip_at, water, mixing, rims, warm_o, top_o):
    tile_count, sub_count, lev_count, place = where_am_i
    my_tile, my_sub, my_lev = place()
    levels, rows, width = water.shape
    halo = {}
    for dt in (-1, 0, 1):
        for ds in (-1, 0, 1):
            if dt == 0 and ds == 0:
                continue
            t, s = my_tile + dt, my_sub + ds
            inside = (t >= 0) & (t < tile_count) & (s >= 0) & (s < sub_count)
            device = jnp.where(inside, (t * sub_count + s) * lev_count + my_lev, 0)
            strip = rims[device, strip_at : strip_at + TILE_ROWS].astype(F32)[: 2 * levels]
            halo[dt, ds] = strip * flag(inside)
    left_cols = halo[0, -1].T
    right_cols = halo[0, 1].T
    row = iota((rows, width), 0)
    lane = iota((rows, width), 1)
    line = iota((1, width), 1)
    total = None

    def laplacian(x, top, bottom, left, right):
        up = jnp.where(row == 0, top, roll(x, 1, 0))
        down = jnp.where(row == rows - 1, bottom, roll(x, -1, 0))
        west = jnp.where(lane == 0, left, roll(x, 1, 1))
        east = jnp.where(lane == width - 1, right, roll(x, -1, 1))
        return up + down + west + east - 4.0 * x

    for l in range(levels):
        x = water[l]
        near, far = 2 * l, 2 * l + 1
        top, top_far = halo[-1, 0][near : near + 1], halo[-1, 0][far : far + 1]
        bottom, bottom_far = halo[1, 0][near : near + 1], halo[1, 0][far : far + 1]
        left, left_far = left_cols[0:rows, near : near + 1], left_cols[0:rows, far : far + 1]
        right, right_far = right_cols[0:rows, near : near + 1], right_cols[0:rows, far : far + 1]
        corner = {}
        for dt in (-1, 1):
            for ds in (-1, 1):
                corner[dt, ds] = halo[dt, ds][near : near + 1, 0:1]

        def ring_row(mid, out_row, in_row, dt):
            west = jnp.where(line == 0, corner[dt, -1], roll(mid, 1, 1))
            east = jnp.where(line == width - 1, corner[dt, 1], roll(mid, -1, 1))
            return west + east + out_row + in_row - 4.0 * mid

        def ring_col(mid, out_col, in_col, ds):
            up = jnp.concatenate([corner[-1, ds], mid[:-1]], axis=0)
            down = jnp.concatenate([mid[1:], corner[1, ds]], axis=0)
            return up + down + out_col + in_col - 4.0 * mid

        once = laplacian(x, top, bottom, left, right)
        twice = laplacian(
            once,
            ring_row(top, top_far, x[0:1], -1),
            ring_row(bottom, bottom_far, x[rows - 1 :], 1),
            ring_col(left, left_far, x[:, 0:1], -1),
            ring_col(right, right_far, x[:, width - 1 :], 1),
        )
        warm = x - mixing[...] * twice
        warm_o[l] = warm
        total = warm if total is None else total + warm
    top_o[...] = (total / (levels * lev_count)).astype(top_o.dtype)


def subcycles_kernel(me, table, viscous, gain, speed, push, rims, push_rims, out, flat_o):
    size = viscous.shape[0]
    half = DEPTH
    high = 2 * DEPTH
    sub = iota((high, size), 0)
    lane = iota((high, size), 1)
    edge = (sub & (half - 1)) == 0
    turn = jnp.where(sub < half, CORIOLIS_TURN, -CORIOLIS_TURN).astype(F32)
    first, last = lane == 0, lane == size - 1

    def load(device, side, mask, with_push=True):
        block = rims[device, side * 2 * high : (side + 1) * 2 * high].astype(F32)
        velocity, both = block[:high] * mask, block[high:]
        if not with_push:
            return velocity
        other = roll(both, half, 0)
        visc = jnp.where(sub < half, both, other)
        scale = jnp.where(sub < half, other, both) * mask
        start = side // 2 * 2 * high
        pushed = push_rims[device, start : start + 2 * high].astype(F32)
        pushed = pushed[:high] if side % 2 == 0 else pushed[high:]
        return [velocity, visc, scale, pushed]

    def follow(device, side):
        name = table[device, side]
        return jnp.where(name >= 0, name, 0), name >= 0

    def step(state, left, right, inner, outer):
        c, visc, scale, pushed = state
        spread = left + right + inner + outer - 4.0 * c
        return scale * (c + visc * spread + pushed + turn * roll(c, half, 0))

    strips = []
    for q in range(4):
        x, has_x = follow(me(), q)
        strip = load(x, OPPOSITE[q], flag(has_x))
        sides = []
        for s in LATERAL[q]:
            y, has_y = follow(x, s)
            z, has_z = follow(y, OPPOSITE[q])
            w, has_w = follow(z, OPPOSITE[s])
            sides.append(
                [
                    load(y, OPPOSITE[q], flag(has_y)),
                    load(z, q, flag(has_z)),
                    load(w, q, flag(has_w), with_push=False),
                ]
            )
        strips.append((strip, sides))

    row = iota((size, size), 0)
    col = iota((size, size), 1)
    vx, vy = speed[0], speed[1]
    visc, scale, push_x, push_y = viscous[...], gain[...], push[0], push[1]

    def spread_of(v, north, south, east, west):
        up = jnp.where(row == size - 1, north, roll(v, -1, 0))
        down = jnp.where(row == 0, south, roll(v, 1, 0))
        right = jnp.where(col == size - 1, east, roll(v, -1, 1))
        left = jnp.where(col == 0, west, roll(v, 1, 1))
        return up + down + right + left - 4.0 * v

    for t in range(SUBCYCLES):
        cells = [strip[0] for strip, _ in strips]
        if t < SUBCYCLES - 1:
            mixed = jnp.where(col < half, roll(vx, 1, 1), roll(vy, 1 + half, 1))
            across = mixed.T[0:high]
            own = [
                jnp.where(sub < half, vx[size - 1 :], vy[size - 1 :]),
                jnp.where(sub < half, vx[0:1], vy[0:1]),
                across,
                roll(across, -1, 0),
            ]
            for q in range(4):
                strip, (beyond, before) = strips[q]
                c, y_hi, y_lo = strip[0], beyond[0][0], before[0][0]
                left = jnp.where(first, roll(y_lo, 1, 1), roll(c, 1, 1))
                right = jnp.where(last, roll(y_hi, -1, 1), roll(c, -1, 1))
                inner = jnp.where(edge, own[q], roll(c, 1, 0))
                new_strip = step(strip, left, right, inner, roll(c, -1, 0))
                if t < SUBCYCLES - 2:
                    new_sides = []
                    for i, (y, z, w) in enumerate((beyond, before)):
                        away = 1 if i == 0 else -1
                        boundary = first if i == 0 else last
                        yc, zc = y[0], z[0]
                        toward = jnp.where(boundary, roll(c, away, 1), roll(yc, away, 1))
                        inner = jnp.where(edge, zc, roll(yc, 1, 0))
                        new_y = step(y, toward, roll(yc, -away, 1), inner, roll(yc, -1, 0))
                        new_z = zc
                        if t < SUBCYCLES - 3:
                            toward = jnp.where(boundary, roll(w, away, 1), roll(zc, away, 1))
                            inner = jnp.where(edge, yc, roll(zc, 1, 0))
                            new_z = step(z, toward, roll(zc, -away, 1), inner, roll(zc, -1, 0))
                        new_sides.append((new_y, new_z))
                    for item, (new_y, new_z) in zip((beyond, before), new_sides):
                        item[0][0] = new_y
                        item[1][0] = new_z
                strip[0] = new_strip
        north, south = cells[0], cells[1]
        sides = jnp.where(edge, cells[2], roll(cells[3], 1, 0)).T
        east_x, west_x = sides[:, 0:1], sides[:, 1:2]
        east_y, west_y = sides[:, half : half + 1], sides[:, half + 1 : half + 2]
        spread_x = spread_of(vx, north[0:1], south[0:1], east_x, west_x)
        spread_y = spread_of(
            vy, north[half : half + 1], south[half : half + 1], east_y, west_y
        )
        new_x = scale * (vx + visc * spread_x + push_x + CORIOLIS_TURN * vy)
        new_y = scale * (vy + visc * spread_y + push_y - CORIOLIS_TURN * vx)
        vx, vy = new_x, new_y
    out[0] = vx
    out[1] = vy
    flat_o[pl.ds(0, size, stride=2), :] = vx
    flat_o[pl.ds(1, size, stride=2), :] = vy


def back_kernel(group, side, drag, conduct, current, speed, *refs):
    chunks = refs[:group]
    tops = refs[group : 2 * group]
    outs = refs[2 * group :]
    size = drag.shape[0]
    depth = chunks[0].shape[0] - 3 * side
    warm = remap_forward(chunks, [[t[...]] for t in tops], side, depth)
    heat = conduct[...] * warm
    fluxes = [heat.astype(BF16)]
    for c in range(2):
        fluxes.append((drag[...] * (speed[c] - current[c])).astype(BF16))
    wide = jnp.concatenate(fluxes, axis=1)
    for chunk, out in zip(chunks, outs):
        part = jnp.dot(chunk[0:side], wide, preferred_element_type=F32).astype(BF16)
        part = jnp.concatenate([part[:, c * size : (c + 1) * size] for c in range(3)], axis=0)
        reply = jnp.dot(part, chunk[side : side + depth], preferred_element_type=F32)
        out[...] = reply.astype(BF16)


def finish_kernel(warm, currents, *refs):
    replies, (heat_o, current_o) = refs[:-2], refs[-2:]
    total = replies[0][...].astype(F32)
    for reply in replies[1:]:
        total = total + reply[...].astype(F32)
    side = currents.shape[1]
    heat = THERMAL_DIFFUSE * total[0:side]
    for l in range(warm.shape[0]):
        heat_o[l] = warm[l] + heat
    for c in range(2):
        current_o[c] = currents[c] + STRESS_MIXING * total[(c + 1) * side : (c + 2) * side]


def shards(
    water_heat_state,
    diffusion_coefficient,
    upper_current_vector,
    remap_blocks,
    remap_rows,
    remap_cols,
    neighbors,
    thickness,
    concentration,
    ice_velocity,
    wind_stress,
):
    tile_count, sub_count, lev_count = (lax.axis_size(a) for a in ("tile", "sub", "lev"))
    group = sub_count * lev_count
    devices = tile_count * group
    group_axes = ("sub", "lev")
    member_axes = ("tile", "sub", "lev")
    levels, side, width = water_heat_state.shape
    pairs, size = remap_rows.shape[1:3]
    categories = thickness.shape[2]

    def place():
        return tuple(lax.axis_index(a) for a in member_axes)

    def group_place():
        return lax.axis_index("sub") * lev_count + lax.axis_index("lev")

    def device_place():
        return lax.axis_index("tile") * group + group_place()

    def swap(value, k):
        return lax.ppermute(value, group_axes, [(i, i ^ k) for i in range(group)])

    def shape(*dims, dtype=F32):
        return jax.ShapeDtypeStruct(dims, dtype)

    def interleaved(value):
        return value.reshape(2, size, size).transpose(1, 0, 2).reshape(2 * size, size)

    grid = (tile_count, sub_count, lev_count, place)
    plane = shape(size, size)
    planes = shape(2, size, size)
    wind = interleaved(wind_stress)

    chunk_rows = 3 * side + width
    sent = call(
        functools.partial(forward_kernel, (devices, group, group_place)),
        [shape(chunk_rows, width, dtype=BF16)] * group,
        (remap_blocks, remap_rows[0].swapaxes(1, 2), remap_cols[0], upper_current_vector),
        smem=(0,),
    )
    chunks = [sent[0]] + [swap(sent[k], k) for k in range(1, group)]

    side_rows = 16 * DEPTH
    message_rows = side_rows + -(-(2 * levels + 1) // TILE_ROWS) * TILE_ROWS
    message, viscous, gain, step_mass, drag, conduct, speed = call(
        functools.partial(rims_kernel, grid),
        [shape(devices, message_rows, size, dtype=BF16)] + [plane] * 5 + [planes],
        (
            neighbors,
            thickness.reshape(categories, size, size),
            concentration.reshape(categories, size, size),
            interleaved(ice_velocity),
            water_heat_state,
        ),
        scratch=[pltpu.VMEM((side_rows, size), F32)],
        smem=(0,),
    )
    rims = lax.all_to_all(message, member_axes, split_axis=0, concat_axis=0, tiled=True)

    push_message, current_ice, push = call(
        functools.partial(forcing_kernel, group, side),
        [shape(devices, 8 * DEPTH, size, dtype=BF16), planes, planes],
        (step_mass, drag, wind, *chunks),
        scratch=[pltpu.VMEM((8 * DEPTH, size), F32)],
    )
    push_rims = lax.all_to_all(push_message, member_axes, split_axis=0, concat_axis=0, tiled=True)

    warm, top = call(
        functools.partial(ocean_kernel, grid, side_rows),
        [shape(levels, side, width), shape(side, width, dtype=BF16 if lev_count == 1 else F32)],
        (water_heat_state, diffusion_coefficient, rims),
    )
    if lev_count > 1:
        top = lax.psum(top, "lev").astype(BF16)
    tops = [top] + [swap(top, k) for k in range(1, group)]

    names = rims[:, side_rows + 2 * levels, 0:8].astype(jnp.int32)
    table = names[:, 0:4] * 128 + names[:, 4:8]
    speed, flat = call(
        functools.partial(subcycles_kernel, device_place),
        [planes, shape(2 * size, size)],
        (table, viscous, gain, speed, push, rims, push_rims),
        smem=(0,),
    )

    replies = call(
        functools.partial(back_kernel, group, side),
        [shape(3 * side, width, dtype=BF16)] * group,
        (drag, conduct, current_ice, speed, *chunks, *tops),
    )
    replies = [replies[0]] + [swap(replies[k], k) for k in range(1, group)]
    if lev_count > 1:
        replies = [lax.psum(sum(r.astype(F32) for r in replies), "lev")]
    heat, current = call(
        finish_kernel,
        [shape(levels, side, width), shape(2, side, width)],
        (warm, upper_current_vector, *replies),
    )
    velocity = flat.reshape(size, 2, size).transpose(1, 0, 2).reshape(1, 1, 2, size * size)
    return heat, current, velocity


def solution(mesh):
    member = ("tile", "sub", "lev")
    whole = ("copies",) + member
    ice = P(None, whole, None, None)
    water = P("lev", ("copies", "tile"), "sub")
    current = P(None, ("copies", "tile"), "sub")
    return jax.shard_map(
        shards,
        mesh=mesh,
        in_specs=(
            water,
            P("tile", "sub"),
            current,
            P(member, None),
            P(member, None, None, None),
            P(member, None, None, None),
            P(None, member, None),
            ice,
            ice,
            ice,
            ice,
        ),
        out_specs=(water, current, ice),
        check_vma=False,
    )
```

```python
import functools

import jax
import jax.numpy as jnp
from jax import lax
from jax.experimental import pallas as pl
from jax.experimental.pallas import tpu as pltpu
from jax.sharding import PartitionSpec as P

SUBCYCLES = 4
STRENGTH_DECAY = 5.0
VISCOUS_STEP = 0.24
SUBCYCLE_STEP = 0.5
CORIOLIS_TURN = 0.1
BASE_MASS = 0.5
HEAT_RATE = 0.2
THIN_ICE = 0.1
THERMAL_DIFFUSE = 0.5
STRESS_MIXING = 0.5

OPPOSITE = (1, 0, 3, 2)
LATERAL = ((2, 3), (2, 3), (0, 1), (0, 1))
DEPTH = SUBCYCLES
SIDE_ROWS = 16 * DEPTH
PUSH_ROWS = 8 * DEPTH
NAMES_ROW = 4 * DEPTH - 1
TILE_ROWS = 16
F32 = jnp.float32
BF16 = jnp.bfloat16
VMEM_LIMIT = 16 * 1024 * 1024
FLOPS_PER_MICRO = 1.15e9


def call(kernel, outs, args, scratch=(), smem=(), hbm=(), out_space=pltpu.VMEM, grant=VMEM_LIMIT, micros=0.01):
    def space(i):
        return pltpu.SMEM if i in smem else pltpu.HBM if i in hbm else pltpu.VMEM

    specs = [pl.BlockSpec(memory_space=space(i)) for i in range(len(args))]
    size = sum(a.size * a.dtype.itemsize for a in args)
    return pl.pallas_call(
        kernel,
        out_shape=outs,
        in_specs=specs,
        out_specs=jax.tree.map(lambda _: pl.BlockSpec(memory_space=out_space), outs),
        scratch_shapes=list(scratch),
        compiler_params=pltpu.CompilerParams(vmem_limit_bytes=grant),
        cost_estimate=pl.CostEstimate(
            flops=int(micros * FLOPS_PER_MICRO), bytes_accessed=size, transcendentals=0
        ),
    )(*args)


def iota(shape, axis):
    return lax.broadcasted_iota(jnp.int32, shape, axis)


def roll(x, shift, axis):
    return pltpu.roll(x, shift % x.shape[axis], axis)


def flag(condition):
    return jnp.where(condition, 1.0, 0.0).astype(F32)


def forward_kernel(group, blocks_h, rows_h, cols_h, currents_h, *refs):
    devices, members, place = group
    outs, (blocks, currents, fields, arrived, left) = refs[:members], refs[members:]
    pairs, side, width = rows_h.shape
    depth = cols_h.shape[1]
    names = pltpu.make_async_copy(blocks_h, blocks, arrived.at[0])
    water = pltpu.make_async_copy(currents_h, currents, arrived.at[1])
    names.start()
    water.start()
    names.wait()
    me = place()
    owners = [lax.rem(lax.rem(blocks[0, m], devices), members) for m in range(pairs)]
    copies = []
    for k, out in enumerate(outs):
        partner = me ^ k
        pair, found = jnp.int32(0), jnp.int32(0)
        for m in range(pairs):
            pair = jnp.where(owners[m] == partner, m, pair)
            found = jnp.where(owners[m] == partner, 1, found)
        copies.append(
            pltpu.make_async_copy(rows_h.at[pair], out.at[pl.ds(0, side)], left.at[3 * k])
        )
        copies.append(
            pltpu.make_async_copy(cols_h.at[pair], out.at[pl.ds(side, depth)], left.at[3 * k + 1])
        )
        if pairs < members:
            keep = jnp.where(found > 0, 1.0, 0.0).astype(F32)
        else:
            keep = None
        copies[-2].start()
        copies[-1].start()
        if k == 0:
            water.wait()
        if k == 0 or keep is not None:
            for c in range(2):
                field = currents[c] if keep is None else currents[c] * keep
                fields[0 if keep is None else k, c * side : (c + 1) * side] = field.astype(BF16)
        copies.append(
            pltpu.make_async_copy(
                fields.at[0 if keep is None else k],
                out.at[pl.ds(side + depth, 2 * side)],
                left.at[3 * k + 2],
            )
        )
        copies[-1].start()
    for copy in copies:
        copy.wait()


def put_side_rims(store, planes, at):
    size = planes[0].shape[0]
    lane = iota((size, size), 1)
    mixed = jnp.zeros((size, size), F32)
    for i, plane in enumerate(planes):
        turned = roll(plane, DEPTH + 2 * DEPTH * i, 1)
        mixed = jnp.where(lane // (2 * DEPTH) == i, turned, mixed)
    across = mixed.T
    for i, plane in enumerate(planes):
        for k in range(DEPTH):
            base = i * DEPTH + k
            store[at(0) + base : at(0) + base + 1] = plane[size - 1 - k : size - k]
            store[at(1) + base : at(1) + base + 1] = plane[k : k + 1]
            east = 2 * DEPTH * i + DEPTH - 1 - k
            west = 2 * DEPTH * i + DEPTH + k
            store[at(2) + base : at(2) + base + 1] = across[east : east + 1]
            store[at(3) + base : at(3) + base + 1] = across[west : west + 1]


def rims_kernel(
    links, thick, conc, ice, water, out, cols_o, viscous_o, gain_o, mass_o, drag_o, conduct_o,
    speed_o, store,
):
    size = thick.shape[1]
    cover = jnp.zeros((size, size), F32)
    volume = jnp.zeros((size, size), F32)
    conduct = jnp.zeros((size, size), F32)
    for c in range(thick.shape[0]):
        h, a = thick[c], conc[c]
        cover = cover + a
        volume = volume + a * h
        conduct = conduct + a / (h + THIN_ICE)
    mass = volume + BASE_MASS
    viscous = VISCOUS_STEP * (volume * jnp.exp(-STRENGTH_DECAY * (1.0 - cover))) / mass
    step_mass = SUBCYCLE_STEP / mass
    gain = 1.0 / (1.0 + step_mass * cover)
    speed_x = ice[pl.ds(0, size, stride=2), :]
    speed_y = ice[pl.ds(1, size, stride=2), :]
    viscous_o[...] = viscous
    gain_o[...] = gain
    mass_o[...] = step_mass
    drag_o[...] = cover
    conduct_o[...] = -HEAT_RATE * conduct
    speed_o[0] = speed_x
    speed_o[1] = speed_y
    put_side_rims(store, [speed_x, speed_y, viscous, gain], lambda side: side * 4 * DEPTH)
    line = iota((1, size), 1)
    names = jnp.zeros((1, size), F32)
    for q in range(4):
        names = jnp.where(line == q, (links[0, 0, q] >> 7).astype(F32), names)
        names = jnp.where(line == 4 + q, (links[0, 0, q] & 127).astype(F32), names)
    store[NAMES_ROW : NAMES_ROW + 1] = names
    levels, rows, width = water.shape
    start = SIDE_ROWS
    for l in range(levels):
        for j in range(2):
            at = start + 2 * l + j
            store[at : at + 1] = water[l, rows - 1 - j : rows - j]
            store[at + 2 * levels : at + 2 * levels + 1] = water[l, j : j + 1]
    out[...] = store[...].astype(BF16)
    lane = iota((rows, width), 1)
    mixed = jnp.zeros((rows, width), F32)
    for l in range(levels):
        mixed = jnp.where(lane // 4 == l, roll(water[l], 2 + 4 * l, 1), mixed)
    across = jnp.concatenate([mixed, jnp.zeros((width - rows, width), F32)], axis=0).T
    beside = []
    for l in range(levels):
        for j in range(2):
            last = across[4 * l + 1 - j : 4 * l + 2 - j]
            lead = across[4 * l + 2 + j : 4 * l + 3 + j]
            beside.append(jnp.where(line < rows, last, roll(lead, rows, 1)))
    cols_o[...] = jnp.concatenate(beside, axis=0)


def relay_kernel(tiles, place, cols, *refs):
    messages, out = refs[:tiles], refs[tiles]
    for k, message in enumerate(messages):
        out[k * SIDE_ROWS : (k + 1) * SIDE_ROWS] = message[0:SIDE_ROWS]
    levels = cols.shape[0] // 2
    before, after = around(place(), tiles, messages, levels)
    rows = []
    for strip in (before, after):
        rows += [strip[2 * l : 2 * l + 1] for l in range(levels)]
    out[tiles * SIDE_ROWS :] = jnp.concatenate([cols[...]] + rows, axis=0).astype(BF16)


def around(me, tiles, messages, levels):
    before, after = 0.0, 0.0
    for k in range(1, tiles):
        strips = messages[k][SIDE_ROWS : SIDE_ROWS + 4 * levels].astype(F32)
        before = before + strips[: 2 * levels] * flag((me > 0) & ((me ^ k) == me - 1))
        after = after + strips[2 * levels :] * flag((me < tiles - 1) & ((me ^ k) == me + 1))
    return before, after


def remap_forward(chunks, field_rows, side, depth):
    total = None
    for chunk, fields in zip(chunks, field_rows):
        down = chunk[0:side]
        right = chunk[side : side + depth]
        wide = jnp.concatenate(fields, axis=1) if len(fields) > 1 else fields[0]
        part = lax.dot_general(down, wide, (((0,), (0,)), ((), ())), preferred_element_type=F32)
        part = part.astype(BF16)
        width = fields[0].shape[1]
        if len(fields) > 1:
            part = jnp.concatenate(
                [part[:, c * width : (c + 1) * width] for c in range(len(fields))], axis=0
            )
        piece = lax.dot_general(part, right, (((1,), (1,)), ((), ())), preferred_element_type=F32)
        piece = piece.astype(BF16).astype(F32)
        total = piece if total is None else total + piece
    return total


def forcing_kernel(group, side, mass, drag, wind, *refs):
    chunks = refs[:group]
    out, current_o, push_o, store = refs[group:]
    size = mass.shape[0]
    depth = chunks[0].shape[0] - 3 * side
    fields = [
        [c[side + depth : 2 * side + depth], c[2 * side + depth : 3 * side + depth]] for c in chunks
    ]
    total = remap_forward(chunks, fields, side, depth)
    pushes = []
    for c in range(2):
        current = total[c * size : (c + 1) * size]
        current_o[c] = current
        force = wind[pl.ds(c, size, stride=2), :]
        push = mass[...] * (force + drag[...] * current)
        push_o[c] = push
        pushes.append(push)
    put_side_rims(store, pushes, lambda q: q * 2 * DEPTH)
    out[...] = store[...].astype(BF16)


def ocean_kernel(counts, tile_place, member_place, water, mixing, *refs):
    tiles, subs, levs = counts
    members = subs * levs
    messages, relays = refs[:tiles], refs[tiles : tiles + members]
    warm_o, top_o, table_o = refs[tiles + members :]
    levels, rows, width = water.shape
    my_tile, me = tile_place(), member_place()
    halo = {}
    halo[-1, 0], halo[1, 0] = around(my_tile, tiles, messages, levels)
    for ds in (-1, 1):
        beyond = me + ds * levs
        inside = (beyond >= 0) & (beyond < members)
        found = 0.0
        for k in range(1, members):
            strip = relays[k][tiles * SIDE_ROWS : tiles * SIDE_ROWS + 4 * levels].astype(F32)
            found = found + strip * flag(inside & ((me ^ k) == beyond))
        beside, corners = found[: 2 * levels], found[2 * levels :]
        if ds > 0:
            beside = roll(beside, -rows, 1)
        halo[0, ds] = beside
        at = width - 1 if ds < 0 else 0
        halo[-1, ds] = corners[:levels, at : at + 1]
        halo[1, ds] = corners[levels:, at : at + 1]
    mine = my_tile * members + me
    column = iota((table_o.shape[0], width), 1)
    names = []
    for k in range(tiles):
        for m in range(members):
            at = k * SIDE_ROWS
            names.append(relays[m][at : at + TILE_ROWS].astype(F32)[NAMES_ROW : NAMES_ROW + 1])
    names = jnp.concatenate(names, axis=0)
    table = (128.0 * names + roll(names, -4, 1)).astype(jnp.int32)
    table_o[...] = jnp.where((table >= 0) & (column < 4), table ^ mine, -1)
    left_cols = halo[0, -1].T
    right_cols = halo[0, 1].T
    row = iota((rows, width), 0)
    lane = iota((rows, width), 1)
    line = iota((1, width), 1)
    total = None

    def laplacian(x, top, bottom, left, right):
        up = jnp.where(row == 0, top, roll(x, 1, 0))
        down = jnp.where(row == rows - 1, bottom, roll(x, -1, 0))
        west = jnp.where(lane == 0, left, roll(x, 1, 1))
        east = jnp.where(lane == width - 1, right, roll(x, -1, 1))
        return up + down + west + east - 4.0 * x

    for l in range(levels):
        x = water[l]
        near, far = 2 * l, 2 * l + 1
        top, top_far = halo[-1, 0][near : near + 1], halo[-1, 0][far : far + 1]
        bottom, bottom_far = halo[1, 0][near : near + 1], halo[1, 0][far : far + 1]
        left, left_far = left_cols[0:rows, near : near + 1], left_cols[0:rows, far : far + 1]
        right, right_far = right_cols[0:rows, near : near + 1], right_cols[0:rows, far : far + 1]
        corner = {}
        for dt in (-1, 1):
            for ds in (-1, 1):
                corner[dt, ds] = halo[dt, ds][l : l + 1]

        def ring_row(mid, out_row, in_row, dt):
            west = jnp.where(line == 0, corner[dt, -1], roll(mid, 1, 1))
            east = jnp.where(line == width - 1, corner[dt, 1], roll(mid, -1, 1))
            return west + east + out_row + in_row - 4.0 * mid

        def ring_col(mid, out_col, in_col, ds):
            up = jnp.concatenate([corner[-1, ds], mid[:-1]], axis=0)
            down = jnp.concatenate([mid[1:], corner[1, ds]], axis=0)
            return up + down + out_col + in_col - 4.0 * mid

        once = laplacian(x, top, bottom, left, right)
        twice = laplacian(
            once,
            ring_row(top, top_far, x[0:1], -1),
            ring_row(bottom, bottom_far, x[rows - 1 :], 1),
            ring_col(left, left_far, x[:, 0:1], -1),
            ring_col(right, right_far, x[:, width - 1 :], 1),
        )
        warm = x - mixing[...] * twice
        warm_o[l] = warm
        total = warm if total is None else total + warm
    top_o[...] = (total / (levels * levs)).astype(top_o.dtype)


def subcycles_kernel(tiles, members, table, viscous, gain, speed, push, *refs):
    relays, push_relays = refs[:members], refs[members : 2 * members]
    out, rims, push_rims = refs[2 * members :]
    size = viscous.shape[0]
    for k in range(tiles):
        for m in range(members):
            rims[k * members + m] = relays[m][k * SIDE_ROWS : (k + 1) * SIDE_ROWS]
            push_rims[k * members + m] = push_relays[m][k * PUSH_ROWS : (k + 1) * PUSH_ROWS]
    half = DEPTH
    high = 2 * DEPTH
    sub = iota((high, size), 0)
    lane = iota((high, size), 1)
    edge = (sub & (half - 1)) == 0
    turn = jnp.where(sub < half, CORIOLIS_TURN, -CORIOLIS_TURN).astype(F32)
    first, last = lane == 0, lane == size - 1

    def load(device, side, mask, with_push=True):
        block = rims[device, side * 2 * high : (side + 1) * 2 * high].astype(F32)
        velocity, both = block[:high] * mask, block[high:]
        if not with_push:
            return velocity
        other = roll(both, half, 0)
        visc = jnp.where(sub < half, both, other)
        scale = jnp.where(sub < half, other, both) * mask
        start = side // 2 * 2 * high
        pushed = push_rims[device, start : start + 2 * high].astype(F32)
        pushed = pushed[:high] if side % 2 == 0 else pushed[high:]
        return [velocity, visc, scale, pushed]

    def follow(device, side):
        name = table[device, side]
        return jnp.where(name >= 0, name, 0), name >= 0

    def step(state, left, right, inner, outer):
        c, visc, scale, pushed = state
        spread = left + right + inner + outer - 4.0 * c
        return scale * (c + visc * spread + pushed + turn * roll(c, half, 0))

    strips = []
    for q in range(4):
        x, has_x = follow(0, q)
        strip = load(x, OPPOSITE[q], flag(has_x))
        sides = []
        for s in LATERAL[q]:
            y, has_y = follow(x, s)
            z, has_z = follow(y, OPPOSITE[q])
            w, has_w = follow(z, OPPOSITE[s])
            sides.append(
                [
                    load(y, OPPOSITE[q], flag(has_y)),
                    load(z, q, flag(has_z)),
                    load(w, q, flag(has_w), with_push=False),
                ]
            )
        strips.append((strip, sides))

    row = iota((size, size), 0)
    col = iota((size, size), 1)
    vx, vy = speed[0], speed[1]
    visc, scale, push_x, push_y = viscous[...], gain[...], push[0], push[1]

    def spread_of(v, north, south, east, west):
        up = jnp.where(row == size - 1, north, roll(v, -1, 0))
        down = jnp.where(row == 0, south, roll(v, 1, 0))
        right = jnp.where(col == size - 1, east, roll(v, -1, 1))
        left = jnp.where(col == 0, west, roll(v, 1, 1))
        return up + down + right + left - 4.0 * v

    for t in range(SUBCYCLES):
        cells = [strip[0] for strip, _ in strips]
        if t < SUBCYCLES - 1:
            mixed = jnp.where(col < half, roll(vx, 1, 1), roll(vy, 1 + half, 1))
            across = mixed.T[0:high]
            own = [
                jnp.where(sub < half, vx[size - 1 :], vy[size - 1 :]),
                jnp.where(sub < half, vx[0:1], vy[0:1]),
                across,
                roll(across, -1, 0),
            ]
            for q in range(4):
                strip, (beyond, before) = strips[q]
                c, y_hi, y_lo = strip[0], beyond[0][0], before[0][0]
                left = jnp.where(first, roll(y_lo, 1, 1), roll(c, 1, 1))
                right = jnp.where(last, roll(y_hi, -1, 1), roll(c, -1, 1))
                inner = jnp.where(edge, own[q], roll(c, 1, 0))
                new_strip = step(strip, left, right, inner, roll(c, -1, 0))
                if t < SUBCYCLES - 2:
                    new_sides = []
                    for i, (y, z, w) in enumerate((beyond, before)):
                        away = 1 if i == 0 else -1
                        boundary = first if i == 0 else last
                        yc, zc = y[0], z[0]
                        toward = jnp.where(boundary, roll(c, away, 1), roll(yc, away, 1))
                        inner = jnp.where(edge, zc, roll(yc, 1, 0))
                        new_y = step(y, toward, roll(yc, -away, 1), inner, roll(yc, -1, 0))
                        new_z = zc
                        if t < SUBCYCLES - 3:
                            toward = jnp.where(boundary, roll(w, away, 1), roll(zc, away, 1))
                            inner = jnp.where(edge, yc, roll(zc, 1, 0))
                            new_z = step(z, toward, roll(zc, -away, 1), inner, roll(zc, -1, 0))
                        new_sides.append((new_y, new_z))
                    for item, (new_y, new_z) in zip((beyond, before), new_sides):
                        item[0][0] = new_y
                        item[1][0] = new_z
                strip[0] = new_strip
        north, south = cells[0], cells[1]
        sides = jnp.where(edge, cells[2], roll(cells[3], 1, 0)).T
        east_x, west_x = sides[:, 0:1], sides[:, 1:2]
        east_y, west_y = sides[:, half : half + 1], sides[:, half + 1 : half + 2]
        spread_x = spread_of(vx, north[0:1], south[0:1], east_x, west_x)
        spread_y = spread_of(
            vy, north[half : half + 1], south[half : half + 1], east_y, west_y
        )
        new_x = scale * (vx + visc * spread_x + push_x + CORIOLIS_TURN * vy)
        new_y = scale * (vy + visc * spread_y + push_y - CORIOLIS_TURN * vx)
        vx, vy = new_x, new_y
    out[0] = vx
    out[1] = vy


def back_kernel(group, side, drag, conduct, current, speed, *refs):
    chunks = refs[:group]
    tops = refs[group : 2 * group]
    outs = refs[2 * group :]
    size = drag.shape[0]
    depth = chunks[0].shape[0] - 3 * side
    warm = remap_forward(chunks, [[t[...]] for t in tops], side, depth)
    heat = conduct[...] * warm
    fluxes = [heat.astype(BF16)]
    for c in range(2):
        fluxes.append((drag[...] * (speed[c] - current[c])).astype(BF16))
    wide = jnp.concatenate(fluxes, axis=1)
    for chunk, out in zip(chunks, outs):
        part = jnp.dot(chunk[0:side], wide, preferred_element_type=F32).astype(BF16)
        part = jnp.concatenate([part[:, c * size : (c + 1) * size] for c in range(3)], axis=0)
        reply = jnp.dot(part, chunk[side : side + depth], preferred_element_type=F32)
        out[...] = reply.astype(BF16)


def finish_kernel(warm, currents, speed, *refs):
    outs, (flat, heat_v, current_v, left) = refs[-7:-4], refs[-4:]
    replies = refs[:-7]
    flat_o, heat_o, current_o = outs
    size = speed.shape[1]
    copies = [
        pltpu.make_async_copy(source, target, left.at[i])
        for i, (source, target) in enumerate(
            ((flat, flat_o), (heat_v, heat_o), (current_v, current_o))
        )
    ]
    for c in range(2):
        flat[pl.ds(c, size, stride=2), :] = speed[c]
    copies[0].start()
    total = replies[0][...].astype(F32)
    for reply in replies[1:]:
        total = total + reply[...].astype(F32)
    side = currents.shape[1]
    heat = THERMAL_DIFFUSE * total[0:side]
    for l in range(warm.shape[0]):
        heat_v[l] = warm[l] + heat
    copies[1].start()
    for c in range(2):
        current_v[c] = currents[c] + STRESS_MIXING * total[(c + 1) * side : (c + 2) * side]
    copies[2].start()
    for copy in copies:
        copy.wait()


def shards(
    water_heat_state,
    diffusion_coefficient,
    upper_current_vector,
    remap_blocks,
    remap_rows,
    remap_cols,
    neighbors,
    thickness,
    concentration,
    ice_velocity,
    wind_stress,
):
    tile_count, sub_count, lev_count = (lax.axis_size(a) for a in ("tile", "sub", "lev"))
    group = sub_count * lev_count
    devices = tile_count * group
    group_axes = ("sub", "lev")
    member_axes = ("tile", "sub", "lev")
    levels, side, width = water_heat_state.shape
    pairs, size = remap_rows.shape[1:3]
    categories = thickness.shape[2]

    def tile_place():
        return lax.axis_index("tile")

    def member_place():
        return lax.axis_index("sub") * lev_count + lax.axis_index("lev")

    def swap(value, axes, count):
        return [value] + [
            lax.ppermute(value, axes, [(i, i ^ k) for i in range(count)]) for k in range(1, count)
        ]

    def swap_each(values):
        return [values[0]] + [
            lax.ppermute(values[k], group_axes, [(i, i ^ k) for i in range(group)])
            for k in range(1, group)
        ]

    def shape(*dims, dtype=F32):
        return jax.ShapeDtypeStruct(dims, dtype)

    def interleaved(value):
        return value.reshape(2, size, size).transpose(1, 0, 2).reshape(2 * size, size)

    plane = shape(size, size)
    planes = shape(2, size, size)
    wind = interleaved(wind_stress)

    chunk_rows = 3 * side + width
    sent = call(
        functools.partial(forward_kernel, (devices, group, member_place)),
        [shape(chunk_rows, width, dtype=BF16)] * group,
        (remap_blocks, remap_rows[0].swapaxes(1, 2), remap_cols[0], upper_current_vector),
        scratch=[
            pltpu.SMEM((1, pairs), jnp.int32),
            pltpu.VMEM((2, side, width), F32),
            pltpu.VMEM((1 if pairs == group else group, 2 * side, width), BF16),
            pltpu.SemaphoreType.DMA((2,)),
            pltpu.SemaphoreType.DMA((3 * group,)),
        ],
        hbm=(0, 1, 2, 3),
        grant=60 * 2**20,
        micros=2,
    )
    chunks = swap_each(sent)

    links, sent = lax.optimization_barrier((neighbors, sent))
    message, cols, viscous, gain, step_mass, drag, conduct, speed = call(
        rims_kernel,
        [shape(SIDE_ROWS + 4 * levels, size, dtype=BF16), shape(2 * levels, width)]
        + [plane] * 5
        + [planes],
        (
            links,
            thickness.reshape(categories, size, size),
            concentration.reshape(categories, size, size),
            interleaved(ice_velocity),
            water_heat_state,
        ),
        scratch=[pltpu.VMEM((SIDE_ROWS + 4 * levels, size), F32)],
        smem=(0,),
    )
    messages = swap(message, "tile", tile_count)

    push_message, current_ice, push = call(
        functools.partial(forcing_kernel, group, side),
        [shape(PUSH_ROWS, size, dtype=BF16), planes, planes],
        (step_mass, drag, wind, *chunks),
        scratch=[pltpu.VMEM((PUSH_ROWS, size), F32)],
    )
    cols, push_message = lax.optimization_barrier((cols, push_message))
    push_messages = swap(push_message, "tile", tile_count)

    relay = call(
        functools.partial(relay_kernel, tile_count, tile_place),
        shape(tile_count * SIDE_ROWS + 4 * levels, size, dtype=BF16),
        (cols, *messages),
    )
    relays = swap(relay, group_axes, group)
    push_relays = swap(jnp.concatenate(push_messages, axis=0), group_axes, group)

    warm, top, table = call(
        functools.partial(
            ocean_kernel, (tile_count, sub_count, lev_count), tile_place, member_place
        ),
        [
            shape(levels, side, width),
            shape(side, width, dtype=BF16 if lev_count == 1 else F32),
            shape(devices, width, dtype=jnp.int32),
        ],
        (water_heat_state, diffusion_coefficient, *messages, *relays),
    )
    if lev_count > 1:
        top = lax.psum(top, "lev").astype(BF16)
    tops = swap(top, group_axes, group)

    speed = call(
        functools.partial(subcycles_kernel, tile_count, group),
        planes,
        (table, viscous, gain, speed, push, *relays, *push_relays),
        scratch=[
            pltpu.VMEM((devices, SIDE_ROWS, size), BF16),
            pltpu.VMEM((devices, PUSH_ROWS, size), BF16),
        ],
        smem=(0,),
    )

    replies = call(
        functools.partial(back_kernel, group, side),
        [shape(3 * side, width, dtype=BF16)] * group,
        (drag, conduct, current_ice, speed, *chunks, *tops),
    )
    replies = swap_each(replies)
    if lev_count > 1:
        replies = [lax.psum(sum(r.astype(F32) for r in replies), "lev")]
    flat, heat, current = call(
        finish_kernel,
        [shape(2 * size, size), shape(levels, side, width), shape(2, side, width)],
        (warm, upper_current_vector, speed, *replies),
        scratch=[
            pltpu.VMEM((2 * size, size), F32),
            pltpu.VMEM((levels, side, width), F32),
            pltpu.VMEM((2, side, width), F32),
            pltpu.SemaphoreType.DMA((3,)),
        ],
        out_space=pltpu.HBM,
    )
    velocity = flat.reshape(size, 2, size).transpose(1, 0, 2).reshape(1, 1, 2, size * size)
    return heat, current, velocity


def solution(mesh):
    member = ("tile", "sub", "lev")
    whole = ("copies",) + member
    ice = P(None, whole, None, None)
    water = P("lev", ("copies", "tile"), "sub")
    current = P(None, ("copies", "tile"), "sub")
    return jax.shard_map(
        shards,
        mesh=mesh,
        in_specs=(
            water,
            P("tile", "sub"),
            current,
            P(member, None),
            P(member, None, None, None),
            P(member, None, None, None),
            P(None, member, None),
            ice,
            ice,
            ice,
            ice,
        ),
        out_specs=(water, current, ice),
        check_vma=False,
    )
```

```python
import functools

import jax
import jax.numpy as jnp
from jax import lax
from jax.experimental import pallas as pl
from jax.experimental.pallas import tpu as pltpu
from jax.sharding import PartitionSpec as P

SUBCYCLES = 4
STRENGTH_DECAY = 5.0
VISCOUS_STEP = 0.24
SUBCYCLE_STEP = 0.5
CORIOLIS_TURN = 0.1
BASE_MASS = 0.5
HEAT_RATE = 0.2
THIN_ICE = 0.1
THERMAL_DIFFUSE = 0.5
STRESS_MIXING = 0.5

OPPOSITE = (1, 0, 3, 2)
LATERAL = ((2, 3), (2, 3), (0, 1), (0, 1))
DEPTH = SUBCYCLES
SIDE_ROWS = 16 * DEPTH
PUSH_ROWS = 8 * DEPTH
TILE_ROWS = 16
F32 = jnp.float32
BF16 = jnp.bfloat16
VMEM_LIMIT = 16 * 1024 * 1024
FLOPS_PER_MICRO = 1.15e9


def call(kernel, outs, args, scratch=(), smem=(), hbm=(), out_space=pltpu.VMEM, grant=VMEM_LIMIT, micros=0.01):
    def space(i):
        return pltpu.SMEM if i in smem else pltpu.HBM if i in hbm else pltpu.VMEM

    specs = [pl.BlockSpec(memory_space=space(i)) for i in range(len(args))]
    size = sum(a.size * a.dtype.itemsize for a in args)
    return pl.pallas_call(
        kernel,
        out_shape=outs,
        in_specs=specs,
        out_specs=jax.tree.map(lambda _: pl.BlockSpec(memory_space=out_space), outs),
        scratch_shapes=list(scratch),
        compiler_params=pltpu.CompilerParams(vmem_limit_bytes=grant),
        cost_estimate=pl.CostEstimate(
            flops=int(micros * FLOPS_PER_MICRO), bytes_accessed=size, transcendentals=0
        ),
    )(*args)


def iota(shape, axis):
    return lax.broadcasted_iota(jnp.int32, shape, axis)


def roll(x, shift, axis):
    return pltpu.roll(x, shift % x.shape[axis], axis)


def flag(condition):
    return jnp.where(condition, 1.0, 0.0).astype(F32)


def forward_kernel(group, blocks_h, rows_h, cols_h, currents_h, *refs):
    devices, members, place = group
    outs, (blocks, currents, rows, cols, fields, arrived, left) = refs[:members], refs[members:]
    pairs, side, width = rows_h.shape
    depth = cols_h.shape[1]
    loads = [
        pltpu.make_async_copy(source, target, arrived.at[i])
        for i, (source, target) in enumerate(
            ((blocks_h, blocks), (currents_h, currents), (rows_h, rows), (cols_h, cols))
        )
    ]
    for load in loads:
        load.start()
    for load in loads:
        load.wait()
    me = place()
    owners = [lax.rem(lax.rem(blocks[0, m], devices), members) for m in range(pairs)]
    copies = []
    for k, out in enumerate(outs):
        partner = me ^ k
        pair, found = jnp.int32(0), jnp.int32(0)
        for m in range(pairs):
            pair = jnp.where(owners[m] == partner, m, pair)
            found = jnp.where(owners[m] == partner, 1, found)
        copies.append(
            pltpu.make_async_copy(rows.at[pair], out.at[pl.ds(0, side)], left.at[3 * k])
        )
        copies.append(
            pltpu.make_async_copy(cols.at[pair], out.at[pl.ds(side, depth)], left.at[3 * k + 1])
        )
        if pairs < members:
            keep = jnp.where(found > 0, 1.0, 0.0).astype(F32)
        else:
            keep = None
        copies[-2].start()
        copies[-1].start()
        if k == 0 or keep is not None:
            for c in range(2):
                field = currents[c] if keep is None else currents[c] * keep
                fields[0 if keep is None else k, c * side : (c + 1) * side] = field.astype(BF16)
        copies.append(
            pltpu.make_async_copy(
                fields.at[0 if keep is None else k],
                out.at[pl.ds(side + depth, 2 * side)],
                left.at[3 * k + 2],
            )
        )
        copies[-1].start()
    for copy in copies:
        copy.wait()


def put_side_rims(store, planes, at):
    size = planes[0].shape[0]
    lane = iota((size, size), 1)
    mixed = jnp.zeros((size, size), F32)
    for i, plane in enumerate(planes):
        turned = roll(plane, DEPTH + 2 * DEPTH * i, 1)
        mixed = jnp.where(lane // (2 * DEPTH) == i, turned, mixed)
    across = mixed.T
    for i, plane in enumerate(planes):
        for k in range(DEPTH):
            base = i * DEPTH + k
            store[at(0) + base : at(0) + base + 1] = plane[size - 1 - k : size - k]
            store[at(1) + base : at(1) + base + 1] = plane[k : k + 1]
            east = 2 * DEPTH * i + DEPTH - 1 - k
            west = 2 * DEPTH * i + DEPTH + k
            store[at(2) + base : at(2) + base + 1] = across[east : east + 1]
            store[at(3) + base : at(3) + base + 1] = across[west : west + 1]


def rims_kernel(
    where_am_i, links, thick, conc, ice, water, out, viscous_o, gain_o, mass_o, drag_o, conduct_o,
    speed_o, store,
):
    tile_count, sub_count, lev_count, place = where_am_i
    my_tile, my_sub, my_lev = place()
    size = thick.shape[1]
    cover = jnp.zeros((size, size), F32)
    volume = jnp.zeros((size, size), F32)
    conduct = jnp.zeros((size, size), F32)
    for c in range(thick.shape[0]):
        h, a = thick[c], conc[c]
        cover = cover + a
        volume = volume + a * h
        conduct = conduct + a / (h + THIN_ICE)
    mass = volume + BASE_MASS
    viscous = VISCOUS_STEP * (volume * jnp.exp(-STRENGTH_DECAY * (1.0 - cover))) / mass
    step_mass = SUBCYCLE_STEP / mass
    gain = 1.0 / (1.0 + step_mass * cover)
    speed_x = ice[pl.ds(0, size, stride=2), :]
    speed_y = ice[pl.ds(1, size, stride=2), :]
    viscous_o[...] = viscous
    gain_o[...] = gain
    mass_o[...] = step_mass
    drag_o[...] = cover
    conduct_o[...] = -HEAT_RATE * conduct
    speed_o[0] = speed_x
    speed_o[1] = speed_y
    side_rows = SIDE_ROWS
    put_side_rims(store, [speed_x, speed_y, viscous, gain], lambda side: side * 4 * DEPTH)
    rim_rows = store[0:side_rows].astype(BF16)
    for d in range(out.shape[0]):
        out[d, 0:side_rows] = rim_rows
    levels, rows, width = water.shape
    lane = iota((rows, width), 1)
    mixed = jnp.zeros((rows, width), F32)
    for l in range(levels):
        mixed = jnp.where(lane // 4 == l, roll(water[l], 2 + 4 * l, 1), mixed)
    across = jnp.concatenate([mixed, jnp.zeros((width - rows, width), F32)], axis=0).T
    row_lane = iota((1, width), 1)
    names = jnp.zeros((1, width), F32)
    for q in range(4):
        high = links[0, 0, q] >> 7
        low = links[0, 0, q] & 127
        names = jnp.where(row_lane == q, high.astype(F32), names)
        names = jnp.where(row_lane == 4 + q, low.astype(F32), names)
    spare = out.shape[1] - side_rows
    blank = jnp.concatenate(
        [jnp.zeros((2 * levels, width), F32), names, jnp.zeros((spare - 2 * levels - 1, width), F32)]
    )
    empty = blank.astype(BF16)
    for d in range(out.shape[0]):
        out[d, side_rows:] = empty
    tail = blank[2 * levels :]
    for dt in (-1, 0, 1):
        for ds in (-1, 0, 1):
            if dt == 0 and ds == 0:
                continue
            strip = []
            for l in range(levels):
                for j in range(2):
                    r = rows - 1 - j if dt > 0 else j
                    if ds == 0:
                        strip.append(water[l, r : r + 1])
                    elif dt == 0:
                        at = 4 * l + (1 - j if ds > 0 else 2 + j)
                        strip.append(across[at : at + 1])
                    else:
                        line = water[l, r : r + 1]
                        strip.append(roll(line, 1, 1) if ds > 0 else line)
            message = jnp.concatenate(strip + [tail], axis=0).astype(BF16)
            to_tile, to_sub = my_tile + dt, my_sub + ds
            inside = (to_tile >= 0) & (to_tile < tile_count) & (to_sub >= 0) & (to_sub < sub_count)

            @pl.when(inside)
            def _():
                out[(to_tile * sub_count + to_sub) * lev_count + my_lev, side_rows:] = message


def remap_forward(chunks, field_rows, side, depth):
    total = None
    for chunk, fields in zip(chunks, field_rows):
        down = chunk[0:side]
        right = chunk[side : side + depth]
        wide = jnp.concatenate(fields, axis=1) if len(fields) > 1 else fields[0]
        part = lax.dot_general(down, wide, (((0,), (0,)), ((), ())), preferred_element_type=F32)
        part = part.astype(BF16)
        width = fields[0].shape[1]
        if len(fields) > 1:
            part = jnp.concatenate(
                [part[:, c * width : (c + 1) * width] for c in range(len(fields))], axis=0
            )
        piece = lax.dot_general(part, right, (((1,), (1,)), ((), ())), preferred_element_type=F32)
        piece = piece.astype(BF16).astype(F32)
        total = piece if total is None else total + piece
    return total


def forcing_kernel(group, side, mass, drag, wind, *refs):
    chunks = refs[:group]
    out, current_o, push_o, store = refs[group:]
    size = mass.shape[0]
    depth = chunks[0].shape[0] - 3 * side
    fields = [
        [c[side + depth : 2 * side + depth], c[2 * side + depth : 3 * side + depth]] for c in chunks
    ]
    total = remap_forward(chunks, fields, side, depth)
    pushes = []
    for c in range(2):
        current = total[c * size : (c + 1) * size]
        current_o[c] = current
        force = wind[pl.ds(c, size, stride=2), :]
        push = mass[...] * (force + drag[...] * current)
        push_o[c] = push
        pushes.append(push)
    put_side_rims(store, pushes, lambda q: q * 2 * DEPTH)
    out[...] = store[...].astype(BF16)


def ocean_kernel(where_am_i, strip_at, water, mixing, rims, warm_o, top_o):
    tile_count, sub_count, lev_count, place = where_am_i
    my_tile, my_sub, my_lev = place()
    levels, rows, width = water.shape
    halo = {}
    for dt in (-1, 0, 1):
        for ds in (-1, 0, 1):
            if dt == 0 and ds == 0:
                continue
            t, s = my_tile + dt, my_sub + ds
            inside = (t >= 0) & (t < tile_count) & (s >= 0) & (s < sub_count)
            device = jnp.where(inside, (t * sub_count + s) * lev_count + my_lev, 0)
            strip = rims[device, strip_at : strip_at + TILE_ROWS].astype(F32)[: 2 * levels]
            halo[dt, ds] = strip * flag(inside)
    left_cols = halo[0, -1].T
    right_cols = halo[0, 1].T
    row = iota((rows, width), 0)
    lane = iota((rows, width), 1)
    line = iota((1, width), 1)
    total = None

    def laplacian(x, top, bottom, left, right):
        up = jnp.where(row == 0, top, roll(x, 1, 0))
        down = jnp.where(row == rows - 1, bottom, roll(x, -1, 0))
        west = jnp.where(lane == 0, left, roll(x, 1, 1))
        east = jnp.where(lane == width - 1, right, roll(x, -1, 1))
        return up + down + west + east - 4.0 * x

    for l in range(levels):
        x = water[l]
        near, far = 2 * l, 2 * l + 1
        top, top_far = halo[-1, 0][near : near + 1], halo[-1, 0][far : far + 1]
        bottom, bottom_far = halo[1, 0][near : near + 1], halo[1, 0][far : far + 1]
        left, left_far = left_cols[0:rows, near : near + 1], left_cols[0:rows, far : far + 1]
        right, right_far = right_cols[0:rows, near : near + 1], right_cols[0:rows, far : far + 1]
        corner = {}
        for dt in (-1, 1):
            for ds in (-1, 1):
                corner[dt, ds] = halo[dt, ds][near : near + 1, 0:1]

        def ring_row(mid, out_row, in_row, dt):
            west = jnp.where(line == 0, corner[dt, -1], roll(mid, 1, 1))
            east = jnp.where(line == width - 1, corner[dt, 1], roll(mid, -1, 1))
            return west + east + out_row + in_row - 4.0 * mid

        def ring_col(mid, out_col, in_col, ds):
            up = jnp.concatenate([corner[-1, ds], mid[:-1]], axis=0)
            down = jnp.concatenate([mid[1:], corner[1, ds]], axis=0)
            return up + down + out_col + in_col - 4.0 * mid

        once = laplacian(x, top, bottom, left, right)
        twice = laplacian(
            once,
            ring_row(top, top_far, x[0:1], -1),
            ring_row(bottom, bottom_far, x[rows - 1 :], 1),
            ring_col(left, left_far, x[:, 0:1], -1),
            ring_col(right, right_far, x[:, width - 1 :], 1),
        )
        warm = x - mixing[...] * twice
        warm_o[l] = warm
        total = warm if total is None else total + warm
    top_o[...] = (total / (levels * lev_count)).astype(top_o.dtype)


def subcycles_kernel(tiles, members, place, table, viscous, gain, speed, push, rims, *refs):
    push_relays, (out, push_rims) = refs[:members], refs[members:]
    size = viscous.shape[0]
    me = place()
    for k in range(tiles):
        for m in range(members):
            device = me ^ (k * members + m)
            push_rims[device] = push_relays[m][k * PUSH_ROWS : (k + 1) * PUSH_ROWS]
    half = DEPTH
    high = 2 * DEPTH
    sub = iota((high, size), 0)
    lane = iota((high, size), 1)
    edge = (sub & (half - 1)) == 0
    turn = jnp.where(sub < half, CORIOLIS_TURN, -CORIOLIS_TURN).astype(F32)
    first, last = lane == 0, lane == size - 1

    def load(device, side, mask, with_push=True):
        block = rims[device, side * 2 * high : (side + 1) * 2 * high].astype(F32)
        velocity, both = block[:high] * mask, block[high:]
        if not with_push:
            return velocity
        other = roll(both, half, 0)
        visc = jnp.where(sub < half, both, other)
        scale = jnp.where(sub < half, other, both) * mask
        start = side // 2 * 2 * high
        pushed = push_rims[device, start : start + 2 * high].astype(F32)
        pushed = pushed[:high] if side % 2 == 0 else pushed[high:]
        return [velocity, visc, scale, pushed]

    def follow(device, side):
        name = table[device, side]
        return jnp.where(name >= 0, name, 0), name >= 0

    def step(state, left, right, inner, outer):
        c, visc, scale, pushed = state
        spread = left + right + inner + outer - 4.0 * c
        return scale * (c + visc * spread + pushed + turn * roll(c, half, 0))

    strips = []
    for q in range(4):
        x, has_x = follow(me, q)
        strip = load(x, OPPOSITE[q], flag(has_x))
        sides = []
        for s in LATERAL[q]:
            y, has_y = follow(x, s)
            z, has_z = follow(y, OPPOSITE[q])
            w, has_w = follow(z, OPPOSITE[s])
            sides.append(
                [
                    load(y, OPPOSITE[q], flag(has_y)),
                    load(z, q, flag(has_z)),
                    load(w, q, flag(has_w), with_push=False),
                ]
            )
        strips.append((strip, sides))

    row = iota((size, size), 0)
    col = iota((size, size), 1)
    vx, vy = speed[0], speed[1]
    visc, scale, push_x, push_y = viscous[...], gain[...], push[0], push[1]

    def spread_of(v, north, south, east, west):
        up = jnp.where(row == size - 1, north, roll(v, -1, 0))
        down = jnp.where(row == 0, south, roll(v, 1, 0))
        right = jnp.where(col == size - 1, east, roll(v, -1, 1))
        left = jnp.where(col == 0, west, roll(v, 1, 1))
        return up + down + right + left - 4.0 * v

    for t in range(SUBCYCLES):
        cells = [strip[0] for strip, _ in strips]
        if t < SUBCYCLES - 1:
            mixed = jnp.where(col < half, roll(vx, 1, 1), roll(vy, 1 + half, 1))
            across = mixed.T[0:high]
            own = [
                jnp.where(sub < half, vx[size - 1 :], vy[size - 1 :]),
                jnp.where(sub < half, vx[0:1], vy[0:1]),
                across,
                roll(across, -1, 0),
            ]
            for q in range(4):
                strip, (beyond, before) = strips[q]
                c, y_hi, y_lo = strip[0], beyond[0][0], before[0][0]
                left = jnp.where(first, roll(y_lo, 1, 1), roll(c, 1, 1))
                right = jnp.where(last, roll(y_hi, -1, 1), roll(c, -1, 1))
                inner = jnp.where(edge, own[q], roll(c, 1, 0))
                new_strip = step(strip, left, right, inner, roll(c, -1, 0))
                if t < SUBCYCLES - 2:
                    new_sides = []
                    for i, (y, z, w) in enumerate((beyond, before)):
                        away = 1 if i == 0 else -1
                        boundary = first if i == 0 else last
                        yc, zc = y[0], z[0]
                        toward = jnp.where(boundary, roll(c, away, 1), roll(yc, away, 1))
                        inner = jnp.where(edge, zc, roll(yc, 1, 0))
                        new_y = step(y, toward, roll(yc, -away, 1), inner, roll(yc, -1, 0))
                        new_z = zc
                        if t < SUBCYCLES - 3:
                            toward = jnp.where(boundary, roll(w, away, 1), roll(zc, away, 1))
                            inner = jnp.where(edge, yc, roll(zc, 1, 0))
                            new_z = step(z, toward, roll(zc, -away, 1), inner, roll(zc, -1, 0))
                        new_sides.append((new_y, new_z))
                    for item, (new_y, new_z) in zip((beyond, before), new_sides):
                        item[0][0] = new_y
                        item[1][0] = new_z
                strip[0] = new_strip
        north, south = cells[0], cells[1]
        sides = jnp.where(edge, cells[2], roll(cells[3], 1, 0)).T
        east_x, west_x = sides[:, 0:1], sides[:, 1:2]
        east_y, west_y = sides[:, half : half + 1], sides[:, half + 1 : half + 2]
        spread_x = spread_of(vx, north[0:1], south[0:1], east_x, west_x)
        spread_y = spread_of(
            vy, north[half : half + 1], south[half : half + 1], east_y, west_y
        )
        new_x = scale * (vx + visc * spread_x + push_x + CORIOLIS_TURN * vy)
        new_y = scale * (vy + visc * spread_y + push_y - CORIOLIS_TURN * vx)
        vx, vy = new_x, new_y
    out[0] = vx
    out[1] = vy


def back_kernel(group, side, drag, conduct, current, speed, *refs):
    chunks = refs[:group]
    tops = refs[group : 2 * group]
    outs = refs[2 * group :]
    size = drag.shape[0]
    depth = chunks[0].shape[0] - 3 * side
    warm = remap_forward(chunks, [[t[...]] for t in tops], side, depth)
    heat = conduct[...] * warm
    fluxes = [heat.astype(BF16)]
    for c in range(2):
        fluxes.append((drag[...] * (speed[c] - current[c])).astype(BF16))
    wide = jnp.concatenate(fluxes, axis=1)
    for chunk, out in zip(chunks, outs):
        part = jnp.dot(chunk[0:side], wide, preferred_element_type=F32).astype(BF16)
        part = jnp.concatenate([part[:, c * size : (c + 1) * size] for c in range(3)], axis=0)
        reply = jnp.dot(part, chunk[side : side + depth], preferred_element_type=F32)
        out[...] = reply.astype(BF16)


def finish_kernel(warm, currents, speed, *refs):
    outs, (flat, heat_v, current_v, left) = refs[-7:-4], refs[-4:]
    replies = refs[:-7]
    flat_o, heat_o, current_o = outs
    size = speed.shape[1]
    copies = [
        pltpu.make_async_copy(source, target, left.at[i])
        for i, (source, target) in enumerate(
            ((flat, flat_o), (heat_v, heat_o), (current_v, current_o))
        )
    ]
    for c in range(2):
        flat[pl.ds(c, size, stride=2), :] = speed[c]
    copies[0].start()
    total = replies[0][...].astype(F32)
    for reply in replies[1:]:
        total = total + reply[...].astype(F32)
    side = currents.shape[1]
    heat = THERMAL_DIFFUSE * total[0:side]
    for l in range(warm.shape[0]):
        heat_v[l] = warm[l] + heat
    copies[1].start()
    for c in range(2):
        current_v[c] = currents[c] + STRESS_MIXING * total[(c + 1) * side : (c + 2) * side]
    copies[2].start()
    for copy in copies:
        copy.wait()


def shards(
    water_heat_state,
    diffusion_coefficient,
    upper_current_vector,
    remap_blocks,
    remap_rows,
    remap_cols,
    neighbors,
    thickness,
    concentration,
    ice_velocity,
    wind_stress,
):
    tile_count, sub_count, lev_count = (lax.axis_size(a) for a in ("tile", "sub", "lev"))
    group = sub_count * lev_count
    devices = tile_count * group
    group_axes = ("sub", "lev")
    member_axes = ("tile", "sub", "lev")
    levels, side, width = water_heat_state.shape
    pairs, size = remap_rows.shape[1:3]
    categories = thickness.shape[2]

    def place():
        return tuple(lax.axis_index(a) for a in member_axes)

    def member_place():
        return lax.axis_index("sub") * lev_count + lax.axis_index("lev")

    def device_place():
        return lax.axis_index("tile") * group + member_place()

    def swap(value, axes, count):
        return [value] + [
            lax.ppermute(value, axes, [(i, i ^ k) for i in range(count)]) for k in range(1, count)
        ]

    def swap_each(values):
        return [values[0]] + [
            lax.ppermute(values[k], group_axes, [(i, i ^ k) for i in range(group)])
            for k in range(1, group)
        ]

    def shape(*dims, dtype=F32):
        return jax.ShapeDtypeStruct(dims, dtype)

    def interleaved(value):
        return value.reshape(2, size, size).transpose(1, 0, 2).reshape(2 * size, size)

    grid = (tile_count, sub_count, lev_count, place)
    plane = shape(size, size)
    planes = shape(2, size, size)
    wind = interleaved(wind_stress)

    chunk_rows = 3 * side + width
    sent = call(
        functools.partial(forward_kernel, (devices, group, member_place)),
        [shape(chunk_rows, width, dtype=BF16)] * group,
        (remap_blocks, remap_rows[0].swapaxes(1, 2), remap_cols[0], upper_current_vector),
        scratch=[
            pltpu.SMEM((1, pairs), jnp.int32),
            pltpu.VMEM((2, side, width), F32),
            pltpu.VMEM((pairs, side, size), BF16),
            pltpu.VMEM((pairs, size, width), BF16),
            pltpu.VMEM((1 if pairs == group else group, 2 * side, width), BF16),
            pltpu.SemaphoreType.DMA((4,)),
            pltpu.SemaphoreType.DMA((3 * group,)),
        ],
        hbm=(0, 1, 2, 3),
        grant=60 * 2**20,
        micros=2,
    )
    chunks = swap_each(sent)

    message_rows = SIDE_ROWS + -(-(2 * levels + 1) // TILE_ROWS) * TILE_ROWS
    message, viscous, gain, step_mass, drag, conduct, speed = call(
        functools.partial(rims_kernel, grid),
        [shape(devices, message_rows, size, dtype=BF16)] + [plane] * 5 + [planes],
        (
            neighbors,
            thickness.reshape(categories, size, size),
            concentration.reshape(categories, size, size),
            interleaved(ice_velocity),
            water_heat_state,
        ),
        scratch=[pltpu.VMEM((SIDE_ROWS, size), F32)],
        smem=(0,),
    )
    rims = lax.all_to_all(message, member_axes, split_axis=0, concat_axis=0, tiled=True)

    push_message, current_ice, push = call(
        functools.partial(forcing_kernel, group, side),
        [shape(PUSH_ROWS, size, dtype=BF16), planes, planes],
        (step_mass, drag, wind, *chunks),
        scratch=[pltpu.VMEM((PUSH_ROWS, size), F32)],
    )
    push_messages = swap(push_message, "tile", tile_count)
    push_relay, rims = lax.optimization_barrier((jnp.concatenate(push_messages, axis=0), rims))
    push_relays = swap(push_relay, group_axes, group)

    warm, top = call(
        functools.partial(ocean_kernel, grid, SIDE_ROWS),
        [shape(levels, side, width), shape(side, width, dtype=BF16 if lev_count == 1 else F32)],
        (water_heat_state, diffusion_coefficient, rims),
    )
    if lev_count > 1:
        top = lax.psum(top, "lev").astype(BF16)
    tops = swap(top, group_axes, group)

    names = rims[:, SIDE_ROWS + 2 * levels, 0:8].astype(jnp.int32)
    table = names[:, 0:4] * 128 + names[:, 4:8]
    speed = call(
        functools.partial(subcycles_kernel, tile_count, group, device_place),
        planes,
        (table, viscous, gain, speed, push, rims, *push_relays),
        scratch=[pltpu.VMEM((devices, PUSH_ROWS, size), BF16)],
        smem=(0,),
    )

    replies = call(
        functools.partial(back_kernel, group, side),
        [shape(3 * side, width, dtype=BF16)] * group,
        (drag, conduct, current_ice, speed, *chunks, *tops),
    )
    replies = swap_each(replies)
    if lev_count > 1:
        replies = [lax.psum(sum(r.astype(F32) for r in replies), "lev")]
    flat, heat, current = call(
        finish_kernel,
        [shape(2 * size, size), shape(levels, side, width), shape(2, side, width)],
        (warm, upper_current_vector, speed, *replies),
        scratch=[
            pltpu.VMEM((2 * size, size), F32),
            pltpu.VMEM((levels, side, width), F32),
            pltpu.VMEM((2, side, width), F32),
            pltpu.SemaphoreType.DMA((3,)),
        ],
        out_space=pltpu.HBM,
    )
    velocity = flat.reshape(size, 2, size).transpose(1, 0, 2).reshape(1, 1, 2, size * size)
    return heat, current, velocity


def solution(mesh):
    member = ("tile", "sub", "lev")
    whole = ("copies",) + member
    ice = P(None, whole, None, None)
    water = P("lev", ("copies", "tile"), "sub")
    current = P(None, ("copies", "tile"), "sub")
    return jax.shard_map(
        shards,
        mesh=mesh,
        in_specs=(
            water,
            P("tile", "sub"),
            current,
            P(member, None),
            P(member, None, None, None),
            P(member, None, None, None),
            P(None, member, None),
            ice,
            ice,
            ice,
            ice,
        ),
        out_specs=(water, current, ice),
        check_vma=False,
    )
```

```python
import functools
import math

import jax
import jax.numpy as jnp
from jax import lax
from jax.experimental import pallas as pl
from jax.experimental.pallas import tpu as pltpu
from jax.sharding import PartitionSpec as P

SUBCYCLES = 4
STRENGTH_DECAY = 5.0
VISCOUS_STEP = 0.24
SUBCYCLE_STEP = 0.5
CORIOLIS_TURN = 0.1
BASE_MASS = 0.5
HEAT_RATE = 0.2
THIN_ICE = 0.1
THERMAL_DIFFUSE = 0.5
STRESS_MIXING = 0.5

OPPOSITE = (1, 0, 3, 2)
LATERAL = ((2, 3), (2, 3), (0, 1), (0, 1))
DEPTH = SUBCYCLES
SIDE_ROWS = 16 * DEPTH
PUSH_ROWS = 8 * DEPTH
NAMES_ROW = 4 * DEPTH - 1
TILE_ROWS = 16
F32 = jnp.float32
BF16 = jnp.bfloat16
VMEM_LIMIT = 16 * 1024 * 1024
FLOPS_PER_MICRO = 1.15e9


def call(kernel, outs, args, scratch=(), smem=(), hbm=(), out_space=pltpu.VMEM, grant=VMEM_LIMIT, micros=0.01):
    def space(i):
        return pltpu.SMEM if i in smem else pltpu.HBM if i in hbm else pltpu.VMEM

    specs = [pl.BlockSpec(memory_space=space(i)) for i in range(len(args))]
    size = sum(a.size * a.dtype.itemsize for a in args)
    return pl.pallas_call(
        kernel,
        out_shape=outs,
        in_specs=specs,
        out_specs=jax.tree.map(lambda _: pl.BlockSpec(memory_space=out_space), outs),
        scratch_shapes=list(scratch),
        compiler_params=pltpu.CompilerParams(vmem_limit_bytes=grant),
        cost_estimate=pl.CostEstimate(
            flops=int(micros * FLOPS_PER_MICRO), bytes_accessed=size, transcendentals=0
        ),
    )(*args)


def iota(shape, axis):
    return lax.broadcasted_iota(jnp.int32, shape, axis)


def roll(x, shift, axis):
    return pltpu.roll(x, shift % x.shape[axis], axis)


def flag(condition):
    return jnp.where(condition, 1.0, 0.0).astype(F32)


def forward_kernel(group, blocks_h, rows_h, cols_h, currents_h, *refs):
    devices, members, place = group
    outs, (blocks, currents, rows, cols, fields, arrived, left) = refs[:members], refs[members:]
    pairs, side, width = rows_h.shape
    depth = cols_h.shape[1]
    loads = [
        pltpu.make_async_copy(source, target, arrived.at[i])
        for i, (source, target) in enumerate(
            ((blocks_h, blocks), (currents_h, currents), (rows_h, rows), (cols_h, cols))
        )
    ]
    for load in loads:
        load.start()
    for load in loads:
        load.wait()
    me = place()
    owners = [lax.rem(lax.rem(blocks[0, m], devices), members) for m in range(pairs)]
    copies = []
    for k, out in enumerate(outs):
        partner = me ^ k
        pair, found = jnp.int32(0), jnp.int32(0)
        for m in range(pairs):
            pair = jnp.where(owners[m] == partner, m, pair)
            found = jnp.where(owners[m] == partner, 1, found)
        copies.append(
            pltpu.make_async_copy(rows.at[pair], out.at[pl.ds(0, side)], left.at[3 * k])
        )
        copies.append(
            pltpu.make_async_copy(cols.at[pair], out.at[pl.ds(side, depth)], left.at[3 * k + 1])
        )
        if pairs < members:
            keep = jnp.where(found > 0, 1.0, 0.0).astype(F32)
        else:
            keep = None
        copies[-2].start()
        copies[-1].start()
        if k == 0 or keep is not None:
            for c in range(2):
                field = currents[c] if keep is None else currents[c] * keep
                fields[0 if keep is None else k, c * side : (c + 1) * side] = field.astype(BF16)
        copies.append(
            pltpu.make_async_copy(
                fields.at[0 if keep is None else k],
                out.at[pl.ds(side + depth, 2 * side)],
                left.at[3 * k + 2],
            )
        )
        copies[-1].start()
    for copy in copies:
        copy.wait()


def put_side_rims(store, planes, at):
    size = planes[0].shape[0]
    lane = iota((size, size), 1)
    mixed = jnp.zeros((size, size), F32)
    for i, plane in enumerate(planes):
        turned = roll(plane, DEPTH + 2 * DEPTH * i, 1)
        mixed = jnp.where(lane // (2 * DEPTH) == i, turned, mixed)
    across = mixed.T
    for i, plane in enumerate(planes):
        for k in range(DEPTH):
            base = i * DEPTH + k
            store[at(0) + base : at(0) + base + 1] = plane[size - 1 - k : size - k]
            store[at(1) + base : at(1) + base + 1] = plane[k : k + 1]
            east = 2 * DEPTH * i + DEPTH - 1 - k
            west = 2 * DEPTH * i + DEPTH + k
            store[at(2) + base : at(2) + base + 1] = across[east : east + 1]
            store[at(3) + base : at(3) + base + 1] = across[west : west + 1]


def rims_kernel(
    links, thick, conc, ice, water, out, cols_o, viscous_o, gain_o, mass_o, drag_o, conduct_o,
    speed_o, store,
):
    size = thick.shape[1]
    cover = jnp.zeros((size, size), F32)
    volume = jnp.zeros((size, size), F32)
    conduct = jnp.zeros((size, size), F32)
    for c in range(thick.shape[0]):
        h, a = thick[c], conc[c]
        cover = cover + a
        volume = volume + a * h
        conduct = conduct + a / (h + THIN_ICE)
    mass = volume + BASE_MASS
    viscous = VISCOUS_STEP * (volume * jnp.exp(-STRENGTH_DECAY * (1.0 - cover))) / mass
    step_mass = SUBCYCLE_STEP / mass
    gain = 1.0 / (1.0 + step_mass * cover)
    speed_x = ice[pl.ds(0, size, stride=2), :]
    speed_y = ice[pl.ds(1, size, stride=2), :]
    viscous_o[...] = viscous
    gain_o[...] = gain
    mass_o[...] = step_mass
    drag_o[...] = cover
    conduct_o[...] = -HEAT_RATE * conduct
    speed_o[0] = speed_x
    speed_o[1] = speed_y
    put_side_rims(store, [speed_x, speed_y, viscous, gain], lambda side: side * 4 * DEPTH)
    line = iota((1, size), 1)
    names = jnp.zeros((1, size), F32)
    for q in range(4):
        names = jnp.where(line == q, (links[0, 0, q] >> 7).astype(F32), names)
        names = jnp.where(line == 4 + q, (links[0, 0, q] & 127).astype(F32), names)
    store[NAMES_ROW : NAMES_ROW + 1] = names
    levels, rows, width = water.shape
    start = SIDE_ROWS
    for l in range(levels):
        for j in range(2):
            at = start + 2 * l + j
            store[at : at + 1] = water[l, rows - 1 - j : rows - j]
            store[at + 2 * levels : at + 2 * levels + 1] = water[l, j : j + 1]
    out[...] = store[...].astype(BF16)
    lane = iota((rows, width), 1)
    mixed = jnp.zeros((rows, width), F32)
    for l in range(levels):
        mixed = jnp.where(lane // 4 == l, roll(water[l], 2 + 4 * l, 1), mixed)
    across = jnp.concatenate([mixed, jnp.zeros((width - rows, width), F32)], axis=0).T
    beside = []
    for l in range(levels):
        for j in range(2):
            last = across[4 * l + 1 - j : 4 * l + 2 - j]
            lead = across[4 * l + 2 + j : 4 * l + 3 + j]
            beside.append(jnp.where(line < rows, last, roll(lead, rows, 1)))
    cols_o[...] = jnp.concatenate(beside, axis=0)


def relay_kernel(tiles, place, cols, messages, out):
    step = messages.shape[0] // tiles
    for k in range(tiles):
        out[k * SIDE_ROWS : (k + 1) * SIDE_ROWS] = messages[k * step : k * step + SIDE_ROWS]
    levels = cols.shape[0] // 2
    before, after = around(place(), tiles, messages, levels)
    rows = []
    for strip in (before, after):
        rows += [strip[2 * l : 2 * l + 1] for l in range(levels)]
    out[tiles * SIDE_ROWS :] = jnp.concatenate([cols[...]] + rows, axis=0).astype(BF16)


def around(me, tiles, messages, levels):
    before, after = 0.0, 0.0
    step = messages.shape[0] // tiles
    for k in range(1, tiles):
        at = k * step + SIDE_ROWS
        strips = messages[at : at + 4 * levels].astype(F32)
        before = before + strips[: 2 * levels] * flag((me > 0) & ((me ^ k) == me - 1))
        after = after + strips[2 * levels :] * flag((me < tiles - 1) & ((me ^ k) == me + 1))
    return before, after


def remap_forward(chunks, field_rows, side, depth):
    total = None
    for chunk, fields in zip(chunks, field_rows):
        down = chunk[0:side]
        right = chunk[side : side + depth]
        wide = jnp.concatenate(fields, axis=1) if len(fields) > 1 else fields[0]
        part = lax.dot_general(down, wide, (((0,), (0,)), ((), ())), preferred_element_type=F32)
        part = part.astype(BF16)
        width = fields[0].shape[1]
        if len(fields) > 1:
            part = jnp.concatenate(
                [part[:, c * width : (c + 1) * width] for c in range(len(fields))], axis=0
            )
        piece = lax.dot_general(part, right, (((1,), (1,)), ((), ())), preferred_element_type=F32)
        piece = piece.astype(BF16).astype(F32)
        total = piece if total is None else total + piece
    return total


def forcing_kernel(group, side, mass, drag, wind, *refs):
    chunks = refs[:group]
    out, current_o, push_o, store = refs[group:]
    size = mass.shape[0]
    depth = chunks[0].shape[0] - 3 * side
    fields = [
        [c[side + depth : 2 * side + depth], c[2 * side + depth : 3 * side + depth]] for c in chunks
    ]
    total = remap_forward(chunks, fields, side, depth)
    pushes = []
    for c in range(2):
        current = total[c * size : (c + 1) * size]
        current_o[c] = current
        force = wind[pl.ds(c, size, stride=2), :]
        push = mass[...] * (force + drag[...] * current)
        push_o[c] = push
        pushes.append(push)
    put_side_rims(store, pushes, lambda q: q * 2 * DEPTH)
    out[...] = store[...].astype(BF16)


def ocean_kernel(
    counts, tile_place, member_place, water, mixing, messages, relays, warm_o, top_o, table_o
):
    tiles, subs, levs = counts
    members = subs * levs
    step = relays.shape[0] // members
    levels, rows, width = water.shape
    my_tile, me = tile_place(), member_place()
    halo = {}
    halo[-1, 0], halo[1, 0] = around(my_tile, tiles, messages, levels)
    for ds in (-1, 1):
        beyond = me + ds * levs
        inside = (beyond >= 0) & (beyond < members)
        found = 0.0
        for k in range(1, members):
            at = k * step + tiles * SIDE_ROWS
            strip = relays[at : at + 4 * levels].astype(F32)
            found = found + strip * flag(inside & ((me ^ k) == beyond))
        beside, corners = found[: 2 * levels], found[2 * levels :]
        if ds > 0:
            beside = roll(beside, -rows, 1)
        halo[0, ds] = beside
        at = width - 1 if ds < 0 else 0
        halo[-1, ds] = corners[:levels, at : at + 1]
        halo[1, ds] = corners[levels:, at : at + 1]
    mine = my_tile * members + me
    column = iota((table_o.shape[0], width), 1)
    names = []
    for k in range(tiles):
        for m in range(members):
            at = m * step + k * SIDE_ROWS
            names.append(relays[at : at + TILE_ROWS].astype(F32)[NAMES_ROW : NAMES_ROW + 1])
    names = jnp.concatenate(names, axis=0)
    table = (128.0 * names + roll(names, -4, 1)).astype(jnp.int32)
    table_o[...] = jnp.where((table >= 0) & (column < 4), table ^ mine, -1)
    left_cols = halo[0, -1].T
    right_cols = halo[0, 1].T
    row = iota((rows, width), 0)
    lane = iota((rows, width), 1)
    line = iota((1, width), 1)
    total = None

    def laplacian(x, top, bottom, left, right):
        up = jnp.where(row == 0, top, roll(x, 1, 0))
        down = jnp.where(row == rows - 1, bottom, roll(x, -1, 0))
        west = jnp.where(lane == 0, left, roll(x, 1, 1))
        east = jnp.where(lane == width - 1, right, roll(x, -1, 1))
        return up + down + west + east - 4.0 * x

    for l in range(levels):
        x = water[l]
        near, far = 2 * l, 2 * l + 1
        top, top_far = halo[-1, 0][near : near + 1], halo[-1, 0][far : far + 1]
        bottom, bottom_far = halo[1, 0][near : near + 1], halo[1, 0][far : far + 1]
        left, left_far = left_cols[0:rows, near : near + 1], left_cols[0:rows, far : far + 1]
        right, right_far = right_cols[0:rows, near : near + 1], right_cols[0:rows, far : far + 1]
        corner = {}
        for dt in (-1, 1):
            for ds in (-1, 1):
                corner[dt, ds] = halo[dt, ds][l : l + 1]

        def ring_row(mid, out_row, in_row, dt):
            west = jnp.where(line == 0, corner[dt, -1], roll(mid, 1, 1))
            east = jnp.where(line == width - 1, corner[dt, 1], roll(mid, -1, 1))
            return west + east + out_row + in_row - 4.0 * mid

        def ring_col(mid, out_col, in_col, ds):
            up = jnp.concatenate([corner[-1, ds], mid[:-1]], axis=0)
            down = jnp.concatenate([mid[1:], corner[1, ds]], axis=0)
            return up + down + out_col + in_col - 4.0 * mid

        once = laplacian(x, top, bottom, left, right)
        twice = laplacian(
            once,
            ring_row(top, top_far, x[0:1], -1),
            ring_row(bottom, bottom_far, x[rows - 1 :], 1),
            ring_col(left, left_far, x[:, 0:1], -1),
            ring_col(right, right_far, x[:, width - 1 :], 1),
        )
        warm = x - mixing[...] * twice
        warm_o[l] = warm
        total = warm if total is None else total + warm
    top_o[...] = (total / (levels * levs)).astype(top_o.dtype)


def subcycles_kernel(tiles, members, table, viscous, gain, speed, push, *refs):
    relays, push_relays, out, rims, push_rims = refs
    step = relays.shape[0] // members
    size = viscous.shape[0]
    for k in range(tiles):
        for m in range(members):
            at = m * step + k * SIDE_ROWS
            rims[k * members + m] = relays[at : at + SIDE_ROWS]
            at = (m * tiles + k) * PUSH_ROWS
            push_rims[k * members + m] = push_relays[at : at + PUSH_ROWS]
    half = DEPTH
    high = 2 * DEPTH
    sub = iota((high, size), 0)
    lane = iota((high, size), 1)
    edge = (sub & (half - 1)) == 0
    turn = jnp.where(sub < half, CORIOLIS_TURN, -CORIOLIS_TURN).astype(F32)
    first, last = lane == 0, lane == size - 1

    def load(device, side, mask, with_push=True):
        block = rims[device, side * 2 * high : (side + 1) * 2 * high].astype(F32)
        velocity, both = block[:high] * mask, block[high:]
        if not with_push:
            return velocity
        other = roll(both, half, 0)
        visc = jnp.where(sub < half, both, other)
        scale = jnp.where(sub < half, other, both) * mask
        start = side // 2 * 2 * high
        pushed = push_rims[device, start : start + 2 * high].astype(F32)
        pushed = pushed[:high] if side % 2 == 0 else pushed[high:]
        return [velocity, visc, scale, pushed]

    def follow(device, side):
        name = table[device, side]
        return jnp.where(name >= 0, name, 0), name >= 0

    def step(state, left, right, inner, outer):
        c, visc, scale, pushed = state
        spread = left + right + inner + outer - 4.0 * c
        return scale * (c + visc * spread + pushed + turn * roll(c, half, 0))

    strips = []
    for q in range(4):
        x, has_x = follow(0, q)
        strip = load(x, OPPOSITE[q], flag(has_x))
        sides = []
        for s in LATERAL[q]:
            y, has_y = follow(x, s)
            z, has_z = follow(y, OPPOSITE[q])
            w, has_w = follow(z, OPPOSITE[s])
            sides.append(
                [
                    load(y, OPPOSITE[q], flag(has_y)),
                    load(z, q, flag(has_z)),
                    load(w, q, flag(has_w), with_push=False),
                ]
            )
        strips.append((strip, sides))

    row = iota((size, size), 0)
    col = iota((size, size), 1)
    vx, vy = speed[0], speed[1]
    visc, scale, push_x, push_y = viscous[...], gain[...], push[0], push[1]

    def spread_of(v, north, south, east, west):
        up = jnp.where(row == size - 1, north, roll(v, -1, 0))
        down = jnp.where(row == 0, south, roll(v, 1, 0))
        right = jnp.where(col == size - 1, east, roll(v, -1, 1))
        left = jnp.where(col == 0, west, roll(v, 1, 1))
        return up + down + right + left - 4.0 * v

    for t in range(SUBCYCLES):
        cells = [strip[0] for strip, _ in strips]
        if t < SUBCYCLES - 1:
            mixed = jnp.where(col < half, roll(vx, 1, 1), roll(vy, 1 + half, 1))
            across = mixed.T[0:high]
            own = [
                jnp.where(sub < half, vx[size - 1 :], vy[size - 1 :]),
                jnp.where(sub < half, vx[0:1], vy[0:1]),
                across,
                roll(across, -1, 0),
            ]
            for q in range(4):
                strip, (beyond, before) = strips[q]
                c, y_hi, y_lo = strip[0], beyond[0][0], before[0][0]
                left = jnp.where(first, roll(y_lo, 1, 1), roll(c, 1, 1))
                right = jnp.where(last, roll(y_hi, -1, 1), roll(c, -1, 1))
                inner = jnp.where(edge, own[q], roll(c, 1, 0))
                new_strip = step(strip, left, right, inner, roll(c, -1, 0))
                if t < SUBCYCLES - 2:
                    new_sides = []
                    for i, (y, z, w) in enumerate((beyond, before)):
                        away = 1 if i == 0 else -1
                        boundary = first if i == 0 else last
                        yc, zc = y[0], z[0]
                        toward = jnp.where(boundary, roll(c, away, 1), roll(yc, away, 1))
                        inner = jnp.where(edge, zc, roll(yc, 1, 0))
                        new_y = step(y, toward, roll(yc, -away, 1), inner, roll(yc, -1, 0))
                        new_z = zc
                        if t < SUBCYCLES - 3:
                            toward = jnp.where(boundary, roll(w, away, 1), roll(zc, away, 1))
                            inner = jnp.where(edge, yc, roll(zc, 1, 0))
                            new_z = step(z, toward, roll(zc, -away, 1), inner, roll(zc, -1, 0))
                        new_sides.append((new_y, new_z))
                    for item, (new_y, new_z) in zip((beyond, before), new_sides):
                        item[0][0] = new_y
                        item[1][0] = new_z
                strip[0] = new_strip
        north, south = cells[0], cells[1]
        sides = jnp.where(edge, cells[2], roll(cells[3], 1, 0)).T
        east_x, west_x = sides[:, 0:1], sides[:, 1:2]
        east_y, west_y = sides[:, half : half + 1], sides[:, half + 1 : half + 2]
        spread_x = spread_of(vx, north[0:1], south[0:1], east_x, west_x)
        spread_y = spread_of(
            vy, north[half : half + 1], south[half : half + 1], east_y, west_y
        )
        new_x = scale * (vx + visc * spread_x + push_x + CORIOLIS_TURN * vy)
        new_y = scale * (vy + visc * spread_y + push_y - CORIOLIS_TURN * vx)
        vx, vy = new_x, new_y
    out[0] = vx
    out[1] = vy


def back_kernel(group, side, drag, conduct, current, speed, *refs):
    chunks, tops, outs = refs[:group], refs[group], refs[group + 1 :]
    size = drag.shape[0]
    depth = chunks[0].shape[0] - 3 * side
    warm = remap_forward(chunks, [[tops[k * side : (k + 1) * side]] for k in range(group)], side, depth)
    heat = conduct[...] * warm
    fluxes = [heat.astype(BF16)]
    for c in range(2):
        fluxes.append((drag[...] * (speed[c] - current[c])).astype(BF16))
    wide = jnp.concatenate(fluxes, axis=1)
    for chunk, out in zip(chunks, outs):
        part = jnp.dot(chunk[0:side], wide, preferred_element_type=F32).astype(BF16)
        part = jnp.concatenate([part[:, c * size : (c + 1) * size] for c in range(3)], axis=0)
        reply = jnp.dot(part, chunk[side : side + depth], preferred_element_type=F32)
        out[...] = reply.astype(BF16)


def finish_kernel(warm, currents, speed, *refs):
    outs, (flat, heat_v, current_v, left) = refs[-7:-4], refs[-4:]
    replies = refs[:-7]
    flat_o, heat_o, current_o = outs
    size = speed.shape[1]
    copies = [
        pltpu.make_async_copy(source, target, left.at[i])
        for i, (source, target) in enumerate(
            ((flat, flat_o), (heat_v, heat_o), (current_v, current_o))
        )
    ]
    for c in range(2):
        flat[pl.ds(c, size, stride=2), :] = speed[c]
    copies[0].start()
    total = replies[0][...].astype(F32)
    for reply in replies[1:]:
        total = total + reply[...].astype(F32)
    side = currents.shape[1]
    heat = THERMAL_DIFFUSE * total[0:side]
    for l in range(warm.shape[0]):
        heat_v[l] = warm[l] + heat
    copies[1].start()
    for c in range(2):
        current_v[c] = currents[c] + STRESS_MIXING * total[(c + 1) * side : (c + 2) * side]
    copies[2].start()
    for copy in copies:
        copy.wait()


def shards(
    water_heat_state,
    diffusion_coefficient,
    upper_current_vector,
    remap_blocks,
    remap_rows,
    remap_cols,
    neighbors,
    thickness,
    concentration,
    ice_velocity,
    wind_stress,
):
    tile_count, sub_count, lev_count = (lax.axis_size(a) for a in ("tile", "sub", "lev"))
    group = sub_count * lev_count
    devices = tile_count * group
    group_axes = ("sub", "lev")
    member_axes = ("tile", "sub", "lev")
    levels, side, width = water_heat_state.shape
    pairs, size = remap_rows.shape[1:3]
    categories = thickness.shape[2]

    def tile_place():
        return lax.axis_index("tile")

    def member_place():
        return lax.axis_index("sub") * lev_count + lax.axis_index("lev")

    def swap(value, axes, count, k):
        return lax.ppermute(value, axes, [(i, i ^ k) for i in range(count)])

    def gather(value, axes, steps):
        count = math.prod(lax.axis_size(a) for a in axes)
        for k in steps:
            value = jnp.concatenate([value, swap(value, axes, count, k)], axis=0)
        return value

    def doublings(count):
        return [1 << i for i in range(count.bit_length() - 1)]

    def gather_members(value):
        for k in reversed(doublings(group)):
            value = jnp.stack([value, swap(value, group_axes, group, k)], axis=-3)
        return value.reshape(group * value.shape[-2], value.shape[-1])

    def swap_each(values):
        return [values[0]] + [
            lax.ppermute(values[k], group_axes, [(i, i ^ k) for i in range(group)])
            for k in range(1, group)
        ]

    def shape(*dims, dtype=F32):
        return jax.ShapeDtypeStruct(dims, dtype)

    def interleaved(value):
        return value.reshape(2, size, size).transpose(1, 0, 2).reshape(2 * size, size)

    plane = shape(size, size)
    planes = shape(2, size, size)
    wind = interleaved(wind_stress)

    chunk_rows = 3 * side + width
    sent = call(
        functools.partial(forward_kernel, (devices, group, member_place)),
        [shape(chunk_rows, width, dtype=BF16)] * group,
        (remap_blocks, remap_rows[0].swapaxes(1, 2), remap_cols[0], upper_current_vector),
        scratch=[
            pltpu.SMEM((1, pairs), jnp.int32),
            pltpu.VMEM((2, side, width), F32),
            pltpu.VMEM((pairs, side, size), BF16),
            pltpu.VMEM((pairs, size, width), BF16),
            pltpu.VMEM((1 if pairs == group else group, 2 * side, width), BF16),
            pltpu.SemaphoreType.DMA((4,)),
            pltpu.SemaphoreType.DMA((3 * group,)),
        ],
        hbm=(0, 1, 2, 3),
        grant=60 * 2**20,
        micros=2,
    )
    chunks = swap_each(sent)

    links, sent = lax.optimization_barrier((neighbors, sent))
    message, cols, viscous, gain, step_mass, drag, conduct, speed = call(
        rims_kernel,
        [shape(SIDE_ROWS + 4 * levels, size, dtype=BF16), shape(2 * levels, width)]
        + [plane] * 5
        + [planes],
        (
            links,
            thickness.reshape(categories, size, size),
            concentration.reshape(categories, size, size),
            interleaved(ice_velocity),
            water_heat_state,
        ),
        scratch=[pltpu.VMEM((SIDE_ROWS + 4 * levels, size), F32)],
        smem=(0,),
    )
    messages = gather(message, ("tile",), doublings(tile_count))

    push_message, current_ice, push = call(
        functools.partial(forcing_kernel, group, side),
        [shape(PUSH_ROWS, size, dtype=BF16), planes, planes],
        (step_mass, drag, wind, *chunks),
        scratch=[pltpu.VMEM((PUSH_ROWS, size), F32)],
    )
    cols, push_message = lax.optimization_barrier((cols, push_message))
    push_messages = gather(push_message, ("tile",), doublings(tile_count))

    relay = call(
        functools.partial(relay_kernel, tile_count, tile_place),
        shape(tile_count * SIDE_ROWS + 4 * levels, size, dtype=BF16),
        (cols, messages),
    )
    relays = gather_members(relay)
    push_relays = gather_members(push_messages)

    warm, top, table = call(
        functools.partial(
            ocean_kernel, (tile_count, sub_count, lev_count), tile_place, member_place
        ),
        [
            shape(levels, side, width),
            shape(side, width, dtype=BF16 if lev_count == 1 else F32),
            shape(devices, width, dtype=jnp.int32),
        ],
        (water_heat_state, diffusion_coefficient, messages, relays),
    )
    if lev_count > 1:
        top = lax.psum(top, "lev").astype(BF16)
    tops = gather_members(top)

    speed = call(
        functools.partial(subcycles_kernel, tile_count, group),
        planes,
        (table, viscous, gain, speed, push, relays, push_relays),
        scratch=[
            pltpu.VMEM((devices, SIDE_ROWS, size), BF16),
            pltpu.VMEM((devices, PUSH_ROWS, size), BF16),
        ],
        smem=(0,),
    )

    replies = call(
        functools.partial(back_kernel, group, side),
        [shape(3 * side, width, dtype=BF16)] * group,
        (drag, conduct, current_ice, speed, *chunks, tops),
    )
    replies = swap_each(replies)
    if lev_count > 1:
        replies = [lax.psum(sum(r.astype(F32) for r in replies), "lev")]
    flat, heat, current = call(
        finish_kernel,
        [shape(2 * size, size), shape(levels, side, width), shape(2, side, width)],
        (warm, upper_current_vector, speed, *replies),
        scratch=[
            pltpu.VMEM((2 * size, size), F32),
            pltpu.VMEM((levels, side, width), F32),
            pltpu.VMEM((2, side, width), F32),
            pltpu.SemaphoreType.DMA((3,)),
        ],
        out_space=pltpu.HBM,
    )
    velocity = flat.reshape(size, 2, size).transpose(1, 0, 2).reshape(1, 1, 2, size * size)
    return heat, current, velocity


def solution(mesh):
    member = ("tile", "sub", "lev")
    whole = ("copies",) + member
    ice = P(None, whole, None, None)
    water = P("lev", ("copies", "tile"), "sub")
    current = P(None, ("copies", "tile"), "sub")
    return jax.shard_map(
        shards,
        mesh=mesh,
        in_specs=(
            water,
            P("tile", "sub"),
            current,
            P(member, None),
            P(member, None, None, None),
            P(member, None, None, None),
            P(None, member, None),
            ice,
            ice,
            ice,
            ice,
        ),
        out_specs=(water, current, ice),
        check_vma=False,
    )
```

```python
import functools

import jax
import jax.numpy as jnp
from jax import lax
from jax.experimental import pallas as pl
from jax.experimental.pallas import tpu as pltpu
from jax.sharding import PartitionSpec as P

SUBCYCLES = 4
STRENGTH_DECAY = 5.0
VISCOUS_STEP = 0.24
SUBCYCLE_STEP = 0.5
CORIOLIS_TURN = 0.1
BASE_MASS = 0.5
HEAT_RATE = 0.2
THIN_ICE = 0.1
THERMAL_DIFFUSE = 0.5
STRESS_MIXING = 0.5

OPPOSITE = (1, 0, 3, 2)
LATERAL = ((2, 3), (2, 3), (0, 1), (0, 1))
DEPTH = SUBCYCLES
SIDE_ROWS = 16 * DEPTH
PUSH_ROWS = 8 * DEPTH
NAMES_ROW = 2 * DEPTH - 1
TILE_ROWS = 16
F32 = jnp.float32
BF16 = jnp.bfloat16
VMEM_LIMIT = 16 * 1024 * 1024
FLOPS_PER_MICRO = 1.15e9


def call(kernel, outs, args, scratch=(), smem=(), hbm=(), out_space=pltpu.VMEM, grant=VMEM_LIMIT, micros=0.01):
    def space(i):
        return pltpu.SMEM if i in smem else pltpu.HBM if i in hbm else pltpu.VMEM

    specs = [pl.BlockSpec(memory_space=space(i)) for i in range(len(args))]
    size = sum(a.size * a.dtype.itemsize for a in args)
    return pl.pallas_call(
        kernel,
        out_shape=outs,
        in_specs=specs,
        out_specs=jax.tree.map(lambda _: pl.BlockSpec(memory_space=out_space), outs),
        scratch_shapes=list(scratch),
        compiler_params=pltpu.CompilerParams(vmem_limit_bytes=grant),
        cost_estimate=pl.CostEstimate(
            flops=int(micros * FLOPS_PER_MICRO), bytes_accessed=size, transcendentals=0
        ),
    )(*args)


def iota(shape, axis):
    return lax.broadcasted_iota(jnp.int32, shape, axis)


def roll(x, shift, axis):
    return pltpu.roll(x, shift % x.shape[axis], axis)


def flag(condition):
    return jnp.where(condition, 1.0, 0.0).astype(F32)


def forward_kernel(group, links_h, blocks_h, rows_h, cols_h, currents_h, *refs):
    devices, members, place = group
    outs, scratch = refs[:members], refs[members:]
    links, blocks, currents, rows, cols, fields, names, arrived, left = scratch
    pairs, side, width = rows_h.shape
    depth = cols_h.shape[1]
    loads = [
        pltpu.make_async_copy(source, target, arrived.at[i])
        for i, (source, target) in enumerate(
            (
                (links_h, links),
                (blocks_h, blocks),
                (currents_h, currents),
                (rows_h, rows),
                (cols_h, cols),
            )
        )
    ]
    for load in loads:
        load.start()
    for load in loads:
        load.wait()
    me = place()
    owners = [lax.rem(lax.rem(blocks[0, m], devices), members) for m in range(pairs)]
    lane = iota((TILE_ROWS, width), 1)
    numbers = jnp.zeros((TILE_ROWS, width), F32)
    for q in range(4):
        numbers = jnp.where(lane == q, (links[0, 0, q] >> 7).astype(F32), numbers)
        numbers = jnp.where(lane == 4 + q, (links[0, 0, q] & 127).astype(F32), numbers)
    names[...] = numbers.astype(BF16)
    copies = [
        pltpu.make_async_copy(
            names, outs[0].at[pl.ds(3 * side + depth, TILE_ROWS)], left.at[3 * members]
        )
    ]
    copies[0].start()
    for k, out in enumerate(outs):
        partner = me ^ k
        pair, found = jnp.int32(0), jnp.int32(0)
        for m in range(pairs):
            pair = jnp.where(owners[m] == partner, m, pair)
            found = jnp.where(owners[m] == partner, 1, found)
        copies.append(
            pltpu.make_async_copy(rows.at[pair], out.at[pl.ds(0, side)], left.at[3 * k])
        )
        copies.append(
            pltpu.make_async_copy(cols.at[pair], out.at[pl.ds(side, depth)], left.at[3 * k + 1])
        )
        if pairs < members:
            keep = jnp.where(found > 0, 1.0, 0.0).astype(F32)
        else:
            keep = None
        copies[-2].start()
        copies[-1].start()
        if k == 0 or keep is not None:
            for c in range(2):
                field = currents[c] if keep is None else currents[c] * keep
                fields[0 if keep is None else k, c * side : (c + 1) * side] = field.astype(BF16)
        copies.append(
            pltpu.make_async_copy(
                fields.at[0 if keep is None else k],
                out.at[pl.ds(side + depth, 2 * side)],
                left.at[3 * k + 2],
            )
        )
        copies[-1].start()
    for copy in copies:
        copy.wait()


def put_side_rims(store, planes, at):
    size = planes[0].shape[0]
    lane = iota((size, size), 1)
    mixed = jnp.zeros((size, size), F32)
    for i, plane in enumerate(planes):
        turned = roll(plane, DEPTH + 2 * DEPTH * i, 1)
        mixed = jnp.where(lane // (2 * DEPTH) == i, turned, mixed)
    across = mixed.T
    for i, plane in enumerate(planes):
        for k in range(DEPTH):
            base = i * DEPTH + k
            store[at(0) + base : at(0) + base + 1] = plane[size - 1 - k : size - k]
            store[at(1) + base : at(1) + base + 1] = plane[k : k + 1]
            east = 2 * DEPTH * i + DEPTH - 1 - k
            west = 2 * DEPTH * i + DEPTH + k
            store[at(2) + base : at(2) + base + 1] = across[east : east + 1]
            store[at(3) + base : at(3) + base + 1] = across[west : west + 1]


def rims_kernel(
    thick, conc, ice, water, out, cols_o, viscous_o, gain_o, mass_o, drag_o, conduct_o,
    speed_o, store,
):
    size = thick.shape[1]
    cover = jnp.zeros((size, size), F32)
    volume = jnp.zeros((size, size), F32)
    conduct = jnp.zeros((size, size), F32)
    for c in range(thick.shape[0]):
        h, a = thick[c], conc[c]
        cover = cover + a
        volume = volume + a * h
        conduct = conduct + a / (h + THIN_ICE)
    mass = volume + BASE_MASS
    viscous = VISCOUS_STEP * (volume * jnp.exp(-STRENGTH_DECAY * (1.0 - cover))) / mass
    step_mass = SUBCYCLE_STEP / mass
    gain = 1.0 / (1.0 + step_mass * cover)
    speed_x = ice[pl.ds(0, size, stride=2), :]
    speed_y = ice[pl.ds(1, size, stride=2), :]
    viscous_o[...] = viscous
    gain_o[...] = gain
    mass_o[...] = step_mass
    drag_o[...] = cover
    conduct_o[...] = -HEAT_RATE * conduct
    speed_o[0] = speed_x
    speed_o[1] = speed_y
    put_side_rims(store, [speed_x, speed_y, viscous, gain], lambda side: side * 4 * DEPTH)
    line = iota((1, size), 1)
    levels, rows, width = water.shape
    start = SIDE_ROWS
    for l in range(levels):
        for j in range(2):
            at = start + 2 * l + j
            store[at : at + 1] = water[l, rows - 1 - j : rows - j]
            store[at + 2 * levels : at + 2 * levels + 1] = water[l, j : j + 1]
    out[...] = store[...].astype(BF16)
    lane = iota((rows, width), 1)
    mixed = jnp.zeros((rows, width), F32)
    for l in range(levels):
        mixed = jnp.where(lane // 4 == l, roll(water[l], 2 + 4 * l, 1), mixed)
    across = jnp.concatenate([mixed, jnp.zeros((width - rows, width), F32)], axis=0).T
    beside = []
    for l in range(levels):
        for j in range(2):
            last = across[4 * l + 1 - j : 4 * l + 2 - j]
            lead = across[4 * l + 2 + j : 4 * l + 3 + j]
            beside.append(jnp.where(line < rows, last, roll(lead, rows, 1)))
    cols_o[...] = jnp.concatenate(beside, axis=0)


def relay_kernel(tiles, place, cols, *refs):
    messages, out = refs[:tiles], refs[tiles]
    for k, message in enumerate(messages):
        out[k * SIDE_ROWS : (k + 1) * SIDE_ROWS] = message[0:SIDE_ROWS]
    levels = cols.shape[0] // 2
    before, after = around(place(), tiles, messages, levels)
    rows = []
    for strip in (before, after):
        rows += [strip[2 * l : 2 * l + 1] for l in range(levels)]
    out[tiles * SIDE_ROWS :] = jnp.concatenate([cols[...]] + rows, axis=0).astype(BF16)


def around(me, tiles, messages, levels):
    before, after = 0.0, 0.0
    for k in range(1, tiles):
        strips = messages[k][SIDE_ROWS : SIDE_ROWS + 4 * levels].astype(F32)
        before = before + strips[: 2 * levels] * flag((me > 0) & ((me ^ k) == me - 1))
        after = after + strips[2 * levels :] * flag((me < tiles - 1) & ((me ^ k) == me + 1))
    return before, after


def remap_forward(chunks, field_rows, side, depth):
    total = None
    for chunk, fields in zip(chunks, field_rows):
        down = chunk[0:side]
        right = chunk[side : side + depth]
        wide = jnp.concatenate(fields, axis=1) if len(fields) > 1 else fields[0]
        part = lax.dot_general(down, wide, (((0,), (0,)), ((), ())), preferred_element_type=F32)
        part = part.astype(BF16)
        width = fields[0].shape[1]
        if len(fields) > 1:
            part = jnp.concatenate(
                [part[:, c * width : (c + 1) * width] for c in range(len(fields))], axis=0
            )
        piece = lax.dot_general(part, right, (((1,), (1,)), ((), ())), preferred_element_type=F32)
        piece = piece.astype(BF16).astype(F32)
        total = piece if total is None else total + piece
    return total


def forcing_kernel(group, side, mass, drag, wind, *refs):
    chunks = refs[:group]
    out, current_o, push_o, store = refs[group:]
    size = mass.shape[0]
    depth = chunks[-1].shape[0] - 3 * side
    fields = [
        [c[side + depth : 2 * side + depth], c[2 * side + depth : 3 * side + depth]] for c in chunks
    ]
    total = remap_forward(chunks, fields, side, depth)
    pushes = []
    for c in range(2):
        current = total[c * size : (c + 1) * size]
        current_o[c] = current
        force = wind[pl.ds(c, size, stride=2), :]
        push = mass[...] * (force + drag[...] * current)
        push_o[c] = push
        pushes.append(push)
    put_side_rims(store, pushes, lambda q: q * 2 * DEPTH)
    names = chunks[0][3 * side + depth :].astype(F32)
    store[NAMES_ROW : NAMES_ROW + 1] = names[0:1]
    message = store[...].astype(BF16)
    for d in range(out.shape[0]):
        out[d] = message


def ocean_kernel(counts, tile_place, member_place, water, mixing, *refs):
    tiles, subs, levs = counts
    members = subs * levs
    messages, relays = refs[:tiles], refs[tiles : tiles + members]
    warm_o, top_o = refs[tiles + members :]
    levels, rows, width = water.shape
    my_tile, me = tile_place(), member_place()
    halo = {}
    halo[-1, 0], halo[1, 0] = around(my_tile, tiles, messages, levels)
    for ds in (-1, 1):
        beyond = me + ds * levs
        inside = (beyond >= 0) & (beyond < members)
        found = 0.0
        for k in range(1, members):
            strip = relays[k][tiles * SIDE_ROWS : tiles * SIDE_ROWS + 4 * levels].astype(F32)
            found = found + strip * flag(inside & ((me ^ k) == beyond))
        beside, corners = found[: 2 * levels], found[2 * levels :]
        if ds > 0:
            beside = roll(beside, -rows, 1)
        halo[0, ds] = beside
        at = width - 1 if ds < 0 else 0
        halo[-1, ds] = corners[:levels, at : at + 1]
        halo[1, ds] = corners[levels:, at : at + 1]
    left_cols = halo[0, -1].T
    right_cols = halo[0, 1].T
    row = iota((rows, width), 0)
    lane = iota((rows, width), 1)
    line = iota((1, width), 1)
    total = None

    def laplacian(x, top, bottom, left, right):
        up = jnp.where(row == 0, top, roll(x, 1, 0))
        down = jnp.where(row == rows - 1, bottom, roll(x, -1, 0))
        west = jnp.where(lane == 0, left, roll(x, 1, 1))
        east = jnp.where(lane == width - 1, right, roll(x, -1, 1))
        return up + down + west + east - 4.0 * x

    for l in range(levels):
        x = water[l]
        near, far = 2 * l, 2 * l + 1
        top, top_far = halo[-1, 0][near : near + 1], halo[-1, 0][far : far + 1]
        bottom, bottom_far = halo[1, 0][near : near + 1], halo[1, 0][far : far + 1]
        left, left_far = left_cols[0:rows, near : near + 1], left_cols[0:rows, far : far + 1]
        right, right_far = right_cols[0:rows, near : near + 1], right_cols[0:rows, far : far + 1]
        corner = {}
        for dt in (-1, 1):
            for ds in (-1, 1):
                corner[dt, ds] = halo[dt, ds][l : l + 1]

        def ring_row(mid, out_row, in_row, dt):
            west = jnp.where(line == 0, corner[dt, -1], roll(mid, 1, 1))
            east = jnp.where(line == width - 1, corner[dt, 1], roll(mid, -1, 1))
            return west + east + out_row + in_row - 4.0 * mid

        def ring_col(mid, out_col, in_col, ds):
            up = jnp.concatenate([corner[-1, ds], mid[:-1]], axis=0)
            down = jnp.concatenate([mid[1:], corner[1, ds]], axis=0)
            return up + down + out_col + in_col - 4.0 * mid

        once = laplacian(x, top, bottom, left, right)
        twice = laplacian(
            once,
            ring_row(top, top_far, x[0:1], -1),
            ring_row(bottom, bottom_far, x[rows - 1 :], 1),
            ring_col(left, left_far, x[:, 0:1], -1),
            ring_col(right, right_far, x[:, width - 1 :], 1),
        )
        warm = x - mixing[...] * twice
        warm_o[l] = warm
        total = warm if total is None else total + warm
    top_o[...] = (total / (levels * levs)).astype(top_o.dtype)


def subcycles_kernel(tiles, members, place, table, viscous, gain, speed, push, push_rims, *refs):
    relays, (out, rims) = refs[:members], refs[members:]
    size = viscous.shape[0]
    me = place()
    for k in range(tiles):
        for m in range(members):
            rims[me ^ (k * members + m)] = relays[m][k * SIDE_ROWS : (k + 1) * SIDE_ROWS]
    half = DEPTH
    high = 2 * DEPTH
    sub = iota((high, size), 0)
    lane = iota((high, size), 1)
    edge = (sub & (half - 1)) == 0
    turn = jnp.where(sub < half, CORIOLIS_TURN, -CORIOLIS_TURN).astype(F32)
    first, last = lane == 0, lane == size - 1

    def load(device, side, mask, with_push=True):
        block = rims[device, side * 2 * high : (side + 1) * 2 * high].astype(F32)
        velocity, both = block[:high] * mask, block[high:]
        if not with_push:
            return velocity
        other = roll(both, half, 0)
        visc = jnp.where(sub < half, both, other)
        scale = jnp.where(sub < half, other, both) * mask
        start = side // 2 * 2 * high
        pushed = push_rims[device, start : start + 2 * high].astype(F32)
        pushed = pushed[:high] if side % 2 == 0 else pushed[high:]
        return [velocity, visc, scale, pushed]

    def follow(device, side):
        name = table[device, side]
        return jnp.where(name >= 0, name, 0), name >= 0

    def step(state, left, right, inner, outer):
        c, visc, scale, pushed = state
        spread = left + right + inner + outer - 4.0 * c
        return scale * (c + visc * spread + pushed + turn * roll(c, half, 0))

    strips = []
    for q in range(4):
        x, has_x = follow(me, q)
        strip = load(x, OPPOSITE[q], flag(has_x))
        sides = []
        for s in LATERAL[q]:
            y, has_y = follow(x, s)
            z, has_z = follow(y, OPPOSITE[q])
            w, has_w = follow(z, OPPOSITE[s])
            sides.append(
                [
                    load(y, OPPOSITE[q], flag(has_y)),
                    load(z, q, flag(has_z)),
                    load(w, q, flag(has_w), with_push=False),
                ]
            )
        strips.append((strip, sides))

    row = iota((size, size), 0)
    col = iota((size, size), 1)
    vx, vy = speed[0], speed[1]
    visc, scale, push_x, push_y = viscous[...], gain[...], push[0], push[1]

    def spread_of(v, north, south, east, west):
        up = jnp.where(row == size - 1, north, roll(v, -1, 0))
        down = jnp.where(row == 0, south, roll(v, 1, 0))
        right = jnp.where(col == size - 1, east, roll(v, -1, 1))
        left = jnp.where(col == 0, west, roll(v, 1, 1))
        return up + down + right + left - 4.0 * v

    for t in range(SUBCYCLES):
        cells = [strip[0] for strip, _ in strips]
        if t < SUBCYCLES - 1:
            mixed = jnp.where(col < half, roll(vx, 1, 1), roll(vy, 1 + half, 1))
            across = mixed.T[0:high]
            own = [
                jnp.where(sub < half, vx[size - 1 :], vy[size - 1 :]),
                jnp.where(sub < half, vx[0:1], vy[0:1]),
                across,
                roll(across, -1, 0),
            ]
            for q in range(4):
                strip, (beyond, before) = strips[q]
                c, y_hi, y_lo = strip[0], beyond[0][0], before[0][0]
                left = jnp.where(first, roll(y_lo, 1, 1), roll(c, 1, 1))
                right = jnp.where(last, roll(y_hi, -1, 1), roll(c, -1, 1))
                inner = jnp.where(edge, own[q], roll(c, 1, 0))
                new_strip = step(strip, left, right, inner, roll(c, -1, 0))
                if t < SUBCYCLES - 2:
                    new_sides = []
                    for i, (y, z, w) in enumerate((beyond, before)):
                        away = 1 if i == 0 else -1
                        boundary = first if i == 0 else last
                        yc, zc = y[0], z[0]
                        toward = jnp.where(boundary, roll(c, away, 1), roll(yc, away, 1))
                        inner = jnp.where(edge, zc, roll(yc, 1, 0))
                        new_y = step(y, toward, roll(yc, -away, 1), inner, roll(yc, -1, 0))
                        new_z = zc
                        if t < SUBCYCLES - 3:
                            toward = jnp.where(boundary, roll(w, away, 1), roll(zc, away, 1))
                            inner = jnp.where(edge, yc, roll(zc, 1, 0))
                            new_z = step(z, toward, roll(zc, -away, 1), inner, roll(zc, -1, 0))
                        new_sides.append((new_y, new_z))
                    for item, (new_y, new_z) in zip((beyond, before), new_sides):
                        item[0][0] = new_y
                        item[1][0] = new_z
                strip[0] = new_strip
        north, south = cells[0], cells[1]
        sides = jnp.where(edge, cells[2], roll(cells[3], 1, 0)).T
        east_x, west_x = sides[:, 0:1], sides[:, 1:2]
        east_y, west_y = sides[:, half : half + 1], sides[:, half + 1 : half + 2]
        spread_x = spread_of(vx, north[0:1], south[0:1], east_x, west_x)
        spread_y = spread_of(
            vy, north[half : half + 1], south[half : half + 1], east_y, west_y
        )
        new_x = scale * (vx + visc * spread_x + push_x + CORIOLIS_TURN * vy)
        new_y = scale * (vy + visc * spread_y + push_y - CORIOLIS_TURN * vx)
        vx, vy = new_x, new_y
    out[0] = vx
    out[1] = vy


def back_kernel(group, side, drag, conduct, current, speed, *refs):
    chunks = refs[:group]
    tops = refs[group : 2 * group]
    outs = refs[2 * group :]
    size = drag.shape[0]
    depth = chunks[-1].shape[0] - 3 * side
    warm = remap_forward(chunks, [[t[...]] for t in tops], side, depth)
    heat = conduct[...] * warm
    fluxes = [heat.astype(BF16)]
    for c in range(2):
        fluxes.append((drag[...] * (speed[c] - current[c])).astype(BF16))
    wide = jnp.concatenate(fluxes, axis=1)
    for chunk, out in zip(chunks, outs):
        part = jnp.dot(chunk[0:side], wide, preferred_element_type=F32).astype(BF16)
        part = jnp.concatenate([part[:, c * size : (c + 1) * size] for c in range(3)], axis=0)
        reply = jnp.dot(part, chunk[side : side + depth], preferred_element_type=F32)
        out[...] = reply.astype(BF16)


def finish_kernel(warm, currents, speed, *refs):
    outs, (flat, heat_v, current_v, left) = refs[-7:-4], refs[-4:]
    replies = refs[:-7]
    flat_o, heat_o, current_o = outs
    size = speed.shape[1]
    copies = [
        pltpu.make_async_copy(source, target, left.at[i])
        for i, (source, target) in enumerate(
            ((flat, flat_o), (heat_v, heat_o), (current_v, current_o))
        )
    ]
    for c in range(2):
        flat[pl.ds(c, size, stride=2), :] = speed[c]
    copies[0].start()
    total = replies[0][...].astype(F32)
    for reply in replies[1:]:
        total = total + reply[...].astype(F32)
    side = currents.shape[1]
    heat = THERMAL_DIFFUSE * total[0:side]
    for l in range(warm.shape[0]):
        heat_v[l] = warm[l] + heat
    copies[1].start()
    for c in range(2):
        current_v[c] = currents[c] + STRESS_MIXING * total[(c + 1) * side : (c + 2) * side]
    copies[2].start()
    for copy in copies:
        copy.wait()


def shards(
    water_heat_state,
    diffusion_coefficient,
    upper_current_vector,
    remap_blocks,
    remap_rows,
    remap_cols,
    neighbors,
    thickness,
    concentration,
    ice_velocity,
    wind_stress,
):
    tile_count, sub_count, lev_count = (lax.axis_size(a) for a in ("tile", "sub", "lev"))
    group = sub_count * lev_count
    devices = tile_count * group
    group_axes = ("sub", "lev")
    member_axes = ("tile", "sub", "lev")
    levels, side, width = water_heat_state.shape
    pairs, size = remap_rows.shape[1:3]
    categories = thickness.shape[2]

    def tile_place():
        return lax.axis_index("tile")

    def member_place():
        return lax.axis_index("sub") * lev_count + lax.axis_index("lev")

    def device_place():
        return lax.axis_index("tile") * group + member_place()

    def swap(value, axes, count):
        return [value] + [
            lax.ppermute(value, axes, [(i, i ^ k) for i in range(count)]) for k in range(1, count)
        ]

    def swap_each(values):
        return [values[0]] + [
            lax.ppermute(values[k], group_axes, [(i, i ^ k) for i in range(group)])
            for k in range(1, group)
        ]

    def shape(*dims, dtype=F32):
        return jax.ShapeDtypeStruct(dims, dtype)

    def interleaved(value):
        return value.reshape(2, size, size).transpose(1, 0, 2).reshape(2 * size, size)

    plane = shape(size, size)
    planes = shape(2, size, size)
    wind = interleaved(wind_stress)

    chunk_rows = 3 * side + width
    sent = call(
        functools.partial(forward_kernel, (devices, group, member_place)),
        [shape(chunk_rows + TILE_ROWS, width, dtype=BF16)]
        + [shape(chunk_rows, width, dtype=BF16)] * (group - 1),
        (neighbors, remap_blocks, remap_rows[0].swapaxes(1, 2), remap_cols[0], upper_current_vector),
        scratch=[
            pltpu.SMEM(neighbors.shape, jnp.int32),
            pltpu.SMEM((1, pairs), jnp.int32),
            pltpu.VMEM((2, side, width), F32),
            pltpu.VMEM((pairs, side, size), BF16),
            pltpu.VMEM((pairs, size, width), BF16),
            pltpu.VMEM((1 if pairs == group else group, 2 * side, width), BF16),
            pltpu.VMEM((TILE_ROWS, width), BF16),
            pltpu.SemaphoreType.DMA((5,)),
            pltpu.SemaphoreType.DMA((3 * group + 1,)),
        ],
        hbm=(0, 1, 2, 3, 4),
        grant=60 * 2**20,
        micros=10,
    )
    chunks = swap_each(sent)

    message, cols, viscous, gain, step_mass, drag, conduct, speed = call(
        rims_kernel,
        [shape(SIDE_ROWS + 4 * levels, size, dtype=BF16), shape(2 * levels, width)]
        + [plane] * 5
        + [planes],
        (
            thickness.reshape(categories, size, size),
            concentration.reshape(categories, size, size),
            interleaved(ice_velocity),
            water_heat_state,
        ),
        scratch=[pltpu.VMEM((SIDE_ROWS + 4 * levels, size), F32)],
    )
    messages = swap(message, "tile", tile_count)

    push_message, current_ice, push = call(
        functools.partial(forcing_kernel, group, side),
        [shape(devices, PUSH_ROWS, size, dtype=BF16), planes, planes],
        (step_mass, drag, wind, *chunks),
        scratch=[pltpu.VMEM((PUSH_ROWS, size), F32)],
    )
    cols, push_message = lax.optimization_barrier((cols, push_message))
    push_rims = lax.all_to_all(push_message, member_axes, split_axis=0, concat_axis=0, tiled=True)

    relay = call(
        functools.partial(relay_kernel, tile_count, tile_place),
        shape(tile_count * SIDE_ROWS + 4 * levels, size, dtype=BF16),
        (cols, *messages),
    )
    relays = swap(relay, group_axes, group)

    warm, top = call(
        functools.partial(
            ocean_kernel, (tile_count, sub_count, lev_count), tile_place, member_place
        ),
        [
            shape(levels, side, width),
            shape(side, width, dtype=BF16 if lev_count == 1 else F32),
        ],
        (water_heat_state, diffusion_coefficient, *messages, *relays),
    )
    if lev_count > 1:
        top = lax.psum(top, "lev").astype(BF16)
    tops = swap(top, group_axes, group)

    push_rims, _ = lax.optimization_barrier((push_rims, top))
    names = push_rims[:, NAMES_ROW, 0:8].astype(jnp.int32)
    table = names[:, 0:4] * 128 + names[:, 4:8]
    speed = call(
        functools.partial(subcycles_kernel, tile_count, group, device_place),
        planes,
        (table, viscous, gain, speed, push, push_rims, *relays),
        scratch=[pltpu.VMEM((devices, SIDE_ROWS, size), BF16)],
        smem=(0,),
    )

    replies = call(
        functools.partial(back_kernel, group, side),
        [shape(3 * side, width, dtype=BF16)] * group,
        (drag, conduct, current_ice, speed, *chunks, *tops),
    )
    replies = swap_each(replies)
    if lev_count > 1:
        replies = [lax.psum(sum(r.astype(F32) for r in replies), "lev")]
    flat, heat, current = call(
        finish_kernel,
        [shape(2 * size, size), shape(levels, side, width), shape(2, side, width)],
        (warm, upper_current_vector, speed, *replies),
        scratch=[
            pltpu.VMEM((2 * size, size), F32),
            pltpu.VMEM((levels, side, width), F32),
            pltpu.VMEM((2, side, width), F32),
            pltpu.SemaphoreType.DMA((3,)),
        ],
        out_space=pltpu.HBM,
    )
    velocity = flat.reshape(size, 2, size).transpose(1, 0, 2).reshape(1, 1, 2, size * size)
    return heat, current, velocity


def solution(mesh):
    member = ("tile", "sub", "lev")
    whole = ("copies",) + member
    ice = P(None, whole, None, None)
    water = P("lev", ("copies", "tile"), "sub")
    current = P(None, ("copies", "tile"), "sub")
    return jax.shard_map(
        shards,
        mesh=mesh,
        in_specs=(
            water,
            P("tile", "sub"),
            current,
            P(member, None),
            P(member, None, None, None),
            P(member, None, None, None),
            P(None, member, None),
            ice,
            ice,
            ice,
            ice,
        ),
        out_specs=(water, current, ice),
        check_vma=False,
    )
```

```python
import functools

import jax
import jax.numpy as jnp
from jax import lax
from jax.experimental import pallas as pl
from jax.experimental.pallas import tpu as pltpu
from jax.sharding import PartitionSpec as P

SUBCYCLES = 4
STRENGTH_DECAY = 5.0
VISCOUS_STEP = 0.24
SUBCYCLE_STEP = 0.5
CORIOLIS_TURN = 0.1
BASE_MASS = 0.5
HEAT_RATE = 0.2
THIN_ICE = 0.1
THERMAL_DIFFUSE = 0.5
STRESS_MIXING = 0.5

OPPOSITE = (1, 0, 3, 2)
LATERAL = ((2, 3), (2, 3), (0, 1), (0, 1))
DEPTH = SUBCYCLES
SIDE_ROWS = 16 * DEPTH
PUSH_ROWS = 8 * DEPTH
BLOCK_ROWS = SIDE_ROWS + PUSH_ROWS
NAMES_ROW = 2 * DEPTH - 1
CORNER_ROWS = tuple(DEPTH * i - 1 for i in (1, 3, 4, 5, 6, 7, 8))
TILE_ROWS = 16
F32 = jnp.float32
BF16 = jnp.bfloat16
VMEM_LIMIT = 16 * 1024 * 1024
FLOPS_PER_MICRO = 1.15e9


def call(kernel, outs, args, scratch=(), smem=(), hbm=(), out_space=pltpu.VMEM, grant=VMEM_LIMIT, micros=0.01):
    def space(i):
        return pltpu.SMEM if i in smem else pltpu.HBM if i in hbm else pltpu.VMEM

    specs = [pl.BlockSpec(memory_space=space(i)) for i in range(len(args))]
    size = sum(a.size * a.dtype.itemsize for a in args)
    return pl.pallas_call(
        kernel,
        out_shape=outs,
        in_specs=specs,
        out_specs=jax.tree.map(lambda _: pl.BlockSpec(memory_space=out_space), outs),
        scratch_shapes=list(scratch),
        compiler_params=pltpu.CompilerParams(vmem_limit_bytes=grant),
        cost_estimate=pl.CostEstimate(
            flops=int(micros * FLOPS_PER_MICRO), bytes_accessed=size, transcendentals=0
        ),
    )(*args)


def iota(shape, axis):
    return lax.broadcasted_iota(jnp.int32, shape, axis)


def roll(x, shift, axis):
    return pltpu.roll(x, shift % x.shape[axis], axis)


def flag(condition):
    return jnp.where(condition, 1.0, 0.0).astype(F32)


def ocean_columns(water):
    levels, rows, width = water.shape
    lane = iota((rows, width), 1)
    line = iota((1, width), 1)
    mixed = jnp.zeros((rows, width), F32)
    for l in range(levels):
        mixed = jnp.where(lane // 4 == l, roll(water[l], 2 + 4 * l, 1), mixed)
    across = jnp.concatenate([mixed, jnp.zeros((width - rows, width), F32)], axis=0).T
    beside = []
    for l in range(levels):
        for j in range(2):
            last = across[4 * l + 1 - j : 4 * l + 2 - j]
            lead = across[4 * l + 2 + j : 4 * l + 3 + j]
            beside.append(jnp.where(line < rows, last, roll(lead, rows, 1)))
    return beside


def forward_kernel(group, links_h, blocks_h, rows_h, cols_h, currents_h, water_h, *refs):
    devices, members, place = group
    outs, scratch = refs[:members], refs[members:]
    links, blocks, currents, rows, cols, water, fields, tail, arrived, left = scratch
    pairs, side, width = rows_h.shape
    depth = cols_h.shape[1]
    loads = [
        pltpu.make_async_copy(source, target, arrived.at[i])
        for i, (source, target) in enumerate(
            (
                (links_h, links),
                (blocks_h, blocks),
                (currents_h, currents),
                (rows_h, rows),
                (cols_h, cols),
                (water_h, water),
            )
        )
    ]
    for load in loads:
        load.start()
    for load in loads:
        load.wait()
    me = place()
    owners = [lax.rem(lax.rem(blocks[0, m], devices), members) for m in range(pairs)]
    lane = iota((1, width), 1)
    numbers = jnp.zeros((1, width), F32)
    for q in range(4):
        numbers = jnp.where(lane == q, (links[0, 0, q] >> 7).astype(F32), numbers)
        numbers = jnp.where(lane == 4 + q, (links[0, 0, q] & 127).astype(F32), numbers)
    ends = ocean_columns(water) + [numbers]
    blank = jnp.zeros((tail.shape[0] - len(ends), width), F32)
    tail[...] = jnp.concatenate(ends + [blank], axis=0).astype(BF16)
    copies = []
    for k, out in enumerate(outs):
        partner = me ^ k
        pair, found = jnp.int32(0), jnp.int32(0)
        for m in range(pairs):
            pair = jnp.where(owners[m] == partner, m, pair)
            found = jnp.where(owners[m] == partner, 1, found)
        copies.append(
            pltpu.make_async_copy(rows.at[pair], out.at[pl.ds(0, side)], left.at[3 * k])
        )
        copies.append(
            pltpu.make_async_copy(cols.at[pair], out.at[pl.ds(side, depth)], left.at[3 * k + 1])
        )
        if pairs < members:
            keep = jnp.where(found > 0, 1.0, 0.0).astype(F32)
        else:
            keep = None
        copies.append(
            pltpu.make_async_copy(
                tail, out.at[pl.ds(3 * side + depth, tail.shape[0])], left.at[3 * members + k]
            )
        )
        for copy in copies[-3:]:
            copy.start()
        if k == 0 or keep is not None:
            for c in range(2):
                field = currents[c] if keep is None else currents[c] * keep
                fields[0 if keep is None else k, c * side : (c + 1) * side] = field.astype(BF16)
        copies.append(
            pltpu.make_async_copy(
                fields.at[0 if keep is None else k],
                out.at[pl.ds(side + depth, 2 * side)],
                left.at[3 * k + 2],
            )
        )
        copies[-1].start()
    for copy in copies:
        copy.wait()


def put_side_rims(store, planes, at):
    size = planes[0].shape[0]
    lane = iota((size, size), 1)
    mixed = jnp.zeros((size, size), F32)
    for i, plane in enumerate(planes):
        turned = roll(plane, DEPTH + 2 * DEPTH * i, 1)
        mixed = jnp.where(lane // (2 * DEPTH) == i, turned, mixed)
    across = mixed.T
    for i, plane in enumerate(planes):
        for k in range(DEPTH):
            base = i * DEPTH + k
            store[at(0) + base : at(0) + base + 1] = plane[size - 1 - k : size - k]
            store[at(1) + base : at(1) + base + 1] = plane[k : k + 1]
            east = 2 * DEPTH * i + DEPTH - 1 - k
            west = 2 * DEPTH * i + DEPTH + k
            store[at(2) + base : at(2) + base + 1] = across[east : east + 1]
            store[at(3) + base : at(3) + base + 1] = across[west : west + 1]


def rims_kernel(
    thick, conc, ice, water, out, viscous_o, gain_o, mass_o, drag_o, conduct_o,
    speed_o, store,
):
    size = thick.shape[1]
    cover = jnp.zeros((size, size), F32)
    volume = jnp.zeros((size, size), F32)
    conduct = jnp.zeros((size, size), F32)
    for c in range(thick.shape[0]):
        h, a = thick[c], conc[c]
        cover = cover + a
        volume = volume + a * h
        conduct = conduct + a / (h + THIN_ICE)
    mass = volume + BASE_MASS
    viscous = VISCOUS_STEP * (volume * jnp.exp(-STRENGTH_DECAY * (1.0 - cover))) / mass
    step_mass = SUBCYCLE_STEP / mass
    gain = 1.0 / (1.0 + step_mass * cover)
    speed_x = ice[pl.ds(0, size, stride=2), :]
    speed_y = ice[pl.ds(1, size, stride=2), :]
    viscous_o[...] = viscous
    gain_o[...] = gain
    mass_o[...] = step_mass
    drag_o[...] = cover
    conduct_o[...] = -HEAT_RATE * conduct
    speed_o[0] = speed_x
    speed_o[1] = speed_y
    put_side_rims(store, [speed_x, speed_y, viscous, gain], lambda side: side * 4 * DEPTH)
    levels, rows, width = water.shape
    start = SIDE_ROWS
    for l in range(levels):
        for j in range(2):
            at = start + 2 * l + j
            store[at : at + 1] = water[l, rows - 1 - j : rows - j]
            store[at + 2 * levels : at + 2 * levels + 1] = water[l, j : j + 1]
    out[...] = store[...].astype(BF16)


def relay_kernel(tiles, *refs):
    messages, pushes, out = refs[:tiles], refs[tiles : 2 * tiles], refs[2 * tiles]
    for k in range(tiles):
        at = k * BLOCK_ROWS
        out[at : at + SIDE_ROWS] = messages[k][0:SIDE_ROWS]
        out[at + SIDE_ROWS : at + BLOCK_ROWS] = pushes[k][...]


def nearby(me, members, distance, arrays):
    at = me + distance
    inside = (at >= 0) & (at < members)
    found = 0.0
    for k in range(1, members):
        found = found + arrays[k].astype(F32) * flag(inside & ((me ^ k) == at))
    return found


def remap_forward(chunks, field_rows, side, depth):
    total = None
    for chunk, fields in zip(chunks, field_rows):
        down = chunk[0:side]
        right = chunk[side : side + depth]
        wide = jnp.concatenate(fields, axis=1) if len(fields) > 1 else fields[0]
        part = lax.dot_general(down, wide, (((0,), (0,)), ((), ())), preferred_element_type=F32)
        part = part.astype(BF16)
        width = fields[0].shape[1]
        if len(fields) > 1:
            part = jnp.concatenate(
                [part[:, c * width : (c + 1) * width] for c in range(len(fields))], axis=0
            )
        piece = lax.dot_general(part, right, (((1,), (1,)), ((), ())), preferred_element_type=F32)
        piece = piece.astype(BF16).astype(F32)
        total = piece if total is None else total + piece
    return total


def forcing_kernel(group, side, levels, subs, place, mass, drag, wind, *refs):
    chunks = refs[:group][::-1]
    out, current_o, push_o, store = refs[group:]
    size = mass.shape[0]
    depth = chunks[0].shape[1]
    fields = [
        [c[side + depth : 2 * side + depth], c[2 * side + depth : 3 * side + depth]] for c in chunks
    ]
    total = remap_forward(chunks, fields, side, depth)
    pushes = []
    for c in range(2):
        current = total[c * size : (c + 1) * size]
        current_o[c] = current
        force = wind[pl.ds(c, size, stride=2), :]
        push = mass[...] * (force + drag[...] * current)
        push_o[c] = push
        pushes.append(push)
    put_side_rims(store, pushes, lambda q: q * 2 * DEPTH)
    tail = [c[3 * side + depth :] for c in chunks]
    store[NAMES_ROW : NAMES_ROW + 1] = tail[0].astype(F32)[2 * levels : 2 * levels + 1]
    me, step = place(), group // subs
    left, right = (nearby(me, group, d * step, tail) for d in (-1, 1))
    line = iota((1, size), 1)
    for l in range(levels):
        near = slice(2 * l, 2 * l + 1)
        store[CORNER_ROWS[l] : CORNER_ROWS[l] + 1] = jnp.where(line < side, left[near], right[near])
    out[...] = store[...].astype(BF16)


def ocean_kernel(counts, tile_place, member_place, water, mixing, *refs):
    tiles, subs, levs = counts
    members = subs * levs
    messages, pushes = refs[:tiles], refs[tiles : 2 * tiles]
    chunks, (warm_o, top_o) = refs[2 * tiles : -2], refs[-2:]
    levels, rows, width = water.shape
    my_tile, me = tile_place(), member_place()
    halo = {}
    strips = [m[SIDE_ROWS : SIDE_ROWS + 4 * levels] for m in messages]
    rims = [p[...] for p in pushes]
    tails = [c[3 * rows + width :] for c in chunks]
    for dt in (-1, 1):
        beyond = nearby(my_tile, tiles, dt, strips)
        halo[dt, 0] = beyond[: 2 * levels] if dt < 0 else beyond[2 * levels :]
        corners = nearby(my_tile, tiles, dt, rims)
        at = rows - 1 if dt < 0 else 0
        for ds in (-1, 1):
            lane_at = at if ds < 0 else rows + at
            halo[dt, ds] = [
                corners[CORNER_ROWS[l] : CORNER_ROWS[l] + 1, lane_at : lane_at + 1]
                for l in range(levels)
            ]
    for ds in (-1, 1):
        beside = nearby(me, members, ds * levs, tails)[: 2 * levels]
        halo[0, ds] = roll(beside, -rows, 1) if ds > 0 else beside
    left_cols = halo[0, -1].T
    right_cols = halo[0, 1].T
    row = iota((rows, width), 0)
    lane = iota((rows, width), 1)
    line = iota((1, width), 1)
    total = None

    def laplacian(x, top, bottom, left, right):
        up = jnp.where(row == 0, top, roll(x, 1, 0))
        down = jnp.where(row == rows - 1, bottom, roll(x, -1, 0))
        west = jnp.where(lane == 0, left, roll(x, 1, 1))
        east = jnp.where(lane == width - 1, right, roll(x, -1, 1))
        return up + down + west + east - 4.0 * x

    for l in range(levels):
        x = water[l]
        near, far = 2 * l, 2 * l + 1
        top, top_far = halo[-1, 0][near : near + 1], halo[-1, 0][far : far + 1]
        bottom, bottom_far = halo[1, 0][near : near + 1], halo[1, 0][far : far + 1]
        left, left_far = left_cols[0:rows, near : near + 1], left_cols[0:rows, far : far + 1]
        right, right_far = right_cols[0:rows, near : near + 1], right_cols[0:rows, far : far + 1]
        corner = {}
        for dt in (-1, 1):
            for ds in (-1, 1):
                corner[dt, ds] = halo[dt, ds][l]

        def ring_row(mid, out_row, in_row, dt):
            west = jnp.where(line == 0, corner[dt, -1], roll(mid, 1, 1))
            east = jnp.where(line == width - 1, corner[dt, 1], roll(mid, -1, 1))
            return west + east + out_row + in_row - 4.0 * mid

        def ring_col(mid, out_col, in_col, ds):
            up = jnp.concatenate([corner[-1, ds], mid[:-1]], axis=0)
            down = jnp.concatenate([mid[1:], corner[1, ds]], axis=0)
            return up + down + out_col + in_col - 4.0 * mid

        once = laplacian(x, top, bottom, left, right)
        twice = laplacian(
            once,
            ring_row(top, top_far, x[0:1], -1),
            ring_row(bottom, bottom_far, x[rows - 1 :], 1),
            ring_col(left, left_far, x[:, 0:1], -1),
            ring_col(right, right_far, x[:, width - 1 :], 1),
        )
        warm = x - mixing[...] * twice
        warm_o[l] = warm
        total = warm if total is None else total + warm
    top_o[...] = (total / (levels * levs)).astype(top_o.dtype)


def subcycles_kernel(tiles, members, table, viscous, gain, speed, push, *refs):
    relays, (out, rims) = refs[:members], refs[members:]
    size = viscous.shape[0]
    for k in range(tiles):
        for m in range(members):
            rims[k * members + m] = relays[m][k * BLOCK_ROWS : (k + 1) * BLOCK_ROWS]
    half = DEPTH
    high = 2 * DEPTH
    sub = iota((high, size), 0)
    lane = iota((high, size), 1)
    edge = (sub & (half - 1)) == 0
    turn = jnp.where(sub < half, CORIOLIS_TURN, -CORIOLIS_TURN).astype(F32)
    first, last = lane == 0, lane == size - 1

    def load(device, side, mask, with_push=True):
        block = rims[device, side * 2 * high : (side + 1) * 2 * high].astype(F32)
        velocity, both = block[:high] * mask, block[high:]
        if not with_push:
            return velocity
        other = roll(both, half, 0)
        visc = jnp.where(sub < half, both, other)
        scale = jnp.where(sub < half, other, both) * mask
        start = SIDE_ROWS + side // 2 * 2 * high
        pushed = rims[device, start : start + 2 * high].astype(F32)
        pushed = pushed[:high] if side % 2 == 0 else pushed[high:]
        return [velocity, visc, scale, pushed]

    def follow(device, side):
        name = table[device, side]
        return jnp.where(name >= 0, name, 0), name >= 0

    def step(state, left, right, inner, outer):
        c, visc, scale, pushed = state
        spread = left + right + inner + outer - 4.0 * c
        return scale * (c + visc * spread + pushed + turn * roll(c, half, 0))

    strips = []
    for q in range(4):
        x, has_x = follow(0, q)
        strip = load(x, OPPOSITE[q], flag(has_x))
        sides = []
        for s in LATERAL[q]:
            y, has_y = follow(x, s)
            z, has_z = follow(y, OPPOSITE[q])
            w, has_w = follow(z, OPPOSITE[s])
            sides.append(
                [
                    load(y, OPPOSITE[q], flag(has_y)),
                    load(z, q, flag(has_z)),
                    load(w, q, flag(has_w), with_push=False),
                ]
            )
        strips.append((strip, sides))

    row = iota((size, size), 0)
    col = iota((size, size), 1)
    vx, vy = speed[0], speed[1]
    visc, scale, push_x, push_y = viscous[...], gain[...], push[0], push[1]

    def spread_of(v, north, south, east, west):
        up = jnp.where(row == size - 1, north, roll(v, -1, 0))
        down = jnp.where(row == 0, south, roll(v, 1, 0))
        right = jnp.where(col == size - 1, east, roll(v, -1, 1))
        left = jnp.where(col == 0, west, roll(v, 1, 1))
        return up + down + right + left - 4.0 * v

    for t in range(SUBCYCLES):
        cells = [strip[0] for strip, _ in strips]
        if t < SUBCYCLES - 1:
            mixed = jnp.where(col < half, roll(vx, 1, 1), roll(vy, 1 + half, 1))
            across = mixed.T[0:high]
            own = [
                jnp.where(sub < half, vx[size - 1 :], vy[size - 1 :]),
                jnp.where(sub < half, vx[0:1], vy[0:1]),
                across,
                roll(across, -1, 0),
            ]
            for q in range(4):
                strip, (beyond, before) = strips[q]
                c, y_hi, y_lo = strip[0], beyond[0][0], before[0][0]
                left = jnp.where(first, roll(y_lo, 1, 1), roll(c, 1, 1))
                right = jnp.where(last, roll(y_hi, -1, 1), roll(c, -1, 1))
                inner = jnp.where(edge, own[q], roll(c, 1, 0))
                new_strip = step(strip, left, right, inner, roll(c, -1, 0))
                if t < SUBCYCLES - 2:
                    new_sides = []
                    for i, (y, z, w) in enumerate((beyond, before)):
                        away = 1 if i == 0 else -1
                        boundary = first if i == 0 else last
                        yc, zc = y[0], z[0]
                        toward = jnp.where(boundary, roll(c, away, 1), roll(yc, away, 1))
                        inner = jnp.where(edge, zc, roll(yc, 1, 0))
                        new_y = step(y, toward, roll(yc, -away, 1), inner, roll(yc, -1, 0))
                        new_z = zc
                        if t < SUBCYCLES - 3:
                            toward = jnp.where(boundary, roll(w, away, 1), roll(zc, away, 1))
                            inner = jnp.where(edge, yc, roll(zc, 1, 0))
                            new_z = step(z, toward, roll(zc, -away, 1), inner, roll(zc, -1, 0))
                        new_sides.append((new_y, new_z))
                    for item, (new_y, new_z) in zip((beyond, before), new_sides):
                        item[0][0] = new_y
                        item[1][0] = new_z
                strip[0] = new_strip
        north, south = cells[0], cells[1]
        sides = jnp.where(edge, cells[2], roll(cells[3], 1, 0)).T
        east_x, west_x = sides[:, 0:1], sides[:, 1:2]
        east_y, west_y = sides[:, half : half + 1], sides[:, half + 1 : half + 2]
        spread_x = spread_of(vx, north[0:1], south[0:1], east_x, west_x)
        spread_y = spread_of(
            vy, north[half : half + 1], south[half : half + 1], east_y, west_y
        )
        new_x = scale * (vx + visc * spread_x + push_x + CORIOLIS_TURN * vy)
        new_y = scale * (vy + visc * spread_y + push_y - CORIOLIS_TURN * vx)
        vx, vy = new_x, new_y
    out[0] = vx
    out[1] = vy


def back_kernel(group, side, drag, conduct, current, speed, *refs):
    chunks = refs[:group]
    tops = refs[group : 2 * group]
    outs = refs[2 * group :]
    size = drag.shape[0]
    depth = chunks[0].shape[1]
    warm = remap_forward(chunks, [[t[...]] for t in tops], side, depth)
    heat = conduct[...] * warm
    fluxes = [heat.astype(BF16)]
    for c in range(2):
        fluxes.append((drag[...] * (speed[c] - current[c])).astype(BF16))
    wide = jnp.concatenate(fluxes, axis=1)
    for chunk, out in zip(chunks, outs):
        part = jnp.dot(chunk[0:side], wide, preferred_element_type=F32).astype(BF16)
        part = jnp.concatenate([part[:, c * size : (c + 1) * size] for c in range(3)], axis=0)
        reply = jnp.dot(part, chunk[side : side + depth], preferred_element_type=F32)
        out[...] = reply.astype(BF16)


def finish_kernel(warm, currents, speed, *refs):
    outs, (flat, heat_v, current_v, left) = refs[-7:-4], refs[-4:]
    replies = refs[:-7]
    flat_o, heat_o, current_o = outs
    size = speed.shape[1]
    copies = [
        pltpu.make_async_copy(source, target, left.at[i])
        for i, (source, target) in enumerate(
            ((flat, flat_o), (heat_v, heat_o), (current_v, current_o))
        )
    ]
    for c in range(2):
        flat[pl.ds(c, size, stride=2), :] = speed[c]
    copies[0].start()
    total = replies[0][...].astype(F32)
    for reply in replies[1:]:
        total = total + reply[...].astype(F32)
    side = currents.shape[1]
    heat = THERMAL_DIFFUSE * total[0:side]
    for l in range(warm.shape[0]):
        heat_v[l] = warm[l] + heat
    copies[1].start()
    for c in range(2):
        current_v[c] = currents[c] + STRESS_MIXING * total[(c + 1) * side : (c + 2) * side]
    copies[2].start()
    for copy in copies:
        copy.wait()


def shards(
    water_heat_state,
    diffusion_coefficient,
    upper_current_vector,
    remap_blocks,
    remap_rows,
    remap_cols,
    neighbors,
    thickness,
    concentration,
    ice_velocity,
    wind_stress,
):
    tile_count, sub_count, lev_count = (lax.axis_size(a) for a in ("tile", "sub", "lev"))
    group = sub_count * lev_count
    devices = tile_count * group
    group_axes = ("sub", "lev")
    member_axes = ("tile", "sub", "lev")
    levels, side, width = water_heat_state.shape
    pairs, size = remap_rows.shape[1:3]
    categories = thickness.shape[2]

    def tile_place():
        return lax.axis_index("tile")

    def member_place():
        return lax.axis_index("sub") * lev_count + lax.axis_index("lev")

    def device_place():
        return lax.axis_index("tile") * group + member_place()

    def far_first(count):
        return [*range(2, count), 1]

    def swap(value, axes, count):
        got = {0: value}
        for k in far_first(count):
            got[k] = lax.ppermute(value, axes, [(i, i ^ k) for i in range(count)])
        return [got[k] for k in range(count)]

    def swap_each(values):
        got = {0: values[0]}
        for k in far_first(group):
            got[k] = lax.ppermute(values[k], group_axes, [(i, i ^ k) for i in range(group)])
        return [got[k] for k in range(group)]

    def shape(*dims, dtype=F32):
        return jax.ShapeDtypeStruct(dims, dtype)

    def interleaved(value):
        return value.reshape(2, size, size).transpose(1, 0, 2).reshape(2 * size, size)

    plane = shape(size, size)
    planes = shape(2, size, size)
    wind = interleaved(wind_stress)

    tail_rows = -(-(2 * levels + 1) // TILE_ROWS) * TILE_ROWS
    chunk_rows = 3 * side + width + tail_rows
    sent = call(
        functools.partial(forward_kernel, (devices, group, member_place)),
        [shape(chunk_rows, width, dtype=BF16)] * group,
        (
            neighbors,
            remap_blocks,
            remap_rows[0].swapaxes(1, 2),
            remap_cols[0],
            upper_current_vector,
            water_heat_state,
        ),
        scratch=[
            pltpu.SMEM(neighbors.shape, jnp.int32),
            pltpu.SMEM((1, pairs), jnp.int32),
            pltpu.VMEM((2, side, width), F32),
            pltpu.VMEM((pairs, side, size), BF16),
            pltpu.VMEM((pairs, size, width), BF16),
            pltpu.VMEM((levels, side, width), F32),
            pltpu.VMEM((1 if pairs == group else group, 2 * side, width), BF16),
            pltpu.VMEM((tail_rows, width), BF16),
            pltpu.SemaphoreType.DMA((6,)),
            pltpu.SemaphoreType.DMA((4 * group,)),
        ],
        hbm=(0, 1, 2, 3, 4, 5),
        grant=60 * 2**20,
        micros=10,
    )
    chunks = swap_each(sent)

    message, viscous, gain, step_mass, drag, conduct, speed = call(
        rims_kernel,
        [shape(SIDE_ROWS + 4 * levels, size, dtype=BF16)] + [plane] * 5 + [planes],
        (
            thickness.reshape(categories, size, size),
            concentration.reshape(categories, size, size),
            interleaved(ice_velocity),
            water_heat_state,
        ),
        scratch=[pltpu.VMEM((SIDE_ROWS + 4 * levels, size), F32)],
    )
    messages = swap(message, "tile", tile_count)

    forcing_drag, _ = lax.optimization_barrier((drag, messages[2:]))
    push_message, current_ice, push = call(
        functools.partial(forcing_kernel, group, side, levels, sub_count, member_place),
        [shape(PUSH_ROWS, size, dtype=BF16), planes, planes],
        (step_mass, forcing_drag, wind, *chunks[::-1]),
        scratch=[pltpu.VMEM((PUSH_ROWS, size), F32)],
    )
    push_messages = swap(push_message, "tile", tile_count)

    relay = call(
        functools.partial(relay_kernel, tile_count),
        shape(tile_count * BLOCK_ROWS, size, dtype=BF16),
        (*messages, *push_messages),
    )
    relays = swap(relay, group_axes, group)

    mixing, _ = lax.optimization_barrier((diffusion_coefficient, relay))
    warm, top = call(
        functools.partial(
            ocean_kernel, (tile_count, sub_count, lev_count), tile_place, member_place
        ),
        [shape(levels, side, width), shape(side, width, dtype=BF16 if lev_count == 1 else F32)],
        (water_heat_state, mixing, *messages, *push_messages, *chunks),
    )
    if lev_count > 1:
        top = lax.psum(top, "lev").astype(BF16)
    tops = swap(top, group_axes, group)

    names = jnp.stack(
        [r.reshape(tile_count, BLOCK_ROWS, size)[:, SIDE_ROWS + NAMES_ROW, 0:8] for r in relays],
        axis=1,
    )
    names = names.reshape(devices, 8).astype(jnp.int32)
    table = names[:, 0:4] * 128 + names[:, 4:8]
    table = jnp.where(table < 0, -1, table ^ device_place())
    push, _ = lax.optimization_barrier((push, top))
    speed = call(
        functools.partial(subcycles_kernel, tile_count, group),
        planes,
        (table, viscous, gain, speed, push, *relays),
        scratch=[pltpu.VMEM((devices, BLOCK_ROWS, size), BF16)],
        smem=(0,),
    )

    replies = call(
        functools.partial(back_kernel, group, side),
        [shape(3 * side, width, dtype=BF16)] * group,
        (drag, conduct, current_ice, speed, *chunks, *tops),
    )
    replies = swap_each(replies)
    if lev_count > 1:
        replies = [lax.psum(sum(r.astype(F32) for r in replies), "lev")]
    flat, heat, current = call(
        finish_kernel,
        [shape(2 * size, size), shape(levels, side, width), shape(2, side, width)],
        (warm, upper_current_vector, speed, *replies[::-1]),
        scratch=[
            pltpu.VMEM((2 * size, size), F32),
            pltpu.VMEM((levels, side, width), F32),
            pltpu.VMEM((2, side, width), F32),
            pltpu.SemaphoreType.DMA((3,)),
        ],
        out_space=pltpu.HBM,
    )
    velocity = flat.reshape(size, 2, size).transpose(1, 0, 2).reshape(1, 1, 2, size * size)
    return heat, current, velocity


def solution(mesh):
    member = ("tile", "sub", "lev")
    whole = ("copies",) + member
    ice = P(None, whole, None, None)
    water = P("lev", ("copies", "tile"), "sub")
    current = P(None, ("copies", "tile"), "sub")
    return jax.shard_map(
        shards,
        mesh=mesh,
        in_specs=(
            water,
            P("tile", "sub"),
            current,
            P(member, None),
            P(member, None, None, None),
            P(member, None, None, None),
            P(None, member, None),
            ice,
            ice,
            ice,
            ice,
        ),
        out_specs=(water, current, ice),
        check_vma=False,
    )
```

```python
import functools

import jax
import jax.numpy as jnp
from jax import lax
from jax.experimental import pallas as pl
from jax.experimental.pallas import tpu as pltpu
from jax.sharding import PartitionSpec as P

SUBCYCLES = 4
STRENGTH_DECAY = 5.0
VISCOUS_STEP = 0.24
SUBCYCLE_STEP = 0.5
CORIOLIS_TURN = 0.1
BASE_MASS = 0.5
HEAT_RATE = 0.2
THIN_ICE = 0.1
THERMAL_DIFFUSE = 0.5
STRESS_MIXING = 0.5

OPPOSITE = (1, 0, 3, 2)
LATERAL = ((2, 3), (2, 3), (0, 1), (0, 1))
DEPTH = SUBCYCLES
SIDE_ROWS = 16 * DEPTH
PUSH_ROWS = 8 * DEPTH
BLOCK_ROWS = SIDE_ROWS + PUSH_ROWS
NAMES_ROW = 2 * DEPTH - 1
CORNER_ROWS = tuple(DEPTH * i - 1 for i in (1, 3, 4, 5, 6, 7, 8))
TILE_ROWS = 16
F32 = jnp.float32
BF16 = jnp.bfloat16
VMEM_LIMIT = 16 * 1024 * 1024
FLOPS_PER_MICRO = 1.15e9


def call(kernel, outs, args, scratch=(), smem=(), hbm=(), out_space=pltpu.VMEM, grant=VMEM_LIMIT, micros=0.01):
    def space(i):
        return pltpu.SMEM if i in smem else pltpu.HBM if i in hbm else pltpu.VMEM

    specs = [pl.BlockSpec(memory_space=space(i)) for i in range(len(args))]
    size = sum(a.size * a.dtype.itemsize for a in args)
    return pl.pallas_call(
        kernel,
        out_shape=outs,
        in_specs=specs,
        out_specs=jax.tree.map(lambda _: pl.BlockSpec(memory_space=out_space), outs),
        scratch_shapes=list(scratch),
        compiler_params=pltpu.CompilerParams(vmem_limit_bytes=grant),
        cost_estimate=pl.CostEstimate(
            flops=int(micros * FLOPS_PER_MICRO), bytes_accessed=size, transcendentals=0
        ),
    )(*args)


def iota(shape, axis):
    return lax.broadcasted_iota(jnp.int32, shape, axis)


def roll(x, shift, axis):
    return pltpu.roll(x, shift % x.shape[axis], axis)


def flag(condition):
    return jnp.where(condition, 1.0, 0.0).astype(F32)


def ocean_columns(water):
    levels, rows, width = water.shape
    lane = iota((rows, width), 1)
    line = iota((1, width), 1)
    mixed = jnp.zeros((rows, width), F32)
    for l in range(levels):
        mixed = jnp.where(lane // 4 == l, roll(water[l], 2 + 4 * l, 1), mixed)
    across = jnp.concatenate([mixed, jnp.zeros((width - rows, width), F32)], axis=0).T
    beside = []
    for l in range(levels):
        for j in range(2):
            last = across[4 * l + 1 - j : 4 * l + 2 - j]
            lead = across[4 * l + 2 + j : 4 * l + 3 + j]
            beside.append(jnp.where(line < rows, last, roll(lead, rows, 1)))
    return beside


def forward_kernel(group, links_h, blocks_h, rows_h, cols_h, currents_h, water_h, *refs):
    devices, members, place = group
    outs, scratch = refs[:members], refs[members:]
    links, blocks, currents, rows, cols, water, fields, tail, arrived, left = scratch
    pairs, side, width = rows_h.shape
    depth = cols_h.shape[1]
    loads = [
        pltpu.make_async_copy(source, target, arrived.at[i])
        for i, (source, target) in enumerate(
            (
                (links_h, links),
                (blocks_h, blocks),
                (currents_h, currents),
                (rows_h, rows),
                (cols_h, cols),
                (water_h, water),
            )
        )
    ]
    for load in loads:
        load.start()
    for load in loads:
        load.wait()
    me = place()
    owners = [lax.rem(lax.rem(blocks[0, m], devices), members) for m in range(pairs)]
    lane = iota((1, width), 1)
    numbers = jnp.zeros((1, width), F32)
    for q in range(4):
        numbers = jnp.where(lane == q, (links[0, 0, q] >> 7).astype(F32), numbers)
        numbers = jnp.where(lane == 4 + q, (links[0, 0, q] & 127).astype(F32), numbers)
    ends = ocean_columns(water) + [numbers]
    blank = jnp.zeros((tail.shape[0] - len(ends), width), F32)
    tail[...] = jnp.concatenate(ends + [blank], axis=0).astype(BF16)
    copies = []
    for k, out in enumerate(outs):
        partner = me ^ k
        pair, found = jnp.int32(0), jnp.int32(0)
        for m in range(pairs):
            pair = jnp.where(owners[m] == partner, m, pair)
            found = jnp.where(owners[m] == partner, 1, found)
        copies.append(
            pltpu.make_async_copy(rows.at[pair], out.at[pl.ds(0, side)], left.at[3 * k])
        )
        copies.append(
            pltpu.make_async_copy(cols.at[pair], out.at[pl.ds(side, depth)], left.at[3 * k + 1])
        )
        if pairs < members:
            keep = jnp.where(found > 0, 1.0, 0.0).astype(F32)
        else:
            keep = None
        copies.append(
            pltpu.make_async_copy(
                tail, out.at[pl.ds(3 * side + depth, tail.shape[0])], left.at[3 * members + k]
            )
        )
        for copy in copies[-3:]:
            copy.start()
        if k == 0 or keep is not None:
            for c in range(2):
                field = currents[c] if keep is None else currents[c] * keep
                fields[0 if keep is None else k, c * side : (c + 1) * side] = field.astype(BF16)
        copies.append(
            pltpu.make_async_copy(
                fields.at[0 if keep is None else k],
                out.at[pl.ds(side + depth, 2 * side)],
                left.at[3 * k + 2],
            )
        )
        copies[-1].start()
    for copy in copies:
        copy.wait()


def put_side_rims(store, planes, at):
    size = planes[0].shape[0]
    lane = iota((size, size), 1)
    mixed = jnp.zeros((size, size), F32)
    for i, plane in enumerate(planes):
        turned = roll(plane, DEPTH + 2 * DEPTH * i, 1)
        mixed = jnp.where(lane // (2 * DEPTH) == i, turned, mixed)
    across = mixed.T
    for i, plane in enumerate(planes):
        for k in range(DEPTH):
            base = i * DEPTH + k
            store[at(0) + base : at(0) + base + 1] = plane[size - 1 - k : size - k]
            store[at(1) + base : at(1) + base + 1] = plane[k : k + 1]
            east = 2 * DEPTH * i + DEPTH - 1 - k
            west = 2 * DEPTH * i + DEPTH + k
            store[at(2) + base : at(2) + base + 1] = across[east : east + 1]
            store[at(3) + base : at(3) + base + 1] = across[west : west + 1]


def rims_kernel(
    thick, conc, ice, water, out, viscous_o, gain_o, mass_o, drag_o, conduct_o,
    speed_o, store,
):
    size = thick.shape[1]
    cover = jnp.zeros((size, size), F32)
    volume = jnp.zeros((size, size), F32)
    conduct = jnp.zeros((size, size), F32)
    for c in range(thick.shape[0]):
        h, a = thick[c], conc[c]
        cover = cover + a
        volume = volume + a * h
        conduct = conduct + a / (h + THIN_ICE)
    mass = volume + BASE_MASS
    viscous = VISCOUS_STEP * (volume * jnp.exp(-STRENGTH_DECAY * (1.0 - cover))) / mass
    step_mass = SUBCYCLE_STEP / mass
    gain = 1.0 / (1.0 + step_mass * cover)
    speed_x = ice[pl.ds(0, size, stride=2), :]
    speed_y = ice[pl.ds(1, size, stride=2), :]
    viscous_o[...] = viscous
    gain_o[...] = gain
    mass_o[...] = step_mass
    drag_o[...] = cover
    conduct_o[...] = -HEAT_RATE * conduct
    speed_o[0] = speed_x
    speed_o[1] = speed_y
    put_side_rims(store, [speed_x, speed_y, viscous, gain], lambda side: side * 4 * DEPTH)
    levels, rows, width = water.shape
    start = SIDE_ROWS
    for l in range(levels):
        for j in range(2):
            at = start + 2 * l + j
            store[at : at + 1] = water[l, rows - 1 - j : rows - j]
            store[at + 2 * levels : at + 2 * levels + 1] = water[l, j : j + 1]
    out[...] = store[...].astype(BF16)


def relay_kernel(tiles, *refs):
    messages, out = refs[:tiles][::-1], refs[tiles]
    for k in range(tiles):
        out[k * BLOCK_ROWS : (k + 1) * BLOCK_ROWS] = messages[k][0:BLOCK_ROWS]


def nearby(me, members, distance, arrays):
    at = me + distance
    inside = (at >= 0) & (at < members)
    found = 0.0
    for k in range(1, members):
        found = found + arrays[k].astype(F32) * flag(inside & ((me ^ k) == at))
    return found


def remap_forward(chunks, field_rows, side, depth):
    total = None
    for chunk, fields in zip(chunks, field_rows):
        down = chunk[0:side]
        right = chunk[side : side + depth]
        wide = jnp.concatenate(fields, axis=1) if len(fields) > 1 else fields[0]
        part = lax.dot_general(down, wide, (((0,), (0,)), ((), ())), preferred_element_type=F32)
        part = part.astype(BF16)
        width = fields[0].shape[1]
        if len(fields) > 1:
            part = jnp.concatenate(
                [part[:, c * width : (c + 1) * width] for c in range(len(fields))], axis=0
            )
        piece = lax.dot_general(part, right, (((1,), (1,)), ((), ())), preferred_element_type=F32)
        piece = piece.astype(BF16).astype(F32)
        total = piece if total is None else total + piece
    return total


def forcing_kernel(group, side, levels, subs, place, mass, drag, wind, early, *refs):
    chunks = refs[:group][::-1]
    out, current_o, push_o, store = refs[group:]
    size = mass.shape[0]
    depth = chunks[0].shape[1]
    fields = [
        [c[side + depth : 2 * side + depth], c[2 * side + depth : 3 * side + depth]] for c in chunks
    ]
    total = remap_forward(chunks, fields, side, depth)
    pushes = []
    for c in range(2):
        current = total[c * size : (c + 1) * size]
        current_o[c] = current
        force = wind[pl.ds(c, size, stride=2), :]
        push = mass[...] * (force + drag[...] * current)
        push_o[c] = push
        pushes.append(push)
    put_side_rims(store, pushes, lambda q: q * 2 * DEPTH)
    tail = [c[3 * side + depth :] for c in chunks]
    store[NAMES_ROW : NAMES_ROW + 1] = tail[0].astype(F32)[2 * levels : 2 * levels + 1]
    me, step = place(), group // subs
    left, right = (nearby(me, group, d * step, tail) for d in (-1, 1))
    line = iota((1, size), 1)
    for l in range(levels):
        near = slice(2 * l, 2 * l + 1)
        store[CORNER_ROWS[l] : CORNER_ROWS[l] + 1] = jnp.where(line < side, left[near], right[near])
    out[0:PUSH_ROWS] = store[...].astype(BF16)
    out[PUSH_ROWS:] = early[...]


def ocean_kernel(counts, tile_place, member_place, water, mixing, *refs):
    tiles, subs, levs = counts
    members = subs * levs
    messages, chunks, (warm_o, top_o) = refs[:tiles], refs[tiles:-2], refs[-2:]
    levels, rows, width = water.shape
    my_tile, me = tile_place(), member_place()
    halo = {}
    strips = [m[BLOCK_ROWS : BLOCK_ROWS + 4 * levels] for m in messages]
    rims = [m[0:PUSH_ROWS] for m in messages]
    tails = [c[3 * rows + width :] for c in chunks]
    for dt in (-1, 1):
        beyond = nearby(my_tile, tiles, dt, strips)
        halo[dt, 0] = beyond[: 2 * levels] if dt < 0 else beyond[2 * levels :]
        corners = nearby(my_tile, tiles, dt, rims)
        at = rows - 1 if dt < 0 else 0
        for ds in (-1, 1):
            lane_at = at if ds < 0 else rows + at
            halo[dt, ds] = [
                corners[CORNER_ROWS[l] : CORNER_ROWS[l] + 1, lane_at : lane_at + 1]
                for l in range(levels)
            ]
    for ds in (-1, 1):
        beside = nearby(me, members, ds * levs, tails)[: 2 * levels]
        halo[0, ds] = roll(beside, -rows, 1) if ds > 0 else beside
    left_cols = halo[0, -1].T
    right_cols = halo[0, 1].T
    row = iota((rows, width), 0)
    lane = iota((rows, width), 1)
    line = iota((1, width), 1)
    total = None

    def laplacian(x, top, bottom, left, right):
        up = jnp.where(row == 0, top, roll(x, 1, 0))
        down = jnp.where(row == rows - 1, bottom, roll(x, -1, 0))
        west = jnp.where(lane == 0, left, roll(x, 1, 1))
        east = jnp.where(lane == width - 1, right, roll(x, -1, 1))
        return up + down + west + east - 4.0 * x

    for l in range(levels):
        x = water[l]
        near, far = 2 * l, 2 * l + 1
        top, top_far = halo[-1, 0][near : near + 1], halo[-1, 0][far : far + 1]
        bottom, bottom_far = halo[1, 0][near : near + 1], halo[1, 0][far : far + 1]
        left, left_far = left_cols[0:rows, near : near + 1], left_cols[0:rows, far : far + 1]
        right, right_far = right_cols[0:rows, near : near + 1], right_cols[0:rows, far : far + 1]
        corner = {}
        for dt in (-1, 1):
            for ds in (-1, 1):
                corner[dt, ds] = halo[dt, ds][l]

        def ring_row(mid, out_row, in_row, dt):
            west = jnp.where(line == 0, corner[dt, -1], roll(mid, 1, 1))
            east = jnp.where(line == width - 1, corner[dt, 1], roll(mid, -1, 1))
            return west + east + out_row + in_row - 4.0 * mid

        def ring_col(mid, out_col, in_col, ds):
            up = jnp.concatenate([corner[-1, ds], mid[:-1]], axis=0)
            down = jnp.concatenate([mid[1:], corner[1, ds]], axis=0)
            return up + down + out_col + in_col - 4.0 * mid

        once = laplacian(x, top, bottom, left, right)
        twice = laplacian(
            once,
            ring_row(top, top_far, x[0:1], -1),
            ring_row(bottom, bottom_far, x[rows - 1 :], 1),
            ring_col(left, left_far, x[:, 0:1], -1),
            ring_col(right, right_far, x[:, width - 1 :], 1),
        )
        warm = x - mixing[...] * twice
        warm_o[l] = warm
        total = warm if total is None else total + warm
    top_o[...] = (total / (levels * levs)).astype(top_o.dtype)


def subcycles_kernel(tiles, members, table, viscous, gain, speed, push, *refs):
    relays, (out, rims) = refs[:members], refs[members:]
    size = viscous.shape[0]
    for k in range(tiles):
        for m in range(members):
            rims[k * members + m] = relays[m][k * BLOCK_ROWS : (k + 1) * BLOCK_ROWS]
    half = DEPTH
    high = 2 * DEPTH
    sub = iota((high, size), 0)
    lane = iota((high, size), 1)
    edge = (sub & (half - 1)) == 0
    turn = jnp.where(sub < half, CORIOLIS_TURN, -CORIOLIS_TURN).astype(F32)
    first, last = lane == 0, lane == size - 1

    def load(device, side, mask, with_push=True):
        start = PUSH_ROWS + side * 2 * high
        block = rims[device, start : start + 2 * high].astype(F32)
        velocity, both = block[:high] * mask, block[high:]
        if not with_push:
            return velocity
        other = roll(both, half, 0)
        visc = jnp.where(sub < half, both, other)
        scale = jnp.where(sub < half, other, both) * mask
        start = side // 2 * 2 * high
        pushed = rims[device, start : start + 2 * high].astype(F32)
        pushed = pushed[:high] if side % 2 == 0 else pushed[high:]
        return [velocity, visc, scale, pushed]

    def follow(device, side):
        name = table[device, side]
        return jnp.where(name >= 0, name, 0), name >= 0

    def step(state, left, right, inner, outer):
        c, visc, scale, pushed = state
        spread = left + right + inner + outer - 4.0 * c
        return scale * (c + visc * spread + pushed + turn * roll(c, half, 0))

    strips = []
    for q in range(4):
        x, has_x = follow(0, q)
        strip = load(x, OPPOSITE[q], flag(has_x))
        sides = []
        for s in LATERAL[q]:
            y, has_y = follow(x, s)
            z, has_z = follow(y, OPPOSITE[q])
            w, has_w = follow(z, OPPOSITE[s])
            sides.append(
                [
                    load(y, OPPOSITE[q], flag(has_y)),
                    load(z, q, flag(has_z)),
                    load(w, q, flag(has_w), with_push=False),
                ]
            )
        strips.append((strip, sides))

    row = iota((size, size), 0)
    col = iota((size, size), 1)
    vx, vy = speed[0], speed[1]
    visc, scale, push_x, push_y = viscous[...], gain[...], push[0], push[1]

    def spread_of(v, north, south, east, west):
        up = jnp.where(row == size - 1, north, roll(v, -1, 0))
        down = jnp.where(row == 0, south, roll(v, 1, 0))
        right = jnp.where(col == size - 1, east, roll(v, -1, 1))
        left = jnp.where(col == 0, west, roll(v, 1, 1))
        return up + down + right + left - 4.0 * v

    for t in range(SUBCYCLES):
        cells = [strip[0] for strip, _ in strips]
        if t < SUBCYCLES - 1:
            mixed = jnp.where(col < half, roll(vx, 1, 1), roll(vy, 1 + half, 1))
            across = mixed.T[0:high]
            own = [
                jnp.where(sub < half, vx[size - 1 :], vy[size - 1 :]),
                jnp.where(sub < half, vx[0:1], vy[0:1]),
                across,
                roll(across, -1, 0),
            ]
            for q in range(4):
                strip, (beyond, before) = strips[q]
                c, y_hi, y_lo = strip[0], beyond[0][0], before[0][0]
                left = jnp.where(first, roll(y_lo, 1, 1), roll(c, 1, 1))
                right = jnp.where(last, roll(y_hi, -1, 1), roll(c, -1, 1))
                inner = jnp.where(edge, own[q], roll(c, 1, 0))
                new_strip = step(strip, left, right, inner, roll(c, -1, 0))
                if t < SUBCYCLES - 2:
                    new_sides = []
                    for i, (y, z, w) in enumerate((beyond, before)):
                        away = 1 if i == 0 else -1
                        boundary = first if i == 0 else last
                        yc, zc = y[0], z[0]
                        toward = jnp.where(boundary, roll(c, away, 1), roll(yc, away, 1))
                        inner = jnp.where(edge, zc, roll(yc, 1, 0))
                        new_y = step(y, toward, roll(yc, -away, 1), inner, roll(yc, -1, 0))
                        new_z = zc
                        if t < SUBCYCLES - 3:
                            toward = jnp.where(boundary, roll(w, away, 1), roll(zc, away, 1))
                            inner = jnp.where(edge, yc, roll(zc, 1, 0))
                            new_z = step(z, toward, roll(zc, -away, 1), inner, roll(zc, -1, 0))
                        new_sides.append((new_y, new_z))
                    for item, (new_y, new_z) in zip((beyond, before), new_sides):
                        item[0][0] = new_y
                        item[1][0] = new_z
                strip[0] = new_strip
        north, south = cells[0], cells[1]
        sides = jnp.where(edge, cells[2], roll(cells[3], 1, 0)).T
        east_x, west_x = sides[:, 0:1], sides[:, 1:2]
        east_y, west_y = sides[:, half : half + 1], sides[:, half + 1 : half + 2]
        spread_x = spread_of(vx, north[0:1], south[0:1], east_x, west_x)
        spread_y = spread_of(
            vy, north[half : half + 1], south[half : half + 1], east_y, west_y
        )
        new_x = scale * (vx + visc * spread_x + push_x + CORIOLIS_TURN * vy)
        new_y = scale * (vy + visc * spread_y + push_y - CORIOLIS_TURN * vx)
        vx, vy = new_x, new_y
    out[0] = vx
    out[1] = vy


def back_kernel(group, side, drag, conduct, current, speed, *refs):
    chunks = refs[:group]
    tops = refs[group : 2 * group]
    outs = refs[2 * group :]
    size = drag.shape[0]
    depth = chunks[0].shape[1]
    warm = remap_forward(chunks, [[t[...]] for t in tops], side, depth)
    heat = conduct[...] * warm
    fluxes = [heat.astype(BF16)]
    for c in range(2):
        fluxes.append((drag[...] * (speed[c] - current[c])).astype(BF16))
    wide = jnp.concatenate(fluxes, axis=1)
    for chunk, out in zip(chunks, outs):
        part = jnp.dot(chunk[0:side], wide, preferred_element_type=F32).astype(BF16)
        part = jnp.concatenate([part[:, c * size : (c + 1) * size] for c in range(3)], axis=0)
        reply = jnp.dot(part, chunk[side : side + depth], preferred_element_type=F32)
        out[...] = reply.astype(BF16)


def finish_kernel(warm, currents, speed, *refs):
    outs, (flat, heat_v, current_v, left) = refs[-7:-4], refs[-4:]
    replies = refs[:-7]
    flat_o, heat_o, current_o = outs
    size = speed.shape[1]
    copies = [
        pltpu.make_async_copy(source, target, left.at[i])
        for i, (source, target) in enumerate(
            ((flat, flat_o), (heat_v, heat_o), (current_v, current_o))
        )
    ]
    for c in range(2):
        flat[pl.ds(c, size, stride=2), :] = speed[c]
    copies[0].start()
    total = replies[0][...].astype(F32)
    for reply in replies[1:]:
        total = total + reply[...].astype(F32)
    side = currents.shape[1]
    heat = THERMAL_DIFFUSE * total[0:side]
    for l in range(warm.shape[0]):
        heat_v[l] = warm[l] + heat
    copies[1].start()
    for c in range(2):
        current_v[c] = currents[c] + STRESS_MIXING * total[(c + 1) * side : (c + 2) * side]
    copies[2].start()
    for copy in copies:
        copy.wait()


def shards(
    water_heat_state,
    diffusion_coefficient,
    upper_current_vector,
    remap_blocks,
    remap_rows,
    remap_cols,
    neighbors,
    thickness,
    concentration,
    ice_velocity,
    wind_stress,
):
    tile_count, sub_count, lev_count = (lax.axis_size(a) for a in ("tile", "sub", "lev"))
    group = sub_count * lev_count
    devices = tile_count * group
    group_axes = ("sub", "lev")
    member_axes = ("tile", "sub", "lev")
    levels, side, width = water_heat_state.shape
    pairs, size = remap_rows.shape[1:3]
    categories = thickness.shape[2]

    def tile_place():
        return lax.axis_index("tile")

    def member_place():
        return lax.axis_index("sub") * lev_count + lax.axis_index("lev")

    def device_place():
        return lax.axis_index("tile") * group + member_place()

    def far_first(count):
        return [*range(2, count), 1]

    def swap(value, axes, count):
        got = {0: value}
        for k in far_first(count):
            got[k] = lax.ppermute(value, axes, [(i, i ^ k) for i in range(count)])
        return [got[k] for k in range(count)]

    def swap_each(values):
        got = {0: values[0]}
        for k in far_first(group):
            got[k] = lax.ppermute(values[k], group_axes, [(i, i ^ k) for i in range(group)])
        return [got[k] for k in range(group)]

    def shape(*dims, dtype=F32):
        return jax.ShapeDtypeStruct(dims, dtype)

    def interleaved(value):
        return value.reshape(2, size, size).transpose(1, 0, 2).reshape(2 * size, size)

    plane = shape(size, size)
    planes = shape(2, size, size)
    wind = interleaved(wind_stress)

    tail_rows = -(-(2 * levels + 1) // TILE_ROWS) * TILE_ROWS
    chunk_rows = 3 * side + width + tail_rows
    sent = call(
        functools.partial(forward_kernel, (devices, group, member_place)),
        [shape(chunk_rows, width, dtype=BF16)] * group,
        (
            neighbors,
            remap_blocks,
            remap_rows[0].swapaxes(1, 2),
            remap_cols[0],
            upper_current_vector,
            water_heat_state,
        ),
        scratch=[
            pltpu.SMEM(neighbors.shape, jnp.int32),
            pltpu.SMEM((1, pairs), jnp.int32),
            pltpu.VMEM((2, side, width), F32),
            pltpu.VMEM((pairs, side, size), BF16),
            pltpu.VMEM((pairs, size, width), BF16),
            pltpu.VMEM((levels, side, width), F32),
            pltpu.VMEM((1 if pairs == group else group, 2 * side, width), BF16),
            pltpu.VMEM((tail_rows, width), BF16),
            pltpu.SemaphoreType.DMA((6,)),
            pltpu.SemaphoreType.DMA((4 * group,)),
        ],
        hbm=(0, 1, 2, 3, 4, 5),
        grant=60 * 2**20,
        micros=10,
    )
    chunks = swap_each(sent)

    early, viscous, gain, step_mass, drag, conduct, speed = call(
        rims_kernel,
        [shape(SIDE_ROWS + 4 * levels, size, dtype=BF16)] + [plane] * 5 + [planes],
        (
            thickness.reshape(categories, size, size),
            concentration.reshape(categories, size, size),
            interleaved(ice_velocity),
            water_heat_state,
        ),
        scratch=[pltpu.VMEM((SIDE_ROWS + 4 * levels, size), F32)],
    )
    message, current_ice, push = call(
        functools.partial(forcing_kernel, group, side, levels, sub_count, member_place),
        [shape(BLOCK_ROWS + 4 * levels, size, dtype=BF16), planes, planes],
        (step_mass, drag, wind, early, *chunks[::-1]),
        scratch=[pltpu.VMEM((PUSH_ROWS, size), F32)],
    )
    messages = swap(message, "tile", tile_count)

    relay = call(
        functools.partial(relay_kernel, tile_count),
        shape(tile_count * BLOCK_ROWS, size, dtype=BF16),
        messages[::-1],
    )
    relays = swap(relay, group_axes, group)

    mixing, _ = lax.optimization_barrier((diffusion_coefficient, relay))
    warm, top = call(
        functools.partial(
            ocean_kernel, (tile_count, sub_count, lev_count), tile_place, member_place
        ),
        [shape(levels, side, width), shape(side, width, dtype=BF16 if lev_count == 1 else F32)],
        (water_heat_state, mixing, *messages, *chunks),
    )
    if lev_count > 1:
        top = lax.psum(top, "lev").astype(BF16)
    tops = swap(top, group_axes, group)

    names = jnp.stack(
        [r.reshape(tile_count, BLOCK_ROWS, size)[:, NAMES_ROW, 0:8] for r in relays],
        axis=1,
    )
    names = names.reshape(devices, 8).astype(jnp.int32)
    table = names[:, 0:4] * 128 + names[:, 4:8]
    table = jnp.where(table < 0, -1, table ^ device_place())
    push, _ = lax.optimization_barrier((push, top))
    speed = call(
        functools.partial(subcycles_kernel, tile_count, group),
        planes,
        (table, viscous, gain, speed, push, *relays),
        scratch=[pltpu.VMEM((devices, BLOCK_ROWS, size), BF16)],
        smem=(0,),
    )

    replies = call(
        functools.partial(back_kernel, group, side),
        [shape(3 * side, width, dtype=BF16)] * group,
        (drag, conduct, current_ice, speed, *chunks, *tops),
    )
    replies = swap_each(replies)
    if lev_count > 1:
        replies = [lax.psum(sum(r.astype(F32) for r in replies), "lev")]
    flat, heat, current = call(
        finish_kernel,
        [shape(2 * size, size), shape(levels, side, width), shape(2, side, width)],
        (warm, upper_current_vector, speed, *replies[::-1]),
        scratch=[
            pltpu.VMEM((2 * size, size), F32),
            pltpu.VMEM((levels, side, width), F32),
            pltpu.VMEM((2, side, width), F32),
            pltpu.SemaphoreType.DMA((3,)),
        ],
        out_space=pltpu.HBM,
    )
    velocity = flat.reshape(size, 2, size).transpose(1, 0, 2).reshape(1, 1, 2, size * size)
    return heat, current, velocity


def solution(mesh):
    member = ("tile", "sub", "lev")
    whole = ("copies",) + member
    ice = P(None, whole, None, None)
    water = P("lev", ("copies", "tile"), "sub")
    current = P(None, ("copies", "tile"), "sub")
    return jax.shard_map(
        shards,
        mesh=mesh,
        in_specs=(
            water,
            P("tile", "sub"),
            current,
            P(member, None),
            P(member, None, None, None),
            P(member, None, None, None),
            P(None, member, None),
            ice,
            ice,
            ice,
            ice,
        ),
        out_specs=(water, current, ice),
        check_vma=False,
    )
```

```python
import functools

import jax
import jax.numpy as jnp
from jax import lax
from jax.experimental import pallas as pl
from jax.experimental.pallas import tpu as pltpu
from jax.sharding import PartitionSpec as P

SUBCYCLES = 4
STRENGTH_DECAY = 5.0
VISCOUS_STEP = 0.24
SUBCYCLE_STEP = 0.5
CORIOLIS_TURN = 0.1
BASE_MASS = 0.5
HEAT_RATE = 0.2
THIN_ICE = 0.1
THERMAL_DIFFUSE = 0.5
STRESS_MIXING = 0.5

OPPOSITE = (1, 0, 3, 2)
LATERAL = ((2, 3), (2, 3), (0, 1), (0, 1))
DEPTH = SUBCYCLES
SIDE_ROWS = 16 * DEPTH
PUSH_ROWS = 8 * DEPTH
BLOCK_ROWS = SIDE_ROWS + PUSH_ROWS
NAMES_ROW = 2 * DEPTH - 1
CORNER_ROWS = tuple(DEPTH * i - 1 for i in (1, 3, 4, 5, 6, 7, 8))
TILE_ROWS = 16
F32 = jnp.float32
BF16 = jnp.bfloat16
VMEM_LIMIT = 16 * 1024 * 1024
FLOPS_PER_MICRO = 1.15e9


def call(kernel, outs, args, scratch=(), smem=(), hbm=(), out_space=pltpu.VMEM, grant=VMEM_LIMIT, micros=0.01):
    def space(i):
        return pltpu.SMEM if i in smem else pltpu.HBM if i in hbm else pltpu.VMEM

    specs = [pl.BlockSpec(memory_space=space(i)) for i in range(len(args))]
    size = sum(a.size * a.dtype.itemsize for a in args)
    return pl.pallas_call(
        kernel,
        out_shape=outs,
        in_specs=specs,
        out_specs=jax.tree.map(lambda _: pl.BlockSpec(memory_space=out_space), outs),
        scratch_shapes=list(scratch),
        compiler_params=pltpu.CompilerParams(vmem_limit_bytes=grant),
        cost_estimate=pl.CostEstimate(
            flops=int(micros * FLOPS_PER_MICRO), bytes_accessed=size, transcendentals=0
        ),
    )(*args)


def iota(shape, axis):
    return lax.broadcasted_iota(jnp.int32, shape, axis)


def roll(x, shift, axis):
    return pltpu.roll(x, shift % x.shape[axis], axis)


def flag(condition):
    return jnp.where(condition, 1.0, 0.0).astype(F32)


def ocean_columns(water):
    levels, rows, width = water.shape
    lane = iota((rows, width), 1)
    line = iota((1, width), 1)
    mixed = jnp.zeros((rows, width), F32)
    for l in range(levels):
        mixed = jnp.where(lane // 4 == l, roll(water[l], 2 + 4 * l, 1), mixed)
    across = jnp.concatenate([mixed, jnp.zeros((width - rows, width), F32)], axis=0).T
    beside = []
    for l in range(levels):
        for j in range(2):
            last = across[4 * l + 1 - j : 4 * l + 2 - j]
            lead = across[4 * l + 2 + j : 4 * l + 3 + j]
            beside.append(jnp.where(line < rows, last, roll(lead, rows, 1)))
    return beside


def forward_kernel(group, links_h, blocks_h, rows_h, cols_h, currents_h, water_h, *refs):
    devices, members, place = group
    outs, scratch = refs[:members], refs[members:]
    links, blocks, currents, rows, cols, water, fields, tail, arrived, left = scratch
    pairs, side, width = rows_h.shape
    depth = cols_h.shape[1]
    loads = [
        pltpu.make_async_copy(source, target, arrived.at[i])
        for i, (source, target) in enumerate(
            (
                (links_h, links),
                (blocks_h, blocks),
                (currents_h, currents),
                (rows_h, rows),
                (cols_h, cols),
                (water_h, water),
            )
        )
    ]
    for load in loads:
        load.start()
    for i in (1, 3, 4):
        loads[i].wait()
    me = place()
    side, depth, pairs = rows.shape[1], cols.shape[1], rows.shape[0]
    owners = [lax.rem(lax.rem(blocks[0, m], devices), members) for m in range(pairs)]
    copies, keeps = [], []
    for k, out in enumerate(outs):
        partner = me ^ k
        pair, found = jnp.int32(0), jnp.int32(0)
        for m in range(pairs):
            pair = jnp.where(owners[m] == partner, m, pair)
            found = jnp.where(owners[m] == partner, 1, found)
        keeps.append(flag(found > 0))
        at = 0
        for i, source in enumerate((rows, cols)):
            target = out.at[pl.ds(at, source.shape[1])]
            copies.append(pltpu.make_async_copy(source.at[pair], target, left.at[4 * k + i]))
            copies[-1].start()
            at += source.shape[1]
    for i in (0, 2, 5):
        loads[i].wait()
    plain = pairs == members
    for k in range(1 if plain else members):
        for c in range(2):
            field = currents[c] if plain else currents[c] * keeps[k]
            fields[k, c * side : (c + 1) * side] = field.astype(BF16)
    lane = iota((1, width), 1)
    numbers = jnp.zeros((1, width), F32)
    for q in range(4):
        numbers = jnp.where(lane == q, (links[0, 0, q] >> 7).astype(F32), numbers)
        numbers = jnp.where(lane == 4 + q, (links[0, 0, q] & 127).astype(F32), numbers)
    ends = ocean_columns(water) + [numbers]
    blank = jnp.zeros((tail.shape[0] - len(ends), width), F32)
    tail[...] = jnp.concatenate(ends + [blank], axis=0).astype(BF16)
    for k, out in enumerate(outs):
        at = side + depth
        for i, source in enumerate((fields.at[0 if plain else k], tail)):
            target = out.at[pl.ds(at, source.shape[0])]
            copies.append(pltpu.make_async_copy(source, target, left.at[4 * k + 2 + i]))
            copies[-1].start()
            at += source.shape[0]
    for copy in copies:
        copy.wait()


def put_side_rims(store, planes, at):
    size = planes[0].shape[0]
    lane = iota((size, size), 1)
    mixed = jnp.zeros((size, size), F32)
    for i, plane in enumerate(planes):
        turned = roll(plane, DEPTH + 2 * DEPTH * i, 1)
        mixed = jnp.where(lane // (2 * DEPTH) == i, turned, mixed)
    across = mixed.T
    for i, plane in enumerate(planes):
        for k in range(DEPTH):
            base = i * DEPTH + k
            store[at(0) + base : at(0) + base + 1] = plane[size - 1 - k : size - k]
            store[at(1) + base : at(1) + base + 1] = plane[k : k + 1]
            east = 2 * DEPTH * i + DEPTH - 1 - k
            west = 2 * DEPTH * i + DEPTH + k
            store[at(2) + base : at(2) + base + 1] = across[east : east + 1]
            store[at(3) + base : at(3) + base + 1] = across[west : west + 1]


def rims_kernel(
    thick, conc, ice, water, out, viscous_o, gain_o, mass_o, drag_o, conduct_o,
    speed_o, store,
):
    size = thick.shape[1]
    cover = jnp.zeros((size, size), F32)
    volume = jnp.zeros((size, size), F32)
    conduct = jnp.zeros((size, size), F32)
    for c in range(thick.shape[0]):
        h, a = thick[c], conc[c]
        cover = cover + a
        volume = volume + a * h
        conduct = conduct + a / (h + THIN_ICE)
    mass = volume + BASE_MASS
    viscous = VISCOUS_STEP * (volume * jnp.exp(-STRENGTH_DECAY * (1.0 - cover))) / mass
    step_mass = SUBCYCLE_STEP / mass
    gain = 1.0 / (1.0 + step_mass * cover)
    speed_x = ice[pl.ds(0, size, stride=2), :]
    speed_y = ice[pl.ds(1, size, stride=2), :]
    viscous_o[...] = viscous
    gain_o[...] = gain
    mass_o[...] = step_mass
    drag_o[...] = cover
    conduct_o[...] = -HEAT_RATE * conduct
    speed_o[0] = speed_x
    speed_o[1] = speed_y
    put_side_rims(store, [speed_x, speed_y, viscous, gain], lambda side: side * 4 * DEPTH)
    levels, rows, width = water.shape
    start = SIDE_ROWS
    for l in range(levels):
        for j in range(2):
            at = start + 2 * l + j
            store[at : at + 1] = water[l, rows - 1 - j : rows - j]
            store[at + 2 * levels : at + 2 * levels + 1] = water[l, j : j + 1]
    out[...] = store[...].astype(BF16)


def relay_kernel(tiles, *refs):
    messages, out = refs[:tiles][::-1], refs[tiles]
    for k in range(tiles):
        out[k * BLOCK_ROWS : (k + 1) * BLOCK_ROWS] = messages[k][0:BLOCK_ROWS]


def nearby(me, members, distance, arrays):
    at = me + distance
    inside = (at >= 0) & (at < members)
    found = 0.0
    for k in range(1, members):
        found = found + arrays[k].astype(F32) * flag(inside & ((me ^ k) == at))
    return found


def remap_forward(chunks, field_rows, side, depth):
    total = None
    for chunk, fields in zip(chunks, field_rows):
        down = chunk[0:side]
        right = chunk[side : side + depth]
        wide = jnp.concatenate(fields, axis=1) if len(fields) > 1 else fields[0]
        part = lax.dot_general(down, wide, (((0,), (0,)), ((), ())), preferred_element_type=F32)
        part = part.astype(BF16)
        width = fields[0].shape[1]
        if len(fields) > 1:
            part = jnp.concatenate(
                [part[:, c * width : (c + 1) * width] for c in range(len(fields))], axis=0
            )
        piece = lax.dot_general(part, right, (((1,), (1,)), ((), ())), preferred_element_type=F32)
        piece = piece.astype(BF16).astype(F32)
        total = piece if total is None else total + piece
    return total


def forcing_kernel(group, side, levels, subs, place, mass, drag, wind, early, *refs):
    chunks = refs[:group][::-1]
    out, current_o, push_o, store = refs[group:]
    size = mass.shape[0]
    depth = chunks[0].shape[1]
    fields = [
        [c[side + depth : 2 * side + depth], c[2 * side + depth : 3 * side + depth]] for c in chunks
    ]
    total = remap_forward(chunks, fields, side, depth)
    pushes = []
    for c in range(2):
        current = total[c * size : (c + 1) * size]
        current_o[c] = current
        force = wind[pl.ds(c, size, stride=2), :]
        push = mass[...] * (force + drag[...] * current)
        push_o[c] = push
        pushes.append(push)
    put_side_rims(store, pushes, lambda q: q * 2 * DEPTH)
    tail = [c[3 * side + depth :] for c in chunks]
    store[NAMES_ROW : NAMES_ROW + 1] = tail[0].astype(F32)[2 * levels : 2 * levels + 1]
    me, step = place(), group // subs
    left, right = (nearby(me, group, d * step, tail) for d in (-1, 1))
    line = iota((1, size), 1)
    for l in range(levels):
        near = slice(2 * l, 2 * l + 1)
        store[CORNER_ROWS[l] : CORNER_ROWS[l] + 1] = jnp.where(line < side, left[near], right[near])
    out[0:PUSH_ROWS] = store[...].astype(BF16)
    out[PUSH_ROWS:] = early[...]


def ocean_kernel(counts, tile_place, member_place, water, mixing, *refs):
    tiles, subs, levs = counts
    members = subs * levs
    messages, chunks, (warm_o, top_o) = refs[:tiles], refs[tiles:-2], refs[-2:]
    levels, rows, width = water.shape
    my_tile, me = tile_place(), member_place()
    halo = {}
    strips = [m[BLOCK_ROWS : BLOCK_ROWS + 4 * levels] for m in messages]
    rims = [m[0:PUSH_ROWS] for m in messages]
    tails = [c[3 * rows + width :] for c in chunks]
    for dt in (-1, 1):
        beyond = nearby(my_tile, tiles, dt, strips)
        halo[dt, 0] = beyond[: 2 * levels] if dt < 0 else beyond[2 * levels :]
        corners = nearby(my_tile, tiles, dt, rims)
        at = rows - 1 if dt < 0 else 0
        for ds in (-1, 1):
            lane_at = at if ds < 0 else rows + at
            halo[dt, ds] = [
                corners[CORNER_ROWS[l] : CORNER_ROWS[l] + 1, lane_at : lane_at + 1]
                for l in range(levels)
            ]
    for ds in (-1, 1):
        beside = nearby(me, members, ds * levs, tails)[: 2 * levels]
        halo[0, ds] = roll(beside, -rows, 1) if ds > 0 else beside
    left_cols = halo[0, -1].T
    right_cols = halo[0, 1].T
    row = iota((rows, width), 0)
    lane = iota((rows, width), 1)
    line = iota((1, width), 1)
    total = None

    def laplacian(x, top, bottom, left, right):
        up = jnp.where(row == 0, top, roll(x, 1, 0))
        down = jnp.where(row == rows - 1, bottom, roll(x, -1, 0))
        west = jnp.where(lane == 0, left, roll(x, 1, 1))
        east = jnp.where(lane == width - 1, right, roll(x, -1, 1))
        return up + down + west + east - 4.0 * x

    for l in range(levels):
        x = water[l]
        near, far = 2 * l, 2 * l + 1
        top, top_far = halo[-1, 0][near : near + 1], halo[-1, 0][far : far + 1]
        bottom, bottom_far = halo[1, 0][near : near + 1], halo[1, 0][far : far + 1]
        left, left_far = left_cols[0:rows, near : near + 1], left_cols[0:rows, far : far + 1]
        right, right_far = right_cols[0:rows, near : near + 1], right_cols[0:rows, far : far + 1]
        corner = {}
        for dt in (-1, 1):
            for ds in (-1, 1):
                corner[dt, ds] = halo[dt, ds][l]

        def ring_row(mid, out_row, in_row, dt):
            west = jnp.where(line == 0, corner[dt, -1], roll(mid, 1, 1))
            east = jnp.where(line == width - 1, corner[dt, 1], roll(mid, -1, 1))
            return west + east + out_row + in_row - 4.0 * mid

        def ring_col(mid, out_col, in_col, ds):
            up = jnp.concatenate([corner[-1, ds], mid[:-1]], axis=0)
            down = jnp.concatenate([mid[1:], corner[1, ds]], axis=0)
            return up + down + out_col + in_col - 4.0 * mid

        once = laplacian(x, top, bottom, left, right)
        twice = laplacian(
            once,
            ring_row(top, top_far, x[0:1], -1),
            ring_row(bottom, bottom_far, x[rows - 1 :], 1),
            ring_col(left, left_far, x[:, 0:1], -1),
            ring_col(right, right_far, x[:, width - 1 :], 1),
        )
        warm = x - mixing[...] * twice
        warm_o[l] = warm
        total = warm if total is None else total + warm
    top_o[...] = (total / (levels * levs)).astype(top_o.dtype)


def subcycles_kernel(tiles, members, table, viscous, gain, speed, push, *refs):
    relays, (out, rims, names, named) = refs[:members], refs[members:]
    load_names = pltpu.make_async_copy(table, names, named)
    load_names.start()
    size = viscous.shape[0]
    for k in range(tiles):
        for m in range(members):
            rims[k * members + m] = relays[m][k * BLOCK_ROWS : (k + 1) * BLOCK_ROWS]
    half = DEPTH
    high = 2 * DEPTH
    sub = iota((high, size), 0)
    lane = iota((high, size), 1)
    edge = (sub & (half - 1)) == 0
    turn = jnp.where(sub < half, CORIOLIS_TURN, -CORIOLIS_TURN).astype(F32)
    first, last = lane == 0, lane == size - 1

    def load(device, side, mask, with_push=True):
        start = PUSH_ROWS + side * 2 * high
        block = rims[device, start : start + 2 * high].astype(F32)
        velocity, both = block[:high] * mask, block[high:]
        if not with_push:
            return velocity
        other = roll(both, half, 0)
        visc = jnp.where(sub < half, both, other)
        scale = jnp.where(sub < half, other, both) * mask
        start = side // 2 * 2 * high
        pushed = rims[device, start : start + 2 * high].astype(F32)
        pushed = pushed[:high] if side % 2 == 0 else pushed[high:]
        return [velocity, visc, scale, pushed]

    def follow(device, side):
        name = names[device, side]
        return jnp.where(name >= 0, name, 0), name >= 0

    def step(state, left, right, inner, outer):
        c, visc, scale, pushed = state
        spread = left + right + inner + outer - 4.0 * c
        return scale * (c + visc * spread + pushed + turn * roll(c, half, 0))

    row = iota((size, size), 0)
    col = iota((size, size), 1)
    vx, vy = speed[0], speed[1]
    visc, scale, push_x, push_y = viscous[...], gain[...], push[0], push[1]

    def interior(v):
        up = jnp.where(row == size - 1, 0.0, roll(v, -1, 0))
        down = jnp.where(row == 0, 0.0, roll(v, 1, 0))
        right = jnp.where(col == size - 1, 0.0, roll(v, -1, 1))
        left = jnp.where(col == 0, 0.0, roll(v, 1, 1))
        return up + down + right + left - 4.0 * v

    def rim_of(north, south, east, west):
        up = jnp.where(row == size - 1, north, jnp.where(row == 0, south, 0.0))
        return up + jnp.where(col == size - 1, east, jnp.where(col == 0, west, 0.0))

    def own_edges(vx, vy):
        mixed = jnp.where(col < half, roll(vx, 1, 1), roll(vy, 1 + half, 1))
        across = mixed.T[0:high]
        return [
            jnp.where(sub < half, vx[size - 1 :], vy[size - 1 :]),
            jnp.where(sub < half, vx[0:1], vy[0:1]),
            across,
            roll(across, -1, 0),
        ]

    own = own_edges(vx, vy)
    inner_x, inner_y = interior(vx), interior(vy)
    load_names.wait()
    strips = []
    for q in range(4):
        x, has_x = follow(0, q)
        strip = load(x, OPPOSITE[q], flag(has_x))
        sides = []
        for s in LATERAL[q]:
            y, has_y = follow(x, s)
            z, has_z = follow(y, OPPOSITE[q])
            w, has_w = follow(z, OPPOSITE[s])
            sides.append(
                [
                    load(y, OPPOSITE[q], flag(has_y)),
                    load(z, q, flag(has_z)),
                    load(w, q, flag(has_w), with_push=False),
                ]
            )
        strips.append((strip, sides))

    for t in range(SUBCYCLES):
        cells = [strip[0] for strip, _ in strips]
        if t < SUBCYCLES - 1:
            if t > 0:
                own = own_edges(vx, vy)
            for q in range(4):
                strip, (beyond, before) = strips[q]
                c, y_hi, y_lo = strip[0], beyond[0][0], before[0][0]
                left = jnp.where(first, roll(y_lo, 1, 1), roll(c, 1, 1))
                right = jnp.where(last, roll(y_hi, -1, 1), roll(c, -1, 1))
                inner = jnp.where(edge, own[q], roll(c, 1, 0))
                new_strip = step(strip, left, right, inner, roll(c, -1, 0))
                if t < SUBCYCLES - 2:
                    new_sides = []
                    for i, (y, z, w) in enumerate((beyond, before)):
                        away = 1 if i == 0 else -1
                        boundary = first if i == 0 else last
                        yc, zc = y[0], z[0]
                        toward = jnp.where(boundary, roll(c, away, 1), roll(yc, away, 1))
                        inner = jnp.where(edge, zc, roll(yc, 1, 0))
                        new_y = step(y, toward, roll(yc, -away, 1), inner, roll(yc, -1, 0))
                        new_z = zc
                        if t < SUBCYCLES - 3:
                            toward = jnp.where(boundary, roll(w, away, 1), roll(zc, away, 1))
                            inner = jnp.where(edge, yc, roll(zc, 1, 0))
                            new_z = step(z, toward, roll(zc, -away, 1), inner, roll(zc, -1, 0))
                        new_sides.append((new_y, new_z))
                    for item, (new_y, new_z) in zip((beyond, before), new_sides):
                        item[0][0] = new_y
                        item[1][0] = new_z
                strip[0] = new_strip
        north, south = cells[0], cells[1]
        sides = jnp.where(edge, cells[2], roll(cells[3], 1, 0)).T
        east_x, west_x = sides[:, 0:1], sides[:, 1:2]
        east_y, west_y = sides[:, half : half + 1], sides[:, half + 1 : half + 2]
        if t > 0:
            inner_x, inner_y = interior(vx), interior(vy)
        spread_x = inner_x + rim_of(north[0:1], south[0:1], east_x, west_x)
        spread_y = inner_y + rim_of(
            north[half : half + 1], south[half : half + 1], east_y, west_y
        )
        new_x = scale * (vx + visc * spread_x + push_x + CORIOLIS_TURN * vy)
        new_y = scale * (vy + visc * spread_y + push_y - CORIOLIS_TURN * vx)
        vx, vy = new_x, new_y
    out[0] = vx
    out[1] = vy


def back_kernel(group, side, drag, conduct, current, speed, *refs):
    chunks = refs[:group]
    tops = refs[group : 2 * group]
    outs = refs[2 * group :]
    size = drag.shape[0]
    depth = chunks[0].shape[1]
    warm = remap_forward(chunks, [[t[...]] for t in tops], side, depth)
    heat = conduct[...] * warm
    fluxes = [heat.astype(BF16)]
    for c in range(2):
        fluxes.append((drag[...] * (speed[c] - current[c])).astype(BF16))
    wide = jnp.concatenate(fluxes, axis=1)
    for chunk, out in zip(chunks, outs):
        part = jnp.dot(chunk[0:side], wide, preferred_element_type=F32).astype(BF16)
        part = jnp.concatenate([part[:, c * size : (c + 1) * size] for c in range(3)], axis=0)
        reply = jnp.dot(part, chunk[side : side + depth], preferred_element_type=F32)
        out[...] = reply.astype(BF16)


def finish_kernel(warm, currents, speed, *refs):
    outs, (flat, heat_v, current_v, left) = refs[-7:-4], refs[-4:]
    replies = refs[:-7]
    flat_o, heat_o, current_o = outs
    size = speed.shape[1]
    copies = [
        pltpu.make_async_copy(source, target, left.at[i])
        for i, (source, target) in enumerate(
            ((flat, flat_o), (heat_v, heat_o), (current_v, current_o))
        )
    ]
    for c in range(2):
        flat[pl.ds(c, size, stride=2), :] = speed[c]
    copies[0].start()
    total = replies[0][...].astype(F32)
    for reply in replies[1:]:
        total = total + reply[...].astype(F32)
    side = currents.shape[1]
    heat = THERMAL_DIFFUSE * total[0:side]
    for l in range(warm.shape[0]):
        heat_v[l] = warm[l] + heat
    copies[1].start()
    for c in range(2):
        current_v[c] = currents[c] + STRESS_MIXING * total[(c + 1) * side : (c + 2) * side]
    copies[2].start()
    for copy in copies:
        copy.wait()


def shards(
    water_heat_state,
    diffusion_coefficient,
    upper_current_vector,
    remap_blocks,
    remap_rows,
    remap_cols,
    neighbors,
    thickness,
    concentration,
    ice_velocity,
    wind_stress,
):
    tile_count, sub_count, lev_count = (lax.axis_size(a) for a in ("tile", "sub", "lev"))
    group = sub_count * lev_count
    devices = tile_count * group
    group_axes = ("sub", "lev")
    member_axes = ("tile", "sub", "lev")
    levels, side, width = water_heat_state.shape
    pairs, size = remap_rows.shape[1:3]
    categories = thickness.shape[2]

    def tile_place():
        return lax.axis_index("tile")

    def member_place():
        return lax.axis_index("sub") * lev_count + lax.axis_index("lev")

    def device_place():
        return lax.axis_index("tile") * group + member_place()

    def far_first(count):
        return [*range(2, count), 1]

    def swap(value, axes, count):
        got = {0: value}
        for k in far_first(count):
            got[k] = lax.ppermute(value, axes, [(i, i ^ k) for i in range(count)])
        return [got[k] for k in range(count)]

    def swap_chips(value):
        return {0: value} | {
            k: lax.ppermute(value, group_axes, [(i, i ^ k) for i in range(group)])
            for k in range(2, group, 2)
        }

    def swap_cores(got):
        beside = [(i, i ^ 1) for i in range(group)]
        got = got | {k + 1: lax.ppermute(got[k], group_axes, beside) for k in got}
        return [got[k] for k in range(group)]

    def swap_each(values):
        got = {0: values[0]}
        for k in far_first(group):
            got[k] = lax.ppermute(values[k], group_axes, [(i, i ^ k) for i in range(group)])
        return [got[k] for k in range(group)]

    def shape(*dims, dtype=F32):
        return jax.ShapeDtypeStruct(dims, dtype)

    def interleaved(value):
        return value.reshape(2, size, size).transpose(1, 0, 2).reshape(2 * size, size)

    plane = shape(size, size)
    planes = shape(2, size, size)
    wind = interleaved(wind_stress)

    tail_rows = -(-(2 * levels + 1) // TILE_ROWS) * TILE_ROWS
    chunk_rows = 3 * side + width + tail_rows
    sent = call(
        functools.partial(forward_kernel, (devices, group, member_place)),
        [shape(chunk_rows, width, dtype=BF16)] * group,
        (
            neighbors,
            remap_blocks,
            remap_rows[0].swapaxes(1, 2),
            remap_cols[0],
            upper_current_vector,
            water_heat_state,
        ),
        scratch=[
            pltpu.SMEM(neighbors.shape, jnp.int32),
            pltpu.SMEM((1, pairs), jnp.int32),
            pltpu.VMEM((2, side, width), F32),
            pltpu.VMEM((pairs, side, size), BF16),
            pltpu.VMEM((pairs, size, width), BF16),
            pltpu.VMEM((levels, side, width), F32),
            pltpu.VMEM((1 if pairs == group else group, 2 * side, width), BF16),
            pltpu.VMEM((tail_rows, width), BF16),
            pltpu.SemaphoreType.DMA((6,)),
            pltpu.SemaphoreType.DMA((4 * group,)),
        ],
        hbm=(0, 1, 2, 3, 4, 5),
        grant=60 * 2**20,
        micros=10,
    )
    chunks = swap_each(sent)

    early, viscous, gain, step_mass, drag, conduct, speed = call(
        rims_kernel,
        [shape(SIDE_ROWS + 4 * levels, size, dtype=BF16)] + [plane] * 5 + [planes],
        (
            thickness.reshape(categories, size, size),
            concentration.reshape(categories, size, size),
            interleaved(ice_velocity),
            water_heat_state,
        ),
        scratch=[pltpu.VMEM((SIDE_ROWS + 4 * levels, size), F32)],
    )
    message, current_ice, push = call(
        functools.partial(forcing_kernel, group, side, levels, sub_count, member_place),
        [shape(BLOCK_ROWS + 4 * levels, size, dtype=BF16), planes, planes],
        (step_mass, drag, wind, early, *chunks[::-1]),
        scratch=[pltpu.VMEM((PUSH_ROWS, size), F32)],
    )
    messages = swap(message, "tile", tile_count)

    relay = call(
        functools.partial(relay_kernel, tile_count),
        shape(tile_count * BLOCK_ROWS, size, dtype=BF16),
        messages[::-1],
    )
    relays = swap_chips(relay)

    mixing, _ = lax.optimization_barrier((diffusion_coefficient, relay))
    warm, top = call(
        functools.partial(
            ocean_kernel, (tile_count, sub_count, lev_count), tile_place, member_place
        ),
        [shape(levels, side, width), shape(side, width, dtype=BF16 if lev_count == 1 else F32)],
        (water_heat_state, mixing, *messages, *chunks),
    )
    if lev_count > 1:
        top = lax.psum(top, "lev").astype(BF16)
    tops = swap(top, group_axes, group)

    far = sorted(k for k in relays if k)
    relayed, _ = lax.optimization_barrier(([relays[k] for k in far], tops[1]))
    relays = swap_cores({0: relay} | dict(zip(far, relayed)))

    names = jnp.stack(
        [r.reshape(tile_count, BLOCK_ROWS, size)[:, NAMES_ROW, 0:8] for r in relays],
        axis=1,
    )
    names = names.reshape(devices, 8).astype(jnp.int32)
    table = names[:, 0:4] * 128 + names[:, 4:8]
    table = jnp.where(table < 0, -1, table ^ device_place())
    push, _ = lax.optimization_barrier((push, top))
    speed = call(
        functools.partial(subcycles_kernel, tile_count, group),
        planes,
        (table, viscous, gain, speed, push, *relays),
        scratch=[
            pltpu.VMEM((devices, BLOCK_ROWS, size), BF16),
            pltpu.SMEM((devices, 4), jnp.int32),
            pltpu.SemaphoreType.DMA,
        ],
        hbm=(0,),
    )

    replies = call(
        functools.partial(back_kernel, group, side),
        [shape(3 * side, width, dtype=BF16)] * group,
        (drag, conduct, current_ice, speed, *chunks, *tops),
    )
    replies = swap_each(replies)
    if lev_count > 1:
        replies = [lax.psum(sum(r.astype(F32) for r in replies), "lev")]
    flat, heat, current = call(
        finish_kernel,
        [shape(2 * size, size), shape(levels, side, width), shape(2, side, width)],
        (warm, upper_current_vector, speed, *replies[::-1]),
        scratch=[
            pltpu.VMEM((2 * size, size), F32),
            pltpu.VMEM((levels, side, width), F32),
            pltpu.VMEM((2, side, width), F32),
            pltpu.SemaphoreType.DMA((3,)),
        ],
        out_space=pltpu.HBM,
    )
    velocity = flat.reshape(size, 2, size).transpose(1, 0, 2).reshape(1, 1, 2, size * size)
    return heat, current, velocity


def solution(mesh):
    member = ("tile", "sub", "lev")
    whole = ("copies",) + member
    ice = P(None, whole, None, None)
    water = P("lev", ("copies", "tile"), "sub")
    current = P(None, ("copies", "tile"), "sub")
    return jax.shard_map(
        shards,
        mesh=mesh,
        in_specs=(
            water,
            P("tile", "sub"),
            current,
            P(member, None),
            P(member, None, None, None),
            P(member, None, None, None),
            P(None, member, None),
            ice,
            ice,
            ice,
            ice,
        ),
        out_specs=(water, current, ice),
        check_vma=False,
    )
```

```python
import functools

import jax
import jax.numpy as jnp
from jax import lax
from jax.experimental import pallas as pl
from jax.experimental.pallas import tpu as pltpu
from jax.sharding import PartitionSpec as P

SUBCYCLES = 4
STRENGTH_DECAY = 5.0
VISCOUS_STEP = 0.24
SUBCYCLE_STEP = 0.5
CORIOLIS_TURN = 0.1
BASE_MASS = 0.5
HEAT_RATE = 0.2
THIN_ICE = 0.1
THERMAL_DIFFUSE = 0.5
STRESS_MIXING = 0.5

OPPOSITE = (1, 0, 3, 2)
LATERAL = ((2, 3), (2, 3), (0, 1), (0, 1))
DEPTH = SUBCYCLES
SIDE_ROWS = 16 * DEPTH
PUSH_ROWS = 8 * DEPTH
BLOCK_ROWS = SIDE_ROWS + PUSH_ROWS
NAMES_ROW = 2 * DEPTH - 1
CORNER_ROWS = tuple(DEPTH * i - 1 for i in (1, 3, 4, 5, 6, 7, 8))
TILE_ROWS = 16
F32 = jnp.float32
BF16 = jnp.bfloat16
VMEM_LIMIT = 16 * 1024 * 1024
FLOPS_PER_MICRO = 1.15e9


def call(kernel, outs, args, scratch=(), smem=(), hbm=(), out_space=pltpu.VMEM, grant=VMEM_LIMIT, micros=0.01):
    def space(i):
        return pltpu.SMEM if i in smem else pltpu.HBM if i in hbm else pltpu.VMEM

    specs = [pl.BlockSpec(memory_space=space(i)) for i in range(len(args))]
    size = sum(a.size * a.dtype.itemsize for a in args)
    return pl.pallas_call(
        kernel,
        out_shape=outs,
        in_specs=specs,
        out_specs=jax.tree.map(lambda _: pl.BlockSpec(memory_space=out_space), outs),
        scratch_shapes=list(scratch),
        compiler_params=pltpu.CompilerParams(vmem_limit_bytes=grant),
        cost_estimate=pl.CostEstimate(
            flops=int(micros * FLOPS_PER_MICRO), bytes_accessed=size, transcendentals=0
        ),
    )(*args)


def iota(shape, axis):
    return lax.broadcasted_iota(jnp.int32, shape, axis)


def roll(x, shift, axis):
    return pltpu.roll(x, shift % x.shape[axis], axis)


def flag(condition):
    return jnp.where(condition, 1.0, 0.0).astype(F32)


def ocean_columns(water):
    levels, rows, width = water.shape
    lane = iota((rows, width), 1)
    line = iota((1, width), 1)
    mixed = jnp.zeros((rows, width), F32)
    for l in range(levels):
        mixed = jnp.where(lane // 4 == l, roll(water[l], 2 + 4 * l, 1), mixed)
    across = jnp.concatenate([mixed, jnp.zeros((width - rows, width), F32)], axis=0).T
    beside = []
    for l in range(levels):
        for j in range(2):
            last = across[4 * l + 1 - j : 4 * l + 2 - j]
            lead = across[4 * l + 2 + j : 4 * l + 3 + j]
            beside.append(jnp.where(line < rows, last, roll(lead, rows, 1)))
    return beside


def forward_kernel(group, links_h, blocks_h, rows_h, cols_h, currents_h, water_h, *refs):
    devices, members, place = group
    outs, scratch = refs[:members], refs[members:]
    links, blocks, currents, rows, cols, water, fields, tail, kept, arrived, left = scratch
    pairs, side, width = rows_h.shape
    depth = cols_h.shape[1]
    loads = [
        pltpu.make_async_copy(source, target, arrived.at[i])
        for i, (source, target) in enumerate(
            (
                (links_h, links),
                (blocks_h, blocks),
                (currents_h, currents),
                (rows_h, rows),
                (cols_h, cols),
                (water_h, water),
            )
        )
    ]
    for load in loads:
        load.start()
    for i in (1, 3, 4):
        loads[i].wait()
    me = place()
    side, depth, pairs = rows.shape[1], cols.shape[1], rows.shape[0]
    owners = [lax.rem(lax.rem(blocks[0, m], devices), members) for m in range(pairs)]
    copies = []
    for k, out in enumerate(outs):
        partner = me ^ k
        pair = jnp.int32(0)
        for m in range(pairs):
            pair = jnp.where(owners[m] == partner, m, pair)
        if pairs < members:
            found = sum(flag(owners[m] == partner) for m in range(pairs))
            kept[k] = (rows[pair].astype(F32) * found).astype(BF16)
        at = 0
        for i, source in enumerate((rows, cols)):
            if i == 0 and pairs < members:
                source, pair_at = kept, k
            else:
                pair_at = pair
            target = out.at[pl.ds(at, source.shape[1])]
            copies.append(pltpu.make_async_copy(source.at[pair_at], target, left.at[4 * k + i]))
            copies[-1].start()
            at += source.shape[1]
    for i in (0, 2, 5):
        loads[i].wait()
    for c in range(2):
        fields[0, c * side : (c + 1) * side] = currents[c].astype(BF16)
    lane = iota((1, width), 1)
    numbers = jnp.zeros((1, width), F32)
    for q in range(4):
        numbers = jnp.where(lane == q, (links[0, 0, q] >> 7).astype(F32), numbers)
        numbers = jnp.where(lane == 4 + q, (links[0, 0, q] & 127).astype(F32), numbers)
    ends = ocean_columns(water) + [numbers]
    blank = jnp.zeros((tail.shape[0] - len(ends), width), F32)
    tail[...] = jnp.concatenate(ends + [blank], axis=0).astype(BF16)
    for k, out in enumerate(outs):
        at = side + depth
        if out.shape[0] == at:
            continue
        for i, source in enumerate((fields.at[0], tail)):
            target = out.at[pl.ds(at, source.shape[0])]
            copies.append(pltpu.make_async_copy(source, target, left.at[4 * k + 2 + i]))
            copies[-1].start()
            at += source.shape[0]
    for copy in copies:
        copy.wait()


def put_side_rims(store, planes, at):
    size = planes[0].shape[0]
    lane = iota((size, size), 1)
    mixed = jnp.zeros((size, size), F32)
    for i, plane in enumerate(planes):
        turned = roll(plane, DEPTH + 2 * DEPTH * i, 1)
        mixed = jnp.where(lane // (2 * DEPTH) == i, turned, mixed)
    across = mixed.T
    for i, plane in enumerate(planes):
        for k in range(DEPTH):
            base = i * DEPTH + k
            store[at(0) + base : at(0) + base + 1] = plane[size - 1 - k : size - k]
            store[at(1) + base : at(1) + base + 1] = plane[k : k + 1]
            east = 2 * DEPTH * i + DEPTH - 1 - k
            west = 2 * DEPTH * i + DEPTH + k
            store[at(2) + base : at(2) + base + 1] = across[east : east + 1]
            store[at(3) + base : at(3) + base + 1] = across[west : west + 1]


def rims_kernel(
    thick, conc, ice, water, out, viscous_o, gain_o, mass_o, drag_o, conduct_o,
    speed_o, store,
):
    size = thick.shape[1]
    cover = jnp.zeros((size, size), F32)
    volume = jnp.zeros((size, size), F32)
    conduct = jnp.zeros((size, size), F32)
    for c in range(thick.shape[0]):
        h, a = thick[c], conc[c]
        cover = cover + a
        volume = volume + a * h
        conduct = conduct + a / (h + THIN_ICE)
    mass = volume + BASE_MASS
    viscous = VISCOUS_STEP * (volume * jnp.exp(-STRENGTH_DECAY * (1.0 - cover))) / mass
    step_mass = SUBCYCLE_STEP / mass
    gain = 1.0 / (1.0 + step_mass * cover)
    speed_x = ice[pl.ds(0, size, stride=2), :]
    speed_y = ice[pl.ds(1, size, stride=2), :]
    viscous_o[...] = viscous
    gain_o[...] = gain
    mass_o[...] = step_mass
    drag_o[...] = cover
    conduct_o[...] = -HEAT_RATE * conduct
    speed_o[0] = speed_x
    speed_o[1] = speed_y
    put_side_rims(store, [speed_x, speed_y, viscous, gain], lambda side: side * 4 * DEPTH)
    levels, rows, width = water.shape
    start = SIDE_ROWS
    for l in range(levels):
        for j in range(2):
            at = start + 2 * l + j
            store[at : at + 1] = water[l, rows - 1 - j : rows - j]
            store[at + 2 * levels : at + 2 * levels + 1] = water[l, j : j + 1]
    out[...] = store[...].astype(BF16)


def nearby(me, members, distance, arrays):
    at = me + distance
    inside = (at >= 0) & (at < members)
    found = 0.0
    for k in range(1, members):
        found = found + arrays[k].astype(F32) * flag(inside & ((me ^ k) == at))
    return found


def remap_forward(chunks, field_rows, side, depth):
    total = None
    for chunk, fields in zip(chunks, field_rows):
        down = chunk[0:side]
        right = chunk[side : side + depth]
        wide = jnp.concatenate(fields, axis=1) if len(fields) > 1 else fields[0]
        part = lax.dot_general(down, wide, (((0,), (0,)), ((), ())), preferred_element_type=F32)
        part = part.astype(BF16)
        width = fields[0].shape[1]
        if len(fields) > 1:
            part = jnp.concatenate(
                [part[:, c * width : (c + 1) * width] for c in range(len(fields))], axis=0
            )
        piece = lax.dot_general(part, right, (((1,), (1,)), ((), ())), preferred_element_type=F32)
        piece = piece.astype(BF16).astype(F32)
        total = piece if total is None else total + piece
    return total


def tails_of(chunks, hops):
    at = min(c.shape[0] for c in chunks)
    return [hops[k // 2 - 1][...] if k > 1 and k % 2 else c[at:] for k, c in enumerate(chunks)]


def forcing_kernel(group, side, levels, subs, place, mass, drag, wind, early, *refs):
    chunks = refs[:group][::-1]
    hops, (out, current_o, push_o, store) = refs[group:-4], refs[-4:]
    size = mass.shape[0]
    depth = chunks[0].shape[1]
    tails = tails_of(chunks, hops)
    fields = [[t[0:side], t[side : 2 * side]] for t in tails]
    total = remap_forward(chunks, fields, side, depth)
    pushes = []
    for c in range(2):
        current = total[c * size : (c + 1) * size]
        current_o[c] = current
        force = wind[pl.ds(c, size, stride=2), :]
        push = mass[...] * (force + drag[...] * current)
        push_o[c] = push
        pushes.append(push)
    put_side_rims(store, pushes, lambda q: q * 2 * DEPTH)
    tail = [t[2 * side :] for t in tails]
    store[NAMES_ROW : NAMES_ROW + 1] = tail[0].astype(F32)[2 * levels : 2 * levels + 1]
    me, step = place(), group // subs
    left, right = (nearby(me, group, d * step, tail) for d in (-1, 1))
    line = iota((1, size), 1)
    for l in range(levels):
        near = slice(2 * l, 2 * l + 1)
        store[CORNER_ROWS[l] : CORNER_ROWS[l] + 1] = jnp.where(line < side, left[near], right[near])
    out[0:PUSH_ROWS] = store[...].astype(BF16)
    out[PUSH_ROWS:] = early[...]


def ocean_halos(counts, tile_place, member_place, shape, messages, tails):
    tiles, subs, levs = counts
    levels, rows, width = shape
    my_tile, me = tile_place(), member_place()
    halo = {}
    strips = [m[BLOCK_ROWS : BLOCK_ROWS + 4 * levels] for m in messages]
    rims = [m[0:PUSH_ROWS] for m in messages]
    ends = [t[2 * rows :] for t in tails]
    for dt in (-1, 1):
        beyond = nearby(my_tile, tiles, dt, strips)
        halo[dt, 0] = beyond[: 2 * levels] if dt < 0 else beyond[2 * levels :]
        corners = nearby(my_tile, tiles, dt, rims)
        corners = jnp.concatenate([corners[r : r + 1] for r in CORNER_ROWS[:levels]], axis=0)
        at = rows - 1 if dt < 0 else 0
        for ds in (-1, 1):
            lane_at = at if ds < 0 else rows + at
            halo[dt, ds] = corners[:, lane_at : lane_at + 1]
    for ds in (-1, 1):
        beside = nearby(me, subs * levs, ds * levs, ends)[: 2 * levels]
        halo[0, ds] = roll(beside, -rows, 1) if ds > 0 else beside
    return halo


def biharmonic(x, top, bottom, left, right, corner):
    rows, width = x.shape
    row, lane = iota(x.shape, 0), iota(x.shape, 1)
    line = iota((1, width), 1)

    def laplacian(x, top, bottom, left, right):
        up = jnp.where(row == 0, top, roll(x, 1, 0))
        down = jnp.where(row == rows - 1, bottom, roll(x, -1, 0))
        west = jnp.where(lane == 0, left, roll(x, 1, 1))
        east = jnp.where(lane == width - 1, right, roll(x, -1, 1))
        return up + down + west + east - 4.0 * x

    def ring_row(mid, out_row, in_row, dt):
        west = jnp.where(line == 0, corner[dt, -1], roll(mid, 1, 1))
        east = jnp.where(line == width - 1, corner[dt, 1], roll(mid, -1, 1))
        return west + east + out_row + in_row - 4.0 * mid

    def ring_col(mid, out_col, in_col, ds):
        up = jnp.concatenate([corner[-1, ds], mid[:-1]], axis=0)
        down = jnp.concatenate([mid[1:], corner[1, ds]], axis=0)
        return up + down + out_col + in_col - 4.0 * mid

    return laplacian(
        laplacian(x, top[0], bottom[0], left[0], right[0]),
        ring_row(*top, x[0:1], -1),
        ring_row(*bottom, x[rows - 1 :], 1),
        ring_col(*left, x[:, 0:1], -1),
        ring_col(*right, x[:, width - 1 :], 1),
    )


def split_refs(tiles, members, refs, outs):
    messages, chunks = refs[:tiles], refs[tiles : tiles + members]
    return messages, tails_of(chunks, refs[tiles + members : -outs]), refs[-outs:]


def relay_kernel(counts, tile_place, member_place, water, mixing, *refs):
    tiles, subs, levs = counts
    outs = 1 if levs == 1 else 2
    messages, tails, outs = split_refs(tiles, subs * levs, refs, outs)
    for k in range(tiles):
        outs[0][k * BLOCK_ROWS : (k + 1) * BLOCK_ROWS] = messages[k][0:BLOCK_ROWS]
    levels, rows, width = water.shape
    halo = ocean_halos(counts, tile_place, member_place, water.shape, messages, tails)

    def both(strip):
        near = sum(strip[2 * l : 2 * l + 1] for l in range(levels))
        far = sum(strip[2 * l + 1 : 2 * l + 2] for l in range(levels))
        return near, far

    def as_columns(strip):
        near, far = both(strip)
        across = jnp.concatenate([near, far] + [jnp.zeros_like(near)] * 6, axis=0).T
        return across[0:rows, 0:1], across[0:rows, 1:2]

    corner = {
        (dt, ds): jnp.sum(halo[dt, ds], axis=0, keepdims=True) for dt in (-1, 1) for ds in (-1, 1)
    }
    x = sum(water[l] for l in range(levels))
    twice = biharmonic(
        x, both(halo[-1, 0]), both(halo[1, 0]), as_columns(halo[0, -1]), as_columns(halo[0, 1]), corner
    )
    top = (x - mixing[...] * twice) / (levels * levs)
    if levs == 1:
        outs[0][tiles * BLOCK_ROWS :] = top.astype(BF16)
    else:
        outs[1][...] = top


def ocean_kernel(counts, tile_place, member_place, water, mixing, *refs):
    tiles, subs, levs = counts
    messages, tails, (warm_o,) = split_refs(tiles, subs * levs, refs, 1)
    levels, rows, width = water.shape
    halo = ocean_halos(counts, tile_place, member_place, water.shape, messages, tails)
    left, right = halo[0, -1].T, halo[0, 1].T
    for l in range(levels):
        x = water[l]
        pair = (2 * l, 2 * l + 1)
        twice = biharmonic(
            x,
            [halo[-1, 0][i : i + 1] for i in pair],
            [halo[1, 0][i : i + 1] for i in pair],
            [left[0:rows, i : i + 1] for i in pair],
            [right[0:rows, i : i + 1] for i in pair],
            {(dt, ds): halo[dt, ds][l : l + 1] for dt in (-1, 1) for ds in (-1, 1)},
        )
        warm_o[l] = x - mixing[...] * twice


def subcycles_kernel(tiles, members, table, viscous, gain, speed, push, *refs):
    relays, (out, rims, names, named) = refs[:members], refs[members:]
    load_names = pltpu.make_async_copy(table, names, named)
    load_names.start()
    size = viscous.shape[0]
    for k in range(tiles):
        for m in range(members):
            rims[k * members + m] = relays[m][k * BLOCK_ROWS : (k + 1) * BLOCK_ROWS]
    half = DEPTH
    high = 2 * DEPTH
    sub = iota((high, size), 0)
    lane = iota((high, size), 1)
    edge = (sub & (half - 1)) == 0
    turn = jnp.where(sub < half, CORIOLIS_TURN, -CORIOLIS_TURN).astype(F32)
    first, last = lane == 0, lane == size - 1

    def load(device, side, mask, with_push=True):
        start = PUSH_ROWS + side * 2 * high
        block = rims[device, start : start + 2 * high].astype(F32)
        velocity, both = block[:high] * mask, block[high:]
        if not with_push:
            return velocity
        other = roll(both, half, 0)
        visc = jnp.where(sub < half, both, other)
        scale = jnp.where(sub < half, other, both) * mask
        start = side // 2 * 2 * high
        pushed = rims[device, start : start + 2 * high].astype(F32)
        pushed = pushed[:high] if side % 2 == 0 else pushed[high:]
        return [velocity, visc, scale, pushed]

    def follow(device, side):
        name = names[device, side]
        return jnp.where(name >= 0, name, 0), name >= 0

    def step(state, left, right, inner, outer):
        c, visc, scale, pushed = state
        spread = left + right + inner + outer - 4.0 * c
        return scale * (c + visc * spread + pushed + turn * roll(c, half, 0))

    row = iota((size, size), 0)
    col = iota((size, size), 1)
    vx, vy = speed[0], speed[1]
    visc, scale, push_x, push_y = viscous[...], gain[...], push[0], push[1]

    def interior(v):
        up = jnp.where(row == size - 1, 0.0, roll(v, -1, 0))
        down = jnp.where(row == 0, 0.0, roll(v, 1, 0))
        right = jnp.where(col == size - 1, 0.0, roll(v, -1, 1))
        left = jnp.where(col == 0, 0.0, roll(v, 1, 1))
        return up + down + right + left - 4.0 * v

    def rim_of(north, south, east, west):
        up = jnp.where(row == size - 1, north, jnp.where(row == 0, south, 0.0))
        return up + jnp.where(col == size - 1, east, jnp.where(col == 0, west, 0.0))

    def own_edges(vx, vy):
        mixed = jnp.where(col < half, roll(vx, 1, 1), roll(vy, 1 + half, 1))
        across = mixed.T[0:high]
        return [
            jnp.where(sub < half, vx[size - 1 :], vy[size - 1 :]),
            jnp.where(sub < half, vx[0:1], vy[0:1]),
            across,
            roll(across, -1, 0),
        ]

    own = own_edges(vx, vy)
    inner_x, inner_y = interior(vx), interior(vy)
    load_names.wait()
    strips = []
    for q in range(4):
        x, has_x = follow(0, q)
        strip = load(x, OPPOSITE[q], flag(has_x))
        sides = []
        for s in LATERAL[q]:
            y, has_y = follow(x, s)
            z, has_z = follow(y, OPPOSITE[q])
            w, has_w = follow(z, OPPOSITE[s])
            sides.append(
                [
                    load(y, OPPOSITE[q], flag(has_y)),
                    load(z, q, flag(has_z)),
                    load(w, q, flag(has_w), with_push=False),
                ]
            )
        strips.append((strip, sides))

    for t in range(SUBCYCLES):
        cells = [strip[0] for strip, _ in strips]
        if t < SUBCYCLES - 1:
            if t > 0:
                own = own_edges(vx, vy)
            for q in range(4):
                strip, (beyond, before) = strips[q]
                c, y_hi, y_lo = strip[0], beyond[0][0], before[0][0]
                left = jnp.where(first, roll(y_lo, 1, 1), roll(c, 1, 1))
                right = jnp.where(last, roll(y_hi, -1, 1), roll(c, -1, 1))
                inner = jnp.where(edge, own[q], roll(c, 1, 0))
                new_strip = step(strip, left, right, inner, roll(c, -1, 0))
                if t < SUBCYCLES - 2:
                    new_sides = []
                    for i, (y, z, w) in enumerate((beyond, before)):
                        away = 1 if i == 0 else -1
                        boundary = first if i == 0 else last
                        yc, zc = y[0], z[0]
                        toward = jnp.where(boundary, roll(c, away, 1), roll(yc, away, 1))
                        inner = jnp.where(edge, zc, roll(yc, 1, 0))
                        new_y = step(y, toward, roll(yc, -away, 1), inner, roll(yc, -1, 0))
                        new_z = zc
                        if t < SUBCYCLES - 3:
                            toward = jnp.where(boundary, roll(w, away, 1), roll(zc, away, 1))
                            inner = jnp.where(edge, yc, roll(zc, 1, 0))
                            new_z = step(z, toward, roll(zc, -away, 1), inner, roll(zc, -1, 0))
                        new_sides.append((new_y, new_z))
                    for item, (new_y, new_z) in zip((beyond, before), new_sides):
                        item[0][0] = new_y
                        item[1][0] = new_z
                strip[0] = new_strip
        north, south = cells[0], cells[1]
        sides = jnp.where(edge, cells[2], roll(cells[3], 1, 0)).T
        east_x, west_x = sides[:, 0:1], sides[:, 1:2]
        east_y, west_y = sides[:, half : half + 1], sides[:, half + 1 : half + 2]
        if t > 0:
            inner_x, inner_y = interior(vx), interior(vy)
        spread_x = inner_x + rim_of(north[0:1], south[0:1], east_x, west_x)
        spread_y = inner_y + rim_of(
            north[half : half + 1], south[half : half + 1], east_y, west_y
        )
        new_x = scale * (vx + visc * spread_x + push_x + CORIOLIS_TURN * vy)
        new_y = scale * (vy + visc * spread_y + push_y - CORIOLIS_TURN * vx)
        vx, vy = new_x, new_y
    out[0] = vx
    out[1] = vy


def back_kernel(group, side, drag, conduct, current, speed, *refs):
    chunks, relays, outs = refs[:group], refs[group : 2 * group], refs[2 * group :]
    size = drag.shape[0]
    depth = chunks[0].shape[1]
    warm = remap_forward(chunks, [[r[r.shape[0] - side :]] for r in relays], side, depth)
    heat = conduct[...] * warm
    fluxes = [heat.astype(BF16)]
    for c in range(2):
        fluxes.append((drag[...] * (speed[c] - current[c])).astype(BF16))
    wide = jnp.concatenate(fluxes, axis=1)
    for chunk, out in zip(chunks, outs):
        part = jnp.dot(chunk[0:side], wide, preferred_element_type=F32).astype(BF16)
        part = jnp.concatenate([part[:, c * size : (c + 1) * size] for c in range(3)], axis=0)
        reply = jnp.dot(part, chunk[side : side + depth], preferred_element_type=F32)
        out[...] = reply.astype(BF16)


def finish_kernel(warm, currents, speed, *refs):
    outs, (flat, heat_v, current_v, left) = refs[-7:-4], refs[-4:]
    replies = refs[:-7]
    flat_o, heat_o, current_o = outs
    size = speed.shape[1]
    copies = [
        pltpu.make_async_copy(source, target, left.at[i])
        for i, (source, target) in enumerate(
            ((flat, flat_o), (heat_v, heat_o), (current_v, current_o))
        )
    ]
    for c in range(2):
        flat[pl.ds(c, size, stride=2), :] = speed[c]
    copies[0].start()
    total = replies[0][...].astype(F32)
    for reply in replies[1:]:
        total = total + reply[...].astype(F32)
    side = currents.shape[1]
    heat = THERMAL_DIFFUSE * total[0:side]
    for l in range(warm.shape[0]):
        heat_v[l] = warm[l] + heat
    copies[1].start()
    for c in range(2):
        current_v[c] = currents[c] + STRESS_MIXING * total[(c + 1) * side : (c + 2) * side]
    copies[2].start()
    for copy in copies:
        copy.wait()


def shards(
    water_heat_state,
    diffusion_coefficient,
    upper_current_vector,
    remap_blocks,
    remap_rows,
    remap_cols,
    neighbors,
    thickness,
    concentration,
    ice_velocity,
    wind_stress,
):
    tile_count, sub_count, lev_count = (lax.axis_size(a) for a in ("tile", "sub", "lev"))
    group = sub_count * lev_count
    devices = tile_count * group
    group_axes = ("sub", "lev")
    member_axes = ("tile", "sub", "lev")
    levels, side, width = water_heat_state.shape
    pairs, size = remap_rows.shape[1:3]
    categories = thickness.shape[2]

    def tile_place():
        return lax.axis_index("tile")

    def member_place():
        return lax.axis_index("sub") * lev_count + lax.axis_index("lev")

    def device_place():
        return lax.axis_index("tile") * group + member_place()

    def far_first(count):
        return [*range(2, count), 1]

    def swap(value, axes, count):
        got = {0: value}
        for k in far_first(count):
            got[k] = lax.ppermute(value, axes, [(i, i ^ k) for i in range(count)])
        return [got[k] for k in range(count)]

    def swap_chips(value):
        return {0: value} | {
            k: lax.ppermute(value, group_axes, [(i, i ^ k) for i in range(group)])
            for k in range(2, group, 2)
        }

    def swap_cores(got):
        beside = [(i, i ^ 1) for i in range(group)]
        got = got | {k + 1: lax.ppermute(got[k], group_axes, beside) for k in got}
        return [got[k] for k in range(group)]

    def swap_each(values):
        got = {0: values[0]}
        for k in far_first(group):
            got[k] = lax.ppermute(values[k], group_axes, [(i, i ^ k) for i in range(group)])
        return [got[k] for k in range(group)]

    def shape(*dims, dtype=F32):
        return jax.ShapeDtypeStruct(dims, dtype)

    def interleaved(value):
        return value.reshape(2, size, size).transpose(1, 0, 2).reshape(2 * size, size)

    plane = shape(size, size)
    planes = shape(2, size, size)
    wind = interleaved(wind_stress)

    tail_rows = -(-(2 * levels + 1) // TILE_ROWS) * TILE_ROWS
    pair_rows = side + width
    chunk_rows = pair_rows + 2 * side + tail_rows
    sent = call(
        functools.partial(forward_kernel, (devices, group, member_place)),
        [
            shape(pair_rows if k > 1 and k % 2 else chunk_rows, width, dtype=BF16)
            for k in range(group)
        ],
        (
            neighbors,
            remap_blocks,
            remap_rows[0].swapaxes(1, 2),
            remap_cols[0],
            upper_current_vector,
            water_heat_state,
        ),
        scratch=[
            pltpu.SMEM(neighbors.shape, jnp.int32),
            pltpu.SMEM((1, pairs), jnp.int32),
            pltpu.VMEM((2, side, width), F32),
            pltpu.VMEM((pairs, side, size), BF16),
            pltpu.VMEM((pairs, size, width), BF16),
            pltpu.VMEM((levels, side, width), F32),
            pltpu.VMEM((1, 2 * side, width), BF16),
            pltpu.VMEM((tail_rows, width), BF16),
            pltpu.VMEM((1 if pairs == group else group, side, size), BF16),
            pltpu.SemaphoreType.DMA((6,)),
            pltpu.SemaphoreType.DMA((4 * group,)),
        ],
        hbm=(0, 1, 2, 3, 4, 5),
        grant=60 * 2**20,
        micros=10,
    )
    chunks = swap_each(sent)
    hops = [
        lax.ppermute(chunks[k][pair_rows:], group_axes, [(i, i ^ 1) for i in range(group)])
        for k in range(2, group, 2)
    ]

    early, viscous, gain, step_mass, drag, conduct, speed = call(
        rims_kernel,
        [shape(SIDE_ROWS + 4 * levels, size, dtype=BF16)] + [plane] * 5 + [planes],
        (
            thickness.reshape(categories, size, size),
            concentration.reshape(categories, size, size),
            interleaved(ice_velocity),
            water_heat_state,
        ),
        scratch=[pltpu.VMEM((SIDE_ROWS + 4 * levels, size), F32)],
    )
    message, current_ice, push = call(
        functools.partial(forcing_kernel, group, side, levels, sub_count, member_place),
        [shape(BLOCK_ROWS + 4 * levels, size, dtype=BF16), planes, planes],
        (step_mass, drag, wind, early, *chunks[::-1], *hops),
        scratch=[pltpu.VMEM((PUSH_ROWS, size), F32)],
    )
    messages = swap(message, "tile", tile_count)

    counts = (tile_count, sub_count, lev_count)
    ocean = (*messages, *chunks, *hops)
    relay_rows = tile_count * BLOCK_ROWS
    relay_shapes = [shape(relay_rows + (side if lev_count == 1 else 0), size, dtype=BF16)]
    if lev_count > 1:
        relay_shapes.append(shape(side, width))
    relay, *top = call(
        functools.partial(relay_kernel, counts, tile_place, member_place),
        relay_shapes,
        (water_heat_state, diffusion_coefficient, *ocean),
    )
    if lev_count > 1:
        relay = jnp.concatenate([relay, lax.psum(top[0], "lev").astype(BF16)], axis=0)
    relays = swap_chips(relay)

    mixing, _ = lax.optimization_barrier((diffusion_coefficient, relay))
    (warm,) = call(
        functools.partial(ocean_kernel, counts, tile_place, member_place),
        [shape(levels, side, width)],
        (water_heat_state, mixing, *ocean),
    )
    far = sorted(k for k in relays if k)
    relayed, _ = lax.optimization_barrier(([relays[k] for k in far], warm))
    relays = swap_cores({0: relay} | dict(zip(far, relayed)))

    names = jnp.stack(
        [
            r[:relay_rows].reshape(tile_count, BLOCK_ROWS, size)[:, NAMES_ROW, 0:8]
            for r in relays
        ],
        axis=1,
    )
    names = names.reshape(devices, 8).astype(jnp.int32)
    table = names[:, 0:4] * 128 + names[:, 4:8]
    table = jnp.where(table < 0, -1, table ^ device_place())
    speed = call(
        functools.partial(subcycles_kernel, tile_count, group),
        planes,
        (table, viscous, gain, speed, push, *relays),
        scratch=[
            pltpu.VMEM((devices, BLOCK_ROWS, size), BF16),
            pltpu.SMEM((devices, 4), jnp.int32),
            pltpu.SemaphoreType.DMA,
        ],
        hbm=(0,),
    )

    replies = call(
        functools.partial(back_kernel, group, side),
        [shape(3 * side, width, dtype=BF16)] * group,
        (drag, conduct, current_ice, speed, *chunks, *relays),
    )
    replies = swap_each(replies)
    if lev_count > 1:
        replies = [lax.psum(sum(r.astype(F32) for r in replies), "lev")]
    flat, heat, current = call(
        finish_kernel,
        [shape(2 * size, size), shape(levels, side, width), shape(2, side, width)],
        (warm, upper_current_vector, speed, *replies[::-1]),
        scratch=[
            pltpu.VMEM((2 * size, size), F32),
            pltpu.VMEM((levels, side, width), F32),
            pltpu.VMEM((2, side, width), F32),
            pltpu.SemaphoreType.DMA((3,)),
        ],
        out_space=pltpu.HBM,
    )
    velocity = flat.reshape(size, 2, size).transpose(1, 0, 2).reshape(1, 1, 2, size * size)
    return heat, current, velocity


def solution(mesh):
    member = ("tile", "sub", "lev")
    whole = ("copies",) + member
    ice = P(None, whole, None, None)
    water = P("lev", ("copies", "tile"), "sub")
    current = P(None, ("copies", "tile"), "sub")
    return jax.shard_map(
        shards,
        mesh=mesh,
        in_specs=(
            water,
            P("tile", "sub"),
            current,
            P(member, None),
            P(member, None, None, None),
            P(member, None, None, None),
            P(None, member, None),
            ice,
            ice,
            ice,
            ice,
        ),
        out_specs=(water, current, ice),
        check_vma=False,
    )
```

```python
import functools

import jax
import jax.numpy as jnp
from jax import lax
from jax.experimental import pallas as pl
from jax.experimental.pallas import tpu as pltpu
from jax.sharding import PartitionSpec as P

SUBCYCLES = 4
STRENGTH_DECAY = 5.0
VISCOUS_STEP = 0.24
SUBCYCLE_STEP = 0.5
CORIOLIS_TURN = 0.1
BASE_MASS = 0.5
HEAT_RATE = 0.2
THIN_ICE = 0.1
THERMAL_DIFFUSE = 0.5
STRESS_MIXING = 0.5

OPPOSITE = (1, 0, 3, 2)
LATERAL = ((2, 3), (2, 3), (0, 1), (0, 1))
DEPTH = SUBCYCLES
SIDE_ROWS = 16 * DEPTH
PUSH_ROWS = 8 * DEPTH
BLOCK_ROWS = SIDE_ROWS + PUSH_ROWS
NAMES_ROW = 2 * DEPTH - 1
CORNER_ROWS = tuple(DEPTH * i - 1 for i in (1, 3, 4, 5, 6, 7, 8))
TILE_ROWS = 16
F32 = jnp.float32
BF16 = jnp.bfloat16
VMEM_LIMIT = 16 * 1024 * 1024
FLOPS_PER_MICRO = 1.15e9


def call(kernel, outs, args, scratch=(), smem=(), hbm=(), out_space=pltpu.VMEM, grant=VMEM_LIMIT, micros=0.01):
    def space(i):
        return pltpu.SMEM if i in smem else pltpu.HBM if i in hbm else pltpu.VMEM

    specs = [pl.BlockSpec(memory_space=space(i)) for i in range(len(args))]
    size = sum(a.size * a.dtype.itemsize for a in args)
    return pl.pallas_call(
        kernel,
        out_shape=outs,
        in_specs=specs,
        out_specs=jax.tree.map(lambda _: pl.BlockSpec(memory_space=out_space), outs),
        scratch_shapes=list(scratch),
        compiler_params=pltpu.CompilerParams(vmem_limit_bytes=grant),
        cost_estimate=pl.CostEstimate(
            flops=int(micros * FLOPS_PER_MICRO), bytes_accessed=size, transcendentals=0
        ),
    )(*args)


def iota(shape, axis):
    return lax.broadcasted_iota(jnp.int32, shape, axis)


def roll(x, shift, axis):
    return pltpu.roll(x, shift % x.shape[axis], axis)


def flag(condition):
    return jnp.where(condition, 1.0, 0.0).astype(F32)


def ocean_columns(water):
    levels, rows, width = water.shape
    lane = iota((rows, width), 1)
    line = iota((1, width), 1)
    mixed = jnp.zeros((rows, width), F32)
    for l in range(levels):
        mixed = jnp.where(lane // 4 == l, roll(water[l], 2 + 4 * l, 1), mixed)
    across = jnp.concatenate([mixed, jnp.zeros((width - rows, width), F32)], axis=0).T
    beside = []
    for l in range(levels):
        for j in range(2):
            last = across[4 * l + 1 - j : 4 * l + 2 - j]
            lead = across[4 * l + 2 + j : 4 * l + 3 + j]
            beside.append(jnp.where(line < rows, last, roll(lead, rows, 1)))
    return beside


def forward_kernel(group, links_h, blocks_h, rows_h, cols_h, currents_h, water_h, *refs):
    devices, members, place = group
    outs, scratch = refs[:members], refs[members:]
    links, blocks, currents, rows, cols, water, fields, tail, kept, arrived, left = scratch
    pairs, side, width = rows_h.shape
    depth = cols_h.shape[1]
    loads = [
        pltpu.make_async_copy(source, target, arrived.at[i])
        for i, (source, target) in enumerate(
            (
                (links_h, links),
                (blocks_h, blocks),
                (currents_h, currents),
                (rows_h, rows),
                (cols_h, cols),
                (water_h, water),
            )
        )
    ]
    for load in loads:
        load.start()
    for i in (1, 3, 4):
        loads[i].wait()
    me = place()
    side, depth, pairs = rows.shape[1], cols.shape[1], rows.shape[0]
    owners = [lax.rem(lax.rem(blocks[0, m], devices), members) for m in range(pairs)]
    copies = []
    for k, out in enumerate(outs):
        partner = me ^ k
        pair = jnp.int32(0)
        for m in range(pairs):
            pair = jnp.where(owners[m] == partner, m, pair)
        if pairs < members:
            found = sum(flag(owners[m] == partner) for m in range(pairs))
            kept[k] = (rows[pair].astype(F32) * found).astype(BF16)
        at = 0
        for i, source in enumerate((rows, cols)):
            if i == 0 and pairs < members:
                source, pair_at = kept, k
            else:
                pair_at = pair
            target = out.at[pl.ds(at, source.shape[1])]
            copies.append(pltpu.make_async_copy(source.at[pair_at], target, left.at[4 * k + i]))
            copies[-1].start()
            at += source.shape[1]
    for i in (0, 2, 5):
        loads[i].wait()
    for c in range(2):
        fields[0, c * side : (c + 1) * side] = currents[c].astype(BF16)
    lane = iota((1, width), 1)
    numbers = jnp.zeros((1, width), F32)
    for q in range(4):
        numbers = jnp.where(lane == q, (links[0, 0, q] >> 7).astype(F32), numbers)
        numbers = jnp.where(lane == 4 + q, (links[0, 0, q] & 127).astype(F32), numbers)
    ends = ocean_columns(water) + [numbers]
    blank = jnp.zeros((tail.shape[0] - len(ends), width), F32)
    tail[...] = jnp.concatenate(ends + [blank], axis=0).astype(BF16)
    for k, out in enumerate(outs):
        at = side + depth
        if out.shape[0] == at:
            continue
        for i, source in enumerate((fields.at[0], tail)):
            target = out.at[pl.ds(at, source.shape[0])]
            copies.append(pltpu.make_async_copy(source, target, left.at[4 * k + 2 + i]))
            copies[-1].start()
            at += source.shape[0]
    for copy in copies:
        copy.wait()


def put_side_rims(store, planes, at):
    size = planes[0].shape[0]
    lane = iota((size, size), 1)
    mixed = jnp.zeros((size, size), F32)
    for i, plane in enumerate(planes):
        turned = roll(plane, DEPTH + 2 * DEPTH * i, 1)
        mixed = jnp.where(lane // (2 * DEPTH) == i, turned, mixed)
    across = mixed.T
    for i, plane in enumerate(planes):
        for k in range(DEPTH):
            base = i * DEPTH + k
            store[at(0) + base : at(0) + base + 1] = plane[size - 1 - k : size - k]
            store[at(1) + base : at(1) + base + 1] = plane[k : k + 1]
            east = 2 * DEPTH * i + DEPTH - 1 - k
            west = 2 * DEPTH * i + DEPTH + k
            store[at(2) + base : at(2) + base + 1] = across[east : east + 1]
            store[at(3) + base : at(3) + base + 1] = across[west : west + 1]


def rims_kernel(
    thick, conc, ice, water, out, viscous_o, gain_o, mass_o, drag_o, conduct_o,
    speed_o, store,
):
    size = thick.shape[1]
    cover = jnp.zeros((size, size), F32)
    volume = jnp.zeros((size, size), F32)
    conduct = jnp.zeros((size, size), F32)
    for c in range(thick.shape[0]):
        h, a = thick[c], conc[c]
        cover = cover + a
        volume = volume + a * h
        conduct = conduct + a / (h + THIN_ICE)
    mass = volume + BASE_MASS
    viscous = VISCOUS_STEP * (volume * jnp.exp(-STRENGTH_DECAY * (1.0 - cover))) / mass
    step_mass = SUBCYCLE_STEP / mass
    gain = 1.0 / (1.0 + step_mass * cover)
    speed_x = ice[pl.ds(0, size, stride=2), :]
    speed_y = ice[pl.ds(1, size, stride=2), :]
    viscous_o[...] = viscous
    gain_o[...] = gain
    mass_o[...] = step_mass
    drag_o[...] = cover
    conduct_o[...] = -HEAT_RATE * conduct
    speed_o[0] = speed_x
    speed_o[1] = speed_y
    put_side_rims(store, [speed_x, speed_y, viscous, gain], lambda side: side * 4 * DEPTH)
    levels, rows, width = water.shape
    start = SIDE_ROWS
    for l in range(levels):
        for j in range(2):
            at = start + 2 * l + j
            store[at : at + 1] = water[l, rows - 1 - j : rows - j]
            store[at + 2 * levels : at + 2 * levels + 1] = water[l, j : j + 1]
    out[...] = store[...].astype(BF16)


def nearby(me, members, distance, arrays):
    at = me + distance
    inside = (at >= 0) & (at < members)
    found = 0.0
    for k in range(1, members):
        found = found + arrays[k].astype(F32) * flag(inside & ((me ^ k) == at))
    return found


def remap_forward(chunks, field_rows, side, depth):
    total = None
    for chunk, fields in zip(chunks, field_rows):
        down = chunk[0:side]
        right = chunk[side : side + depth]
        wide = jnp.concatenate(fields, axis=1) if len(fields) > 1 else fields[0]
        part = lax.dot_general(down, wide, (((0,), (0,)), ((), ())), preferred_element_type=F32)
        part = part.astype(BF16)
        width = fields[0].shape[1]
        if len(fields) > 1:
            part = jnp.concatenate(
                [part[:, c * width : (c + 1) * width] for c in range(len(fields))], axis=0
            )
        piece = lax.dot_general(part, right, (((1,), (1,)), ((), ())), preferred_element_type=F32)
        piece = piece.astype(BF16).astype(F32)
        total = piece if total is None else total + piece
    return total


def tails_of(chunks, hops):
    at = min(c.shape[0] for c in chunks)
    return [hops[k // 2 - 1][...] if k > 1 and k % 2 else c[at:] for k, c in enumerate(chunks)]


def forcing_kernel(group, side, levels, subs, place, mass, drag, wind, early, *refs):
    chunks = refs[:group][::-1]
    hops, (out, current_o, push_o, store) = refs[group:-4], refs[-4:]
    size = mass.shape[0]
    depth = chunks[0].shape[1]
    tails = tails_of(chunks, hops)
    fields = [[t[0:side], t[side : 2 * side]] for t in tails]
    total = remap_forward(chunks, fields, side, depth)
    pushes = []
    for c in range(2):
        current = total[c * size : (c + 1) * size]
        current_o[c] = current
        force = wind[pl.ds(c, size, stride=2), :]
        push = mass[...] * (force + drag[...] * current)
        push_o[c] = push
        pushes.append(push)
    put_side_rims(store, pushes, lambda q: q * 2 * DEPTH)
    tail = [t[2 * side :] for t in tails]
    store[NAMES_ROW : NAMES_ROW + 1] = tail[0].astype(F32)[2 * levels : 2 * levels + 1]
    me, step = place(), group // subs
    left, right = (nearby(me, group, d * step, tail) for d in (-1, 1))
    line = iota((1, size), 1)
    for l in range(levels):
        near = slice(2 * l, 2 * l + 1)
        store[CORNER_ROWS[l] : CORNER_ROWS[l] + 1] = jnp.where(line < side, left[near], right[near])
    out[0:PUSH_ROWS] = store[...].astype(BF16)
    out[PUSH_ROWS:] = early[...]


def ocean_halos(counts, tile_place, member_place, shape, messages, tails):
    tiles, subs, levs = counts
    levels, rows, width = shape
    my_tile, me = tile_place(), member_place()
    halo = {}
    strips = [m[BLOCK_ROWS : BLOCK_ROWS + 4 * levels] for m in messages]
    rims = [m[0:PUSH_ROWS] for m in messages]
    ends = [t[2 * rows :] for t in tails]
    for dt in (-1, 1):
        beyond = nearby(my_tile, tiles, dt, strips)
        halo[dt, 0] = beyond[: 2 * levels] if dt < 0 else beyond[2 * levels :]
        corners = nearby(my_tile, tiles, dt, rims)
        corners = jnp.concatenate([corners[r : r + 1] for r in CORNER_ROWS[:levels]], axis=0)
        at = rows - 1 if dt < 0 else 0
        for ds in (-1, 1):
            lane_at = at if ds < 0 else rows + at
            halo[dt, ds] = corners[:, lane_at : lane_at + 1]
    for ds in (-1, 1):
        beside = nearby(me, subs * levs, ds * levs, ends)[: 2 * levels]
        halo[0, ds] = roll(beside, -rows, 1) if ds > 0 else beside
    return halo


def biharmonic(x, top, bottom, left, right, corner):
    rows, width = x.shape
    row, lane = iota(x.shape, 0), iota(x.shape, 1)
    line = iota((1, width), 1)

    def laplacian(x, top, bottom, left, right):
        up = jnp.where(row == 0, top, roll(x, 1, 0))
        down = jnp.where(row == rows - 1, bottom, roll(x, -1, 0))
        west = jnp.where(lane == 0, left, roll(x, 1, 1))
        east = jnp.where(lane == width - 1, right, roll(x, -1, 1))
        return up + down + west + east - 4.0 * x

    def ring_row(mid, out_row, in_row, dt):
        west = jnp.where(line == 0, corner[dt, -1], roll(mid, 1, 1))
        east = jnp.where(line == width - 1, corner[dt, 1], roll(mid, -1, 1))
        return west + east + out_row + in_row - 4.0 * mid

    def ring_col(mid, out_col, in_col, ds):
        up = jnp.concatenate([corner[-1, ds], mid[:-1]], axis=0)
        down = jnp.concatenate([mid[1:], corner[1, ds]], axis=0)
        return up + down + out_col + in_col - 4.0 * mid

    return laplacian(
        laplacian(x, top[0], bottom[0], left[0], right[0]),
        ring_row(*top, x[0:1], -1),
        ring_row(*bottom, x[rows - 1 :], 1),
        ring_col(*left, x[:, 0:1], -1),
        ring_col(*right, x[:, width - 1 :], 1),
    )


def split_refs(tiles, members, refs, outs):
    messages, chunks = refs[:tiles], refs[tiles : tiles + members]
    return messages, tails_of(chunks, refs[tiles + members : -outs]), refs[-outs:]


def relay_kernel(counts, tile_place, member_place, water, mixing, *refs):
    tiles, subs, levs = counts
    outs = 1 if levs == 1 else 2
    messages, tails, outs = split_refs(tiles, subs * levs, refs, outs)
    for k in range(tiles):
        outs[0][k * BLOCK_ROWS : (k + 1) * BLOCK_ROWS] = messages[k][0:BLOCK_ROWS]
    levels, rows, width = water.shape
    halo = ocean_halos(counts, tile_place, member_place, water.shape, messages, tails)

    def both(strip):
        near = sum(strip[2 * l : 2 * l + 1] for l in range(levels))
        far = sum(strip[2 * l + 1 : 2 * l + 2] for l in range(levels))
        return near, far

    def as_columns(strip):
        near, far = both(strip)
        across = jnp.concatenate([near, far] + [jnp.zeros_like(near)] * 6, axis=0).T
        return across[0:rows, 0:1], across[0:rows, 1:2]

    corner = {
        (dt, ds): jnp.sum(halo[dt, ds], axis=0, keepdims=True) for dt in (-1, 1) for ds in (-1, 1)
    }
    x = sum(water[l] for l in range(levels))
    twice = biharmonic(
        x, both(halo[-1, 0]), both(halo[1, 0]), as_columns(halo[0, -1]), as_columns(halo[0, 1]), corner
    )
    top = (x - mixing[...] * twice) / (levels * levs)
    if levs == 1:
        outs[0][tiles * BLOCK_ROWS :] = top.astype(BF16)
    else:
        outs[1][...] = top


def ocean_kernel(counts, tile_place, member_place, water, mixing, *refs):
    tiles, subs, levs = counts
    messages, tails, (warm_o,) = split_refs(tiles, subs * levs, refs, 1)
    levels, rows, width = water.shape
    halo = ocean_halos(counts, tile_place, member_place, water.shape, messages, tails)
    left, right = halo[0, -1].T, halo[0, 1].T
    for l in range(levels):
        x = water[l]
        pair = (2 * l, 2 * l + 1)
        twice = biharmonic(
            x,
            [halo[-1, 0][i : i + 1] for i in pair],
            [halo[1, 0][i : i + 1] for i in pair],
            [left[0:rows, i : i + 1] for i in pair],
            [right[0:rows, i : i + 1] for i in pair],
            {(dt, ds): halo[dt, ds][l : l + 1] for dt in (-1, 1) for ds in (-1, 1)},
        )
        warm_o[l] = x - mixing[...] * twice


def subcycles_kernel(tiles, members, table, viscous, gain, speed, push, *refs):
    relays, (out, rims, names, named) = refs[:members], refs[members:]
    load_names = pltpu.make_async_copy(table, names, named)
    load_names.start()
    size = viscous.shape[0]
    for k in range(tiles):
        for m in range(members):
            rims[k * members + m] = relays[m][k * BLOCK_ROWS : (k + 1) * BLOCK_ROWS]
    half = DEPTH
    high = 2 * DEPTH
    sub = iota((high, size), 0)
    lane = iota((high, size), 1)
    edge = (sub & (half - 1)) == 0
    turn = jnp.where(sub < half, CORIOLIS_TURN, -CORIOLIS_TURN).astype(F32)
    first, last = lane == 0, lane == size - 1

    def load(device, side, mask, with_push=True):
        start = PUSH_ROWS + side * 2 * high
        block = rims[device, start : start + 2 * high].astype(F32)
        velocity, both = block[:high] * mask, block[high:]
        if not with_push:
            return velocity
        other = roll(both, half, 0)
        visc = jnp.where(sub < half, both, other)
        scale = jnp.where(sub < half, other, both) * mask
        start = side // 2 * 2 * high
        pushed = rims[device, start : start + 2 * high].astype(F32)
        pushed = pushed[:high] if side % 2 == 0 else pushed[high:]
        return [velocity, visc, scale, pushed]

    def follow(device, side):
        name = names[device, side]
        return jnp.where(name >= 0, name, 0), name >= 0

    def step(state, left, right, inner, outer):
        c, visc, scale, pushed = state
        spread = left + right + inner + outer - 4.0 * c
        return scale * (c + visc * spread + pushed + turn * roll(c, half, 0))

    row = iota((size, size), 0)
    col = iota((size, size), 1)
    vx, vy = speed[0], speed[1]
    visc, scale, push_x, push_y = viscous[...], gain[...], push[0], push[1]

    def interior(v):
        up = jnp.where(row == size - 1, 0.0, roll(v, -1, 0))
        down = jnp.where(row == 0, 0.0, roll(v, 1, 0))
        right = jnp.where(col == size - 1, 0.0, roll(v, -1, 1))
        left = jnp.where(col == 0, 0.0, roll(v, 1, 1))
        return up + down + right + left - 4.0 * v

    def rim_of(north, south, east, west):
        up = jnp.where(row == size - 1, north, jnp.where(row == 0, south, 0.0))
        return up + jnp.where(col == size - 1, east, jnp.where(col == 0, west, 0.0))

    def own_edges(vx, vy):
        mixed = jnp.where(col < half, roll(vx, 1, 1), roll(vy, 1 + half, 1))
        across = mixed.T[0:high]
        return [
            jnp.where(sub < half, vx[size - 1 :], vy[size - 1 :]),
            jnp.where(sub < half, vx[0:1], vy[0:1]),
            across,
            roll(across, -1, 0),
        ]

    own = own_edges(vx, vy)
    inner_x, inner_y = interior(vx), interior(vy)
    load_names.wait()
    strips = []
    for q in range(4):
        x, has_x = follow(0, q)
        strip = load(x, OPPOSITE[q], flag(has_x))
        sides = []
        for s in LATERAL[q]:
            y, has_y = follow(x, s)
            z, has_z = follow(y, OPPOSITE[q])
            w, has_w = follow(z, OPPOSITE[s])
            sides.append(
                [
                    load(y, OPPOSITE[q], flag(has_y)),
                    load(z, q, flag(has_z)),
                    load(w, q, flag(has_w), with_push=False),
                ]
            )
        strips.append((strip, sides))

    for t in range(SUBCYCLES):
        cells = [strip[0] for strip, _ in strips]
        if t < SUBCYCLES - 1:
            if t > 0:
                own = own_edges(vx, vy)
            for q in range(4):
                strip, (beyond, before) = strips[q]
                c, y_hi, y_lo = strip[0], beyond[0][0], before[0][0]
                left = jnp.where(first, roll(y_lo, 1, 1), roll(c, 1, 1))
                right = jnp.where(last, roll(y_hi, -1, 1), roll(c, -1, 1))
                inner = jnp.where(edge, own[q], roll(c, 1, 0))
                new_strip = step(strip, left, right, inner, roll(c, -1, 0))
                if t < SUBCYCLES - 2:
                    new_sides = []
                    for i, (y, z, w) in enumerate((beyond, before)):
                        away = 1 if i == 0 else -1
                        boundary = first if i == 0 else last
                        yc, zc = y[0], z[0]
                        toward = jnp.where(boundary, roll(c, away, 1), roll(yc, away, 1))
                        inner = jnp.where(edge, zc, roll(yc, 1, 0))
                        new_y = step(y, toward, roll(yc, -away, 1), inner, roll(yc, -1, 0))
                        new_z = zc
                        if t < SUBCYCLES - 3:
                            toward = jnp.where(boundary, roll(w, away, 1), roll(zc, away, 1))
                            inner = jnp.where(edge, yc, roll(zc, 1, 0))
                            new_z = step(z, toward, roll(zc, -away, 1), inner, roll(zc, -1, 0))
                        new_sides.append((new_y, new_z))
                    for item, (new_y, new_z) in zip((beyond, before), new_sides):
                        item[0][0] = new_y
                        item[1][0] = new_z
                strip[0] = new_strip
        north, south = cells[0], cells[1]
        sides = jnp.where(edge, cells[2], roll(cells[3], 1, 0)).T
        east_x, west_x = sides[:, 0:1], sides[:, 1:2]
        east_y, west_y = sides[:, half : half + 1], sides[:, half + 1 : half + 2]
        if t > 0:
            inner_x, inner_y = interior(vx), interior(vy)
        spread_x = inner_x + rim_of(north[0:1], south[0:1], east_x, west_x)
        spread_y = inner_y + rim_of(
            north[half : half + 1], south[half : half + 1], east_y, west_y
        )
        new_x = scale * (vx + visc * spread_x + push_x + CORIOLIS_TURN * vy)
        new_y = scale * (vy + visc * spread_y + push_y - CORIOLIS_TURN * vx)
        vx, vy = new_x, new_y
    out[0] = vx
    out[1] = vy


def back_kernel(group, side, drag, conduct, current, speed, *refs):
    chunks, relays, outs = refs[:group], refs[group : 2 * group], refs[2 * group :]
    size = drag.shape[0]
    depth = chunks[0].shape[1]
    warm = remap_forward(chunks, [[r[r.shape[0] - side :]] for r in relays], side, depth)
    heat = conduct[...] * warm
    fluxes = [heat.astype(BF16)]
    for c in range(2):
        fluxes.append((drag[...] * (speed[c] - current[c])).astype(BF16))
    wide = jnp.concatenate(fluxes, axis=1)
    own, beside = outs
    step = 3 * side
    for k, chunk in enumerate(chunks):
        part = jnp.dot(chunk[0:side], wide, preferred_element_type=F32).astype(BF16)
        part = jnp.concatenate([part[:, c * size : (c + 1) * size] for c in range(3)], axis=0)
        reply = jnp.dot(part, chunk[side : side + depth], preferred_element_type=F32)
        at = k // 2 * step
        if k % 2:
            beside[at : at + step] = reply.astype(BF16)
        else:
            own[at : at + step] = reply


def pair_kernel(own, beside, *outs):
    step = outs[0].shape[0]
    for k, out in enumerate(outs):
        at = (k + 1) * step
        out[...] = (own[at : at + step] + beside[at : at + step].astype(F32)).astype(BF16)


def finish_kernel(warm, currents, speed, own, beside, *refs):
    outs, (flat, heat_v, current_v, left) = refs[-7:-4], refs[-4:]
    replies = refs[:-7]
    flat_o, heat_o, current_o = outs
    size = speed.shape[1]
    copies = [
        pltpu.make_async_copy(source, target, left.at[i])
        for i, (source, target) in enumerate(
            ((flat, flat_o), (heat_v, heat_o), (current_v, current_o))
        )
    ]
    for c in range(2):
        flat[pl.ds(c, size, stride=2), :] = speed[c]
    copies[0].start()
    side = currents.shape[1]
    total = own[0 : 3 * side] + beside[0 : 3 * side].astype(F32)
    for reply in replies:
        total = total + reply[...].astype(F32)
    heat = THERMAL_DIFFUSE * total[0:side]
    for l in range(warm.shape[0]):
        heat_v[l] = warm[l] + heat
    copies[1].start()
    for c in range(2):
        current_v[c] = currents[c] + STRESS_MIXING * total[(c + 1) * side : (c + 2) * side]
    copies[2].start()
    for copy in copies:
        copy.wait()


def shards(
    water_heat_state,
    diffusion_coefficient,
    upper_current_vector,
    remap_blocks,
    remap_rows,
    remap_cols,
    neighbors,
    thickness,
    concentration,
    ice_velocity,
    wind_stress,
):
    tile_count, sub_count, lev_count = (lax.axis_size(a) for a in ("tile", "sub", "lev"))
    group = sub_count * lev_count
    devices = tile_count * group
    group_axes = ("sub", "lev")
    member_axes = ("tile", "sub", "lev")
    levels, side, width = water_heat_state.shape
    pairs, size = remap_rows.shape[1:3]
    categories = thickness.shape[2]

    def tile_place():
        return lax.axis_index("tile")

    def member_place():
        return lax.axis_index("sub") * lev_count + lax.axis_index("lev")

    def device_place():
        return lax.axis_index("tile") * group + member_place()

    def swap(value, axes, count):
        got = {0: value}
        for k in range(1, count):
            got[k] = lax.ppermute(value, axes, [(i, i ^ k) for i in range(count)])
        return [got[k] for k in range(count)]

    def swap_chips(value):
        return {0: value} | {
            k: lax.ppermute(value, group_axes, [(i, i ^ k) for i in range(group)])
            for k in range(2, group, 2)
        }

    def swap_cores(got):
        beside = [(i, i ^ 1) for i in range(group)]
        got = got | {k + 1: lax.ppermute(got[k], group_axes, beside) for k in got}
        return [got[k] for k in range(group)]

    def swap_each(values):
        got = {0: values[0]}
        for k in range(1, group):
            got[k] = lax.ppermute(values[k], group_axes, [(i, i ^ k) for i in range(group)])
        return [got[k] for k in range(group)]

    def shape(*dims, dtype=F32):
        return jax.ShapeDtypeStruct(dims, dtype)

    def interleaved(value):
        return value.reshape(2, size, size).transpose(1, 0, 2).reshape(2 * size, size)

    plane = shape(size, size)
    planes = shape(2, size, size)
    wind = interleaved(wind_stress)

    tail_rows = -(-(2 * levels + 1) // TILE_ROWS) * TILE_ROWS
    pair_rows = side + width
    chunk_rows = pair_rows + 2 * side + tail_rows
    sent = call(
        functools.partial(forward_kernel, (devices, group, member_place)),
        [
            shape(pair_rows if k > 1 and k % 2 else chunk_rows, width, dtype=BF16)
            for k in range(group)
        ],
        (
            neighbors,
            remap_blocks,
            remap_rows[0].swapaxes(1, 2),
            remap_cols[0],
            upper_current_vector,
            water_heat_state,
        ),
        scratch=[
            pltpu.SMEM(neighbors.shape, jnp.int32),
            pltpu.SMEM((1, pairs), jnp.int32),
            pltpu.VMEM((2, side, width), F32),
            pltpu.VMEM((pairs, side, size), BF16),
            pltpu.VMEM((pairs, size, width), BF16),
            pltpu.VMEM((levels, side, width), F32),
            pltpu.VMEM((1, 2 * side, width), BF16),
            pltpu.VMEM((tail_rows, width), BF16),
            pltpu.VMEM((1 if pairs == group else group, side, size), BF16),
            pltpu.SemaphoreType.DMA((6,)),
            pltpu.SemaphoreType.DMA((4 * group,)),
        ],
        hbm=(0, 1, 2, 3, 4, 5),
        grant=60 * 2**20,
        micros=10,
    )
    chunks = swap_each(sent)
    hops = [
        lax.ppermute(chunks[k][pair_rows:], group_axes, [(i, i ^ 1) for i in range(group)])
        for k in range(2, group, 2)
    ]

    early, viscous, gain, step_mass, drag, conduct, speed = call(
        rims_kernel,
        [shape(SIDE_ROWS + 4 * levels, size, dtype=BF16)] + [plane] * 5 + [planes],
        (
            thickness.reshape(categories, size, size),
            concentration.reshape(categories, size, size),
            interleaved(ice_velocity),
            water_heat_state,
        ),
        scratch=[pltpu.VMEM((SIDE_ROWS + 4 * levels, size), F32)],
    )
    message, current_ice, push = call(
        functools.partial(forcing_kernel, group, side, levels, sub_count, member_place),
        [shape(BLOCK_ROWS + 4 * levels, size, dtype=BF16), planes, planes],
        (step_mass, drag, wind, early, *chunks[::-1], *hops),
        scratch=[pltpu.VMEM((PUSH_ROWS, size), F32)],
    )
    messages = swap(message, "tile", tile_count)

    counts = (tile_count, sub_count, lev_count)
    ocean = (*messages, *chunks, *hops)
    relay_rows = tile_count * BLOCK_ROWS
    relay_shapes = [shape(relay_rows + (side if lev_count == 1 else 0), size, dtype=BF16)]
    if lev_count > 1:
        relay_shapes.append(shape(side, width))
    relay, *top = call(
        functools.partial(relay_kernel, counts, tile_place, member_place),
        relay_shapes,
        (water_heat_state, diffusion_coefficient, *ocean),
    )
    if lev_count > 1:
        relay = jnp.concatenate([relay, lax.psum(top[0], "lev").astype(BF16)], axis=0)
    relays = swap_chips(relay)

    mixing, _ = lax.optimization_barrier((diffusion_coefficient, relay))
    (warm,) = call(
        functools.partial(ocean_kernel, counts, tile_place, member_place),
        [shape(levels, side, width)],
        (water_heat_state, mixing, *ocean),
    )
    far = sorted(k for k in relays if k)
    relayed, _ = lax.optimization_barrier(([relays[k] for k in far], warm))
    relays = swap_cores({0: relay} | dict(zip(far, relayed)))

    names = jnp.stack(
        [
            r[:relay_rows].reshape(tile_count, BLOCK_ROWS, size)[:, NAMES_ROW, 0:8]
            for r in relays
        ],
        axis=1,
    )
    names = names.reshape(devices, 8).astype(jnp.int32)
    table = names[:, 0:4] * 128 + names[:, 4:8]
    table = jnp.where(table < 0, -1, table ^ device_place())
    speed = call(
        functools.partial(subcycles_kernel, tile_count, group),
        planes,
        (table, viscous, gain, speed, push, *relays),
        scratch=[
            pltpu.VMEM((devices, BLOCK_ROWS, size), BF16),
            pltpu.SMEM((devices, 4), jnp.int32),
            pltpu.SemaphoreType.DMA,
        ],
        hbm=(0,),
    )

    step = 3 * side
    own, beside = call(
        functools.partial(back_kernel, group, side),
        [shape(group // 2 * step, width), shape(group // 2 * step, width, dtype=BF16)],
        (drag, conduct, current_ice, speed, *chunks, *relays),
    )
    beside = lax.ppermute(beside, group_axes, [(i, i ^ 1) for i in range(group)])
    paired = call(
        pair_kernel, [shape(step, width, dtype=BF16)] * (group // 2 - 1), (own, beside)
    )
    replies = [
        lax.ppermute(value, group_axes, [(i, i ^ (2 * k + 2)) for i in range(group)])
        for k, value in enumerate(paired)
    ]
    if lev_count > 1:
        parts = [r.astype(F32) for r in (own[:step], beside[:step], *replies)]
        own, beside, replies = lax.psum(sum(parts), "lev"), jnp.zeros_like(beside[:step]), []
    flat, heat, current = call(
        finish_kernel,
        [shape(2 * size, size), shape(levels, side, width), shape(2, side, width)],
        (warm, upper_current_vector, speed, own, beside, *replies),
        scratch=[
            pltpu.VMEM((2 * size, size), F32),
            pltpu.VMEM((levels, side, width), F32),
            pltpu.VMEM((2, side, width), F32),
            pltpu.SemaphoreType.DMA((3,)),
        ],
        out_space=pltpu.HBM,
    )
    velocity = flat.reshape(size, 2, size).transpose(1, 0, 2).reshape(1, 1, 2, size * size)
    return heat, current, velocity


def solution(mesh):
    member = ("tile", "sub", "lev")
    whole = ("copies",) + member
    ice = P(None, whole, None, None)
    water = P("lev", ("copies", "tile"), "sub")
    current = P(None, ("copies", "tile"), "sub")
    return jax.shard_map(
        shards,
        mesh=mesh,
        in_specs=(
            water,
            P("tile", "sub"),
            current,
            P(member, None),
            P(member, None, None, None),
            P(member, None, None, None),
            P(None, member, None),
            ice,
            ice,
            ice,
            ice,
        ),
        out_specs=(water, current, ice),
        check_vma=False,
    )
```

```python
import functools

import jax
import jax.numpy as jnp
from jax import lax
from jax.experimental import pallas as pl
from jax.experimental.pallas import tpu as pltpu
from jax.sharding import PartitionSpec as P

SUBCYCLES = 4
STRENGTH_DECAY = 5.0
VISCOUS_STEP = 0.24
SUBCYCLE_STEP = 0.5
CORIOLIS_TURN = 0.1
BASE_MASS = 0.5
HEAT_RATE = 0.2
THIN_ICE = 0.1
THERMAL_DIFFUSE = 0.5
STRESS_MIXING = 0.5

OPPOSITE = (1, 0, 3, 2)
LATERAL = ((2, 3), (2, 3), (0, 1), (0, 1))
DEPTH = SUBCYCLES
SIDE_ROWS = 16 * DEPTH
PUSH_ROWS = 8 * DEPTH
BLOCK_ROWS = SIDE_ROWS + PUSH_ROWS
NAMES_ROW = 2 * DEPTH - 1
CORNER_ROWS = tuple(DEPTH * i - 1 for i in (1, 3, 4, 5, 6, 7, 8))
TILE_ROWS = 16
F32 = jnp.float32
BF16 = jnp.bfloat16
VMEM_LIMIT = 16 * 1024 * 1024
FLOPS_PER_MICRO = 1.15e9


def call(kernel, outs, args, scratch=(), smem=(), hbm=(), out_space=pltpu.VMEM, grant=VMEM_LIMIT, micros=0.01):
    def space(i):
        return pltpu.SMEM if i in smem else pltpu.HBM if i in hbm else pltpu.VMEM

    specs = [pl.BlockSpec(memory_space=space(i)) for i in range(len(args))]
    size = sum(a.size * a.dtype.itemsize for a in args)
    return pl.pallas_call(
        kernel,
        out_shape=outs,
        in_specs=specs,
        out_specs=jax.tree.map(lambda _: pl.BlockSpec(memory_space=out_space), outs),
        scratch_shapes=list(scratch),
        compiler_params=pltpu.CompilerParams(vmem_limit_bytes=grant),
        cost_estimate=pl.CostEstimate(
            flops=int(micros * FLOPS_PER_MICRO), bytes_accessed=size, transcendentals=0
        ),
    )(*args)


def iota(shape, axis):
    return lax.broadcasted_iota(jnp.int32, shape, axis)


def roll(x, shift, axis):
    return pltpu.roll(x, shift % x.shape[axis], axis)


def flag(condition):
    return jnp.where(condition, 1.0, 0.0).astype(F32)


def ocean_columns(water):
    levels, rows, width = water.shape
    lane = iota((rows, width), 1)
    line = iota((1, width), 1)
    mixed = jnp.zeros((rows, width), F32)
    for l in range(levels):
        mixed = jnp.where(lane // 4 == l, roll(water[l], 2 + 4 * l, 1), mixed)
    across = jnp.concatenate([mixed, jnp.zeros((width - rows, width), F32)], axis=0).T
    beside = []
    for l in range(levels):
        for j in range(2):
            last = across[4 * l + 1 - j : 4 * l + 2 - j]
            lead = across[4 * l + 2 + j : 4 * l + 3 + j]
            beside.append(jnp.where(line < rows, last, roll(lead, rows, 1)))
    return beside


def forward_kernel(group, links_h, blocks_h, rows_h, cols_h, currents_h, water_h, *refs):
    devices, members, place = group
    outs, scratch = refs[:members], refs[members:]
    links, blocks, currents, weights, water, fields, kept, arrived, left = scratch
    pairs, side, width = rows_h.shape
    both = weights.shape[1]
    loads = [
        pltpu.make_async_copy(source, target, arrived.at[i])
        for i, (source, target) in enumerate(
            (
                (links_h, links),
                (blocks_h, blocks),
                (currents_h, currents),
                (rows_h, weights.at[:, pl.ds(0, side)]),
                (cols_h, weights.at[:, pl.ds(side, both - side)]),
                (water_h, water),
            )
        )
    ]
    for load in loads:
        load.start()
    for i in (1, 3, 4):
        loads[i].wait()
    me = place()
    owners = [lax.rem(lax.rem(blocks[0, m], devices), members) for m in range(pairs)]
    copies = []
    for k, out in enumerate(outs):
        partner = me ^ k
        pair = jnp.int32(0)
        for m in range(pairs):
            pair = jnp.where(owners[m] == partner, m, pair)
        source = weights.at[pair]
        if pairs < members:
            found = sum(flag(owners[m] == partner) for m in range(pairs))
            kept[k] = (weights[pair].astype(F32) * found).astype(BF16)
            source = kept.at[k]
        copies.append(pltpu.make_async_copy(source, out.at[pl.ds(0, both)], left.at[2 * k]))
        copies[-1].start()
    for i in (0, 2, 5):
        loads[i].wait()
    for c in range(2):
        fields[c * side : (c + 1) * side] = currents[c].astype(BF16)
    lane = iota((1, width), 1)
    numbers = jnp.zeros((1, width), F32)
    for q in range(4):
        numbers = jnp.where(lane == q, (links[0, 0, q] >> 7).astype(F32), numbers)
        numbers = jnp.where(lane == 4 + q, (links[0, 0, q] & 127).astype(F32), numbers)
    ends = ocean_columns(water) + [numbers]
    blank = jnp.zeros((fields.shape[0] - 2 * side - len(ends), width), F32)
    fields[2 * side :] = jnp.concatenate(ends + [blank], axis=0).astype(BF16)
    for k, out in enumerate(outs):
        if out.shape[0] > both:
            target = out.at[pl.ds(both, fields.shape[0])]
            copies.append(pltpu.make_async_copy(fields, target, left.at[2 * k + 1]))
            copies[-1].start()
    for copy in copies:
        copy.wait()


def put_side_rims(store, planes, at):
    size = planes[0].shape[0]
    lane = iota((size, size), 1)
    mixed = jnp.zeros((size, size), F32)
    for i, plane in enumerate(planes):
        turned = roll(plane, DEPTH + 2 * DEPTH * i, 1)
        mixed = jnp.where(lane // (2 * DEPTH) == i, turned, mixed)
    across = mixed.T
    for i, plane in enumerate(planes):
        for k in range(DEPTH):
            base = i * DEPTH + k
            store[at(0) + base : at(0) + base + 1] = plane[size - 1 - k : size - k]
            store[at(1) + base : at(1) + base + 1] = plane[k : k + 1]
            east = 2 * DEPTH * i + DEPTH - 1 - k
            west = 2 * DEPTH * i + DEPTH + k
            store[at(2) + base : at(2) + base + 1] = across[east : east + 1]
            store[at(3) + base : at(3) + base + 1] = across[west : west + 1]


def rims_kernel(
    thick, conc, ice, water, out, viscous_o, gain_o, mass_o, drag_o, conduct_o,
    speed_o, store,
):
    size = thick.shape[1]
    cover = jnp.zeros((size, size), F32)
    volume = jnp.zeros((size, size), F32)
    conduct = jnp.zeros((size, size), F32)
    for c in range(thick.shape[0]):
        h, a = thick[c], conc[c]
        cover = cover + a
        volume = volume + a * h
        conduct = conduct + a / (h + THIN_ICE)
    mass = volume + BASE_MASS
    viscous = VISCOUS_STEP * (volume * jnp.exp(-STRENGTH_DECAY * (1.0 - cover))) / mass
    step_mass = SUBCYCLE_STEP / mass
    gain = 1.0 / (1.0 + step_mass * cover)
    speed_x = ice[pl.ds(0, size, stride=2), :]
    speed_y = ice[pl.ds(1, size, stride=2), :]
    viscous_o[...] = viscous
    gain_o[...] = gain
    mass_o[...] = step_mass
    drag_o[...] = cover
    conduct_o[...] = -HEAT_RATE * conduct
    speed_o[0] = speed_x
    speed_o[1] = speed_y
    put_side_rims(store, [speed_x, speed_y, viscous, gain], lambda side: side * 4 * DEPTH)
    levels, rows, width = water.shape
    start = SIDE_ROWS
    for l in range(levels):
        for j in range(2):
            at = start + 2 * l + j
            store[at : at + 1] = water[l, rows - 1 - j : rows - j]
            store[at + 2 * levels : at + 2 * levels + 1] = water[l, j : j + 1]
    out[...] = store[...].astype(BF16)


def nearby(me, members, distance, arrays):
    at = me + distance
    inside = (at >= 0) & (at < members)
    found = 0.0
    for k in range(1, members):
        found = found + arrays[k].astype(F32) * flag(inside & ((me ^ k) == at))
    return found


def remap_forward(chunks, field_rows, side, depth):
    total = None
    for chunk, fields in zip(chunks, field_rows):
        down = chunk[0:side]
        right = chunk[side : side + depth]
        wide = jnp.concatenate(fields, axis=1) if len(fields) > 1 else fields[0]
        part = lax.dot_general(down, wide, (((0,), (0,)), ((), ())), preferred_element_type=F32)
        part = part.astype(BF16)
        width = fields[0].shape[1]
        if len(fields) > 1:
            part = jnp.concatenate(
                [part[:, c * width : (c + 1) * width] for c in range(len(fields))], axis=0
            )
        piece = lax.dot_general(part, right, (((1,), (1,)), ((), ())), preferred_element_type=F32)
        piece = piece.astype(BF16).astype(F32)
        total = piece if total is None else total + piece
    return total


def tails_of(chunks, hops):
    at = min(c.shape[0] for c in chunks)
    return [hops[k // 2 - 1][...] if k > 1 and k % 2 else c[at:] for k, c in enumerate(chunks)]


def forcing_kernel(group, side, levels, subs, place, mass, drag, wind, early, *refs):
    chunks = refs[:group][::-1]
    hops, (out, current_o, push_o, store) = refs[group:-4], refs[-4:]
    size = mass.shape[0]
    depth = chunks[0].shape[1]
    tails = tails_of(chunks, hops)
    fields = [[t[0:side], t[side : 2 * side]] for t in tails]
    total = remap_forward(chunks, fields, side, depth)
    pushes = []
    for c in range(2):
        current = total[c * size : (c + 1) * size]
        current_o[c] = current
        force = wind[pl.ds(c, size, stride=2), :]
        push = mass[...] * (force + drag[...] * current)
        push_o[c] = push
        pushes.append(push)
    put_side_rims(store, pushes, lambda q: q * 2 * DEPTH)
    tail = [t[2 * side :] for t in tails]
    store[NAMES_ROW : NAMES_ROW + 1] = tail[0].astype(F32)[2 * levels : 2 * levels + 1]
    me, step = place(), group // subs
    left, right = (nearby(me, group, d * step, tail) for d in (-1, 1))
    line = iota((1, size), 1)
    for l in range(levels):
        near = slice(2 * l, 2 * l + 1)
        store[CORNER_ROWS[l] : CORNER_ROWS[l] + 1] = jnp.where(line < side, left[near], right[near])
    out[0:PUSH_ROWS] = store[...].astype(BF16)
    out[PUSH_ROWS:] = early[...]


def ocean_halos(counts, tile_place, member_place, shape, messages, tails):
    tiles, subs, levs = counts
    levels, rows, width = shape
    my_tile, me = tile_place(), member_place()
    halo = {}
    strips = [m[BLOCK_ROWS : BLOCK_ROWS + 4 * levels] for m in messages]
    rims = [m[0:PUSH_ROWS] for m in messages]
    ends = [t[2 * rows :] for t in tails]
    for dt in (-1, 1):
        beyond = nearby(my_tile, tiles, dt, strips)
        halo[dt, 0] = beyond[: 2 * levels] if dt < 0 else beyond[2 * levels :]
        corners = nearby(my_tile, tiles, dt, rims)
        corners = jnp.concatenate([corners[r : r + 1] for r in CORNER_ROWS[:levels]], axis=0)
        at = rows - 1 if dt < 0 else 0
        for ds in (-1, 1):
            lane_at = at if ds < 0 else rows + at
            halo[dt, ds] = corners[:, lane_at : lane_at + 1]
    for ds in (-1, 1):
        beside = nearby(me, subs * levs, ds * levs, ends)[: 2 * levels]
        halo[0, ds] = roll(beside, -rows, 1) if ds > 0 else beside
    return halo


def biharmonic(x, top, bottom, left, right, corner):
    rows, width = x.shape
    row, lane = iota(x.shape, 0), iota(x.shape, 1)
    line = iota((1, width), 1)

    def laplacian(x, top, bottom, left, right):
        up = jnp.where(row == 0, top, roll(x, 1, 0))
        down = jnp.where(row == rows - 1, bottom, roll(x, -1, 0))
        west = jnp.where(lane == 0, left, roll(x, 1, 1))
        east = jnp.where(lane == width - 1, right, roll(x, -1, 1))
        return up + down + west + east - 4.0 * x

    def ring_row(mid, out_row, in_row, dt):
        west = jnp.where(line == 0, corner[dt, -1], roll(mid, 1, 1))
        east = jnp.where(line == width - 1, corner[dt, 1], roll(mid, -1, 1))
        return west + east + out_row + in_row - 4.0 * mid

    def ring_col(mid, out_col, in_col, ds):
        up = jnp.concatenate([corner[-1, ds], mid[:-1]], axis=0)
        down = jnp.concatenate([mid[1:], corner[1, ds]], axis=0)
        return up + down + out_col + in_col - 4.0 * mid

    return laplacian(
        laplacian(x, top[0], bottom[0], left[0], right[0]),
        ring_row(*top, x[0:1], -1),
        ring_row(*bottom, x[rows - 1 :], 1),
        ring_col(*left, x[:, 0:1], -1),
        ring_col(*right, x[:, width - 1 :], 1),
    )


def split_refs(tiles, members, refs, outs):
    messages, chunks = refs[:tiles], refs[tiles : tiles + members]
    return messages, tails_of(chunks, refs[tiles + members : -outs]), refs[-outs:]


def relay_kernel(counts, tile_place, member_place, water, mixing, *refs):
    tiles, subs, levs = counts
    outs = 1 if levs == 1 else 2
    messages, tails, outs = split_refs(tiles, subs * levs, refs, outs)
    for k in range(tiles):
        outs[0][k * BLOCK_ROWS : (k + 1) * BLOCK_ROWS] = messages[k][0:BLOCK_ROWS]
    levels, rows, width = water.shape
    halo = ocean_halos(counts, tile_place, member_place, water.shape, messages, tails)

    def both(strip):
        near = sum(strip[2 * l : 2 * l + 1] for l in range(levels))
        far = sum(strip[2 * l + 1 : 2 * l + 2] for l in range(levels))
        return near, far

    def as_columns(strip):
        near, far = both(strip)
        across = jnp.concatenate([near, far] + [jnp.zeros_like(near)] * 6, axis=0).T
        return across[0:rows, 0:1], across[0:rows, 1:2]

    corner = {
        (dt, ds): jnp.sum(halo[dt, ds], axis=0, keepdims=True) for dt in (-1, 1) for ds in (-1, 1)
    }
    x = sum(water[l] for l in range(levels))
    twice = biharmonic(
        x, both(halo[-1, 0]), both(halo[1, 0]), as_columns(halo[0, -1]), as_columns(halo[0, 1]), corner
    )
    top = (x - mixing[...] * twice) / (levels * levs)
    if levs == 1:
        outs[0][tiles * BLOCK_ROWS :] = top.astype(BF16)
    else:
        outs[1][...] = top


def ocean_kernel(counts, tile_place, member_place, water, mixing, *refs):
    tiles, subs, levs = counts
    messages, tails, (warm_o,) = split_refs(tiles, subs * levs, refs, 1)
    levels, rows, width = water.shape
    halo = ocean_halos(counts, tile_place, member_place, water.shape, messages, tails)
    left, right = halo[0, -1].T, halo[0, 1].T
    for l in range(levels):
        x = water[l]
        pair = (2 * l, 2 * l + 1)
        twice = biharmonic(
            x,
            [halo[-1, 0][i : i + 1] for i in pair],
            [halo[1, 0][i : i + 1] for i in pair],
            [left[0:rows, i : i + 1] for i in pair],
            [right[0:rows, i : i + 1] for i in pair],
            {(dt, ds): halo[dt, ds][l : l + 1] for dt in (-1, 1) for ds in (-1, 1)},
        )
        warm_o[l] = x - mixing[...] * twice


def ice_kernel(
    tiles, members, side, table, viscous, gain, drag, conduct, current, speed, push, *refs
):
    chunks, relays = refs[:members], refs[members : 2 * members]
    out, own_o, beside_o, rims, names, named = refs[2 * members :]
    load_names = pltpu.make_async_copy(table, names, named)
    load_names.start()
    size = viscous.shape[0]
    depth = chunks[0].shape[1]
    warm = remap_forward(chunks, [[r[r.shape[0] - side :]] for r in relays], side, depth)
    heat = (conduct[...] * warm).astype(BF16)
    for k in range(tiles):
        for m in range(members):
            rims[k * members + m] = relays[m][k * BLOCK_ROWS : (k + 1) * BLOCK_ROWS]
    half = DEPTH
    high = 2 * DEPTH
    sub = iota((high, size), 0)
    lane = iota((high, size), 1)
    edge = (sub & (half - 1)) == 0
    turn = jnp.where(sub < half, CORIOLIS_TURN, -CORIOLIS_TURN).astype(F32)
    first, last = lane == 0, lane == size - 1

    def load(device, side, mask, with_push=True):
        start = PUSH_ROWS + side * 2 * high
        block = rims[device, start : start + 2 * high].astype(F32)
        velocity, both = block[:high] * mask, block[high:]
        if not with_push:
            return velocity
        other = roll(both, half, 0)
        visc = jnp.where(sub < half, both, other)
        scale = jnp.where(sub < half, other, both) * mask
        start = side // 2 * 2 * high
        pushed = rims[device, start : start + 2 * high].astype(F32)
        pushed = pushed[:high] if side % 2 == 0 else pushed[high:]
        return [velocity, visc, scale, pushed]

    def follow(device, side):
        name = names[device, side]
        return jnp.where(name >= 0, name, 0), name >= 0

    def step(state, left, right, inner, outer):
        c, visc, scale, pushed = state
        spread = left + right + inner + outer - 4.0 * c
        return scale * (c + visc * spread + pushed + turn * roll(c, half, 0))

    row = iota((size, size), 0)
    col = iota((size, size), 1)
    vx, vy = speed[0], speed[1]
    visc, scale, push_x, push_y = viscous[...], gain[...], push[0], push[1]

    def interior(v):
        up = jnp.where(row == size - 1, 0.0, roll(v, -1, 0))
        down = jnp.where(row == 0, 0.0, roll(v, 1, 0))
        right = jnp.where(col == size - 1, 0.0, roll(v, -1, 1))
        left = jnp.where(col == 0, 0.0, roll(v, 1, 1))
        return up + down + right + left - 4.0 * v

    def rim_of(north, south, east, west):
        up = jnp.where(row == size - 1, north, jnp.where(row == 0, south, 0.0))
        return up + jnp.where(col == size - 1, east, jnp.where(col == 0, west, 0.0))

    def own_edges(vx, vy):
        mixed = jnp.where(col < half, roll(vx, 1, 1), roll(vy, 1 + half, 1))
        across = mixed.T[0:high]
        return [
            jnp.where(sub < half, vx[size - 1 :], vy[size - 1 :]),
            jnp.where(sub < half, vx[0:1], vy[0:1]),
            across,
            roll(across, -1, 0),
        ]

    own = own_edges(vx, vy)
    inner_x, inner_y = interior(vx), interior(vy)
    load_names.wait()
    strips = []
    for q in range(4):
        x, has_x = follow(0, q)
        strip = load(x, OPPOSITE[q], flag(has_x))
        sides = []
        for s in LATERAL[q]:
            y, has_y = follow(x, s)
            z, has_z = follow(y, OPPOSITE[q])
            w, has_w = follow(z, OPPOSITE[s])
            sides.append(
                [
                    load(y, OPPOSITE[q], flag(has_y)),
                    load(z, q, flag(has_z)),
                    load(w, q, flag(has_w), with_push=False),
                ]
            )
        strips.append((strip, sides))

    for t in range(SUBCYCLES):
        cells = [strip[0] for strip, _ in strips]
        if t < SUBCYCLES - 1:
            if t > 0:
                own = own_edges(vx, vy)
            for q in range(4):
                strip, (beyond, before) = strips[q]
                c, y_hi, y_lo = strip[0], beyond[0][0], before[0][0]
                left = jnp.where(first, roll(y_lo, 1, 1), roll(c, 1, 1))
                right = jnp.where(last, roll(y_hi, -1, 1), roll(c, -1, 1))
                inner = jnp.where(edge, own[q], roll(c, 1, 0))
                new_strip = step(strip, left, right, inner, roll(c, -1, 0))
                if t < SUBCYCLES - 2:
                    new_sides = []
                    for i, (y, z, w) in enumerate((beyond, before)):
                        away = 1 if i == 0 else -1
                        boundary = first if i == 0 else last
                        yc, zc = y[0], z[0]
                        toward = jnp.where(boundary, roll(c, away, 1), roll(yc, away, 1))
                        inner = jnp.where(edge, zc, roll(yc, 1, 0))
                        new_y = step(y, toward, roll(yc, -away, 1), inner, roll(yc, -1, 0))
                        new_z = zc
                        if t < SUBCYCLES - 3:
                            toward = jnp.where(boundary, roll(w, away, 1), roll(zc, away, 1))
                            inner = jnp.where(edge, yc, roll(zc, 1, 0))
                            new_z = step(z, toward, roll(zc, -away, 1), inner, roll(zc, -1, 0))
                        new_sides.append((new_y, new_z))
                    for item, (new_y, new_z) in zip((beyond, before), new_sides):
                        item[0][0] = new_y
                        item[1][0] = new_z
                strip[0] = new_strip
        north, south = cells[0], cells[1]
        sides = jnp.where(edge, cells[2], roll(cells[3], 1, 0)).T
        east_x, west_x = sides[:, 0:1], sides[:, 1:2]
        east_y, west_y = sides[:, half : half + 1], sides[:, half + 1 : half + 2]
        if t > 0:
            inner_x, inner_y = interior(vx), interior(vy)
        spread_x = inner_x + rim_of(north[0:1], south[0:1], east_x, west_x)
        spread_y = inner_y + rim_of(
            north[half : half + 1], south[half : half + 1], east_y, west_y
        )
        new_x = scale * (vx + visc * spread_x + push_x + CORIOLIS_TURN * vy)
        new_y = scale * (vy + visc * spread_y + push_y - CORIOLIS_TURN * vx)
        vx, vy = new_x, new_y
    out[0] = vx
    out[1] = vy
    stress = [(drag[...] * (v - current[c])).astype(BF16) for c, v in enumerate((vx, vy))]
    return_fluxes([heat, *stress], chunks, side, depth, own_o, beside_o)


def return_fluxes(fluxes, chunks, side, depth, own, beside):
    size = fluxes[0].shape[0]
    wide = jnp.concatenate(fluxes, axis=1)
    step = 3 * side
    for k, chunk in enumerate(chunks):
        part = jnp.dot(chunk[0:side], wide, preferred_element_type=F32).astype(BF16)
        part = jnp.concatenate([part[:, c * size : (c + 1) * size] for c in range(3)], axis=0)
        reply = jnp.dot(part, chunk[side : side + depth], preferred_element_type=F32)
        at = k // 2 * step
        if k % 2:
            beside[at : at + step] = reply.astype(BF16)
        else:
            own[at : at + step] = reply


def pair_kernel(own, beside, *outs):
    step = outs[0].shape[0]
    for k, out in enumerate(outs):
        at = (k + 1) * step
        out[...] = (own[at : at + step] + beside[at : at + step].astype(F32)).astype(BF16)


def finish_kernel(warm, currents, speed, own, beside, *refs):
    outs, (flat, heat_v, current_v, left) = refs[-7:-4], refs[-4:]
    replies = refs[:-7]
    flat_o, heat_o, current_o = outs
    size = speed.shape[1]
    copies = [
        pltpu.make_async_copy(source, target, left.at[i])
        for i, (source, target) in enumerate(
            ((flat, flat_o), (heat_v, heat_o), (current_v, current_o))
        )
    ]
    for c in range(2):
        flat[pl.ds(c, size, stride=2), :] = speed[c]
    copies[0].start()
    side = currents.shape[1]
    total = own[0 : 3 * side] + beside[0 : 3 * side].astype(F32)
    for reply in replies:
        total = total + reply[...].astype(F32)
    heat = THERMAL_DIFFUSE * total[0:side]
    for l in range(warm.shape[0]):
        heat_v[l] = warm[l] + heat
    copies[1].start()
    for c in range(2):
        current_v[c] = currents[c] + STRESS_MIXING * total[(c + 1) * side : (c + 2) * side]
    copies[2].start()
    for copy in copies:
        copy.wait()


def shards(
    water_heat_state,
    diffusion_coefficient,
    upper_current_vector,
    remap_blocks,
    remap_rows,
    remap_cols,
    neighbors,
    thickness,
    concentration,
    ice_velocity,
    wind_stress,
):
    tile_count, sub_count, lev_count = (lax.axis_size(a) for a in ("tile", "sub", "lev"))
    group = sub_count * lev_count
    devices = tile_count * group
    group_axes = ("sub", "lev")
    member_axes = ("tile", "sub", "lev")
    levels, side, width = water_heat_state.shape
    pairs, size = remap_rows.shape[1:3]
    categories = thickness.shape[2]

    def tile_place():
        return lax.axis_index("tile")

    def member_place():
        return lax.axis_index("sub") * lev_count + lax.axis_index("lev")

    def device_place():
        return lax.axis_index("tile") * group + member_place()

    def swap(value, axes, count):
        got = {0: value}
        for k in range(1, count):
            got[k] = lax.ppermute(value, axes, [(i, i ^ k) for i in range(count)])
        return [got[k] for k in range(count)]

    def swap_chips(value):
        return {0: value} | {
            k: lax.ppermute(value, group_axes, [(i, i ^ k) for i in range(group)])
            for k in range(2, group, 2)
        }

    def swap_cores(got):
        beside = [(i, i ^ 1) for i in range(group)]
        got = got | {k + 1: lax.ppermute(got[k], group_axes, beside) for k in got}
        return [got[k] for k in range(group)]

    def swap_each(values):
        got = {0: values[0]}
        for k in range(1, group):
            got[k] = lax.ppermute(values[k], group_axes, [(i, i ^ k) for i in range(group)])
        return [got[k] for k in range(group)]

    def shape(*dims, dtype=F32):
        return jax.ShapeDtypeStruct(dims, dtype)

    def interleaved(value):
        return value.reshape(2, size, size).transpose(1, 0, 2).reshape(2 * size, size)

    plane = shape(size, size)
    planes = shape(2, size, size)
    wind = interleaved(wind_stress)

    tail_rows = -(-(2 * levels + 1) // TILE_ROWS) * TILE_ROWS
    pair_rows = side + width
    chunk_rows = pair_rows + 2 * side + tail_rows
    sent = call(
        functools.partial(forward_kernel, (devices, group, member_place)),
        [
            shape(pair_rows if k > 1 and k % 2 else chunk_rows, width, dtype=BF16)
            for k in range(group)
        ],
        (
            neighbors,
            remap_blocks,
            remap_rows[0].swapaxes(1, 2),
            remap_cols[0],
            upper_current_vector,
            water_heat_state,
        ),
        scratch=[
            pltpu.SMEM(neighbors.shape, jnp.int32),
            pltpu.SMEM((1, pairs), jnp.int32),
            pltpu.VMEM((2, side, width), F32),
            pltpu.VMEM((pairs, pair_rows, width), BF16),
            pltpu.VMEM((levels, side, width), F32),
            pltpu.VMEM((chunk_rows - pair_rows, width), BF16),
            pltpu.VMEM((1 if pairs == group else group, pair_rows, width), BF16),
            pltpu.SemaphoreType.DMA((6,)),
            pltpu.SemaphoreType.DMA((2 * group,)),
        ],
        hbm=(0, 1, 2, 3, 4, 5),
        grant=60 * 2**20,
        micros=10,
    )
    chunks = swap_each(sent)
    hops = [
        lax.ppermute(chunks[k][pair_rows:], group_axes, [(i, i ^ 1) for i in range(group)])
        for k in range(2, group, 2)
    ]

    early, viscous, gain, step_mass, drag, conduct, speed = call(
        rims_kernel,
        [shape(SIDE_ROWS + 4 * levels, size, dtype=BF16)] + [plane] * 5 + [planes],
        (
            thickness.reshape(categories, size, size),
            concentration.reshape(categories, size, size),
            interleaved(ice_velocity),
            water_heat_state,
        ),
        scratch=[pltpu.VMEM((SIDE_ROWS + 4 * levels, size), F32)],
    )
    message, current_ice, push = call(
        functools.partial(forcing_kernel, group, side, levels, sub_count, member_place),
        [shape(BLOCK_ROWS + 4 * levels, size, dtype=BF16), planes, planes],
        (step_mass, drag, wind, early, *chunks[::-1], *hops),
        scratch=[pltpu.VMEM((PUSH_ROWS, size), F32)],
    )
    messages = swap(message, "tile", tile_count)

    counts = (tile_count, sub_count, lev_count)
    ocean = (*messages, *chunks, *hops)
    relay_rows = tile_count * BLOCK_ROWS
    relay_shapes = [shape(relay_rows + (side if lev_count == 1 else 0), size, dtype=BF16)]
    if lev_count > 1:
        relay_shapes.append(shape(side, width))
    relay, *top = call(
        functools.partial(relay_kernel, counts, tile_place, member_place),
        relay_shapes,
        (water_heat_state, diffusion_coefficient, *ocean),
    )
    if lev_count > 1:
        relay = jnp.concatenate([relay, lax.psum(top[0], "lev").astype(BF16)], axis=0)
    relays = swap_chips(relay)

    mixing, _ = lax.optimization_barrier((diffusion_coefficient, relay))
    (warm,) = call(
        functools.partial(ocean_kernel, counts, tile_place, member_place),
        [shape(levels, side, width)],
        (water_heat_state, mixing, *ocean),
    )
    far = sorted(k for k in relays if k)
    relayed, _ = lax.optimization_barrier(([relays[k] for k in far], warm))
    relays = swap_cores({0: relay} | dict(zip(far, relayed)))

    names = jnp.stack(
        [
            r[:relay_rows].reshape(tile_count, BLOCK_ROWS, size)[:, NAMES_ROW, 0:8]
            for r in relays
        ],
        axis=1,
    )
    names = names.reshape(devices, 8).astype(jnp.int32)
    table = names[:, 0:4] * 128 + names[:, 4:8]
    table = jnp.where(table < 0, -1, table ^ device_place())
    step = 3 * side
    speed, own, beside = call(
        functools.partial(ice_kernel, tile_count, group, side),
        [
            planes,
            shape(group // 2 * step, width),
            shape(group // 2 * step, width, dtype=BF16),
        ],
        (table, viscous, gain, drag, conduct, current_ice, speed, push, *chunks, *relays),
        scratch=[
            pltpu.VMEM((devices, BLOCK_ROWS, size), BF16),
            pltpu.SMEM((devices, 4), jnp.int32),
            pltpu.SemaphoreType.DMA,
        ],
        hbm=(0,),
    )
    beside = lax.ppermute(beside, group_axes, [(i, i ^ 1) for i in range(group)])
    paired = call(
        pair_kernel, [shape(step, width, dtype=BF16)] * (group // 2 - 1), (own, beside)
    )
    replies = [
        lax.ppermute(value, group_axes, [(i, i ^ (2 * k + 2)) for i in range(group)])
        for k, value in enumerate(paired)
    ]
    if lev_count > 1:
        parts = [r.astype(F32) for r in (own[:step], beside[:step], *replies)]
        own, beside, replies = lax.psum(sum(parts), "lev"), jnp.zeros_like(beside[:step]), []
    flat, heat, current = call(
        finish_kernel,
        [shape(2 * size, size), shape(levels, side, width), shape(2, side, width)],
        (warm, upper_current_vector, speed, own, beside, *replies),
        scratch=[
            pltpu.VMEM((2 * size, size), F32),
            pltpu.VMEM((levels, side, width), F32),
            pltpu.VMEM((2, side, width), F32),
            pltpu.SemaphoreType.DMA((3,)),
        ],
        out_space=pltpu.HBM,
    )
    velocity = flat.reshape(size, 2, size).transpose(1, 0, 2).reshape(1, 1, 2, size * size)
    return heat, current, velocity


def solution(mesh):
    member = ("tile", "sub", "lev")
    whole = ("copies",) + member
    ice = P(None, whole, None, None)
    water = P("lev", ("copies", "tile"), "sub")
    current = P(None, ("copies", "tile"), "sub")
    return jax.shard_map(
        shards,
        mesh=mesh,
        in_specs=(
            water,
            P("tile", "sub"),
            current,
            P(member, None),
            P(member, None, None, None),
            P(member, None, None, None),
            P(None, member, None),
            ice,
            ice,
            ice,
            ice,
        ),
        out_specs=(water, current, ice),
        check_vma=False,
    )
```

```python
import functools

import jax
import jax.numpy as jnp
from jax import lax
from jax.experimental import pallas as pl
from jax.experimental.pallas import tpu as pltpu
from jax.sharding import PartitionSpec as P

SUBCYCLES = 4
STRENGTH_DECAY = 5.0
VISCOUS_STEP = 0.24
SUBCYCLE_STEP = 0.5
CORIOLIS_TURN = 0.1
BASE_MASS = 0.5
HEAT_RATE = 0.2
THIN_ICE = 0.1
THERMAL_DIFFUSE = 0.5
STRESS_MIXING = 0.5

OPPOSITE = (1, 0, 3, 2)
LATERAL = ((2, 3), (2, 3), (0, 1), (0, 1))
DEPTH = SUBCYCLES
SIDE_ROWS = 16 * DEPTH
PUSH_ROWS = 8 * DEPTH
BLOCK_ROWS = SIDE_ROWS + PUSH_ROWS
NAMES_ROW = 2 * DEPTH - 1
CORNER_ROWS = tuple(DEPTH * i - 1 for i in (1, 3, 4, 5, 6, 7, 8))
TILE_ROWS = 16
F32 = jnp.float32
BF16 = jnp.bfloat16
VMEM_LIMIT = 16 * 1024 * 1024
FLOPS_PER_MICRO = 1.15e9


def call(kernel, outs, args, scratch=(), smem=(), hbm=(), out_space=pltpu.VMEM, grant=VMEM_LIMIT, micros=0.01):
    def space(i):
        return pltpu.SMEM if i in smem else pltpu.HBM if i in hbm else pltpu.VMEM

    specs = [pl.BlockSpec(memory_space=space(i)) for i in range(len(args))]
    size = sum(a.size * a.dtype.itemsize for a in args)
    return pl.pallas_call(
        kernel,
        out_shape=outs,
        in_specs=specs,
        out_specs=jax.tree.map(lambda _: pl.BlockSpec(memory_space=out_space), outs),
        scratch_shapes=list(scratch),
        compiler_params=pltpu.CompilerParams(vmem_limit_bytes=grant),
        cost_estimate=pl.CostEstimate(
            flops=int(micros * FLOPS_PER_MICRO), bytes_accessed=size, transcendentals=0
        ),
    )(*args)


def iota(shape, axis):
    return lax.broadcasted_iota(jnp.int32, shape, axis)


def roll(x, shift, axis):
    return pltpu.roll(x, shift % x.shape[axis], axis)


def flag(condition):
    return jnp.where(condition, 1.0, 0.0).astype(F32)


def ocean_columns(water):
    levels, rows, width = water.shape
    lane = iota((rows, width), 1)
    line = iota((1, width), 1)
    mixed = jnp.zeros((rows, width), F32)
    for l in range(levels):
        mixed = jnp.where(lane // 4 == l, roll(water[l], 2 + 4 * l, 1), mixed)
    across = jnp.concatenate([mixed, jnp.zeros((width - rows, width), F32)], axis=0).T
    beside = []
    for l in range(levels):
        for j in range(2):
            last = across[4 * l + 1 - j : 4 * l + 2 - j]
            lead = across[4 * l + 2 + j : 4 * l + 3 + j]
            beside.append(jnp.where(line < rows, last, roll(lead, rows, 1)))
    return beside


def forward_kernel(group, links_h, blocks_h, rows_h, cols_h, currents_h, water_h, *refs):
    devices, members, place = group
    outs, scratch = refs[:members], refs[members:]
    links, blocks, currents, weights, water, fields, kept, arrived, left = scratch
    pairs, side, width = rows_h.shape
    both = weights.shape[1]
    loads = [
        pltpu.make_async_copy(source, target, arrived.at[i])
        for i, (source, target) in enumerate(
            (
                (links_h, links),
                (blocks_h, blocks),
                (currents_h, currents),
                (rows_h, weights.at[:, pl.ds(0, side)]),
                (cols_h, weights.at[:, pl.ds(side, both - side)]),
                (water_h, water),
            )
        )
    ]
    for load in loads:
        load.start()
    for i in (1, 3, 4):
        loads[i].wait()
    me = place()
    owners = [lax.rem(lax.rem(blocks[0, m], devices), members) for m in range(pairs)]
    copies = []
    for k, out in enumerate(outs):
        partner = me ^ k
        pair = jnp.int32(0)
        for m in range(pairs):
            pair = jnp.where(owners[m] == partner, m, pair)
        source = weights.at[pair]
        if pairs < members:
            found = sum(flag(owners[m] == partner) for m in range(pairs))
            kept[k] = (weights[pair].astype(F32) * found).astype(BF16)
            source = kept.at[k]
        copies.append(pltpu.make_async_copy(source, out.at[pl.ds(0, both)], left.at[2 * k]))
        copies[-1].start()
    for i in (0, 2, 5):
        loads[i].wait()
    for c in range(2):
        fields[c * side : (c + 1) * side] = currents[c].astype(BF16)
    lane = iota((1, width), 1)
    numbers = jnp.zeros((1, width), F32)
    for q in range(4):
        numbers = jnp.where(lane == q, (links[0, 0, q] >> 7).astype(F32), numbers)
        numbers = jnp.where(lane == 4 + q, (links[0, 0, q] & 127).astype(F32), numbers)
    ends = ocean_columns(water) + [numbers]
    blank = jnp.zeros((fields.shape[0] - 2 * side - len(ends), width), F32)
    fields[2 * side :] = jnp.concatenate(ends + [blank], axis=0).astype(BF16)
    for k, out in enumerate(outs):
        if out.shape[0] > both:
            target = out.at[pl.ds(both, fields.shape[0])]
            copies.append(pltpu.make_async_copy(fields, target, left.at[2 * k + 1]))
            copies[-1].start()
    for copy in copies:
        copy.wait()


def put_side_rims(store, planes, at):
    size = planes[0].shape[0]
    lane = iota((size, size), 1)
    mixed = jnp.zeros((size, size), F32)
    for i, plane in enumerate(planes):
        turned = roll(plane, DEPTH + 2 * DEPTH * i, 1)
        mixed = jnp.where(lane // (2 * DEPTH) == i, turned, mixed)
    across = mixed.T
    for i, plane in enumerate(planes):
        for k in range(DEPTH):
            base = i * DEPTH + k
            store[at(0) + base : at(0) + base + 1] = plane[size - 1 - k : size - k]
            store[at(1) + base : at(1) + base + 1] = plane[k : k + 1]
            east = 2 * DEPTH * i + DEPTH - 1 - k
            west = 2 * DEPTH * i + DEPTH + k
            store[at(2) + base : at(2) + base + 1] = across[east : east + 1]
            store[at(3) + base : at(3) + base + 1] = across[west : west + 1]


def rims_kernel(
    thick, conc, ice, water, out, viscous_o, gain_o, mass_o, drag_o, conduct_o,
    speed_o, store,
):
    size = thick.shape[1]
    cover = jnp.zeros((size, size), F32)
    volume = jnp.zeros((size, size), F32)
    conduct = jnp.zeros((size, size), F32)
    for c in range(thick.shape[0]):
        h, a = thick[c], conc[c]
        cover = cover + a
        volume = volume + a * h
        conduct = conduct + a / (h + THIN_ICE)
    mass = volume + BASE_MASS
    viscous = VISCOUS_STEP * (volume * jnp.exp(-STRENGTH_DECAY * (1.0 - cover))) / mass
    step_mass = SUBCYCLE_STEP / mass
    gain = 1.0 / (1.0 + step_mass * cover)
    speed_x = ice[pl.ds(0, size, stride=2), :]
    speed_y = ice[pl.ds(1, size, stride=2), :]
    viscous_o[...] = viscous
    gain_o[...] = gain
    mass_o[...] = step_mass
    drag_o[...] = cover
    conduct_o[...] = -HEAT_RATE * conduct
    speed_o[0] = speed_x
    speed_o[1] = speed_y
    put_side_rims(store, [speed_x, speed_y, viscous, gain], lambda side: side * 4 * DEPTH)
    levels, rows, width = water.shape
    start = SIDE_ROWS
    for l in range(levels):
        for j in range(2):
            at = start + 2 * l + j
            store[at : at + 1] = water[l, rows - 1 - j : rows - j]
            store[at + 2 * levels : at + 2 * levels + 1] = water[l, j : j + 1]
    out[...] = store[...].astype(BF16)


def nearby(me, members, distance, arrays):
    at = me + distance
    inside = (at >= 0) & (at < members)
    found = 0.0
    for k in range(1, members):
        found = found + arrays[k].astype(F32) * flag(inside & ((me ^ k) == at))
    return found


def remap_forward(chunks, field_rows, side, depth):
    total = None
    for chunk, fields in zip(chunks, field_rows):
        down = chunk[0:side]
        right = chunk[side : side + depth]
        wide = jnp.concatenate(fields, axis=1) if len(fields) > 1 else fields[0]
        part = lax.dot_general(down, wide, (((0,), (0,)), ((), ())), preferred_element_type=F32)
        part = part.astype(BF16)
        width = fields[0].shape[1]
        if len(fields) > 1:
            part = jnp.concatenate(
                [part[:, c * width : (c + 1) * width] for c in range(len(fields))], axis=0
            )
        piece = lax.dot_general(part, right, (((1,), (1,)), ((), ())), preferred_element_type=F32)
        piece = piece.astype(BF16).astype(F32)
        total = piece if total is None else total + piece
    return total


def tails_of(chunks, hops):
    at = min(c.shape[0] for c in chunks)
    return [hops[k // 2 - 1][...] if k > 1 and k % 2 else c[at:] for k, c in enumerate(chunks)]


def forcing_kernel(group, side, levels, subs, place, mass, drag, wind, early, *refs):
    chunks = refs[:group][::-1]
    hops, (out, current_o, push_o, store) = refs[group:-4], refs[-4:]
    size = mass.shape[0]
    depth = chunks[0].shape[1]
    tails = tails_of(chunks, hops)
    fields = [[t[0:side], t[side : 2 * side]] for t in tails]
    total = remap_forward(chunks, fields, side, depth)
    pushes = []
    for c in range(2):
        current = total[c * size : (c + 1) * size]
        current_o[c] = current
        force = wind[pl.ds(c, size, stride=2), :]
        push = mass[...] * (force + drag[...] * current)
        push_o[c] = push
        pushes.append(push)
    put_side_rims(store, pushes, lambda q: q * 2 * DEPTH)
    tail = [t[2 * side :] for t in tails]
    store[NAMES_ROW : NAMES_ROW + 1] = tail[0].astype(F32)[2 * levels : 2 * levels + 1]
    me, step = place(), group // subs
    left, right = (nearby(me, group, d * step, tail) for d in (-1, 1))
    line = iota((1, size), 1)
    for l in range(levels):
        near = slice(2 * l, 2 * l + 1)
        store[CORNER_ROWS[l] : CORNER_ROWS[l] + 1] = jnp.where(line < side, left[near], right[near])
    out[0:PUSH_ROWS] = store[...].astype(BF16)
    out[PUSH_ROWS:] = early[...]


def ocean_halos(counts, tile_place, member_place, shape, messages, tails):
    tiles, subs, levs = counts
    levels, rows, width = shape
    my_tile, me = tile_place(), member_place()
    halo = {}
    strips = [m[BLOCK_ROWS : BLOCK_ROWS + 4 * levels] for m in messages]
    rims = [m[0:PUSH_ROWS] for m in messages]
    ends = [t[2 * rows :] for t in tails]
    for dt in (-1, 1):
        beyond = nearby(my_tile, tiles, dt, strips)
        halo[dt, 0] = beyond[: 2 * levels] if dt < 0 else beyond[2 * levels :]
        corners = nearby(my_tile, tiles, dt, rims)
        corners = jnp.concatenate([corners[r : r + 1] for r in CORNER_ROWS[:levels]], axis=0)
        at = rows - 1 if dt < 0 else 0
        for ds in (-1, 1):
            lane_at = at if ds < 0 else rows + at
            halo[dt, ds] = corners[:, lane_at : lane_at + 1]
    for ds in (-1, 1):
        beside = nearby(me, subs * levs, ds * levs, ends)[: 2 * levels]
        halo[0, ds] = roll(beside, -rows, 1) if ds > 0 else beside
    return halo


def biharmonic(x, top, bottom, left, right, corner):
    rows, width = x.shape
    row, lane = iota(x.shape, 0), iota(x.shape, 1)
    line = iota((1, width), 1)

    def laplacian(x, top, bottom, left, right):
        up = jnp.where(row == 0, top, roll(x, 1, 0))
        down = jnp.where(row == rows - 1, bottom, roll(x, -1, 0))
        west = jnp.where(lane == 0, left, roll(x, 1, 1))
        east = jnp.where(lane == width - 1, right, roll(x, -1, 1))
        return up + down + west + east - 4.0 * x

    def ring_row(mid, out_row, in_row, dt):
        west = jnp.where(line == 0, corner[dt, -1], roll(mid, 1, 1))
        east = jnp.where(line == width - 1, corner[dt, 1], roll(mid, -1, 1))
        return west + east + out_row + in_row - 4.0 * mid

    def ring_col(mid, out_col, in_col, ds):
        up = jnp.concatenate([corner[-1, ds], mid[:-1]], axis=0)
        down = jnp.concatenate([mid[1:], corner[1, ds]], axis=0)
        return up + down + out_col + in_col - 4.0 * mid

    return laplacian(
        laplacian(x, top[0], bottom[0], left[0], right[0]),
        ring_row(*top, x[0:1], -1),
        ring_row(*bottom, x[rows - 1 :], 1),
        ring_col(*left, x[:, 0:1], -1),
        ring_col(*right, x[:, width - 1 :], 1),
    )


def split_refs(tiles, members, refs, outs):
    messages, chunks = refs[:tiles], refs[tiles : tiles + members]
    return messages, tails_of(chunks, refs[tiles + members : -outs]), refs[-outs:]


def relay_kernel(counts, tile_place, member_place, water, mixing, *refs):
    tiles, subs, levs = counts
    outs = 1 if levs == 1 else 2
    messages, tails, outs = split_refs(tiles, subs * levs, refs, outs)
    for k in range(tiles):
        outs[0][k * BLOCK_ROWS : (k + 1) * BLOCK_ROWS] = messages[k][0:BLOCK_ROWS]
    levels, rows, width = water.shape
    halo = ocean_halos(counts, tile_place, member_place, water.shape, messages, tails)

    def both(strip):
        near = sum(strip[2 * l : 2 * l + 1] for l in range(levels))
        far = sum(strip[2 * l + 1 : 2 * l + 2] for l in range(levels))
        return near, far

    def as_columns(strip):
        near, far = both(strip)
        across = jnp.concatenate([near, far] + [jnp.zeros_like(near)] * 6, axis=0).T
        return across[0:rows, 0:1], across[0:rows, 1:2]

    corner = {
        (dt, ds): jnp.sum(halo[dt, ds], axis=0, keepdims=True) for dt in (-1, 1) for ds in (-1, 1)
    }
    x = sum(water[l] for l in range(levels))
    twice = biharmonic(
        x, both(halo[-1, 0]), both(halo[1, 0]), as_columns(halo[0, -1]), as_columns(halo[0, 1]), corner
    )
    top = (x - mixing[...] * twice) / (levels * levs)
    if levs == 1:
        outs[0][tiles * BLOCK_ROWS :] = top.astype(BF16)
    else:
        outs[1][...] = top


def ocean_kernel(counts, tile_place, member_place, water, mixing, *refs):
    tiles, subs, levs = counts
    messages, tails, (warm_o,) = split_refs(tiles, subs * levs, refs, 1)
    levels, rows, width = water.shape
    halo = ocean_halos(counts, tile_place, member_place, water.shape, messages, tails)
    left, right = halo[0, -1].T, halo[0, 1].T
    for l in range(levels):
        x = water[l]
        pair = (2 * l, 2 * l + 1)
        twice = biharmonic(
            x,
            [halo[-1, 0][i : i + 1] for i in pair],
            [halo[1, 0][i : i + 1] for i in pair],
            [left[0:rows, i : i + 1] for i in pair],
            [right[0:rows, i : i + 1] for i in pair],
            {(dt, ds): halo[dt, ds][l : l + 1] for dt in (-1, 1) for ds in (-1, 1)},
        )
        warm_o[l] = x - mixing[...] * twice


def ice_kernel(
    tiles, members, side, table, viscous, gain, drag, conduct, current, speed, push, *refs
):
    chunks, relays = refs[:members], refs[members : 2 * members]
    out, own_o, beside_o, rims, names, named, field = refs[2 * members :]
    load_names = pltpu.make_async_copy(table, names, named)
    load_names.start()
    size = viscous.shape[0]
    depth = chunks[0].shape[1]
    warm = remap_forward(chunks, [[r[r.shape[0] - side :]] for r in relays], side, depth)
    heat = (conduct[...] * warm).astype(BF16)
    for k in range(tiles):
        for m in range(members):
            rims[k * members + m] = relays[m][k * BLOCK_ROWS : (k + 1) * BLOCK_ROWS]
    half = DEPTH
    high = 2 * DEPTH
    sub = iota((high, size), 0)
    lane = iota((high, size), 1)
    edge = (sub & (half - 1)) == 0
    turn = jnp.where(sub < half, CORIOLIS_TURN, -CORIOLIS_TURN).astype(F32)
    first, last = lane == 0, lane == size - 1

    def load(device, side, mask, with_push=True):
        start = PUSH_ROWS + side * 2 * high
        block = rims[device, start : start + 2 * high].astype(F32)
        velocity, both = block[:high] * mask, block[high:]
        if not with_push:
            return velocity
        other = roll(both, half, 0)
        visc = jnp.where(sub < half, both, other)
        scale = jnp.where(sub < half, other, both) * mask
        start = side // 2 * 2 * high
        pushed = rims[device, start : start + 2 * high].astype(F32)
        pushed = pushed[:high] if side % 2 == 0 else pushed[high:]
        return [velocity, visc, scale, pushed]

    def follow(device, side):
        name = names[device, side]
        return jnp.where(name >= 0, name, 0), name >= 0

    def step(state, left, right, inner, outer):
        c, visc, scale, pushed = state
        spread = left + right + inner + outer - 4.0 * c
        return scale * (c + visc * spread + pushed + turn * roll(c, half, 0))

    col = iota((size, size), 1)
    base = high
    for c in range(2):
        field[0, c, base : base + size] = speed[c]

    def own_edges(now):
        vx, vy = (field[now, c, base : base + size] for c in range(2))
        mixed = jnp.where(col < half, roll(vx, 1, 1), roll(vy, 1 + half, 1))
        across = mixed.T[0:high]
        return [
            jnp.where(sub < half, vx[size - 1 :], vy[size - 1 :]),
            jnp.where(sub < half, vx[0:1], vy[0:1]),
            across,
            roll(across, -1, 0),
        ]

    own = own_edges(0)
    load_names.wait()
    strips = []
    for q in range(4):
        x, has_x = follow(0, q)
        strip = load(x, OPPOSITE[q], flag(has_x))
        sides = []
        for s in LATERAL[q]:
            y, has_y = follow(x, s)
            z, has_z = follow(y, OPPOSITE[q])
            w, has_w = follow(z, OPPOSITE[s])
            sides.append(
                [
                    load(y, OPPOSITE[q], flag(has_y)),
                    load(z, q, flag(has_z)),
                    load(w, q, flag(has_w), with_push=False),
                ]
            )
        strips.append((strip, sides))

    for t in range(SUBCYCLES):
        cells = [strip[0] for strip, _ in strips]
        if t < SUBCYCLES - 1:
            if t > 0:
                own = own_edges(t % 2)
            for q in range(4):
                strip, (beyond, before) = strips[q]
                c, y_hi, y_lo = strip[0], beyond[0][0], before[0][0]
                left = jnp.where(first, roll(y_lo, 1, 1), roll(c, 1, 1))
                right = jnp.where(last, roll(y_hi, -1, 1), roll(c, -1, 1))
                inner = jnp.where(edge, own[q], roll(c, 1, 0))
                new_strip = step(strip, left, right, inner, roll(c, -1, 0))
                if t < SUBCYCLES - 2:
                    new_sides = []
                    for i, (y, z, w) in enumerate((beyond, before)):
                        away = 1 if i == 0 else -1
                        boundary = first if i == 0 else last
                        yc, zc = y[0], z[0]
                        toward = jnp.where(boundary, roll(c, away, 1), roll(yc, away, 1))
                        inner = jnp.where(edge, zc, roll(yc, 1, 0))
                        new_y = step(y, toward, roll(yc, -away, 1), inner, roll(yc, -1, 0))
                        new_z = zc
                        if t < SUBCYCLES - 3:
                            toward = jnp.where(boundary, roll(w, away, 1), roll(zc, away, 1))
                            inner = jnp.where(edge, yc, roll(zc, 1, 0))
                            new_z = step(z, toward, roll(zc, -away, 1), inner, roll(zc, -1, 0))
                        new_sides.append((new_y, new_z))
                    for item, (new_y, new_z) in zip((beyond, before), new_sides):
                        item[0][0] = new_y
                        item[1][0] = new_z
                strip[0] = new_strip
        now, later = t % 2, (t + 1) % 2
        sides = jnp.where(edge, cells[2], roll(cells[3], 1, 0)).T
        for c in range(2):
            at = c * half
            field[now, c, base + size : base + size + 1] = cells[0][at : at + 1]
            field[now, c, base - 1 : base] = cells[1][at : at + 1]
        for i in range(size // high):
            rows = slice(i * high, (i + 1) * high)
            held = [field[now, c, base + i * high : base + (i + 1) * high] for c in range(2)]
            for c in range(2):
                v, at = held[c], base + i * high
                up = field[now, c, at + 1 : at + 1 + high]
                down = field[now, c, at - 1 : at - 1 + high]
                east = jnp.where(last, sides[rows, c * half : c * half + 1], roll(v, -1, 1))
                west = jnp.where(first, sides[rows, c * half + 1 : c * half + 2], roll(v, 1, 1))
                spread = up + down + east + west - 4.0 * v
                turned = (CORIOLIS_TURN if c == 0 else -CORIOLIS_TURN) * held[1 - c]
                new = gain[rows] * (v + viscous[rows] * spread + push[c, rows] + turned)
                if t == SUBCYCLES - 1:
                    out[c, rows] = new
                else:
                    field[later, c, at : at + high] = new
    stress = [(drag[...] * (out[c] - current[c])).astype(BF16) for c in range(2)]
    return_fluxes([heat, *stress], chunks, side, depth, own_o, beside_o)


def return_fluxes(fluxes, chunks, side, depth, own, beside):
    size = fluxes[0].shape[0]
    wide = jnp.concatenate(fluxes, axis=1)
    step = 3 * side
    for k, chunk in enumerate(chunks):
        part = jnp.dot(chunk[0:side], wide, preferred_element_type=F32).astype(BF16)
        part = jnp.concatenate([part[:, c * size : (c + 1) * size] for c in range(3)], axis=0)
        reply = jnp.dot(part, chunk[side : side + depth], preferred_element_type=F32)
        at = k // 2 * step
        if k % 2:
            beside[at : at + step] = reply.astype(BF16)
        else:
            own[at : at + step] = reply


def pair_kernel(own, beside, *outs):
    step = outs[0].shape[0]
    for k, out in enumerate(outs):
        at = (k + 1) * step
        out[...] = (own[at : at + step] + beside[at : at + step].astype(F32)).astype(BF16)


def finish_kernel(warm, currents, speed, own, beside, *refs):
    outs, (flat, heat_v, current_v, left) = refs[-7:-4], refs[-4:]
    replies = refs[:-7]
    flat_o, heat_o, current_o = outs
    size = speed.shape[1]
    copies = [
        pltpu.make_async_copy(source, target, left.at[i])
        for i, (source, target) in enumerate(
            ((flat, flat_o), (heat_v, heat_o), (current_v, current_o))
        )
    ]
    for c in range(2):
        flat[pl.ds(c, size, stride=2), :] = speed[c]
    copies[0].start()
    side = currents.shape[1]
    total = own[0 : 3 * side] + beside[0 : 3 * side].astype(F32)
    for reply in replies:
        total = total + reply[...].astype(F32)
    heat = THERMAL_DIFFUSE * total[0:side]
    for l in range(warm.shape[0]):
        heat_v[l] = warm[l] + heat
    copies[1].start()
    for c in range(2):
        current_v[c] = currents[c] + STRESS_MIXING * total[(c + 1) * side : (c + 2) * side]
    copies[2].start()
    for copy in copies:
        copy.wait()


def shards(
    water_heat_state,
    diffusion_coefficient,
    upper_current_vector,
    remap_blocks,
    remap_rows,
    remap_cols,
    neighbors,
    thickness,
    concentration,
    ice_velocity,
    wind_stress,
):
    tile_count, sub_count, lev_count = (lax.axis_size(a) for a in ("tile", "sub", "lev"))
    group = sub_count * lev_count
    devices = tile_count * group
    group_axes = ("sub", "lev")
    member_axes = ("tile", "sub", "lev")
    levels, side, width = water_heat_state.shape
    pairs, size = remap_rows.shape[1:3]
    categories = thickness.shape[2]

    def tile_place():
        return lax.axis_index("tile")

    def member_place():
        return lax.axis_index("sub") * lev_count + lax.axis_index("lev")

    def device_place():
        return lax.axis_index("tile") * group + member_place()

    def swap(value, axes, count):
        got = {0: value}
        for k in range(1, count):
            got[k] = lax.ppermute(value, axes, [(i, i ^ k) for i in range(count)])
        return [got[k] for k in range(count)]

    def swap_chips(value):
        return {0: value} | {
            k: lax.ppermute(value, group_axes, [(i, i ^ k) for i in range(group)])
            for k in range(2, group, 2)
        }

    def swap_cores(got):
        beside = [(i, i ^ 1) for i in range(group)]
        got = got | {k + 1: lax.ppermute(got[k], group_axes, beside) for k in got}
        return [got[k] for k in range(group)]

    def swap_each(values):
        got = {0: values[0]}
        for k in range(1, group):
            got[k] = lax.ppermute(values[k], group_axes, [(i, i ^ k) for i in range(group)])
        return [got[k] for k in range(group)]

    def shape(*dims, dtype=F32):
        return jax.ShapeDtypeStruct(dims, dtype)

    def interleaved(value):
        return value.reshape(2, size, size).transpose(1, 0, 2).reshape(2 * size, size)

    plane = shape(size, size)
    planes = shape(2, size, size)
    wind = interleaved(wind_stress)

    tail_rows = -(-(2 * levels + 1) // TILE_ROWS) * TILE_ROWS
    pair_rows = side + width
    chunk_rows = pair_rows + 2 * side + tail_rows
    sent = call(
        functools.partial(forward_kernel, (devices, group, member_place)),
        [
            shape(pair_rows if k > 1 and k % 2 else chunk_rows, width, dtype=BF16)
            for k in range(group)
        ],
        (
            neighbors,
            remap_blocks,
            remap_rows[0].swapaxes(1, 2),
            remap_cols[0],
            upper_current_vector,
            water_heat_state,
        ),
        scratch=[
            pltpu.SMEM(neighbors.shape, jnp.int32),
            pltpu.SMEM((1, pairs), jnp.int32),
            pltpu.VMEM((2, side, width), F32),
            pltpu.VMEM((pairs, pair_rows, width), BF16),
            pltpu.VMEM((levels, side, width), F32),
            pltpu.VMEM((chunk_rows - pair_rows, width), BF16),
            pltpu.VMEM((1 if pairs == group else group, pair_rows, width), BF16),
            pltpu.SemaphoreType.DMA((6,)),
            pltpu.SemaphoreType.DMA((2 * group,)),
        ],
        hbm=(0, 1, 2, 3, 4, 5),
        grant=60 * 2**20,
        micros=10,
    )
    chunks = swap_each(sent)
    hops = [
        lax.ppermute(chunks[k][pair_rows:], group_axes, [(i, i ^ 1) for i in range(group)])
        for k in range(2, group, 2)
    ]

    early, viscous, gain, step_mass, drag, conduct, speed = call(
        rims_kernel,
        [shape(SIDE_ROWS + 4 * levels, size, dtype=BF16)] + [plane] * 5 + [planes],
        (
            thickness.reshape(categories, size, size),
            concentration.reshape(categories, size, size),
            interleaved(ice_velocity),
            water_heat_state,
        ),
        scratch=[pltpu.VMEM((SIDE_ROWS + 4 * levels, size), F32)],
    )
    message, current_ice, push = call(
        functools.partial(forcing_kernel, group, side, levels, sub_count, member_place),
        [shape(BLOCK_ROWS + 4 * levels, size, dtype=BF16), planes, planes],
        (step_mass, drag, wind, early, *chunks[::-1], *hops),
        scratch=[pltpu.VMEM((PUSH_ROWS, size), F32)],
    )
    messages = swap(message, "tile", tile_count)

    counts = (tile_count, sub_count, lev_count)
    ocean = (*messages, *chunks, *hops)
    relay_rows = tile_count * BLOCK_ROWS
    relay_shapes = [shape(relay_rows + (side if lev_count == 1 else 0), size, dtype=BF16)]
    if lev_count > 1:
        relay_shapes.append(shape(side, width))
    relay, *top = call(
        functools.partial(relay_kernel, counts, tile_place, member_place),
        relay_shapes,
        (water_heat_state, diffusion_coefficient, *ocean),
    )
    if lev_count > 1:
        relay = jnp.concatenate([relay, lax.psum(top[0], "lev").astype(BF16)], axis=0)
    relays = swap_chips(relay)

    mixing, _ = lax.optimization_barrier((diffusion_coefficient, relay))
    (warm,) = call(
        functools.partial(ocean_kernel, counts, tile_place, member_place),
        [shape(levels, side, width)],
        (water_heat_state, mixing, *ocean),
    )
    far = sorted(k for k in relays if k)
    relayed, _ = lax.optimization_barrier(([relays[k] for k in far], warm))
    relays = swap_cores({0: relay} | dict(zip(far, relayed)))

    names = jnp.stack(
        [
            r[:relay_rows].reshape(tile_count, BLOCK_ROWS, size)[:, NAMES_ROW, 0:8]
            for r in relays
        ],
        axis=1,
    )
    names = names.reshape(devices, 8).astype(jnp.int32)
    table = names[:, 0:4] * 128 + names[:, 4:8]
    table = jnp.where(table < 0, -1, table ^ device_place())
    step = 3 * side
    speed, own, beside = call(
        functools.partial(ice_kernel, tile_count, group, side),
        [
            planes,
            shape(group // 2 * step, width),
            shape(group // 2 * step, width, dtype=BF16),
        ],
        (table, viscous, gain, drag, conduct, current_ice, speed, push, *chunks, *relays),
        scratch=[
            pltpu.VMEM((devices, BLOCK_ROWS, size), BF16),
            pltpu.SMEM((devices, 4), jnp.int32),
            pltpu.SemaphoreType.DMA,
            pltpu.VMEM((2, 2, size + 4 * DEPTH, size), F32),
        ],
        hbm=(0,),
    )
    beside = lax.ppermute(beside, group_axes, [(i, i ^ 1) for i in range(group)])
    paired = call(
        pair_kernel, [shape(step, width, dtype=BF16)] * (group // 2 - 1), (own, beside)
    )
    replies = [
        lax.ppermute(value, group_axes, [(i, i ^ (2 * k + 2)) for i in range(group)])
        for k, value in enumerate(paired)
    ]
    if lev_count > 1:
        parts = [r.astype(F32) for r in (own[:step], beside[:step], *replies)]
        own, beside, replies = lax.psum(sum(parts), "lev"), jnp.zeros_like(beside[:step]), []
    flat, heat, current = call(
        finish_kernel,
        [shape(2 * size, size), shape(levels, side, width), shape(2, side, width)],
        (warm, upper_current_vector, speed, own, beside, *replies),
        scratch=[
            pltpu.VMEM((2 * size, size), F32),
            pltpu.VMEM((levels, side, width), F32),
            pltpu.VMEM((2, side, width), F32),
            pltpu.SemaphoreType.DMA((3,)),
        ],
        out_space=pltpu.HBM,
    )
    velocity = flat.reshape(size, 2, size).transpose(1, 0, 2).reshape(1, 1, 2, size * size)
    return heat, current, velocity


def solution(mesh):
    member = ("tile", "sub", "lev")
    whole = ("copies",) + member
    ice = P(None, whole, None, None)
    water = P("lev", ("copies", "tile"), "sub")
    current = P(None, ("copies", "tile"), "sub")
    return jax.shard_map(
        shards,
        mesh=mesh,
        in_specs=(
            water,
            P("tile", "sub"),
            current,
            P(member, None),
            P(member, None, None, None),
            P(member, None, None, None),
            P(None, member, None),
            ice,
            ice,
            ice,
            ice,
        ),
        out_specs=(water, current, ice),
        check_vma=False,
    )
```

```python
import functools

import jax
import jax.numpy as jnp
from jax import lax
from jax.experimental import pallas as pl
from jax.experimental.pallas import tpu as pltpu
from jax.sharding import PartitionSpec as P

SUBCYCLES = 4
STRENGTH_DECAY = 5.0
VISCOUS_STEP = 0.24
SUBCYCLE_STEP = 0.5
CORIOLIS_TURN = 0.1
BASE_MASS = 0.5
HEAT_RATE = 0.2
THIN_ICE = 0.1
THERMAL_DIFFUSE = 0.5
STRESS_MIXING = 0.5

OPPOSITE = (1, 0, 3, 2)
LATERAL = ((2, 3), (2, 3), (0, 1), (0, 1))
DEPTH = SUBCYCLES
EARLY_DEPTHS = (DEPTH, DEPTH, DEPTH - 1, DEPTH - 1)
LATE_DEPTHS = (DEPTH - 1, DEPTH - 1)
EARLY_SIDE, LATE_SIDE = sum(EARLY_DEPTHS), sum(LATE_DEPTHS)
EARLY_ROWS = 4 * EARLY_SIDE
BLOCK_ROWS = EARLY_ROWS + 4 * LATE_SIDE
TILE_ROWS = 16
F32 = jnp.float32
BF16 = jnp.bfloat16
VMEM_LIMIT = 16 * 1024 * 1024
FLOPS_PER_MICRO = 1.15e9


def call(kernel, outs, args, scratch=(), smem=(), hbm=(), out_space=pltpu.VMEM, grant=VMEM_LIMIT, micros=0.01):
    def space(i):
        return pltpu.SMEM if i in smem else pltpu.HBM if i in hbm else pltpu.VMEM

    specs = [pl.BlockSpec(memory_space=space(i)) for i in range(len(args))]
    size = sum(a.size * a.dtype.itemsize for a in args)
    return pl.pallas_call(
        kernel,
        out_shape=outs,
        in_specs=specs,
        out_specs=jax.tree.map(lambda _: pl.BlockSpec(memory_space=out_space), outs),
        scratch_shapes=list(scratch),
        compiler_params=pltpu.CompilerParams(vmem_limit_bytes=grant),
        cost_estimate=pl.CostEstimate(
            flops=int(micros * FLOPS_PER_MICRO), bytes_accessed=size, transcendentals=0
        ),
    )(*args)


def iota(shape, axis):
    return lax.broadcasted_iota(jnp.int32, shape, axis)


def roll(x, shift, axis):
    return pltpu.roll(x, shift % x.shape[axis], axis)


def flag(condition):
    return jnp.where(condition, 1.0, 0.0).astype(F32)


def ocean_columns(water):
    levels, rows, width = water.shape
    lane = iota((rows, width), 1)
    line = iota((1, width), 1)
    mixed = jnp.zeros((rows, width), F32)
    for l in range(levels):
        mixed = jnp.where(lane // 4 == l, roll(water[l], 2 + 4 * l, 1), mixed)
    across = jnp.concatenate([mixed, jnp.zeros((width - rows, width), F32)], axis=0).T
    beside = []
    for l in range(levels):
        for j in range(2):
            last = across[4 * l + 1 - j : 4 * l + 2 - j]
            lead = across[4 * l + 2 + j : 4 * l + 3 + j]
            beside.append(jnp.where(line < rows, last, roll(lead, rows, 1)))
    return beside


def forward_kernel(group, links_h, blocks_h, rows_h, cols_h, currents_h, water_h, *refs):
    devices, members, place = group
    outs, scratch = refs[:members], refs[members:]
    links, blocks, currents, weights, water, fields, kept, arrived, left = scratch
    pairs, side, width = rows_h.shape
    both = weights.shape[1]
    loads = [
        pltpu.make_async_copy(source, target, arrived.at[i])
        for i, (source, target) in enumerate(
            (
                (links_h, links),
                (blocks_h, blocks),
                (currents_h, currents),
                (rows_h, weights.at[:, pl.ds(0, side)]),
                (cols_h, weights.at[:, pl.ds(side, both - side)]),
                (water_h, water),
            )
        )
    ]
    for load in loads:
        load.start()
    for i in (1, 3, 4):
        loads[i].wait()
    me = place()
    owners = [lax.rem(lax.rem(blocks[0, m], devices), members) for m in range(pairs)]
    copies = []
    for k, out in enumerate(outs):
        partner = me ^ k
        pair = jnp.int32(0)
        for m in range(pairs):
            pair = jnp.where(owners[m] == partner, m, pair)
        source = weights.at[pair]
        if pairs < members:
            found = sum(flag(owners[m] == partner) for m in range(pairs))
            kept[k] = (weights[pair].astype(F32) * found).astype(BF16)
            source = kept.at[k]
        copies.append(pltpu.make_async_copy(source, out.at[pl.ds(0, both)], left.at[2 * k]))
        copies[-1].start()
    for i in (0, 2, 5):
        loads[i].wait()
    for c in range(2):
        fields[c * side : (c + 1) * side] = currents[c].astype(BF16)
    lane = iota((1, width), 1)
    numbers = jnp.zeros((1, width), F32)
    for q in range(4):
        numbers = jnp.where(lane == q, (links[0, 0, q] >> 7).astype(F32), numbers)
        numbers = jnp.where(lane == 4 + q, (links[0, 0, q] & 127).astype(F32), numbers)
    ends = ocean_columns(water) + [numbers]
    blank = jnp.zeros((fields.shape[0] - 2 * side - len(ends), width), F32)
    fields[2 * side :] = jnp.concatenate(ends + [blank], axis=0).astype(BF16)
    for k, out in enumerate(outs):
        if out.shape[0] > both:
            target = out.at[pl.ds(both, fields.shape[0])]
            copies.append(pltpu.make_async_copy(fields, target, left.at[2 * k + 1]))
            copies[-1].start()
    for copy in copies:
        copy.wait()


def put_side_rims(store, planes, depths, at):
    size = planes[0].shape[0]
    lane = iota((size, size), 1)
    mixed = jnp.zeros((size, size), F32)
    for i, plane in enumerate(planes):
        turned = roll(plane, DEPTH + 2 * DEPTH * i, 1)
        mixed = jnp.where(lane // (2 * DEPTH) == i, turned, mixed)
    across = mixed.T
    base = 0
    for i, plane in enumerate(planes):
        for k in range(depths[i]):
            east = 2 * DEPTH * i + DEPTH - 1 - k
            west = 2 * DEPTH * i + DEPTH + k
            store[at(0) + base : at(0) + base + 1] = plane[size - 1 - k : size - k]
            store[at(1) + base : at(1) + base + 1] = plane[k : k + 1]
            store[at(2) + base : at(2) + base + 1] = across[east : east + 1]
            store[at(3) + base : at(3) + base + 1] = across[west : west + 1]
            base += 1


def rims_kernel(
    thick, conc, ice, water, out, viscous_o, gain_o, mass_o, drag_o, conduct_o,
    speed_o,
):
    size = thick.shape[1]
    cover = jnp.zeros((size, size), F32)
    volume = jnp.zeros((size, size), F32)
    conduct = jnp.zeros((size, size), F32)
    for c in range(thick.shape[0]):
        h, a = thick[c], conc[c]
        cover = cover + a
        volume = volume + a * h
        conduct = conduct + a / (h + THIN_ICE)
    mass = volume + BASE_MASS
    viscous = VISCOUS_STEP * (volume * jnp.exp(-STRENGTH_DECAY * (1.0 - cover))) / mass
    step_mass = SUBCYCLE_STEP / mass
    gain = 1.0 / (1.0 + step_mass * cover)
    speed_x = ice[pl.ds(0, size, stride=2), :]
    speed_y = ice[pl.ds(1, size, stride=2), :]
    viscous_o[...] = viscous
    gain_o[...] = gain
    mass_o[...] = step_mass
    drag_o[...] = cover
    conduct_o[...] = -HEAT_RATE * conduct
    speed_o[0] = speed_x
    speed_o[1] = speed_y
    put_side_rims(
        out, [speed_x, speed_y, viscous, gain], EARLY_DEPTHS, lambda side: side * EARLY_SIDE
    )
    levels, rows, width = water.shape
    for l in range(levels):
        for j in range(2):
            at = EARLY_ROWS + 2 * l + j
            out[at : at + 1] = water[l, rows - 1 - j : rows - j]
            out[at + 2 * levels : at + 2 * levels + 1] = water[l, j : j + 1]


def nearby(me, members, distance, arrays):
    at = me + distance
    inside = (at >= 0) & (at < members)
    found = 0.0
    for k in range(1, members):
        found = found + arrays[k].astype(F32) * flag(inside & ((me ^ k) == at))
    return found


def remap_forward(chunks, field_rows, side, depth):
    total = None
    for chunk, fields in zip(chunks, field_rows):
        down = chunk[0:side]
        right = chunk[side : side + depth]
        wide = jnp.concatenate(fields, axis=1) if len(fields) > 1 else fields[0]
        part = lax.dot_general(down, wide, (((0,), (0,)), ((), ())), preferred_element_type=F32)
        part = part.astype(BF16)
        width = fields[0].shape[1]
        if len(fields) > 1:
            part = jnp.concatenate(
                [part[:, c * width : (c + 1) * width] for c in range(len(fields))], axis=0
            )
        piece = lax.dot_general(part, right, (((1,), (1,)), ((), ())), preferred_element_type=F32)
        piece = piece.astype(BF16).astype(F32)
        total = piece if total is None else total + piece
    return total


def tails_of(chunks, hops):
    at = min(c.shape[0] for c in chunks)
    return [hops[k // 2 - 1][...] if k > 1 and k % 2 else c[at:] for k, c in enumerate(chunks)]


def forcing_kernel(group, side, levels, subs, place, mass, drag, wind, early, *refs):
    chunks = refs[:group][::-1]
    hops, (out, current_o, push_o, store) = refs[group:-4], refs[-4:]
    size = mass.shape[0]
    depth = chunks[0].shape[1]
    tails = tails_of(chunks, hops)
    fields = [[t[0:side], t[side : 2 * side]] for t in tails]
    total = remap_forward(chunks, fields, side, depth)
    pushes = []
    for c in range(2):
        current = total[c * size : (c + 1) * size]
        current_o[c] = current
        force = wind[pl.ds(c, size, stride=2), :]
        push = mass[...] * (force + drag[...] * current)
        push_o[c] = push
        pushes.append(push)
    store[0:EARLY_ROWS] = early[0:EARLY_ROWS]
    put_side_rims(store, pushes, LATE_DEPTHS, lambda side: EARLY_ROWS + side * LATE_SIDE)
    tail = [t[2 * side :].astype(F32) for t in tails]
    line = iota((1, size), 1)
    names = jnp.zeros((1, size), F32)
    for k in range(group):
        names = jnp.where(line // 8 == k, roll(tail[k][2 * levels : 2 * levels + 1], 8 * k, 1), names)
    me, step = place(), group // subs
    left, right = (nearby(me, group, d * step, tail) for d in (-1, 1))
    extra = [names]
    for l in range(levels):
        near = slice(2 * l, 2 * l + 1)
        extra.append(jnp.where(line < side, left[near], right[near]))
    extra.append(early[EARLY_ROWS:])
    used = BLOCK_ROWS + 1 + 5 * levels
    store[BLOCK_ROWS:] = jnp.concatenate(
        extra + [jnp.zeros((store.shape[0] - used, size), F32)], axis=0
    )
    out[...] = store[...].astype(BF16)


def ocean_halos(counts, tile_place, member_place, shape, messages, tails):
    tiles, subs, levs = counts
    levels, rows, width = shape
    my_tile, me = tile_place(), member_place()
    halo = {}
    extras = [m[BLOCK_ROWS:] for m in messages]
    ends = [t[2 * rows :] for t in tails]
    for dt in (-1, 1):
        extra = nearby(my_tile, tiles, dt, extras)
        corners, strips = extra[1 : 1 + levels], extra[1 + levels : 1 + 5 * levels]
        halo[dt, 0] = strips[: 2 * levels] if dt < 0 else strips[2 * levels :]
        at = rows - 1 if dt < 0 else 0
        for ds in (-1, 1):
            lane_at = at if ds < 0 else rows + at
            halo[dt, ds] = corners[:, lane_at : lane_at + 1]
    for ds in (-1, 1):
        beside = nearby(me, subs * levs, ds * levs, ends)[: 2 * levels]
        halo[0, ds] = roll(beside, -rows, 1) if ds > 0 else beside
    return halo


def biharmonic(x, top, bottom, left, right, corner):
    rows, width = x.shape
    row, lane = iota(x.shape, 0), iota(x.shape, 1)
    line = iota((1, width), 1)

    def laplacian(x, top, bottom, left, right):
        up = jnp.where(row == 0, top, roll(x, 1, 0))
        down = jnp.where(row == rows - 1, bottom, roll(x, -1, 0))
        west = jnp.where(lane == 0, left, roll(x, 1, 1))
        east = jnp.where(lane == width - 1, right, roll(x, -1, 1))
        return up + down + west + east - 4.0 * x

    def ring_row(mid, out_row, in_row, dt):
        west = jnp.where(line == 0, corner[dt, -1], roll(mid, 1, 1))
        east = jnp.where(line == width - 1, corner[dt, 1], roll(mid, -1, 1))
        return west + east + out_row + in_row - 4.0 * mid

    def ring_col(mid, out_col, in_col, ds):
        up = jnp.concatenate([corner[-1, ds], mid[:-1]], axis=0)
        down = jnp.concatenate([mid[1:], corner[1, ds]], axis=0)
        return up + down + out_col + in_col - 4.0 * mid

    return laplacian(
        laplacian(x, top[0], bottom[0], left[0], right[0]),
        ring_row(*top, x[0:1], -1),
        ring_row(*bottom, x[rows - 1 :], 1),
        ring_col(*left, x[:, 0:1], -1),
        ring_col(*right, x[:, width - 1 :], 1),
    )


def split_refs(tiles, members, refs, outs):
    messages, chunks = refs[:tiles], refs[tiles : tiles + members]
    return messages, tails_of(chunks, refs[tiles + members : -outs]), refs[-outs:]


def relay_kernel(counts, tile_place, member_place, water, mixing, *refs):
    tiles, subs, levs = counts
    outs = 1 if levs == 1 else 2
    messages, tails, outs = split_refs(tiles, subs * levs, refs, outs)
    for k in range(tiles):
        outs[0][k * BLOCK_ROWS : (k + 1) * BLOCK_ROWS] = messages[k][0:BLOCK_ROWS]
    levels, rows, width = water.shape
    halo = ocean_halos(counts, tile_place, member_place, water.shape, messages, tails)

    def both(strip):
        near = sum(strip[2 * l : 2 * l + 1] for l in range(levels))
        far = sum(strip[2 * l + 1 : 2 * l + 2] for l in range(levels))
        return near, far

    def as_columns(strip):
        near, far = both(strip)
        across = jnp.concatenate([near, far] + [jnp.zeros_like(near)] * 6, axis=0).T
        return across[0:rows, 0:1], across[0:rows, 1:2]

    corner = {
        (dt, ds): jnp.sum(halo[dt, ds], axis=0, keepdims=True) for dt in (-1, 1) for ds in (-1, 1)
    }
    x = sum(water[l] for l in range(levels))
    twice = biharmonic(
        x, both(halo[-1, 0]), both(halo[1, 0]), as_columns(halo[0, -1]), as_columns(halo[0, 1]), corner
    )
    top = (x - mixing[...] * twice) / (levels * levs)
    if levs == 1:
        outs[0][tiles * BLOCK_ROWS :] = top.astype(BF16)
    else:
        outs[1][...] = top


def ocean_kernel(counts, tile_place, member_place, water, mixing, *refs):
    tiles, subs, levs = counts
    messages, tails, (warm_o,) = split_refs(tiles, subs * levs, refs, 1)
    levels, rows, width = water.shape
    halo = ocean_halos(counts, tile_place, member_place, water.shape, messages, tails)
    left, right = halo[0, -1].T, halo[0, 1].T
    for l in range(levels):
        x = water[l]
        pair = (2 * l, 2 * l + 1)
        twice = biharmonic(
            x,
            [halo[-1, 0][i : i + 1] for i in pair],
            [halo[1, 0][i : i + 1] for i in pair],
            [left[0:rows, i : i + 1] for i in pair],
            [right[0:rows, i : i + 1] for i in pair],
            {(dt, ds): halo[dt, ds][l : l + 1] for dt in (-1, 1) for ds in (-1, 1)},
        )
        warm_o[l] = x - mixing[...] * twice


def ice_kernel(
    tiles, members, side, table, viscous, gain, drag, conduct, current, speed, push, *refs
):
    chunks, relays = refs[:members], refs[members : 2 * members]
    out, own_o, beside_o, rims, names, named, field = refs[2 * members :]
    load_names = pltpu.make_async_copy(table, names, named)
    load_names.start()
    size = viscous.shape[0]
    depth = chunks[0].shape[1]
    warm = remap_forward(chunks, [[r[r.shape[0] - side :]] for r in relays], side, depth)
    heat = (conduct[...] * warm).astype(BF16)
    for k in range(tiles):
        for m in range(members):
            block = relays[m][k * BLOCK_ROWS : (k + 1) * BLOCK_ROWS]
            rims[k * members + m, 0:BLOCK_ROWS] = block.astype(F32)
            rims[k * members + m, BLOCK_ROWS:] = jnp.zeros((2 * DEPTH, size), F32)
    half = DEPTH
    high = 2 * DEPTH
    sub = iota((high, size), 0)
    lane = iota((high, size), 1)
    edge = (sub & (half - 1)) == 0
    turn = jnp.where(sub < half, CORIOLIS_TURN, -CORIOLIS_TURN).astype(F32)
    first, last = lane == 0, lane == size - 1

    def load(device, side, mask, with_push=True):
        start = side * EARLY_SIDE
        velocity = rims[device, start : start + high] * mask
        if not with_push:
            return velocity
        both = rims[device, start + high : start + 2 * high]
        visc = jnp.where(sub < half, both, roll(both, half, 0))
        scale = jnp.where(sub < half, roll(both, 1 - half, 0), roll(both, 1, 0)) * mask
        start = EARLY_ROWS + side * LATE_SIDE
        late = rims[device, start : start + high]
        pushed = jnp.where(sub < half, late, roll(late, 1, 0))
        return [velocity, visc, scale, pushed]

    def follow(device, side):
        name = names[device, side]
        return jnp.where(name >= 0, name, 0), name >= 0

    def step(state, left, right, inner, outer):
        c, visc, scale, pushed = state
        spread = left + right + inner + outer - 4.0 * c
        return scale * (c + visc * spread + pushed + turn * roll(c, half, 0))

    col = iota((size, size), 1)
    base = high
    for c in range(2):
        field[0, c, base : base + size] = speed[c]

    def own_edges(now):
        vx, vy = (field[now, c, base : base + size] for c in range(2))
        mixed = jnp.where(col < half, roll(vx, 1, 1), roll(vy, 1 + half, 1))
        across = mixed.T[0:high]
        return [
            jnp.where(sub < half, vx[size - 1 :], vy[size - 1 :]),
            jnp.where(sub < half, vx[0:1], vy[0:1]),
            across,
            roll(across, -1, 0),
        ]

    own = own_edges(0)
    load_names.wait()
    strips = []
    for q in range(4):
        x, has_x = follow(0, q)
        strip = load(x, OPPOSITE[q], flag(has_x))
        sides = []
        for s in LATERAL[q]:
            y, has_y = follow(x, s)
            z, has_z = follow(y, OPPOSITE[q])
            w, has_w = follow(z, OPPOSITE[s])
            sides.append(
                [
                    load(y, OPPOSITE[q], flag(has_y)),
                    load(z, q, flag(has_z)),
                    load(w, q, flag(has_w), with_push=False),
                ]
            )
        strips.append((strip, sides))

    for t in range(SUBCYCLES):
        cells = [strip[0] for strip, _ in strips]
        if t < SUBCYCLES - 1:
            if t > 0:
                own = own_edges(t % 2)
            for q in range(4):
                strip, (beyond, before) = strips[q]
                c, y_hi, y_lo = strip[0], beyond[0][0], before[0][0]
                left = jnp.where(first, roll(y_lo, 1, 1), roll(c, 1, 1))
                right = jnp.where(last, roll(y_hi, -1, 1), roll(c, -1, 1))
                inner = jnp.where(edge, own[q], roll(c, 1, 0))
                new_strip = step(strip, left, right, inner, roll(c, -1, 0))
                if t < SUBCYCLES - 2:
                    new_sides = []
                    for i, (y, z, w) in enumerate((beyond, before)):
                        away = 1 if i == 0 else -1
                        boundary = first if i == 0 else last
                        yc, zc = y[0], z[0]
                        toward = jnp.where(boundary, roll(c, away, 1), roll(yc, away, 1))
                        inner = jnp.where(edge, zc, roll(yc, 1, 0))
                        new_y = step(y, toward, roll(yc, -away, 1), inner, roll(yc, -1, 0))
                        new_z = zc
                        if t < SUBCYCLES - 3:
                            toward = jnp.where(boundary, roll(w, away, 1), roll(zc, away, 1))
                            inner = jnp.where(edge, yc, roll(zc, 1, 0))
                            new_z = step(z, toward, roll(zc, -away, 1), inner, roll(zc, -1, 0))
                        new_sides.append((new_y, new_z))
                    for item, (new_y, new_z) in zip((beyond, before), new_sides):
                        item[0][0] = new_y
                        item[1][0] = new_z
                strip[0] = new_strip
        now, later = t % 2, (t + 1) % 2
        sides = jnp.where(edge, cells[2], roll(cells[3], 1, 0)).T
        for c in range(2):
            at = c * half
            field[now, c, base + size : base + size + 1] = cells[0][at : at + 1]
            field[now, c, base - 1 : base] = cells[1][at : at + 1]
        for i in range(size // high):
            rows = slice(i * high, (i + 1) * high)
            held = [field[now, c, base + i * high : base + (i + 1) * high] for c in range(2)]
            for c in range(2):
                v, at = held[c], base + i * high
                up = field[now, c, at + 1 : at + 1 + high]
                down = field[now, c, at - 1 : at - 1 + high]
                east = jnp.where(last, sides[rows, c * half : c * half + 1], roll(v, -1, 1))
                west = jnp.where(first, sides[rows, c * half + 1 : c * half + 2], roll(v, 1, 1))
                spread = up + down + east + west - 4.0 * v
                turned = (CORIOLIS_TURN if c == 0 else -CORIOLIS_TURN) * held[1 - c]
                new = gain[rows] * (v + viscous[rows] * spread + push[c, rows] + turned)
                if t == SUBCYCLES - 1:
                    out[c, rows] = new
                else:
                    field[later, c, at : at + high] = new
    stress = [(drag[...] * (out[c] - current[c])).astype(BF16) for c in range(2)]
    return_fluxes([heat, *stress], chunks, side, depth, own_o, beside_o)


def return_fluxes(fluxes, chunks, side, depth, own, beside):
    size = fluxes[0].shape[0]
    wide = jnp.concatenate(fluxes, axis=1)
    step = 3 * side
    for k, chunk in enumerate(chunks):
        part = jnp.dot(chunk[0:side], wide, preferred_element_type=F32).astype(BF16)
        part = jnp.concatenate([part[:, c * size : (c + 1) * size] for c in range(3)], axis=0)
        reply = jnp.dot(part, chunk[side : side + depth], preferred_element_type=F32)
        at = k // 2 * step
        if k % 2:
            beside[at : at + step] = reply.astype(BF16)
        else:
            own[at : at + step] = reply


def pair_kernel(own, beside, *outs):
    step = outs[0].shape[0]
    for k, out in enumerate(outs):
        at = (k + 1) * step
        out[...] = (own[at : at + step] + beside[at : at + step].astype(F32)).astype(BF16)


def finish_kernel(warm, currents, speed, own, beside, *refs):
    outs, (flat, heat_v, current_v, left) = refs[-7:-4], refs[-4:]
    replies = refs[:-7]
    flat_o, heat_o, current_o = outs
    size = speed.shape[1]
    copies = [
        pltpu.make_async_copy(source, target, left.at[i])
        for i, (source, target) in enumerate(
            ((flat, flat_o), (heat_v, heat_o), (current_v, current_o))
        )
    ]
    for c in range(2):
        flat[pl.ds(c, size, stride=2), :] = speed[c]
    copies[0].start()
    side = currents.shape[1]
    total = own[0 : 3 * side] + beside[0 : 3 * side].astype(F32)
    for reply in replies:
        total = total + reply[...].astype(F32)
    heat = THERMAL_DIFFUSE * total[0:side]
    for l in range(warm.shape[0]):
        heat_v[l] = warm[l] + heat
    copies[1].start()
    for c in range(2):
        current_v[c] = currents[c] + STRESS_MIXING * total[(c + 1) * side : (c + 2) * side]
    copies[2].start()
    for copy in copies:
        copy.wait()


def shards(
    water_heat_state,
    diffusion_coefficient,
    upper_current_vector,
    remap_blocks,
    remap_rows,
    remap_cols,
    neighbors,
    thickness,
    concentration,
    ice_velocity,
    wind_stress,
):
    tile_count, sub_count, lev_count = (lax.axis_size(a) for a in ("tile", "sub", "lev"))
    group = sub_count * lev_count
    devices = tile_count * group
    group_axes = ("sub", "lev")
    member_axes = ("tile", "sub", "lev")
    levels, side, width = water_heat_state.shape
    pairs, size = remap_rows.shape[1:3]
    categories = thickness.shape[2]

    def tile_place():
        return lax.axis_index("tile")

    def member_place():
        return lax.axis_index("sub") * lev_count + lax.axis_index("lev")

    def device_place():
        return lax.axis_index("tile") * group + member_place()

    def swap(value, axes, count):
        got = {0: value}
        for k in range(1, count):
            got[k] = lax.ppermute(value, axes, [(i, i ^ k) for i in range(count)])
        return [got[k] for k in range(count)]

    def swap_chips(value):
        return {0: value} | {
            k: lax.ppermute(value, group_axes, [(i, i ^ k) for i in range(group)])
            for k in range(2, group, 2)
        }

    def swap_cores(got):
        beside = [(i, i ^ 1) for i in range(group)]
        got = got | {k + 1: lax.ppermute(got[k], group_axes, beside) for k in got}
        return [got[k] for k in range(group)]

    def swap_each(values):
        got = {0: values[0]}
        for k in range(1, group):
            got[k] = lax.ppermute(values[k], group_axes, [(i, i ^ k) for i in range(group)])
        return [got[k] for k in range(group)]

    def shape(*dims, dtype=F32):
        return jax.ShapeDtypeStruct(dims, dtype)

    def interleaved(value):
        return value.reshape(2, size, size).transpose(1, 0, 2).reshape(2 * size, size)

    plane = shape(size, size)
    planes = shape(2, size, size)
    wind = interleaved(wind_stress)

    tail_rows = -(-(2 * levels + 1) // TILE_ROWS) * TILE_ROWS
    pair_rows = side + width
    chunk_rows = pair_rows + 2 * side + tail_rows
    sent = call(
        functools.partial(forward_kernel, (devices, group, member_place)),
        [
            shape(pair_rows if k > 1 and k % 2 else chunk_rows, width, dtype=BF16)
            for k in range(group)
        ],
        (
            neighbors,
            remap_blocks,
            remap_rows[0].swapaxes(1, 2),
            remap_cols[0],
            upper_current_vector,
            water_heat_state,
        ),
        scratch=[
            pltpu.SMEM(neighbors.shape, jnp.int32),
            pltpu.SMEM((1, pairs), jnp.int32),
            pltpu.VMEM((2, side, width), F32),
            pltpu.VMEM((pairs, pair_rows, width), BF16),
            pltpu.VMEM((levels, side, width), F32),
            pltpu.VMEM((chunk_rows - pair_rows, width), BF16),
            pltpu.VMEM((1 if pairs == group else group, pair_rows, width), BF16),
            pltpu.SemaphoreType.DMA((6,)),
            pltpu.SemaphoreType.DMA((2 * group,)),
        ],
        hbm=(0, 1, 2, 3, 4, 5),
        grant=60 * 2**20,
        micros=10,
    )
    chunks = swap_each(sent)
    hops = [
        lax.ppermute(chunks[k][pair_rows:], group_axes, [(i, i ^ 1) for i in range(group)])
        for k in range(2, group, 2)
    ]

    early, viscous, gain, step_mass, drag, conduct, speed = call(
        rims_kernel,
        [shape(EARLY_ROWS + 4 * levels, size)] + [plane] * 5 + [planes],
        (
            thickness.reshape(categories, size, size),
            concentration.reshape(categories, size, size),
            interleaved(ice_velocity),
            water_heat_state,
        ),
    )
    extra_rows = -(-(1 + 5 * levels) // TILE_ROWS) * TILE_ROWS
    message, current_ice, push = call(
        functools.partial(forcing_kernel, group, side, levels, sub_count, member_place),
        [shape(BLOCK_ROWS + extra_rows, size, dtype=BF16), planes, planes],
        (step_mass, drag, wind, early, *chunks[::-1], *hops),
        scratch=[pltpu.VMEM((BLOCK_ROWS + extra_rows, size), F32)],
    )
    messages = swap(message, "tile", tile_count)

    counts = (tile_count, sub_count, lev_count)
    ocean = (*messages, *chunks, *hops)
    relay_rows = tile_count * BLOCK_ROWS
    relay_shapes = [shape(relay_rows + (side if lev_count == 1 else 0), size, dtype=BF16)]
    if lev_count > 1:
        relay_shapes.append(shape(side, width))
    relay, *top = call(
        functools.partial(relay_kernel, counts, tile_place, member_place),
        relay_shapes,
        (water_heat_state, diffusion_coefficient, *ocean),
    )
    if lev_count > 1:
        relay = jnp.concatenate([relay, lax.psum(top[0], "lev").astype(BF16)], axis=0)
    relays = swap_chips(relay)

    mixing, _ = lax.optimization_barrier((diffusion_coefficient, relay))
    (warm,) = call(
        functools.partial(ocean_kernel, counts, tile_place, member_place),
        [shape(levels, side, width)],
        (water_heat_state, mixing, *ocean),
    )
    far = sorted(k for k in relays if k)
    relayed, _ = lax.optimization_barrier(([relays[k] for k in far], warm))
    relays = swap_cores({0: relay} | dict(zip(far, relayed)))

    names = jnp.stack([m[BLOCK_ROWS, : 8 * group] for m in messages])
    names = names.reshape(devices, 8).astype(jnp.int32)
    table = names[:, 0:4] * 128 + names[:, 4:8]
    table = jnp.where(table < 0, -1, table ^ device_place())
    step = 3 * side
    speed, own, beside = call(
        functools.partial(ice_kernel, tile_count, group, side),
        [
            planes,
            shape(group // 2 * step, width),
            shape(group // 2 * step, width, dtype=BF16),
        ],
        (table, viscous, gain, drag, conduct, current_ice, speed, push, *chunks, *relays),
        scratch=[
            pltpu.VMEM((devices, BLOCK_ROWS + 2 * DEPTH, size), F32),
            pltpu.SMEM((devices, 4), jnp.int32),
            pltpu.SemaphoreType.DMA,
            pltpu.VMEM((2, 2, size + 4 * DEPTH, size), F32),
        ],
        hbm=(0,),
    )
    beside = lax.ppermute(beside, group_axes, [(i, i ^ 1) for i in range(group)])
    paired = call(
        pair_kernel, [shape(step, width, dtype=BF16)] * (group // 2 - 1), (own, beside)
    )
    replies = [
        lax.ppermute(value, group_axes, [(i, i ^ (2 * k + 2)) for i in range(group)])
        for k, value in enumerate(paired)
    ]
    if lev_count > 1:
        parts = [r.astype(F32) for r in (own[:step], beside[:step], *replies)]
        own, beside, replies = lax.psum(sum(parts), "lev"), jnp.zeros_like(beside[:step]), []
    flat, heat, current = call(
        finish_kernel,
        [shape(2 * size, size), shape(levels, side, width), shape(2, side, width)],
        (warm, upper_current_vector, speed, own, beside, *replies),
        scratch=[
            pltpu.VMEM((2 * size, size), F32),
            pltpu.VMEM((levels, side, width), F32),
            pltpu.VMEM((2, side, width), F32),
            pltpu.SemaphoreType.DMA((3,)),
        ],
        out_space=pltpu.HBM,
    )
    velocity = flat.reshape(size, 2, size).transpose(1, 0, 2).reshape(1, 1, 2, size * size)
    return heat, current, velocity


def solution(mesh):
    member = ("tile", "sub", "lev")
    whole = ("copies",) + member
    ice = P(None, whole, None, None)
    water = P("lev", ("copies", "tile"), "sub")
    current = P(None, ("copies", "tile"), "sub")
    return jax.shard_map(
        shards,
        mesh=mesh,
        in_specs=(
            water,
            P("tile", "sub"),
            current,
            P(member, None),
            P(member, None, None, None),
            P(member, None, None, None),
            P(None, member, None),
            ice,
            ice,
            ice,
            ice,
        ),
        out_specs=(water, current, ice),
        check_vma=False,
    )
```

```python
import functools

import jax
import jax.numpy as jnp
from jax import lax
from jax.experimental import pallas as pl
from jax.experimental.pallas import tpu as pltpu
from jax.sharding import PartitionSpec as P

SUBCYCLES = 4
STRENGTH_DECAY = 5.0
VISCOUS_STEP = 0.24
SUBCYCLE_STEP = 0.5
CORIOLIS_TURN = 0.1
BASE_MASS = 0.5
HEAT_RATE = 0.2
THIN_ICE = 0.1
THERMAL_DIFFUSE = 0.5
STRESS_MIXING = 0.5

OPPOSITE = (1, 0, 3, 2)
LATERAL = ((2, 3), (2, 3), (0, 1), (0, 1))
DEPTH = SUBCYCLES
EARLY_DEPTHS = (DEPTH, DEPTH, DEPTH - 1, DEPTH - 1)
LATE_DEPTHS = (DEPTH - 1, DEPTH - 1)
EARLY_SIDE, LATE_SIDE = sum(EARLY_DEPTHS), sum(LATE_DEPTHS)
EARLY_ROWS = 4 * EARLY_SIDE
BLOCK_ROWS = EARLY_ROWS + 4 * LATE_SIDE
TILE_ROWS = 16
F32 = jnp.float32
BF16 = jnp.bfloat16
VMEM_LIMIT = 16 * 1024 * 1024
FLOPS_PER_MICRO = 1.15e9


def call(kernel, outs, args, scratch=(), smem=(), hbm=(), out_space=pltpu.VMEM, grant=VMEM_LIMIT, micros=0.01):
    def space(i):
        return pltpu.SMEM if i in smem else pltpu.HBM if i in hbm else pltpu.VMEM

    specs = [pl.BlockSpec(memory_space=space(i)) for i in range(len(args))]
    size = sum(a.size * a.dtype.itemsize for a in args)
    return pl.pallas_call(
        kernel,
        out_shape=outs,
        in_specs=specs,
        out_specs=jax.tree.map(lambda _: pl.BlockSpec(memory_space=out_space), outs),
        scratch_shapes=list(scratch),
        compiler_params=pltpu.CompilerParams(vmem_limit_bytes=grant),
        cost_estimate=pl.CostEstimate(
            flops=int(micros * FLOPS_PER_MICRO), bytes_accessed=size, transcendentals=0
        ),
    )(*args)


def iota(shape, axis):
    return lax.broadcasted_iota(jnp.int32, shape, axis)


def roll(x, shift, axis):
    return pltpu.roll(x, shift % x.shape[axis], axis)


def flag(condition):
    return jnp.where(condition, 1.0, 0.0).astype(F32)


def ocean_columns(water):
    levels, rows, width = water.shape
    lane = iota((rows, width), 1)
    line = iota((1, width), 1)
    mixed = jnp.zeros((rows, width), F32)
    for l in range(levels):
        mixed = jnp.where(lane // 4 == l, roll(water[l], 2 + 4 * l, 1), mixed)
    across = jnp.concatenate([mixed, jnp.zeros((width - rows, width), F32)], axis=0).T
    beside = []
    for l in range(levels):
        for j in range(2):
            last = across[4 * l + 1 - j : 4 * l + 2 - j]
            lead = across[4 * l + 2 + j : 4 * l + 3 + j]
            beside.append(jnp.where(line < rows, last, roll(lead, rows, 1)))
    return beside


def forward_kernel(group, links_h, blocks_h, rows_h, cols_h, currents_h, water_h, *refs):
    devices, members, place = group
    outs, scratch = refs[:members], refs[members:]
    links, blocks, currents, weights, water, fields, kept, arrived, left = scratch
    pairs, side, width = rows_h.shape
    both = weights.shape[1]
    loads = [
        pltpu.make_async_copy(source, target, arrived.at[i])
        for i, (source, target) in enumerate(
            (
                (links_h, links),
                (blocks_h, blocks),
                (currents_h, currents),
                (rows_h, weights.at[:, pl.ds(0, side)]),
                (cols_h, weights.at[:, pl.ds(side, both - side)]),
                (water_h, water),
            )
        )
    ]
    for load in loads:
        load.start()
    for i in (1, 3, 4):
        loads[i].wait()
    me = place()
    owners = [lax.rem(lax.rem(blocks[0, m], devices), members) for m in range(pairs)]
    copies = []
    for k, out in enumerate(outs):
        partner = me ^ k
        pair = jnp.int32(0)
        for m in range(pairs):
            pair = jnp.where(owners[m] == partner, m, pair)
        source = weights.at[pair]
        if pairs < members:
            found = sum(flag(owners[m] == partner) for m in range(pairs))
            kept[k] = (weights[pair].astype(F32) * found).astype(BF16)
            source = kept.at[k]
        copies.append(pltpu.make_async_copy(source, out.at[pl.ds(0, both)], left.at[2 * k]))
        copies[-1].start()
    for i in (0, 2, 5):
        loads[i].wait()
    for c in range(2):
        fields[c * side : (c + 1) * side] = currents[c].astype(BF16)
    lane = iota((1, width), 1)
    numbers = jnp.zeros((1, width), F32)
    for q in range(4):
        numbers = jnp.where(lane == q, (links[0, 0, q] >> 7).astype(F32), numbers)
        numbers = jnp.where(lane == 4 + q, (links[0, 0, q] & 127).astype(F32), numbers)
    ends = ocean_columns(water) + [numbers]
    blank = jnp.zeros((fields.shape[0] - 2 * side - len(ends), width), F32)
    fields[2 * side :] = jnp.concatenate(ends + [blank], axis=0).astype(BF16)
    for k, out in enumerate(outs):
        if out.shape[0] > both:
            target = out.at[pl.ds(both, fields.shape[0])]
            copies.append(pltpu.make_async_copy(fields, target, left.at[2 * k + 1]))
            copies[-1].start()
    for copy in copies:
        copy.wait()


def put_side_rims(store, planes, depths, at):
    size = planes[0].shape[0]
    lane = iota((size, size), 1)
    mixed = jnp.zeros((size, size), F32)
    for i, plane in enumerate(planes):
        turned = roll(plane, DEPTH + 2 * DEPTH * i, 1)
        mixed = jnp.where(lane // (2 * DEPTH) == i, turned, mixed)
    across = mixed.T
    base = 0
    for i, plane in enumerate(planes):
        for k in range(depths[i]):
            east = 2 * DEPTH * i + DEPTH - 1 - k
            west = 2 * DEPTH * i + DEPTH + k
            store[at(0) + base : at(0) + base + 1] = plane[size - 1 - k : size - k]
            store[at(1) + base : at(1) + base + 1] = plane[k : k + 1]
            store[at(2) + base : at(2) + base + 1] = across[east : east + 1]
            store[at(3) + base : at(3) + base + 1] = across[west : west + 1]
            base += 1


def rims_kernel(
    thick, conc, ice, water, out, viscous_o, gain_o, mass_o, drag_o, conduct_o,
    speed_o,
):
    size = thick.shape[1]
    cover = jnp.zeros((size, size), F32)
    volume = jnp.zeros((size, size), F32)
    conduct = jnp.zeros((size, size), F32)
    for c in range(thick.shape[0]):
        h, a = thick[c], conc[c]
        cover = cover + a
        volume = volume + a * h
        conduct = conduct + a / (h + THIN_ICE)
    mass = volume + BASE_MASS
    viscous = VISCOUS_STEP * (volume * jnp.exp(-STRENGTH_DECAY * (1.0 - cover))) / mass
    step_mass = SUBCYCLE_STEP / mass
    gain = 1.0 / (1.0 + step_mass * cover)
    speed_x = ice[pl.ds(0, size, stride=2), :]
    speed_y = ice[pl.ds(1, size, stride=2), :]
    viscous_o[...] = viscous
    gain_o[...] = gain
    mass_o[...] = step_mass
    drag_o[...] = cover
    conduct_o[...] = -HEAT_RATE * conduct
    speed_o[0] = speed_x
    speed_o[1] = speed_y
    put_side_rims(
        out, [speed_x, speed_y, viscous, gain], EARLY_DEPTHS, lambda side: side * EARLY_SIDE
    )
    levels, rows, width = water.shape
    for l in range(levels):
        for j in range(2):
            at = EARLY_ROWS + 2 * l + j
            out[at : at + 1] = water[l, rows - 1 - j : rows - j]
            out[at + 2 * levels : at + 2 * levels + 1] = water[l, j : j + 1]


def nearby(me, members, distance, arrays):
    at = me + distance
    inside = (at >= 0) & (at < members)
    found = 0.0
    for k in range(1, members):
        found = found + arrays[k].astype(F32) * flag(inside & ((me ^ k) == at))
    return found


def remap_forward(chunks, field_rows, side, depth):
    total = None
    for chunk, fields in zip(chunks, field_rows):
        down = chunk[0:side]
        right = chunk[side : side + depth]
        wide = jnp.concatenate(fields, axis=1) if len(fields) > 1 else fields[0]
        part = lax.dot_general(down, wide, (((0,), (0,)), ((), ())), preferred_element_type=F32)
        part = part.astype(BF16)
        width = fields[0].shape[1]
        if len(fields) > 1:
            part = jnp.concatenate(
                [part[:, c * width : (c + 1) * width] for c in range(len(fields))], axis=0
            )
        piece = lax.dot_general(part, right, (((1,), (1,)), ((), ())), preferred_element_type=F32)
        piece = piece.astype(BF16).astype(F32)
        total = piece if total is None else total + piece
    return total


def tails_of(chunks, hops):
    at = min(c.shape[0] for c in chunks)
    return [hops[k // 2 - 1][...] if k > 1 and k % 2 else c[at:] for k, c in enumerate(chunks)]


def forcing_kernel(group, side, levels, subs, place, mass, drag, wind, early, *refs):
    chunks = refs[:group][::-1]
    hops, (out, current_o, push_o, store) = refs[group:-4], refs[-4:]
    size = mass.shape[0]
    depth = chunks[0].shape[1]
    tails = tails_of(chunks, hops)
    fields = [[t[0:side], t[side : 2 * side]] for t in tails]
    total = remap_forward(chunks, fields, side, depth)
    pushes = []
    for c in range(2):
        current = total[c * size : (c + 1) * size]
        current_o[c] = current
        force = wind[pl.ds(c, size, stride=2), :]
        push = mass[...] * (force + drag[...] * current)
        push_o[c] = push
        pushes.append(push)
    store[0:EARLY_ROWS] = early[0:EARLY_ROWS]
    put_side_rims(store, pushes, LATE_DEPTHS, lambda side: EARLY_ROWS + side * LATE_SIDE)
    tail = [t[2 * side :].astype(F32) for t in tails]
    line = iota((1, size), 1)
    names = jnp.zeros((1, size), F32)
    for k in range(group):
        names = jnp.where(line // 8 == k, roll(tail[k][2 * levels : 2 * levels + 1], 8 * k, 1), names)
    me, step = place(), group // subs
    left, right = (nearby(me, group, d * step, tail) for d in (-1, 1))
    extra = [names]
    for l in range(levels):
        near = slice(2 * l, 2 * l + 1)
        extra.append(jnp.where(line < side, left[near], right[near]))
    extra.append(early[EARLY_ROWS:])
    used = BLOCK_ROWS + 1 + 5 * levels
    store[BLOCK_ROWS:] = jnp.concatenate(
        extra + [jnp.zeros((store.shape[0] - used, size), F32)], axis=0
    )
    out[...] = store[...].astype(BF16)


def ocean_halos(counts, tile_place, member_place, shape, messages, tails):
    tiles, subs, levs = counts
    levels, rows, width = shape
    my_tile, me = tile_place(), member_place()
    halo = {}
    extras = [m[BLOCK_ROWS:] for m in messages]
    ends = [t[2 * rows :] for t in tails]
    for dt in (-1, 1):
        extra = nearby(my_tile, tiles, dt, extras)
        corners, strips = extra[1 : 1 + levels], extra[1 + levels : 1 + 5 * levels]
        halo[dt, 0] = strips[: 2 * levels] if dt < 0 else strips[2 * levels :]
        at = rows - 1 if dt < 0 else 0
        for ds in (-1, 1):
            lane_at = at if ds < 0 else rows + at
            halo[dt, ds] = corners[:, lane_at : lane_at + 1]
    for ds in (-1, 1):
        beside = nearby(me, subs * levs, ds * levs, ends)[: 2 * levels]
        halo[0, ds] = roll(beside, -rows, 1) if ds > 0 else beside
    return halo


def biharmonic(x, top, bottom, left, right, corner):
    rows, width = x.shape
    row, lane = iota(x.shape, 0), iota(x.shape, 1)
    line = iota((1, width), 1)

    def laplacian(x, top, bottom, left, right):
        up = jnp.where(row == 0, top, roll(x, 1, 0))
        down = jnp.where(row == rows - 1, bottom, roll(x, -1, 0))
        west = jnp.where(lane == 0, left, roll(x, 1, 1))
        east = jnp.where(lane == width - 1, right, roll(x, -1, 1))
        return up + down + west + east - 4.0 * x

    def ring_row(mid, out_row, in_row, dt):
        west = jnp.where(line == 0, corner[dt, -1], roll(mid, 1, 1))
        east = jnp.where(line == width - 1, corner[dt, 1], roll(mid, -1, 1))
        return west + east + out_row + in_row - 4.0 * mid

    def ring_col(mid, out_col, in_col, ds):
        up = jnp.concatenate([corner[-1, ds], mid[:-1]], axis=0)
        down = jnp.concatenate([mid[1:], corner[1, ds]], axis=0)
        return up + down + out_col + in_col - 4.0 * mid

    return laplacian(
        laplacian(x, top[0], bottom[0], left[0], right[0]),
        ring_row(*top, x[0:1], -1),
        ring_row(*bottom, x[rows - 1 :], 1),
        ring_col(*left, x[:, 0:1], -1),
        ring_col(*right, x[:, width - 1 :], 1),
    )


def spread_out(count):
    return sorted(range(count), key=lambda k: (k == count // 2, k))


def split_refs(tiles, members, refs, outs):
    messages = [refs[spread_out(tiles).index(k)] for k in range(tiles)]
    chunks = refs[tiles : tiles + members]
    return messages, tails_of(chunks, refs[tiles + members : -outs]), refs[-outs:]


def relay_kernel(counts, tile_place, member_place, water, mixing, *refs):
    tiles, subs, levs = counts
    outs = 1 if levs == 1 else 2
    messages, tails, outs = split_refs(tiles, subs * levs, refs, outs)
    for k in range(tiles):
        outs[0][k * BLOCK_ROWS : (k + 1) * BLOCK_ROWS] = messages[k][0:BLOCK_ROWS]
    levels, rows, width = water.shape
    halo = ocean_halos(counts, tile_place, member_place, water.shape, messages, tails)

    def both(strip):
        near = sum(strip[2 * l : 2 * l + 1] for l in range(levels))
        far = sum(strip[2 * l + 1 : 2 * l + 2] for l in range(levels))
        return near, far

    def as_columns(strip):
        near, far = both(strip)
        across = jnp.concatenate([near, far] + [jnp.zeros_like(near)] * 6, axis=0).T
        return across[0:rows, 0:1], across[0:rows, 1:2]

    corner = {
        (dt, ds): jnp.sum(halo[dt, ds], axis=0, keepdims=True) for dt in (-1, 1) for ds in (-1, 1)
    }
    x = sum(water[l] for l in range(levels))
    twice = biharmonic(
        x, both(halo[-1, 0]), both(halo[1, 0]), as_columns(halo[0, -1]), as_columns(halo[0, 1]), corner
    )
    top = (x - mixing[...] * twice) / (levels * levs)
    if levs == 1:
        outs[0][tiles * BLOCK_ROWS :] = top.astype(BF16)
    else:
        outs[1][...] = top


def ocean_kernel(counts, tile_place, member_place, water, mixing, *refs):
    tiles, subs, levs = counts
    messages, tails, (warm_o,) = split_refs(tiles, subs * levs, refs, 1)
    levels, rows, width = water.shape
    halo = ocean_halos(counts, tile_place, member_place, water.shape, messages, tails)
    left, right = halo[0, -1].T, halo[0, 1].T
    for l in range(levels):
        x = water[l]
        pair = (2 * l, 2 * l + 1)
        twice = biharmonic(
            x,
            [halo[-1, 0][i : i + 1] for i in pair],
            [halo[1, 0][i : i + 1] for i in pair],
            [left[0:rows, i : i + 1] for i in pair],
            [right[0:rows, i : i + 1] for i in pair],
            {(dt, ds): halo[dt, ds][l : l + 1] for dt in (-1, 1) for ds in (-1, 1)},
        )
        warm_o[l] = x - mixing[...] * twice


def ice_kernel(
    tiles, members, side, table, viscous, gain, drag, conduct, current, speed, push, *refs
):
    chunks, relays = refs[:members], refs[members : 2 * members]
    out, own_o, beside_o, rims, names, named, field = refs[2 * members :]
    load_names = pltpu.make_async_copy(table, names, named)
    load_names.start()
    size = viscous.shape[0]
    depth = chunks[0].shape[1]
    for k in range(tiles):
        for m in range(members):
            block = relays[m][k * BLOCK_ROWS : (k + 1) * BLOCK_ROWS]
            rims[k * members + m, 0:BLOCK_ROWS] = block.astype(F32)
            rims[k * members + m, BLOCK_ROWS:] = jnp.zeros((2 * DEPTH, size), F32)
    half = DEPTH
    high = 2 * DEPTH
    sub = iota((high, size), 0)
    lane = iota((high, size), 1)
    edge = (sub & (half - 1)) == 0
    turn = jnp.where(sub < half, CORIOLIS_TURN, -CORIOLIS_TURN).astype(F32)
    first, last = lane == 0, lane == size - 1

    def load(device, side, mask, with_push=True):
        start = side * EARLY_SIDE
        velocity = rims[device, start : start + high] * mask
        if not with_push:
            return velocity
        both = rims[device, start + high : start + 2 * high]
        visc = jnp.where(sub < half, both, roll(both, half, 0))
        scale = jnp.where(sub < half, roll(both, 1 - half, 0), roll(both, 1, 0)) * mask
        start = EARLY_ROWS + side * LATE_SIDE
        late = rims[device, start : start + high]
        pushed = jnp.where(sub < half, late, roll(late, 1, 0))
        return [velocity, visc, scale, pushed]

    def follow(device, side):
        name = names[device, side]
        return jnp.where(name >= 0, name, 0), name >= 0

    def step(state, left, right, inner, outer):
        c, visc, scale, pushed = state
        spread = left + right + inner + outer - 4.0 * c
        return scale * (c + visc * spread + pushed + turn * roll(c, half, 0))

    col = iota((size, size), 1)
    base = high
    for c in range(2):
        field[0, c, base : base + size] = speed[c]

    def own_edges(now):
        vx, vy = (field[now, c, base : base + size] for c in range(2))
        mixed = jnp.where(col < half, roll(vx, 1, 1), roll(vy, 1 + half, 1))
        across = mixed.T[0:high]
        return [
            jnp.where(sub < half, vx[size - 1 :], vy[size - 1 :]),
            jnp.where(sub < half, vx[0:1], vy[0:1]),
            across,
            roll(across, -1, 0),
        ]

    own = own_edges(0)
    load_names.wait()
    strips = []
    for q in range(4):
        x, has_x = follow(0, q)
        strip = load(x, OPPOSITE[q], flag(has_x))
        sides = []
        for s in LATERAL[q]:
            y, has_y = follow(x, s)
            z, has_z = follow(y, OPPOSITE[q])
            w, has_w = follow(z, OPPOSITE[s])
            sides.append(
                [
                    load(y, OPPOSITE[q], flag(has_y)),
                    load(z, q, flag(has_z)),
                    load(w, q, flag(has_w), with_push=False),
                ]
            )
        strips.append((strip, sides))

    warm = remap_forward(chunks, [[r[r.shape[0] - side :]] for r in relays], side, depth)
    heat = (conduct[...] * warm).astype(BF16)

    for t in range(SUBCYCLES):
        cells = [strip[0] for strip, _ in strips]
        if t < SUBCYCLES - 1:
            if t > 0:
                own = own_edges(t % 2)
            for q in range(4):
                strip, (beyond, before) = strips[q]
                c, y_hi, y_lo = strip[0], beyond[0][0], before[0][0]
                left = jnp.where(first, roll(y_lo, 1, 1), roll(c, 1, 1))
                right = jnp.where(last, roll(y_hi, -1, 1), roll(c, -1, 1))
                inner = jnp.where(edge, own[q], roll(c, 1, 0))
                new_strip = step(strip, left, right, inner, roll(c, -1, 0))
                if t < SUBCYCLES - 2:
                    new_sides = []
                    for i, (y, z, w) in enumerate((beyond, before)):
                        away = 1 if i == 0 else -1
                        boundary = first if i == 0 else last
                        yc, zc = y[0], z[0]
                        toward = jnp.where(boundary, roll(c, away, 1), roll(yc, away, 1))
                        inner = jnp.where(edge, zc, roll(yc, 1, 0))
                        new_y = step(y, toward, roll(yc, -away, 1), inner, roll(yc, -1, 0))
                        new_z = zc
                        if t < SUBCYCLES - 3:
                            toward = jnp.where(boundary, roll(w, away, 1), roll(zc, away, 1))
                            inner = jnp.where(edge, yc, roll(zc, 1, 0))
                            new_z = step(z, toward, roll(zc, -away, 1), inner, roll(zc, -1, 0))
                        new_sides.append((new_y, new_z))
                    for item, (new_y, new_z) in zip((beyond, before), new_sides):
                        item[0][0] = new_y
                        item[1][0] = new_z
                strip[0] = new_strip
        now, later = t % 2, (t + 1) % 2
        sides = jnp.where(edge, cells[2], roll(cells[3], 1, 0)).T
        for c in range(2):
            at = c * half
            field[now, c, base + size : base + size + 1] = cells[0][at : at + 1]
            field[now, c, base - 1 : base] = cells[1][at : at + 1]
        for i in range(size // high):
            rows = slice(i * high, (i + 1) * high)
            held = [field[now, c, base + i * high : base + (i + 1) * high] for c in range(2)]
            for c in range(2):
                v, at = held[c], base + i * high
                up = field[now, c, at + 1 : at + 1 + high]
                down = field[now, c, at - 1 : at - 1 + high]
                east = jnp.where(last, sides[rows, c * half : c * half + 1], roll(v, -1, 1))
                west = jnp.where(first, sides[rows, c * half + 1 : c * half + 2], roll(v, 1, 1))
                spread = up + down + east + west - 4.0 * v
                turned = (CORIOLIS_TURN if c == 0 else -CORIOLIS_TURN) * held[1 - c]
                new = gain[rows] * (v + viscous[rows] * spread + push[c, rows] + turned)
                if t == SUBCYCLES - 1:
                    out[c, rows] = new
                else:
                    field[later, c, at : at + high] = new
    stress = [(drag[...] * (out[c] - current[c])).astype(BF16) for c in range(2)]
    return_fluxes([heat, *stress], chunks, side, depth, own_o, beside_o)


def return_fluxes(fluxes, chunks, side, depth, own, beside):
    size = fluxes[0].shape[0]
    wide = jnp.concatenate(fluxes, axis=1)
    step = 3 * side
    for k, chunk in enumerate(chunks):
        part = jnp.dot(chunk[0:side], wide, preferred_element_type=F32).astype(BF16)
        part = jnp.concatenate([part[:, c * size : (c + 1) * size] for c in range(3)], axis=0)
        reply = jnp.dot(part, chunk[side : side + depth], preferred_element_type=F32)
        at = k // 2 * step
        if k % 2:
            beside[at : at + step] = reply.astype(BF16)
        else:
            own[at : at + step] = reply


def pair_kernel(own, beside, *outs):
    step = outs[0].shape[0]
    for k, out in enumerate(outs):
        at = (k + 1) * step
        out[...] = (own[at : at + step] + beside[at : at + step].astype(F32)).astype(BF16)


def finish_kernel(warm, currents, speed, own, beside, *refs):
    outs, (flat, heat_v, current_v, left) = refs[-7:-4], refs[-4:]
    replies = refs[:-7]
    flat_o, heat_o, current_o = outs
    size = speed.shape[1]
    copies = [
        pltpu.make_async_copy(source, target, left.at[i])
        for i, (source, target) in enumerate(
            ((flat, flat_o), (heat_v, heat_o), (current_v, current_o))
        )
    ]
    for c in range(2):
        flat[pl.ds(c, size, stride=2), :] = speed[c]
    copies[0].start()
    side = currents.shape[1]
    total = own[0 : 3 * side] + beside[0 : 3 * side].astype(F32)
    for reply in replies:
        total = total + reply[...].astype(F32)
    heat = THERMAL_DIFFUSE * total[0:side]
    for l in range(warm.shape[0]):
        heat_v[l] = warm[l] + heat
    copies[1].start()
    for c in range(2):
        current_v[c] = currents[c] + STRESS_MIXING * total[(c + 1) * side : (c + 2) * side]
    copies[2].start()
    for copy in copies:
        copy.wait()


def shards(
    water_heat_state,
    diffusion_coefficient,
    upper_current_vector,
    remap_blocks,
    remap_rows,
    remap_cols,
    neighbors,
    thickness,
    concentration,
    ice_velocity,
    wind_stress,
):
    tile_count, sub_count, lev_count = (lax.axis_size(a) for a in ("tile", "sub", "lev"))
    group = sub_count * lev_count
    devices = tile_count * group
    group_axes = ("sub", "lev")
    member_axes = ("tile", "sub", "lev")
    levels, side, width = water_heat_state.shape
    pairs, size = remap_rows.shape[1:3]
    categories = thickness.shape[2]

    def tile_place():
        return lax.axis_index("tile")

    def member_place():
        return lax.axis_index("sub") * lev_count + lax.axis_index("lev")

    def device_place():
        return lax.axis_index("tile") * group + member_place()

    def swap(value, axes, count):
        got = {0: value}
        for k in range(1, count):
            got[k] = lax.ppermute(value, axes, [(i, i ^ k) for i in range(count)])
        return [got[k] for k in range(count)]

    def swap_chips(value):
        return {0: value} | {
            k: lax.ppermute(value, group_axes, [(i, i ^ k) for i in range(group)])
            for k in range(2, group, 2)
        }

    def swap_cores(got):
        beside = [(i, i ^ 1) for i in range(group)]
        got = got | {k + 1: lax.ppermute(got[k], group_axes, beside) for k in got}
        return [got[k] for k in range(group)]

    def swap_each(values):
        got = {0: values[0]}
        for k in range(1, group):
            got[k] = lax.ppermute(values[k], group_axes, [(i, i ^ k) for i in range(group)])
        return [got[k] for k in range(group)]

    def shape(*dims, dtype=F32):
        return jax.ShapeDtypeStruct(dims, dtype)

    def interleaved(value):
        return value.reshape(2, size, size).transpose(1, 0, 2).reshape(2 * size, size)

    plane = shape(size, size)
    planes = shape(2, size, size)
    wind = interleaved(wind_stress)

    tail_rows = -(-(2 * levels + 1) // TILE_ROWS) * TILE_ROWS
    pair_rows = side + width
    chunk_rows = pair_rows + 2 * side + tail_rows
    sent = call(
        functools.partial(forward_kernel, (devices, group, member_place)),
        [
            shape(pair_rows if k > 1 and k % 2 else chunk_rows, width, dtype=BF16)
            for k in range(group)
        ],
        (
            neighbors,
            remap_blocks,
            remap_rows[0].swapaxes(1, 2),
            remap_cols[0],
            upper_current_vector,
            water_heat_state,
        ),
        scratch=[
            pltpu.SMEM(neighbors.shape, jnp.int32),
            pltpu.SMEM((1, pairs), jnp.int32),
            pltpu.VMEM((2, side, width), F32),
            pltpu.VMEM((pairs, pair_rows, width), BF16),
            pltpu.VMEM((levels, side, width), F32),
            pltpu.VMEM((chunk_rows - pair_rows, width), BF16),
            pltpu.VMEM((1 if pairs == group else group, pair_rows, width), BF16),
            pltpu.SemaphoreType.DMA((6,)),
            pltpu.SemaphoreType.DMA((2 * group,)),
        ],
        hbm=(0, 1, 2, 3, 4, 5),
        grant=60 * 2**20,
        micros=10,
    )
    chunks = swap_each(sent)
    hops = [
        lax.ppermute(chunks[k][pair_rows:], group_axes, [(i, i ^ 1) for i in range(group)])
        for k in range(2, group, 2)
    ]

    early, viscous, gain, step_mass, drag, conduct, speed = call(
        rims_kernel,
        [shape(EARLY_ROWS + 4 * levels, size)] + [plane] * 5 + [planes],
        (
            thickness.reshape(categories, size, size),
            concentration.reshape(categories, size, size),
            interleaved(ice_velocity),
            water_heat_state,
        ),
    )
    extra_rows = -(-(1 + 5 * levels) // TILE_ROWS) * TILE_ROWS
    message, current_ice, push = call(
        functools.partial(forcing_kernel, group, side, levels, sub_count, member_place),
        [shape(BLOCK_ROWS + extra_rows, size, dtype=BF16), planes, planes],
        (step_mass, drag, wind, early, *chunks[::-1], *hops),
        scratch=[pltpu.VMEM((BLOCK_ROWS + extra_rows, size), F32)],
    )
    messages = swap(message, "tile", tile_count)

    counts = (tile_count, sub_count, lev_count)
    ocean = (*(messages[k] for k in spread_out(tile_count)), *chunks, *hops)
    relay_rows = tile_count * BLOCK_ROWS
    relay_shapes = [shape(relay_rows + (side if lev_count == 1 else 0), size, dtype=BF16)]
    if lev_count > 1:
        relay_shapes.append(shape(side, width))
    relay, *top = call(
        functools.partial(relay_kernel, counts, tile_place, member_place),
        relay_shapes,
        (water_heat_state, diffusion_coefficient, *ocean),
    )
    if lev_count > 1:
        relay = jnp.concatenate([relay, lax.psum(top[0], "lev").astype(BF16)], axis=0)
    relays = swap_chips(relay)

    mixing, _ = lax.optimization_barrier((diffusion_coefficient, relay))
    (warm,) = call(
        functools.partial(ocean_kernel, counts, tile_place, member_place),
        [shape(levels, side, width)],
        (water_heat_state, mixing, *ocean),
    )
    far = sorted(k for k in relays if k)
    relayed, _ = lax.optimization_barrier(([relays[k] for k in far], warm))
    relays = swap_cores({0: relay} | dict(zip(far, relayed)))

    names = jnp.stack([m[BLOCK_ROWS, : 8 * group] for m in messages])
    names = names.reshape(devices, 8).astype(jnp.int32)
    table = names[:, 0:4] * 128 + names[:, 4:8]
    table = jnp.where(table < 0, -1, table ^ device_place())
    step = 3 * side
    speed, own, beside = call(
        functools.partial(ice_kernel, tile_count, group, side),
        [
            planes,
            shape(group // 2 * step, width),
            shape(group // 2 * step, width, dtype=BF16),
        ],
        (table, viscous, gain, drag, conduct, current_ice, speed, push, *chunks, *relays),
        scratch=[
            pltpu.VMEM((devices, BLOCK_ROWS + 2 * DEPTH, size), F32),
            pltpu.SMEM((devices, 4), jnp.int32),
            pltpu.SemaphoreType.DMA,
            pltpu.VMEM((2, 2, size + 4 * DEPTH, size), F32),
        ],
        hbm=(0,),
    )
    beside = lax.ppermute(beside, group_axes, [(i, i ^ 1) for i in range(group)])
    paired = call(
        pair_kernel, [shape(step, width, dtype=BF16)] * (group // 2 - 1), (own, beside)
    )
    replies = [
        lax.ppermute(value, group_axes, [(i, i ^ (2 * k + 2)) for i in range(group)])
        for k, value in enumerate(paired)
    ]
    if lev_count > 1:
        parts = [r.astype(F32) for r in (own[:step], beside[:step], *replies)]
        own, beside, replies = lax.psum(sum(parts), "lev"), jnp.zeros_like(beside[:step]), []
    flat, heat, current = call(
        finish_kernel,
        [shape(2 * size, size), shape(levels, side, width), shape(2, side, width)],
        (warm, upper_current_vector, speed, own, beside, *replies),
        scratch=[
            pltpu.VMEM((2 * size, size), F32),
            pltpu.VMEM((levels, side, width), F32),
            pltpu.VMEM((2, side, width), F32),
            pltpu.SemaphoreType.DMA((3,)),
        ],
        out_space=pltpu.HBM,
    )
    velocity = flat.reshape(size, 2, size).transpose(1, 0, 2).reshape(1, 1, 2, size * size)
    return heat, current, velocity


def solution(mesh):
    member = ("tile", "sub", "lev")
    whole = ("copies",) + member
    ice = P(None, whole, None, None)
    water = P("lev", ("copies", "tile"), "sub")
    current = P(None, ("copies", "tile"), "sub")
    return jax.shard_map(
        shards,
        mesh=mesh,
        in_specs=(
            water,
            P("tile", "sub"),
            current,
            P(member, None),
            P(member, None, None, None),
            P(member, None, None, None),
            P(None, member, None),
            ice,
            ice,
            ice,
            ice,
        ),
        out_specs=(water, current, ice),
        check_vma=False,
    )
```

```python
import functools

import jax
import jax.numpy as jnp
from jax import lax
from jax.experimental import pallas as pl
from jax.experimental.pallas import tpu as pltpu
from jax.sharding import PartitionSpec as P

SUBCYCLES = 4
STRENGTH_DECAY = 5.0
VISCOUS_STEP = 0.24
SUBCYCLE_STEP = 0.5
CORIOLIS_TURN = 0.1
BASE_MASS = 0.5
HEAT_RATE = 0.2
THIN_ICE = 0.1
THERMAL_DIFFUSE = 0.5
STRESS_MIXING = 0.5

OPPOSITE = (1, 0, 3, 2)
LATERAL = ((2, 3), (2, 3), (0, 1), (0, 1))
DEPTH = SUBCYCLES
EARLY_DEPTHS = (DEPTH, DEPTH, DEPTH - 1, DEPTH - 1)
LATE_DEPTHS = (DEPTH - 1, DEPTH - 1)
EARLY_SIDE, LATE_SIDE = sum(EARLY_DEPTHS), sum(LATE_DEPTHS)
EARLY_ROWS = 4 * EARLY_SIDE
BLOCK_ROWS = EARLY_ROWS + 4 * LATE_SIDE
TILE_ROWS = 16
F32 = jnp.float32
BF16 = jnp.bfloat16
VMEM_LIMIT = 16 * 1024 * 1024
FLOPS_PER_MICRO = 1.15e9


def call(kernel, outs, args, scratch=(), smem=(), hbm=(), out_space=pltpu.VMEM, grant=VMEM_LIMIT, micros=0.01):
    def space(i):
        return pltpu.SMEM if i in smem else pltpu.HBM if i in hbm else pltpu.VMEM

    specs = [pl.BlockSpec(memory_space=space(i)) for i in range(len(args))]
    size = sum(a.size * a.dtype.itemsize for a in args)
    return pl.pallas_call(
        kernel,
        out_shape=outs,
        in_specs=specs,
        out_specs=jax.tree.map(lambda _: pl.BlockSpec(memory_space=out_space), outs),
        scratch_shapes=list(scratch),
        compiler_params=pltpu.CompilerParams(vmem_limit_bytes=grant),
        cost_estimate=pl.CostEstimate(
            flops=int(micros * FLOPS_PER_MICRO), bytes_accessed=size, transcendentals=0
        ),
    )(*args)


def iota(shape, axis):
    return lax.broadcasted_iota(jnp.int32, shape, axis)


def roll(x, shift, axis):
    return pltpu.roll(x, shift % x.shape[axis], axis)


def flag(condition):
    return jnp.where(condition, 1.0, 0.0).astype(F32)


def ocean_columns(water):
    levels, rows, width = water.shape
    lane = iota((rows, width), 1)
    line = iota((1, width), 1)
    mixed = jnp.zeros((rows, width), F32)
    for l in range(levels):
        mixed = jnp.where(lane // 4 == l, roll(water[l], 2 + 4 * l, 1), mixed)
    across = jnp.concatenate([mixed, jnp.zeros((width - rows, width), F32)], axis=0).T
    beside = []
    for l in range(levels):
        for j in range(2):
            last = across[4 * l + 1 - j : 4 * l + 2 - j]
            lead = across[4 * l + 2 + j : 4 * l + 3 + j]
            beside.append(jnp.where(line < rows, last, roll(lead, rows, 1)))
    return beside


def forward_kernel(group, links_h, blocks_h, rows_h, cols_h, currents_h, water_h, *refs):
    devices, members, place = group
    outs, scratch = refs[:members], refs[members:]
    links, blocks, currents, weights, water, fields, kept, arrived, left = scratch
    pairs, side, width = rows_h.shape
    both = weights.shape[1]
    loads = [
        pltpu.make_async_copy(source, target, arrived.at[i])
        for i, (source, target) in enumerate(
            (
                (links_h, links),
                (blocks_h, blocks),
                (currents_h, currents),
                (rows_h, weights.at[:, pl.ds(0, side)]),
                (cols_h, weights.at[:, pl.ds(side, both - side)]),
                (water_h, water),
            )
        )
    ]
    for load in loads:
        load.start()
    for i in (1, 3, 4):
        loads[i].wait()
    me = place()
    owners = [lax.rem(lax.rem(blocks[0, m], devices), members) for m in range(pairs)]
    copies = []
    for k, out in enumerate(outs):
        partner = me ^ k
        pair = jnp.int32(0)
        for m in range(pairs):
            pair = jnp.where(owners[m] == partner, m, pair)
        source = weights.at[pair]
        if pairs < members:
            found = sum(flag(owners[m] == partner) for m in range(pairs))
            kept[k] = (weights[pair].astype(F32) * found).astype(BF16)
            source = kept.at[k]
        copies.append(pltpu.make_async_copy(source, out.at[pl.ds(0, both)], left.at[2 * k]))
        copies[-1].start()
    for i in (0, 2, 5):
        loads[i].wait()
    for c in range(2):
        fields[c * side : (c + 1) * side] = currents[c].astype(BF16)
    lane = iota((1, width), 1)
    numbers = jnp.zeros((1, width), F32)
    for q in range(4):
        numbers = jnp.where(lane == q, (links[0, 0, q] >> 7).astype(F32), numbers)
        numbers = jnp.where(lane == 4 + q, (links[0, 0, q] & 127).astype(F32), numbers)
    ends = ocean_columns(water) + [numbers]
    blank = jnp.zeros((fields.shape[0] - 2 * side - len(ends), width), F32)
    fields[2 * side :] = jnp.concatenate(ends + [blank], axis=0).astype(BF16)
    for k, out in enumerate(outs):
        if out.shape[0] > both:
            target = out.at[pl.ds(both, fields.shape[0])]
            copies.append(pltpu.make_async_copy(fields, target, left.at[2 * k + 1]))
            copies[-1].start()
    for copy in copies:
        copy.wait()


def put_side_rims(store, planes, depths, at):
    size = planes[0].shape[0]
    lane = iota((size, size), 1)
    mixed = jnp.zeros((size, size), F32)
    for i, plane in enumerate(planes):
        turned = roll(plane, DEPTH + 2 * DEPTH * i, 1)
        mixed = jnp.where(lane // (2 * DEPTH) == i, turned, mixed)
    across = mixed.T
    base = 0
    for i, plane in enumerate(planes):
        for k in range(depths[i]):
            east = 2 * DEPTH * i + DEPTH - 1 - k
            west = 2 * DEPTH * i + DEPTH + k
            store[at(0) + base : at(0) + base + 1] = plane[size - 1 - k : size - k]
            store[at(1) + base : at(1) + base + 1] = plane[k : k + 1]
            store[at(2) + base : at(2) + base + 1] = across[east : east + 1]
            store[at(3) + base : at(3) + base + 1] = across[west : west + 1]
            base += 1


def rims_kernel(
    thick, conc, ice, water, out, viscous_o, gain_o, mass_o, drag_o, conduct_o,
    speed_o,
):
    size = thick.shape[1]
    cover = jnp.zeros((size, size), F32)
    volume = jnp.zeros((size, size), F32)
    conduct = jnp.zeros((size, size), F32)
    for c in range(thick.shape[0]):
        h, a = thick[c], conc[c]
        cover = cover + a
        volume = volume + a * h
        conduct = conduct + a / (h + THIN_ICE)
    mass = volume + BASE_MASS
    viscous = VISCOUS_STEP * (volume * jnp.exp(-STRENGTH_DECAY * (1.0 - cover))) / mass
    step_mass = SUBCYCLE_STEP / mass
    gain = 1.0 / (1.0 + step_mass * cover)
    speed_x = ice[pl.ds(0, size, stride=2), :]
    speed_y = ice[pl.ds(1, size, stride=2), :]
    viscous_o[...] = viscous
    gain_o[...] = gain
    mass_o[...] = step_mass
    drag_o[...] = cover
    conduct_o[...] = -HEAT_RATE * conduct
    speed_o[0] = speed_x
    speed_o[1] = speed_y
    put_side_rims(
        out, [speed_x, speed_y, viscous, gain], EARLY_DEPTHS, lambda side: side * EARLY_SIDE
    )
    levels, rows, width = water.shape
    for l in range(levels):
        for j in range(2):
            at = EARLY_ROWS + 2 * l + j
            out[at : at + 1] = water[l, rows - 1 - j : rows - j]
            out[at + 2 * levels : at + 2 * levels + 1] = water[l, j : j + 1]


def nearby(me, members, distance, arrays):
    at = me + distance
    inside = (at >= 0) & (at < members)
    found = 0.0
    for k in range(1, members):
        found = found + arrays[k].astype(F32) * flag(inside & ((me ^ k) == at))
    return found


def remap_forward(chunks, field_rows, side, depth):
    total = None
    for chunk, fields in zip(chunks, field_rows):
        down = chunk[0:side]
        right = chunk[side : side + depth]
        wide = jnp.concatenate(fields, axis=1) if len(fields) > 1 else fields[0]
        part = lax.dot_general(down, wide, (((0,), (0,)), ((), ())), preferred_element_type=F32)
        part = part.astype(BF16)
        width = fields[0].shape[1]
        if len(fields) > 1:
            part = jnp.concatenate(
                [part[:, c * width : (c + 1) * width] for c in range(len(fields))], axis=0
            )
        piece = lax.dot_general(part, right, (((1,), (1,)), ((), ())), preferred_element_type=F32)
        piece = piece.astype(BF16).astype(F32)
        total = piece if total is None else total + piece
    return total


def tails_of(chunks, hops):
    at = min(c.shape[0] for c in chunks)
    return [hops[k // 2 - 1][...] if k > 1 and k % 2 else c[at:] for k, c in enumerate(chunks)]


def forcing_kernel(group, side, levels, subs, place, mass, drag, wind, early, *refs):
    chunks = refs[:group][::-1]
    hops, (out, current_o, push_o, store) = refs[group:-4], refs[-4:]
    size = mass.shape[0]
    depth = chunks[0].shape[1]
    tails = tails_of(chunks, hops)
    fields = [[t[0:side], t[side : 2 * side]] for t in tails]
    total = remap_forward(chunks, fields, side, depth)
    pushes = []
    for c in range(2):
        current = total[c * size : (c + 1) * size]
        current_o[c] = current
        force = wind[pl.ds(c, size, stride=2), :]
        push = mass[...] * (force + drag[...] * current)
        push_o[c] = push
        pushes.append(push)
    store[0:EARLY_ROWS] = early[0:EARLY_ROWS]
    put_side_rims(store, pushes, LATE_DEPTHS, lambda side: EARLY_ROWS + side * LATE_SIDE)
    tail = [t[2 * side :].astype(F32) for t in tails]
    line = iota((1, size), 1)
    names = jnp.zeros((1, size), F32)
    for k in range(group):
        names = jnp.where(line // 8 == k, roll(tail[k][2 * levels : 2 * levels + 1], 8 * k, 1), names)
    me, step = place(), group // subs
    left, right = (nearby(me, group, d * step, tail) for d in (-1, 1))
    extra = [names]
    for l in range(levels):
        near = slice(2 * l, 2 * l + 1)
        extra.append(jnp.where(line < side, left[near], right[near]))
    extra.append(early[EARLY_ROWS:])
    used = BLOCK_ROWS + 1 + 5 * levels
    store[BLOCK_ROWS:] = jnp.concatenate(
        extra + [jnp.zeros((store.shape[0] - used, size), F32)], axis=0
    )
    out[...] = store[...].astype(BF16)


def ocean_halos(counts, tile_place, member_place, shape, messages, tails):
    tiles, subs, levs = counts
    levels, rows, width = shape
    my_tile, me = tile_place(), member_place()
    halo = {}
    extras = [m[BLOCK_ROWS:] for m in messages]
    ends = [t[2 * rows :] for t in tails]
    for dt in (-1, 1):
        extra = nearby(my_tile, tiles, dt, extras)
        corners, strips = extra[1 : 1 + levels], extra[1 + levels : 1 + 5 * levels]
        halo[dt, 0] = strips[: 2 * levels] if dt < 0 else strips[2 * levels :]
        at = rows - 1 if dt < 0 else 0
        for ds in (-1, 1):
            lane_at = at if ds < 0 else rows + at
            halo[dt, ds] = corners[:, lane_at : lane_at + 1]
    for ds in (-1, 1):
        beside = nearby(me, subs * levs, ds * levs, ends)[: 2 * levels]
        halo[0, ds] = roll(beside, -rows, 1) if ds > 0 else beside
    return halo


def biharmonic(x, top, bottom, left, right, corner):
    rows, width = x.shape
    row, lane = iota(x.shape, 0), iota(x.shape, 1)
    line = iota((1, width), 1)

    def laplacian(x, top, bottom, left, right):
        up = jnp.where(row == 0, top, roll(x, 1, 0))
        down = jnp.where(row == rows - 1, bottom, roll(x, -1, 0))
        west = jnp.where(lane == 0, left, roll(x, 1, 1))
        east = jnp.where(lane == width - 1, right, roll(x, -1, 1))
        return up + down + west + east - 4.0 * x

    def ring_row(mid, out_row, in_row, dt):
        west = jnp.where(line == 0, corner[dt, -1], roll(mid, 1, 1))
        east = jnp.where(line == width - 1, corner[dt, 1], roll(mid, -1, 1))
        return west + east + out_row + in_row - 4.0 * mid

    def ring_col(mid, out_col, in_col, ds):
        up = jnp.concatenate([corner[-1, ds], mid[:-1]], axis=0)
        down = jnp.concatenate([mid[1:], corner[1, ds]], axis=0)
        return up + down + out_col + in_col - 4.0 * mid

    return laplacian(
        laplacian(x, top[0], bottom[0], left[0], right[0]),
        ring_row(*top, x[0:1], -1),
        ring_row(*bottom, x[rows - 1 :], 1),
        ring_col(*left, x[:, 0:1], -1),
        ring_col(*right, x[:, width - 1 :], 1),
    )


def spread_out(count):
    return sorted(range(count), key=lambda k: (k == count // 2, k))


def split_refs(tiles, members, refs, outs):
    messages = [refs[spread_out(tiles).index(k)] for k in range(tiles)]
    chunks = refs[tiles : tiles + members]
    return messages, tails_of(chunks, refs[tiles + members : -outs]), refs[-outs:]


def relay_kernel(counts, tile_place, member_place, water, mixing, *refs):
    tiles, subs, levs = counts
    outs = 1 if levs == 1 else 2
    messages, tails, outs = split_refs(tiles, subs * levs, refs, outs)
    for k in range(tiles):
        outs[0][k * BLOCK_ROWS : (k + 1) * BLOCK_ROWS] = messages[k][0:BLOCK_ROWS]
    levels, rows, width = water.shape
    halo = ocean_halos(counts, tile_place, member_place, water.shape, messages, tails)

    def both(strip):
        near = sum(strip[2 * l : 2 * l + 1] for l in range(levels))
        far = sum(strip[2 * l + 1 : 2 * l + 2] for l in range(levels))
        return near, far

    def as_columns(strip):
        near, far = both(strip)
        across = jnp.concatenate([near, far] + [jnp.zeros_like(near)] * 6, axis=0).T
        return across[0:rows, 0:1], across[0:rows, 1:2]

    corner = {
        (dt, ds): jnp.sum(halo[dt, ds], axis=0, keepdims=True) for dt in (-1, 1) for ds in (-1, 1)
    }
    x = sum(water[l] for l in range(levels))
    twice = biharmonic(
        x, both(halo[-1, 0]), both(halo[1, 0]), as_columns(halo[0, -1]), as_columns(halo[0, 1]), corner
    )
    top = (x - mixing[...] * twice) / (levels * levs)
    if levs == 1:
        outs[0][tiles * BLOCK_ROWS :] = top.astype(BF16)
    else:
        outs[1][...] = top


def ocean_kernel(counts, tile_place, member_place, water, mixing, *refs):
    tiles, subs, levs = counts
    messages, tails, (warm_o,) = split_refs(tiles, subs * levs, refs, 1)
    levels, rows, width = water.shape
    halo = ocean_halos(counts, tile_place, member_place, water.shape, messages, tails)
    left, right = halo[0, -1].T, halo[0, 1].T
    for l in range(levels):
        x = water[l]
        pair = (2 * l, 2 * l + 1)
        twice = biharmonic(
            x,
            [halo[-1, 0][i : i + 1] for i in pair],
            [halo[1, 0][i : i + 1] for i in pair],
            [left[0:rows, i : i + 1] for i in pair],
            [right[0:rows, i : i + 1] for i in pair],
            {(dt, ds): halo[dt, ds][l : l + 1] for dt in (-1, 1) for ds in (-1, 1)},
        )
        warm_o[l] = x - mixing[...] * twice


def ice_kernel(
    tiles, members, side, table, viscous, gain, drag, conduct, current, speed, push, *refs
):
    chunks, relays = refs[:members], refs[members : 2 * members]
    out, own_o, beside_o, rims, names, named, field = refs[2 * members :]
    load_names = pltpu.make_async_copy(table, names, named)
    load_names.start()
    size = viscous.shape[0]
    depth = chunks[0].shape[1]
    for k in range(tiles):
        for m in range(members):
            block = relays[m][k * BLOCK_ROWS : (k + 1) * BLOCK_ROWS]
            rims[k * members + m, 0:BLOCK_ROWS] = block.astype(F32)
            rims[k * members + m, BLOCK_ROWS:] = jnp.zeros((2 * DEPTH, size), F32)
    half = DEPTH
    high = 2 * DEPTH
    sub = iota((high, size), 0)
    lane = iota((high, size), 1)
    edge = (sub & (half - 1)) == 0
    turn = jnp.where(sub < half, CORIOLIS_TURN, -CORIOLIS_TURN).astype(F32)
    first, last = lane == 0, lane == size - 1

    def load(device, side, mask, with_push=True):
        start = side * EARLY_SIDE
        velocity = rims[device, start : start + high] * mask
        if not with_push:
            return velocity
        both = rims[device, start + high : start + 2 * high]
        visc = jnp.where(sub < half, both, roll(both, half, 0))
        scale = jnp.where(sub < half, roll(both, 1 - half, 0), roll(both, 1, 0)) * mask
        start = EARLY_ROWS + side * LATE_SIDE
        late = rims[device, start : start + high]
        pushed = jnp.where(sub < half, late, roll(late, 1, 0))
        return [velocity, visc, scale, pushed]

    def follow(device, side):
        name = names[device, side]
        return jnp.where(name >= 0, name, 0), name >= 0

    def step(state, left, right, inner, outer):
        c, visc, scale, pushed = state
        spread = left + right + inner + outer - 4.0 * c
        return scale * (c + visc * spread + pushed + turn * roll(c, half, 0))

    base = high
    for c in range(2):
        field[0, c, base : base + size] = speed[c]
    load_names.wait()
    def along(cells, before, beyond):
        left = jnp.where(first, roll(before, 1, 1), roll(cells, 1, 1))
        return left, jnp.where(last, roll(beyond, -1, 1), roll(cells, -1, 1))

    def step_end(state, inside, across, away):
        cells = state[0]
        toward = jnp.where(first if away > 0 else last, roll(inside, away, 1), roll(cells, away, 1))
        inner = jnp.where(edge, across, roll(cells, 1, 0))
        return step(state, toward, roll(cells, -away, 1), inner, roll(cells, -1, 0))

    halos = [[] for _ in range(SUBCYCLES)]
    for q in range(4):
        x, has_x = follow(0, q)
        halo = load(x, OPPOSITE[q], flag(has_x))
        own = load(0, q, 1.0)
        ends = []
        for s in LATERAL[q]:
            y, has_y = follow(x, s)
            z, has_z = follow(y, OPPOSITE[q])
            w, has_w = follow(z, OPPOSITE[s])
            u, has_u = follow(0, s)
            v, has_v = follow(u, q)
            ends.append(
                [
                    load(y, OPPOSITE[q], flag(has_y)),
                    load(z, q, flag(has_z)),
                    load(w, q, flag(has_w), with_push=False),
                    load(u, q, flag(has_u)),
                    load(v, OPPOSITE[q], flag(has_v), with_push=False),
                ]
            )
        (y_hi, z_hi, w_hi, u_hi, v_hi), (y_lo, z_lo, w_lo, u_lo, v_lo) = ends
        for t in range(SUBCYCLES):
            halos[t].append(halo[0])
            if t == SUBCYCLES - 1:
                break
            c, o = halo[0], own[0]
            left, right = along(c, y_lo[0], y_hi[0])
            inner = jnp.where(edge, o, roll(c, 1, 0))
            new_halo = step(halo, left, right, inner, roll(c, -1, 0))
            if t < SUBCYCLES - 2:
                left, right = along(o, u_lo[0], u_hi[0])
                inner = jnp.where(edge, c, roll(o, 1, 0))
                new_own = step(own, left, right, inner, roll(o, -1, 0))
                new_y = step_end(y_hi, c, z_hi[0], 1), step_end(y_lo, c, z_lo[0], -1)
            if t < SUBCYCLES - 3:
                z_hi[0], z_lo[0] = (
                    step_end(z_hi, w_hi, y_hi[0], 1),
                    step_end(z_lo, w_lo, y_lo[0], -1),
                )
                u_hi[0], u_lo[0] = step_end(u_hi, o, v_hi, 1), step_end(u_lo, o, v_lo, -1)
            halo[0] = new_halo
            if t < SUBCYCLES - 2:
                own[0] = new_own
                y_hi[0], y_lo[0] = new_y
    columns = [jnp.where(edge, cells[2], roll(cells[3], 1, 0)).T for cells in halos]

    warm = remap_forward(chunks, [[r[r.shape[0] - side :]] for r in relays], side, depth)
    heat = (conduct[...] * warm).astype(BF16)

    for t in range(SUBCYCLES):
        cells, sides = halos[t], columns[t]
        now, later = t % 2, (t + 1) % 2
        for c in range(2):
            at = c * half
            field[now, c, base + size : base + size + 1] = cells[0][at : at + 1]
            field[now, c, base - 1 : base] = cells[1][at : at + 1]
        for i in range(size // high):
            rows = slice(i * high, (i + 1) * high)
            held = [field[now, c, base + i * high : base + (i + 1) * high] for c in range(2)]
            for c in range(2):
                v, at = held[c], base + i * high
                up = field[now, c, at + 1 : at + 1 + high]
                down = field[now, c, at - 1 : at - 1 + high]
                east = jnp.where(last, sides[rows, c * half : c * half + 1], roll(v, -1, 1))
                west = jnp.where(first, sides[rows, c * half + 1 : c * half + 2], roll(v, 1, 1))
                spread = up + down + east + west - 4.0 * v
                turned = (CORIOLIS_TURN if c == 0 else -CORIOLIS_TURN) * held[1 - c]
                new = gain[rows] * (v + viscous[rows] * spread + push[c, rows] + turned)
                if t == SUBCYCLES - 1:
                    out[c, rows] = new
                else:
                    field[later, c, at : at + high] = new
    stress = [(drag[...] * (out[c] - current[c])).astype(BF16) for c in range(2)]
    return_fluxes([heat, *stress], chunks, side, depth, own_o, beside_o)


def return_fluxes(fluxes, chunks, side, depth, own, beside):
    size = fluxes[0].shape[0]
    wide = jnp.concatenate(fluxes, axis=1)
    step = 3 * side
    for k, chunk in enumerate(chunks):
        part = jnp.dot(chunk[0:side], wide, preferred_element_type=F32).astype(BF16)
        part = jnp.concatenate([part[:, c * size : (c + 1) * size] for c in range(3)], axis=0)
        reply = jnp.dot(part, chunk[side : side + depth], preferred_element_type=F32)
        at = k // 2 * step
        if k % 2:
            beside[at : at + step] = reply.astype(BF16)
        else:
            own[at : at + step] = reply


def pair_kernel(own, beside, *outs):
    step = outs[0].shape[0]
    for k, out in enumerate(outs):
        at = (k + 1) * step
        out[...] = (own[at : at + step] + beside[at : at + step].astype(F32)).astype(BF16)


def finish_kernel(warm, currents, speed, own, beside, *refs):
    outs, (flat, heat_v, current_v, left) = refs[-7:-4], refs[-4:]
    replies = refs[:-7]
    flat_o, heat_o, current_o = outs
    size = speed.shape[1]
    copies = [
        pltpu.make_async_copy(source, target, left.at[i])
        for i, (source, target) in enumerate(
            ((flat, flat_o), (heat_v, heat_o), (current_v, current_o))
        )
    ]
    for c in range(2):
        flat[pl.ds(c, size, stride=2), :] = speed[c]
    copies[0].start()
    side = currents.shape[1]
    total = own[0 : 3 * side] + beside[0 : 3 * side].astype(F32)
    for reply in replies:
        total = total + reply[...].astype(F32)
    heat = THERMAL_DIFFUSE * total[0:side]
    for l in range(warm.shape[0]):
        heat_v[l] = warm[l] + heat
    copies[1].start()
    for c in range(2):
        current_v[c] = currents[c] + STRESS_MIXING * total[(c + 1) * side : (c + 2) * side]
    copies[2].start()
    for copy in copies:
        copy.wait()


def shards(
    water_heat_state,
    diffusion_coefficient,
    upper_current_vector,
    remap_blocks,
    remap_rows,
    remap_cols,
    neighbors,
    thickness,
    concentration,
    ice_velocity,
    wind_stress,
):
    tile_count, sub_count, lev_count = (lax.axis_size(a) for a in ("tile", "sub", "lev"))
    group = sub_count * lev_count
    devices = tile_count * group
    group_axes = ("sub", "lev")
    member_axes = ("tile", "sub", "lev")
    levels, side, width = water_heat_state.shape
    pairs, size = remap_rows.shape[1:3]
    categories = thickness.shape[2]

    def tile_place():
        return lax.axis_index("tile")

    def member_place():
        return lax.axis_index("sub") * lev_count + lax.axis_index("lev")

    def device_place():
        return lax.axis_index("tile") * group + member_place()

    def swap(value, axes, count):
        got = {0: value}
        for k in range(1, count):
            got[k] = lax.ppermute(value, axes, [(i, i ^ k) for i in range(count)])
        return [got[k] for k in range(count)]

    def swap_chips(value):
        return {0: value} | {
            k: lax.ppermute(value, group_axes, [(i, i ^ k) for i in range(group)])
            for k in range(2, group, 2)
        }

    def swap_cores(got):
        beside = [(i, i ^ 1) for i in range(group)]
        got = got | {k + 1: lax.ppermute(got[k], group_axes, beside) for k in got}
        return [got[k] for k in range(group)]

    def swap_each(values):
        got = {0: values[0]}
        for k in range(1, group):
            got[k] = lax.ppermute(values[k], group_axes, [(i, i ^ k) for i in range(group)])
        return [got[k] for k in range(group)]

    def shape(*dims, dtype=F32):
        return jax.ShapeDtypeStruct(dims, dtype)

    def interleaved(value):
        return value.reshape(2, size, size).transpose(1, 0, 2).reshape(2 * size, size)

    plane = shape(size, size)
    planes = shape(2, size, size)
    wind = interleaved(wind_stress)

    tail_rows = -(-(2 * levels + 1) // TILE_ROWS) * TILE_ROWS
    pair_rows = side + width
    chunk_rows = pair_rows + 2 * side + tail_rows
    sent = call(
        functools.partial(forward_kernel, (devices, group, member_place)),
        [
            shape(pair_rows if k > 1 and k % 2 else chunk_rows, width, dtype=BF16)
            for k in range(group)
        ],
        (
            neighbors,
            remap_blocks,
            remap_rows[0].swapaxes(1, 2),
            remap_cols[0],
            upper_current_vector,
            water_heat_state,
        ),
        scratch=[
            pltpu.SMEM(neighbors.shape, jnp.int32),
            pltpu.SMEM((1, pairs), jnp.int32),
            pltpu.VMEM((2, side, width), F32),
            pltpu.VMEM((pairs, pair_rows, width), BF16),
            pltpu.VMEM((levels, side, width), F32),
            pltpu.VMEM((chunk_rows - pair_rows, width), BF16),
            pltpu.VMEM((1 if pairs == group else group, pair_rows, width), BF16),
            pltpu.SemaphoreType.DMA((6,)),
            pltpu.SemaphoreType.DMA((2 * group,)),
        ],
        hbm=(0, 1, 2, 3, 4, 5),
        grant=60 * 2**20,
        micros=10,
    )
    chunks = swap_each(sent)
    hops = [
        lax.ppermute(chunks[k][pair_rows:], group_axes, [(i, i ^ 1) for i in range(group)])
        for k in range(2, group, 2)
    ]

    early, viscous, gain, step_mass, drag, conduct, speed = call(
        rims_kernel,
        [shape(EARLY_ROWS + 4 * levels, size)] + [plane] * 5 + [planes],
        (
            thickness.reshape(categories, size, size),
            concentration.reshape(categories, size, size),
            interleaved(ice_velocity),
            water_heat_state,
        ),
    )
    extra_rows = -(-(1 + 5 * levels) // TILE_ROWS) * TILE_ROWS
    message, current_ice, push = call(
        functools.partial(forcing_kernel, group, side, levels, sub_count, member_place),
        [shape(BLOCK_ROWS + extra_rows, size, dtype=BF16), planes, planes],
        (step_mass, drag, wind, early, *chunks[::-1], *hops),
        scratch=[pltpu.VMEM((BLOCK_ROWS + extra_rows, size), F32)],
    )
    messages = swap(message, "tile", tile_count)

    counts = (tile_count, sub_count, lev_count)
    ocean = (*(messages[k] for k in spread_out(tile_count)), *chunks, *hops)
    relay_rows = tile_count * BLOCK_ROWS
    relay_shapes = [shape(relay_rows + (side if lev_count == 1 else 0), size, dtype=BF16)]
    if lev_count > 1:
        relay_shapes.append(shape(side, width))
    relay, *top = call(
        functools.partial(relay_kernel, counts, tile_place, member_place),
        relay_shapes,
        (water_heat_state, diffusion_coefficient, *ocean),
    )
    if lev_count > 1:
        relay = jnp.concatenate([relay, lax.psum(top[0], "lev").astype(BF16)], axis=0)
    relays = swap_chips(relay)

    mixing, _ = lax.optimization_barrier((diffusion_coefficient, relay))
    (warm,) = call(
        functools.partial(ocean_kernel, counts, tile_place, member_place),
        [shape(levels, side, width)],
        (water_heat_state, mixing, *ocean),
    )
    far = sorted(k for k in relays if k)
    relayed, _ = lax.optimization_barrier(([relays[k] for k in far], warm))
    relays = swap_cores({0: relay} | dict(zip(far, relayed)))

    names = jnp.stack([m[BLOCK_ROWS, : 8 * group] for m in messages])
    names = names.reshape(devices, 8).astype(jnp.int32)
    table = names[:, 0:4] * 128 + names[:, 4:8]
    table = jnp.where(table < 0, -1, table ^ device_place())
    step = 3 * side
    speed, own, beside = call(
        functools.partial(ice_kernel, tile_count, group, side),
        [
            planes,
            shape(group // 2 * step, width),
            shape(group // 2 * step, width, dtype=BF16),
        ],
        (table, viscous, gain, drag, conduct, current_ice, speed, push, *chunks, *relays),
        scratch=[
            pltpu.VMEM((devices, BLOCK_ROWS + 2 * DEPTH, size), F32),
            pltpu.SMEM((devices, 4), jnp.int32),
            pltpu.SemaphoreType.DMA,
            pltpu.VMEM((2, 2, size + 4 * DEPTH, size), F32),
        ],
        hbm=(0,),
    )
    beside = lax.ppermute(beside, group_axes, [(i, i ^ 1) for i in range(group)])
    paired = call(
        pair_kernel, [shape(step, width, dtype=BF16)] * (group // 2 - 1), (own, beside)
    )
    replies = [
        lax.ppermute(value, group_axes, [(i, i ^ (2 * k + 2)) for i in range(group)])
        for k, value in enumerate(paired)
    ]
    if lev_count > 1:
        parts = [r.astype(F32) for r in (own[:step], beside[:step], *replies)]
        own, beside, replies = lax.psum(sum(parts), "lev"), jnp.zeros_like(beside[:step]), []
    flat, heat, current = call(
        finish_kernel,
        [shape(2 * size, size), shape(levels, side, width), shape(2, side, width)],
        (warm, upper_current_vector, speed, own, beside, *replies),
        scratch=[
            pltpu.VMEM((2 * size, size), F32),
            pltpu.VMEM((levels, side, width), F32),
            pltpu.VMEM((2, side, width), F32),
            pltpu.SemaphoreType.DMA((3,)),
        ],
        out_space=pltpu.HBM,
    )
    velocity = flat.reshape(size, 2, size).transpose(1, 0, 2).reshape(1, 1, 2, size * size)
    return heat, current, velocity


def solution(mesh):
    member = ("tile", "sub", "lev")
    whole = ("copies",) + member
    ice = P(None, whole, None, None)
    water = P("lev", ("copies", "tile"), "sub")
    current = P(None, ("copies", "tile"), "sub")
    return jax.shard_map(
        shards,
        mesh=mesh,
        in_specs=(
            water,
            P("tile", "sub"),
            current,
            P(member, None),
            P(member, None, None, None),
            P(member, None, None, None),
            P(None, member, None),
            ice,
            ice,
            ice,
            ice,
        ),
        out_specs=(water, current, ice),
        check_vma=False,
    )
```

```python
import functools

import jax
import jax.numpy as jnp
from jax import lax
from jax.experimental import pallas as pl
from jax.experimental.pallas import tpu as pltpu
from jax.sharding import PartitionSpec as P

SUBCYCLES = 4
STRENGTH_DECAY = 5.0
VISCOUS_STEP = 0.24
SUBCYCLE_STEP = 0.5
CORIOLIS_TURN = 0.1
BASE_MASS = 0.5
HEAT_RATE = 0.2
THIN_ICE = 0.1
THERMAL_DIFFUSE = 0.5
STRESS_MIXING = 0.5

OPPOSITE = (1, 0, 3, 2)
LATERAL = ((2, 3), (2, 3), (0, 1), (0, 1))
DEPTH = SUBCYCLES
EARLY_DEPTHS = (DEPTH, DEPTH, DEPTH - 1, DEPTH - 1)
LATE_DEPTHS = (DEPTH - 1, DEPTH - 1)
EARLY_SIDE, LATE_SIDE = sum(EARLY_DEPTHS), sum(LATE_DEPTHS)
EARLY_ROWS = 4 * EARLY_SIDE
BLOCK_ROWS = EARLY_ROWS + 4 * LATE_SIDE
TILE_ROWS = 16
F32 = jnp.float32
BF16 = jnp.bfloat16
VMEM_LIMIT = 16 * 1024 * 1024
FLOPS_PER_MICRO = 1.15e9


def call(
    kernel, outs, args, scratch=(), smem=(), hbm=(), out_space=pltpu.VMEM, out_spaces=None,
    grant=VMEM_LIMIT, micros=0.01,
):
    def space(i):
        return pltpu.SMEM if i in smem else pltpu.HBM if i in hbm else pltpu.VMEM

    specs = [pl.BlockSpec(memory_space=space(i)) for i in range(len(args))]
    size = sum(a.size * a.dtype.itemsize for a in args)
    return pl.pallas_call(
        kernel,
        out_shape=outs,
        in_specs=specs,
        out_specs=(
            jax.tree.map(lambda _: pl.BlockSpec(memory_space=out_space), outs)
            if out_spaces is None
            else [pl.BlockSpec(memory_space=space) for space in out_spaces]
        ),
        scratch_shapes=list(scratch),
        compiler_params=pltpu.CompilerParams(vmem_limit_bytes=grant),
        cost_estimate=pl.CostEstimate(
            flops=int(micros * FLOPS_PER_MICRO), bytes_accessed=size, transcendentals=0
        ),
    )(*args)


def iota(shape, axis):
    return lax.broadcasted_iota(jnp.int32, shape, axis)


def roll(x, shift, axis):
    return pltpu.roll(x, shift % x.shape[axis], axis)


def flag(condition):
    return jnp.where(condition, 1.0, 0.0).astype(F32)


def ocean_columns(water):
    levels, rows, width = water.shape
    lane = iota((rows, width), 1)
    line = iota((1, width), 1)
    mixed = jnp.zeros((rows, width), F32)
    for l in range(levels):
        mixed = jnp.where(lane // 4 == l, roll(water[l], 2 + 4 * l, 1), mixed)
    across = jnp.concatenate([mixed, jnp.zeros((width - rows, width), F32)], axis=0).T
    beside = []
    for l in range(levels):
        for j in range(2):
            last = across[4 * l + 1 - j : 4 * l + 2 - j]
            lead = across[4 * l + 2 + j : 4 * l + 3 + j]
            beside.append(jnp.where(line < rows, last, roll(lead, rows, 1)))
    return beside


def forward_kernel(group, links_h, blocks_h, rows_h, cols_h, currents_h, water_h, *refs):
    devices, members, place = group
    outs, scratch = refs[:members], refs[members:]
    links, blocks, currents, weights, water, fields, kept, arrived, left = scratch
    pairs, side, width = rows_h.shape
    both = weights.shape[1]
    loads = [
        pltpu.make_async_copy(source, target, arrived.at[i])
        for i, (source, target) in enumerate(
            (
                (links_h, links),
                (blocks_h, blocks),
                (currents_h, currents),
                (rows_h, weights.at[:, pl.ds(0, side)]),
                (cols_h, weights.at[:, pl.ds(side, both - side)]),
                (water_h, water),
            )
        )
    ]
    for load in loads:
        load.start()
    for i in (1, 3, 4):
        loads[i].wait()
    me = place()
    owners = [lax.rem(lax.rem(blocks[0, m], devices), members) for m in range(pairs)]
    copies = []
    for k, out in enumerate(outs):
        partner = me ^ k
        pair = jnp.int32(0)
        for m in range(pairs):
            pair = jnp.where(owners[m] == partner, m, pair)
        source = weights.at[pair]
        if pairs < members:
            found = sum(flag(owners[m] == partner) for m in range(pairs))
            kept[k] = (weights[pair].astype(F32) * found).astype(BF16)
            source = kept.at[k]
        copies.append(pltpu.make_async_copy(source, out.at[pl.ds(0, both)], left.at[2 * k]))
        copies[-1].start()
    for i in (0, 2, 5):
        loads[i].wait()
    for c in range(2):
        fields[c * side : (c + 1) * side] = currents[c].astype(BF16)
    lane = iota((1, width), 1)
    numbers = jnp.zeros((1, width), F32)
    for q in range(4):
        numbers = jnp.where(lane == q, (links[0, 0, q] >> 7).astype(F32), numbers)
        numbers = jnp.where(lane == 4 + q, (links[0, 0, q] & 127).astype(F32), numbers)
    ends = ocean_columns(water) + [numbers]
    blank = jnp.zeros((fields.shape[0] - 2 * side - len(ends), width), F32)
    fields[2 * side :] = jnp.concatenate(ends + [blank], axis=0).astype(BF16)
    for k, out in enumerate(outs):
        if out.shape[0] > both:
            target = out.at[pl.ds(both, fields.shape[0])]
            copies.append(pltpu.make_async_copy(fields, target, left.at[2 * k + 1]))
            copies[-1].start()
    for copy in copies:
        copy.wait()


def put_side_rims(store, planes, depths, at):
    size = planes[0].shape[0]
    lane = iota((size, size), 1)
    mixed = jnp.zeros((size, size), F32)
    for i, plane in enumerate(planes):
        turned = roll(plane, DEPTH + 2 * DEPTH * i, 1)
        mixed = jnp.where(lane // (2 * DEPTH) == i, turned, mixed)
    across = mixed.T
    base = 0
    for i, plane in enumerate(planes):
        for k in range(depths[i]):
            east = 2 * DEPTH * i + DEPTH - 1 - k
            west = 2 * DEPTH * i + DEPTH + k
            store[at(0) + base : at(0) + base + 1] = plane[size - 1 - k : size - k]
            store[at(1) + base : at(1) + base + 1] = plane[k : k + 1]
            store[at(2) + base : at(2) + base + 1] = across[east : east + 1]
            store[at(3) + base : at(3) + base + 1] = across[west : west + 1]
            base += 1


def rims_kernel(
    thick, conc, ice, water, out, viscous_o, gain_o, mass_o, drag_o, conduct_o,
    speed_o,
):
    size = thick.shape[1]
    cover = jnp.zeros((size, size), F32)
    volume = jnp.zeros((size, size), F32)
    conduct = jnp.zeros((size, size), F32)
    for c in range(thick.shape[0]):
        h, a = thick[c], conc[c]
        cover = cover + a
        volume = volume + a * h
        conduct = conduct + a / (h + THIN_ICE)
    mass = volume + BASE_MASS
    viscous = VISCOUS_STEP * (volume * jnp.exp(-STRENGTH_DECAY * (1.0 - cover))) / mass
    step_mass = SUBCYCLE_STEP / mass
    gain = 1.0 / (1.0 + step_mass * cover)
    speed_x = ice[pl.ds(0, size, stride=2), :]
    speed_y = ice[pl.ds(1, size, stride=2), :]
    viscous_o[...] = viscous
    gain_o[...] = gain
    mass_o[...] = step_mass
    drag_o[...] = cover
    conduct_o[...] = -HEAT_RATE * conduct
    speed_o[0] = speed_x
    speed_o[1] = speed_y
    put_side_rims(
        out, [speed_x, speed_y, viscous, gain], EARLY_DEPTHS, lambda side: side * EARLY_SIDE
    )
    levels, rows, width = water.shape
    for l in range(levels):
        for j in range(2):
            at = EARLY_ROWS + 2 * l + j
            out[at : at + 1] = water[l, rows - 1 - j : rows - j]
            out[at + 2 * levels : at + 2 * levels + 1] = water[l, j : j + 1]


def nearby(me, members, distance, arrays):
    at = me + distance
    inside = (at >= 0) & (at < members)
    found = 0.0
    for k in range(1, members):
        found = found + arrays[k].astype(F32) * flag(inside & ((me ^ k) == at))
    return found


def remap_forward(chunks, field_rows, side, depth):
    total = None
    for chunk, fields in zip(chunks, field_rows):
        down = chunk[0:side]
        right = chunk[side : side + depth]
        wide = jnp.concatenate(fields, axis=1) if len(fields) > 1 else fields[0]
        part = lax.dot_general(down, wide, (((0,), (0,)), ((), ())), preferred_element_type=F32)
        part = part.astype(BF16)
        width = fields[0].shape[1]
        if len(fields) > 1:
            part = jnp.concatenate(
                [part[:, c * width : (c + 1) * width] for c in range(len(fields))], axis=0
            )
        piece = lax.dot_general(part, right, (((1,), (1,)), ((), ())), preferred_element_type=F32)
        piece = piece.astype(BF16).astype(F32)
        total = piece if total is None else total + piece
    return total


def tails_of(chunks, hops):
    at = min(c.shape[0] for c in chunks)
    return [hops[k // 2 - 1][...] if k > 1 and k % 2 else c[at:] for k, c in enumerate(chunks)]


def forcing_kernel(group, side, levels, subs, place, mass, drag, wind, early, *refs):
    chunks = refs[:group][::-1]
    hops, (out, current_o, push_o, store) = refs[group:-4], refs[-4:]
    size = mass.shape[0]
    depth = chunks[0].shape[1]
    tails = tails_of(chunks, hops)
    fields = [[t[0:side], t[side : 2 * side]] for t in tails]
    total = remap_forward(chunks, fields, side, depth)
    pushes = []
    for c in range(2):
        current = total[c * size : (c + 1) * size]
        current_o[c] = current
        force = wind[pl.ds(c, size, stride=2), :]
        push = mass[...] * (force + drag[...] * current)
        push_o[c] = push
        pushes.append(push)
    store[0:EARLY_ROWS] = early[0:EARLY_ROWS]
    put_side_rims(store, pushes, LATE_DEPTHS, lambda side: EARLY_ROWS + side * LATE_SIDE)
    tail = [t[2 * side :].astype(F32) for t in tails]
    line = iota((1, size), 1)
    names = jnp.zeros((1, size), F32)
    for k in range(group):
        names = jnp.where(line // 8 == k, roll(tail[k][2 * levels : 2 * levels + 1], 8 * k, 1), names)
    me, step = place(), group // subs
    left, right = (nearby(me, group, d * step, tail) for d in (-1, 1))
    extra = [names]
    for l in range(levels):
        near = slice(2 * l, 2 * l + 1)
        extra.append(jnp.where(line < side, left[near], right[near]))
    extra.append(early[EARLY_ROWS:])
    used = BLOCK_ROWS + 1 + 5 * levels
    store[BLOCK_ROWS:] = jnp.concatenate(
        extra + [jnp.zeros((store.shape[0] - used, size), F32)], axis=0
    )
    out[...] = store[...].astype(BF16)


def ocean_halos(counts, tile_place, member_place, shape, messages, tails):
    tiles, subs, levs = counts
    levels, rows, width = shape
    my_tile, me = tile_place(), member_place()
    halo = {}
    extras = [m[BLOCK_ROWS:] for m in messages]
    ends = [t[2 * rows :] for t in tails]
    for dt in (-1, 1):
        extra = nearby(my_tile, tiles, dt, extras)
        corners, strips = extra[1 : 1 + levels], extra[1 + levels : 1 + 5 * levels]
        halo[dt, 0] = strips[: 2 * levels] if dt < 0 else strips[2 * levels :]
        at = rows - 1 if dt < 0 else 0
        for ds in (-1, 1):
            lane_at = at if ds < 0 else rows + at
            halo[dt, ds] = corners[:, lane_at : lane_at + 1]
    for ds in (-1, 1):
        beside = nearby(me, subs * levs, ds * levs, ends)[: 2 * levels]
        halo[0, ds] = roll(beside, -rows, 1) if ds > 0 else beside
    return halo


def biharmonic(x, top, bottom, left, right, corner):
    rows, width = x.shape
    row, lane = iota(x.shape, 0), iota(x.shape, 1)
    line = iota((1, width), 1)

    def laplacian(x, top, bottom, left, right):
        up = jnp.where(row == 0, top, roll(x, 1, 0))
        down = jnp.where(row == rows - 1, bottom, roll(x, -1, 0))
        west = jnp.where(lane == 0, left, roll(x, 1, 1))
        east = jnp.where(lane == width - 1, right, roll(x, -1, 1))
        return up + down + west + east - 4.0 * x

    def ring_row(mid, out_row, in_row, dt):
        west = jnp.where(line == 0, corner[dt, -1], roll(mid, 1, 1))
        east = jnp.where(line == width - 1, corner[dt, 1], roll(mid, -1, 1))
        return west + east + out_row + in_row - 4.0 * mid

    def ring_col(mid, out_col, in_col, ds):
        up = jnp.concatenate([corner[-1, ds], mid[:-1]], axis=0)
        down = jnp.concatenate([mid[1:], corner[1, ds]], axis=0)
        return up + down + out_col + in_col - 4.0 * mid

    return laplacian(
        laplacian(x, top[0], bottom[0], left[0], right[0]),
        ring_row(*top, x[0:1], -1),
        ring_row(*bottom, x[rows - 1 :], 1),
        ring_col(*left, x[:, 0:1], -1),
        ring_col(*right, x[:, width - 1 :], 1),
    )


def spread_out(count):
    return sorted(range(count), key=lambda k: (k == count // 2, k))


def split_refs(tiles, members, refs, outs):
    messages = [refs[spread_out(tiles).index(k)] for k in range(tiles)]
    chunks = refs[tiles : tiles + members]
    return messages, tails_of(chunks, refs[tiles + members : -outs]), refs[-outs:]


def relay_kernel(counts, tile_place, member_place, water, mixing, *refs):
    tiles, subs, levs = counts
    outs = 1 if levs == 1 else 2
    messages, tails, outs = split_refs(tiles, subs * levs, refs, outs)
    for k in range(tiles):
        outs[0][k * BLOCK_ROWS : (k + 1) * BLOCK_ROWS] = messages[k][0:BLOCK_ROWS]
    levels, rows, width = water.shape
    halo = ocean_halos(counts, tile_place, member_place, water.shape, messages, tails)

    def both(strip):
        near = sum(strip[2 * l : 2 * l + 1] for l in range(levels))
        far = sum(strip[2 * l + 1 : 2 * l + 2] for l in range(levels))
        return near, far

    def as_columns(strip):
        near, far = both(strip)
        across = jnp.concatenate([near, far] + [jnp.zeros_like(near)] * 6, axis=0).T
        return across[0:rows, 0:1], across[0:rows, 1:2]

    corner = {
        (dt, ds): jnp.sum(halo[dt, ds], axis=0, keepdims=True) for dt in (-1, 1) for ds in (-1, 1)
    }
    x = sum(water[l] for l in range(levels))
    twice = biharmonic(
        x, both(halo[-1, 0]), both(halo[1, 0]), as_columns(halo[0, -1]), as_columns(halo[0, 1]), corner
    )
    top = (x - mixing[...] * twice) / (levels * levs)
    if levs == 1:
        outs[0][tiles * BLOCK_ROWS :] = top.astype(BF16)
    else:
        outs[1][...] = top


def ocean_kernel(counts, tile_place, member_place, water, mixing, *refs):
    tiles, subs, levs = counts
    messages, tails, (warm_o,) = split_refs(tiles, subs * levs, refs, 1)
    levels, rows, width = water.shape
    halo = ocean_halos(counts, tile_place, member_place, water.shape, messages, tails)
    left, right = halo[0, -1].T, halo[0, 1].T
    for l in range(levels):
        x = water[l]
        pair = (2 * l, 2 * l + 1)
        twice = biharmonic(
            x,
            [halo[-1, 0][i : i + 1] for i in pair],
            [halo[1, 0][i : i + 1] for i in pair],
            [left[0:rows, i : i + 1] for i in pair],
            [right[0:rows, i : i + 1] for i in pair],
            {(dt, ds): halo[dt, ds][l : l + 1] for dt in (-1, 1) for ds in (-1, 1)},
        )
        warm_o[l] = x - mixing[...] * twice


def ice_kernel(
    tiles, members, side, table, viscous, gain, drag, conduct, current, speed, push, *refs
):
    chunks, relays = refs[:members], refs[members : 2 * members]
    out, own_o, beside_o, rims, names, named, field = refs[2 * members :]
    load_names = pltpu.make_async_copy(table, names, named)
    load_names.start()
    size = viscous.shape[0]
    depth = chunks[0].shape[1]
    for k in range(tiles):
        for m in range(members):
            block = relays[m][k * BLOCK_ROWS : (k + 1) * BLOCK_ROWS]
            rims[k * members + m, 0:BLOCK_ROWS] = block.astype(F32)
            rims[k * members + m, BLOCK_ROWS:] = jnp.zeros((2 * DEPTH, size), F32)
    half = DEPTH
    high = 2 * DEPTH
    sub = iota((high, size), 0)
    lane = iota((high, size), 1)
    edge = (sub & (half - 1)) == 0
    turn = jnp.where(sub < half, CORIOLIS_TURN, -CORIOLIS_TURN).astype(F32)
    first, last = lane == 0, lane == size - 1

    def load(device, side, mask, with_push=True):
        start = side * EARLY_SIDE
        velocity = rims[device, start : start + high] * mask
        if not with_push:
            return velocity
        both = rims[device, start + high : start + 2 * high]
        visc = jnp.where(sub < half, both, roll(both, half, 0))
        scale = jnp.where(sub < half, roll(both, 1 - half, 0), roll(both, 1, 0)) * mask
        start = EARLY_ROWS + side * LATE_SIDE
        late = rims[device, start : start + high]
        pushed = jnp.where(sub < half, late, roll(late, 1, 0))
        return [velocity, visc, scale, pushed]

    def follow(device, side):
        name = names[device, side]
        return jnp.where(name >= 0, name, 0), name >= 0

    def step(state, left, right, inner, outer):
        c, visc, scale, pushed = state
        spread = left + right + inner + outer - 4.0 * c
        return scale * (c + visc * spread + pushed + turn * roll(c, half, 0))

    base = high
    for c in range(2):
        field[0, c, base : base + size] = speed[c]
    load_names.wait()
    def along(cells, before, beyond):
        left = jnp.where(first, roll(before, 1, 1), roll(cells, 1, 1))
        return left, jnp.where(last, roll(beyond, -1, 1), roll(cells, -1, 1))

    def step_end(state, inside, across, away):
        cells = state[0]
        toward = jnp.where(first if away > 0 else last, roll(inside, away, 1), roll(cells, away, 1))
        inner = jnp.where(edge, across, roll(cells, 1, 0))
        return step(state, toward, roll(cells, -away, 1), inner, roll(cells, -1, 0))

    halos = [[] for _ in range(SUBCYCLES)]
    for q in range(4):
        x, has_x = follow(0, q)
        halo = load(x, OPPOSITE[q], flag(has_x))
        own = load(0, q, 1.0)
        ends = []
        for s in LATERAL[q]:
            y, has_y = follow(x, s)
            z, has_z = follow(y, OPPOSITE[q])
            w, has_w = follow(z, OPPOSITE[s])
            u, has_u = follow(0, s)
            v, has_v = follow(u, q)
            ends.append(
                [
                    load(y, OPPOSITE[q], flag(has_y)),
                    load(z, q, flag(has_z)),
                    load(w, q, flag(has_w), with_push=False),
                    load(u, q, flag(has_u)),
                    load(v, OPPOSITE[q], flag(has_v), with_push=False),
                ]
            )
        (y_hi, z_hi, w_hi, u_hi, v_hi), (y_lo, z_lo, w_lo, u_lo, v_lo) = ends
        for t in range(SUBCYCLES):
            halos[t].append(halo[0])
            if t == SUBCYCLES - 1:
                break
            c, o = halo[0], own[0]
            left, right = along(c, y_lo[0], y_hi[0])
            inner = jnp.where(edge, o, roll(c, 1, 0))
            new_halo = step(halo, left, right, inner, roll(c, -1, 0))
            if t < SUBCYCLES - 2:
                left, right = along(o, u_lo[0], u_hi[0])
                inner = jnp.where(edge, c, roll(o, 1, 0))
                new_own = step(own, left, right, inner, roll(o, -1, 0))
                new_y = step_end(y_hi, c, z_hi[0], 1), step_end(y_lo, c, z_lo[0], -1)
            if t < SUBCYCLES - 3:
                z_hi[0], z_lo[0] = (
                    step_end(z_hi, w_hi, y_hi[0], 1),
                    step_end(z_lo, w_lo, y_lo[0], -1),
                )
                u_hi[0], u_lo[0] = step_end(u_hi, o, v_hi, 1), step_end(u_lo, o, v_lo, -1)
            halo[0] = new_halo
            if t < SUBCYCLES - 2:
                own[0] = new_own
                y_hi[0], y_lo[0] = new_y
    columns = [jnp.where(edge, cells[2], roll(cells[3], 1, 0)).T for cells in halos]

    warm = remap_forward(chunks, [[r[r.shape[0] - side :]] for r in relays], side, depth)
    heat = (conduct[...] * warm).astype(BF16)

    for t in range(SUBCYCLES):
        cells, sides = halos[t], columns[t]
        now, later = t % 2, (t + 1) % 2
        for c in range(2):
            at = c * half
            field[now, c, base + size : base + size + 1] = cells[0][at : at + 1]
            field[now, c, base - 1 : base] = cells[1][at : at + 1]
        for i in range(size // high):
            rows = slice(i * high, (i + 1) * high)
            held = [field[now, c, base + i * high : base + (i + 1) * high] for c in range(2)]
            for c in range(2):
                v, at = held[c], base + i * high
                up = field[now, c, at + 1 : at + 1 + high]
                down = field[now, c, at - 1 : at - 1 + high]
                east = jnp.where(last, sides[rows, c * half : c * half + 1], roll(v, -1, 1))
                west = jnp.where(first, sides[rows, c * half + 1 : c * half + 2], roll(v, 1, 1))
                spread = up + down + east + west - 4.0 * v
                turned = (CORIOLIS_TURN if c == 0 else -CORIOLIS_TURN) * held[1 - c]
                new = gain[rows] * (v + viscous[rows] * spread + push[c, rows] + turned)
                if t == SUBCYCLES - 1:
                    out[c, rows] = new
                else:
                    field[later, c, at : at + high] = new
    stress = [(drag[...] * (out[c] - current[c])).astype(BF16) for c in range(2)]
    return_fluxes([heat, *stress], chunks, side, depth, own_o, beside_o)


def return_fluxes(fluxes, chunks, side, depth, own, beside):
    size = fluxes[0].shape[0]
    wide = jnp.concatenate(fluxes, axis=1)
    step = 3 * side
    down = jnp.concatenate([chunk[0:side] for chunk in chunks], axis=0)
    parts = jnp.dot(down, wide, preferred_element_type=F32).astype(BF16)
    for k, chunk in enumerate(chunks):
        part = parts[k * side : (k + 1) * side]
        part = jnp.concatenate([part[:, c * size : (c + 1) * size] for c in range(3)], axis=0)
        reply = jnp.dot(part, chunk[side : side + depth], preferred_element_type=F32)
        at = k // 2 * step
        if k % 2:
            beside[at : at + step] = reply.astype(BF16)
        else:
            own[at : at + step] = reply


def pair_kernel(own, beside, *outs):
    step = outs[0].shape[0]
    for k, out in enumerate(outs):
        at = (k + 1) * step
        out[...] = (own[at : at + step] + beside[at : at + step].astype(F32)).astype(BF16)


def settle_kernel(speed, own, beside, flat_o, total_o, flat, left):
    size = speed.shape[1]
    for c in range(2):
        flat[pl.ds(c, size, stride=2), :] = speed[c]
    copy = pltpu.make_async_copy(flat, flat_o, left)
    copy.start()
    rows = total_o.shape[0]
    total_o[...] = own[0:rows] + beside[0:rows].astype(F32)
    copy.wait()


def finish_kernel(warm, currents, total, *refs):
    replies, (heat_o, current_o, heat_v, current_v, left) = refs[:-5], refs[-5:]
    copies = [
        pltpu.make_async_copy(heat_v, heat_o, left.at[0]),
        pltpu.make_async_copy(current_v, current_o, left.at[1]),
    ]
    side = currents.shape[1]
    total = total[...]
    for reply in replies:
        total = total + reply[...].astype(F32)
    heat = THERMAL_DIFFUSE * total[0:side]
    for l in range(warm.shape[0]):
        heat_v[l] = warm[l] + heat
    copies[0].start()
    for c in range(2):
        current_v[c] = currents[c] + STRESS_MIXING * total[(c + 1) * side : (c + 2) * side]
    copies[1].start()
    for copy in copies:
        copy.wait()


def shards(
    water_heat_state,
    diffusion_coefficient,
    upper_current_vector,
    remap_blocks,
    remap_rows,
    remap_cols,
    neighbors,
    thickness,
    concentration,
    ice_velocity,
    wind_stress,
):
    tile_count, sub_count, lev_count = (lax.axis_size(a) for a in ("tile", "sub", "lev"))
    group = sub_count * lev_count
    devices = tile_count * group
    group_axes = ("sub", "lev")
    member_axes = ("tile", "sub", "lev")
    levels, side, width = water_heat_state.shape
    pairs, size = remap_rows.shape[1:3]
    categories = thickness.shape[2]

    def tile_place():
        return lax.axis_index("tile")

    def member_place():
        return lax.axis_index("sub") * lev_count + lax.axis_index("lev")

    def device_place():
        return lax.axis_index("tile") * group + member_place()

    def swap(value, axes, count):
        got = {0: value}
        for k in range(1, count):
            got[k] = lax.ppermute(value, axes, [(i, i ^ k) for i in range(count)])
        return [got[k] for k in range(count)]

    def swap_chips(value):
        return {0: value} | {
            k: lax.ppermute(value, group_axes, [(i, i ^ k) for i in range(group)])
            for k in range(2, group, 2)
        }

    def swap_cores(got):
        beside = [(i, i ^ 1) for i in range(group)]
        got = got | {k + 1: lax.ppermute(got[k], group_axes, beside) for k in got}
        return [got[k] for k in range(group)]

    def swap_each(values):
        got = {0: values[0]}
        for k in range(1, group):
            got[k] = lax.ppermute(values[k], group_axes, [(i, i ^ k) for i in range(group)])
        return [got[k] for k in range(group)]

    def shape(*dims, dtype=F32):
        return jax.ShapeDtypeStruct(dims, dtype)

    def interleaved(value):
        return value.reshape(2, size, size).transpose(1, 0, 2).reshape(2 * size, size)

    plane = shape(size, size)
    planes = shape(2, size, size)
    wind = interleaved(wind_stress)

    tail_rows = -(-(2 * levels + 1) // TILE_ROWS) * TILE_ROWS
    pair_rows = side + width
    chunk_rows = pair_rows + 2 * side + tail_rows
    sent = call(
        functools.partial(forward_kernel, (devices, group, member_place)),
        [
            shape(pair_rows if k > 1 and k % 2 else chunk_rows, width, dtype=BF16)
            for k in range(group)
        ],
        (
            neighbors,
            remap_blocks,
            remap_rows[0].swapaxes(1, 2),
            remap_cols[0],
            upper_current_vector,
            water_heat_state,
        ),
        scratch=[
            pltpu.SMEM(neighbors.shape, jnp.int32),
            pltpu.SMEM((1, pairs), jnp.int32),
            pltpu.VMEM((2, side, width), F32),
            pltpu.VMEM((pairs, pair_rows, width), BF16),
            pltpu.VMEM((levels, side, width), F32),
            pltpu.VMEM((chunk_rows - pair_rows, width), BF16),
            pltpu.VMEM((1 if pairs == group else group, pair_rows, width), BF16),
            pltpu.SemaphoreType.DMA((6,)),
            pltpu.SemaphoreType.DMA((2 * group,)),
        ],
        hbm=(0, 1, 2, 3, 4, 5),
        grant=60 * 2**20,
        micros=10,
    )
    chunks = swap_each(sent)
    hops = [
        lax.ppermute(chunks[k][pair_rows:], group_axes, [(i, i ^ 1) for i in range(group)])
        for k in range(2, group, 2)
    ]

    early, viscous, gain, step_mass, drag, conduct, speed = call(
        rims_kernel,
        [shape(EARLY_ROWS + 4 * levels, size)] + [plane] * 5 + [planes],
        (
            thickness.reshape(categories, size, size),
            concentration.reshape(categories, size, size),
            interleaved(ice_velocity),
            water_heat_state,
        ),
    )
    extra_rows = -(-(1 + 5 * levels) // TILE_ROWS) * TILE_ROWS
    message, current_ice, push = call(
        functools.partial(forcing_kernel, group, side, levels, sub_count, member_place),
        [shape(BLOCK_ROWS + extra_rows, size, dtype=BF16), planes, planes],
        (step_mass, drag, wind, early, *chunks[::-1], *hops),
        scratch=[pltpu.VMEM((BLOCK_ROWS + extra_rows, size), F32)],
    )
    messages = swap(message, "tile", tile_count)

    counts = (tile_count, sub_count, lev_count)
    ocean = (*(messages[k] for k in spread_out(tile_count)), *chunks, *hops)
    relay_rows = tile_count * BLOCK_ROWS
    relay_shapes = [shape(relay_rows + (side if lev_count == 1 else 0), size, dtype=BF16)]
    if lev_count > 1:
        relay_shapes.append(shape(side, width))
    relay, *top = call(
        functools.partial(relay_kernel, counts, tile_place, member_place),
        relay_shapes,
        (water_heat_state, diffusion_coefficient, *ocean),
    )
    if lev_count > 1:
        relay = jnp.concatenate([relay, lax.psum(top[0], "lev").astype(BF16)], axis=0)
    relays = swap_chips(relay)

    mixing, _ = lax.optimization_barrier((diffusion_coefficient, relay))
    (warm,) = call(
        functools.partial(ocean_kernel, counts, tile_place, member_place),
        [shape(levels, side, width)],
        (water_heat_state, mixing, *ocean),
    )
    far = sorted(k for k in relays if k)
    relayed, _ = lax.optimization_barrier(([relays[k] for k in far], warm))
    relays = swap_cores({0: relay} | dict(zip(far, relayed)))

    names = jnp.stack([m[BLOCK_ROWS, : 8 * group] for m in messages])
    names = names.reshape(devices, 8).astype(jnp.int32)
    table = names[:, 0:4] * 128 + names[:, 4:8]
    table = jnp.where(table < 0, -1, table ^ device_place())
    step = 3 * side
    speed, own, beside = call(
        functools.partial(ice_kernel, tile_count, group, side),
        [
            planes,
            shape(group // 2 * step, width),
            shape(group // 2 * step, width, dtype=BF16),
        ],
        (table, viscous, gain, drag, conduct, current_ice, speed, push, *chunks, *relays),
        scratch=[
            pltpu.VMEM((devices, BLOCK_ROWS + 2 * DEPTH, size), F32),
            pltpu.SMEM((devices, 4), jnp.int32),
            pltpu.SemaphoreType.DMA,
            pltpu.VMEM((2, 2, size + 4 * DEPTH, size), F32),
        ],
        hbm=(0,),
    )
    beside = lax.ppermute(beside, group_axes, [(i, i ^ 1) for i in range(group)])
    paired = call(
        pair_kernel, [shape(step, width, dtype=BF16)] * (group // 2 - 1), (own, beside)
    )
    replies = [
        lax.ppermute(value, group_axes, [(i, i ^ (2 * k + 2)) for i in range(group)])
        for k, value in enumerate(paired)
    ]
    flat, total = call(
        settle_kernel,
        [shape(2 * size, size), shape(step, width)],
        (speed, own, beside),
        scratch=[pltpu.VMEM((2 * size, size), F32), pltpu.SemaphoreType.DMA],
        out_spaces=(pltpu.HBM, pltpu.VMEM),
    )
    if lev_count > 1:
        total = lax.psum(total + sum(r.astype(F32) for r in replies), "lev")
        replies = []
    heat, current = call(
        finish_kernel,
        [shape(levels, side, width), shape(2, side, width)],
        (warm, upper_current_vector, total, *replies),
        scratch=[
            pltpu.VMEM((levels, side, width), F32),
            pltpu.VMEM((2, side, width), F32),
            pltpu.SemaphoreType.DMA((2,)),
        ],
        out_space=pltpu.HBM,
    )
    velocity = flat.reshape(size, 2, size).transpose(1, 0, 2).reshape(1, 1, 2, size * size)
    return heat, current, velocity


def solution(mesh):
    member = ("tile", "sub", "lev")
    whole = ("copies",) + member
    ice = P(None, whole, None, None)
    water = P("lev", ("copies", "tile"), "sub")
    current = P(None, ("copies", "tile"), "sub")
    return jax.shard_map(
        shards,
        mesh=mesh,
        in_specs=(
            water,
            P("tile", "sub"),
            current,
            P(member, None),
            P(member, None, None, None),
            P(member, None, None, None),
            P(None, member, None),
            ice,
            ice,
            ice,
            ice,
        ),
        out_specs=(water, current, ice),
        check_vma=False,
    )
```

```python
import functools

import jax
import jax.numpy as jnp
from jax import lax
from jax.experimental import pallas as pl
from jax.experimental.pallas import tpu as pltpu
from jax.sharding import PartitionSpec as P

SUBCYCLES = 4
STRENGTH_DECAY = 5.0
VISCOUS_STEP = 0.24
SUBCYCLE_STEP = 0.5
CORIOLIS_TURN = 0.1
BASE_MASS = 0.5
HEAT_RATE = 0.2
THIN_ICE = 0.1
THERMAL_DIFFUSE = 0.5
STRESS_MIXING = 0.5

OPPOSITE = (1, 0, 3, 2)
LATERAL = ((2, 3), (2, 3), (0, 1), (0, 1))
DEPTH = SUBCYCLES
EARLY_DEPTHS = (DEPTH, DEPTH, DEPTH - 1, DEPTH - 1)
LATE_DEPTHS = (DEPTH - 1, DEPTH - 1)
EARLY_SIDE, LATE_SIDE = sum(EARLY_DEPTHS), sum(LATE_DEPTHS)
EARLY_ROWS = 4 * EARLY_SIDE
BLOCK_ROWS = EARLY_ROWS + 4 * LATE_SIDE
TILE_ROWS = 16
F32 = jnp.float32
BF16 = jnp.bfloat16
VMEM_LIMIT = 16 * 1024 * 1024
FLOPS_PER_MICRO = 1.15e9


def call(
    kernel, outs, args, scratch=(), smem=(), hbm=(), out_space=pltpu.VMEM, out_spaces=None,
    grant=VMEM_LIMIT, micros=0.01,
):
    def space(i):
        return pltpu.SMEM if i in smem else pltpu.HBM if i in hbm else pltpu.VMEM

    specs = [pl.BlockSpec(memory_space=space(i)) for i in range(len(args))]
    size = sum(a.size * a.dtype.itemsize for a in args)
    return pl.pallas_call(
        kernel,
        out_shape=outs,
        in_specs=specs,
        out_specs=(
            jax.tree.map(lambda _: pl.BlockSpec(memory_space=out_space), outs)
            if out_spaces is None
            else [pl.BlockSpec(memory_space=space) for space in out_spaces]
        ),
        scratch_shapes=list(scratch),
        compiler_params=pltpu.CompilerParams(vmem_limit_bytes=grant),
        cost_estimate=pl.CostEstimate(
            flops=int(micros * FLOPS_PER_MICRO), bytes_accessed=size, transcendentals=0
        ),
    )(*args)


def iota(shape, axis):
    return lax.broadcasted_iota(jnp.int32, shape, axis)


def roll(x, shift, axis):
    return pltpu.roll(x, shift % x.shape[axis], axis)


def flag(condition):
    return jnp.where(condition, 1.0, 0.0).astype(F32)


def ocean_columns(water):
    levels, rows, width = water.shape
    lane = iota((rows, width), 1)
    line = iota((1, width), 1)
    mixed = jnp.zeros((rows, width), F32)
    for l in range(levels):
        mixed = jnp.where(lane // 4 == l, roll(water[l], 2 + 4 * l, 1), mixed)
    across = jnp.concatenate([mixed, jnp.zeros((width - rows, width), F32)], axis=0).T
    beside = []
    for l in range(levels):
        for j in range(2):
            last = across[4 * l + 1 - j : 4 * l + 2 - j]
            lead = across[4 * l + 2 + j : 4 * l + 3 + j]
            beside.append(jnp.where(line < rows, last, roll(lead, rows, 1)))
    return beside


def forward_kernel(group, links_h, blocks_h, rows_h, cols_h, currents_h, water_h, *refs):
    devices, members, place = group
    outs, fields_o, scratch = refs[:members], refs[members], refs[members + 1 :]
    links, blocks, currents, weights, water, fields, kept, arrived, left = scratch
    pairs, side, width = rows_h.shape
    both = weights.shape[1]
    loads = [
        pltpu.make_async_copy(source, target, arrived.at[i])
        for i, (source, target) in enumerate(
            (
                (links_h, links),
                (blocks_h, blocks),
                (currents_h, currents),
                (rows_h, weights.at[:, pl.ds(0, side)]),
                (cols_h, weights.at[:, pl.ds(side, both - side)]),
                (water_h, water),
            )
        )
    ]
    for load in loads:
        load.start()
    for i in (1, 3, 4):
        loads[i].wait()
    me = place()
    owners = [lax.rem(lax.rem(blocks[0, m], devices), members) for m in range(pairs)]
    copies = []
    for k, out in enumerate(outs):
        partner = me ^ k
        pair = jnp.int32(0)
        for m in range(pairs):
            pair = jnp.where(owners[m] == partner, m, pair)
        source = weights.at[pair]
        if pairs < members:
            found = sum(flag(owners[m] == partner) for m in range(pairs))
            kept[k] = (weights[pair].astype(F32) * found).astype(BF16)
            source = kept.at[k]
        copies.append(pltpu.make_async_copy(source, out.at[pl.ds(0, both)], left.at[2 * k]))
        copies[-1].start()
    for i in (0, 2, 5):
        loads[i].wait()
    for c in range(2):
        fields[c * side : (c + 1) * side] = currents[c].astype(BF16)
    lane = iota((1, width), 1)
    numbers = jnp.zeros((1, width), F32)
    for q in range(4):
        numbers = jnp.where(lane == q, (links[0, 0, q] >> 7).astype(F32), numbers)
        numbers = jnp.where(lane == 4 + q, (links[0, 0, q] & 127).astype(F32), numbers)
    ends = ocean_columns(water) + [numbers]
    blank = jnp.zeros((fields.shape[0] - 2 * side - len(ends), width), F32)
    fields[2 * side :] = jnp.concatenate(ends + [blank], axis=0).astype(BF16)
    for k, out in enumerate(outs):
        if out.shape[0] > both:
            target = out.at[pl.ds(both, fields.shape[0])]
            copies.append(pltpu.make_async_copy(fields, target, left.at[2 * k + 1]))
            copies[-1].start()
    copies.append(pltpu.make_async_copy(fields, fields_o, left.at[2 * members]))
    copies[-1].start()
    for copy in copies:
        copy.wait()


def put_side_rims(store, planes, depths, at):
    size = planes[0].shape[0]
    lane = iota((size, size), 1)
    mixed = jnp.zeros((size, size), F32)
    for i, plane in enumerate(planes):
        turned = roll(plane, DEPTH + 2 * DEPTH * i, 1)
        mixed = jnp.where(lane // (2 * DEPTH) == i, turned, mixed)
    across = mixed.T
    base = 0
    for i, plane in enumerate(planes):
        for k in range(depths[i]):
            east = 2 * DEPTH * i + DEPTH - 1 - k
            west = 2 * DEPTH * i + DEPTH + k
            store[at(0) + base : at(0) + base + 1] = plane[size - 1 - k : size - k]
            store[at(1) + base : at(1) + base + 1] = plane[k : k + 1]
            store[at(2) + base : at(2) + base + 1] = across[east : east + 1]
            store[at(3) + base : at(3) + base + 1] = across[west : west + 1]
            base += 1


def rims_kernel(
    thick, conc, ice, water, out, viscous_o, gain_o, mass_o, drag_o, conduct_o,
    speed_o,
):
    size = thick.shape[1]
    cover = jnp.zeros((size, size), F32)
    volume = jnp.zeros((size, size), F32)
    conduct = jnp.zeros((size, size), F32)
    for c in range(thick.shape[0]):
        h, a = thick[c], conc[c]
        cover = cover + a
        volume = volume + a * h
        conduct = conduct + a / (h + THIN_ICE)
    mass = volume + BASE_MASS
    viscous = VISCOUS_STEP * (volume * jnp.exp(-STRENGTH_DECAY * (1.0 - cover))) / mass
    step_mass = SUBCYCLE_STEP / mass
    gain = 1.0 / (1.0 + step_mass * cover)
    speed_x = ice[pl.ds(0, size, stride=2), :]
    speed_y = ice[pl.ds(1, size, stride=2), :]
    viscous_o[...] = viscous
    gain_o[...] = gain
    mass_o[...] = step_mass
    drag_o[...] = cover
    conduct_o[...] = -HEAT_RATE * conduct
    speed_o[0] = speed_x
    speed_o[1] = speed_y
    put_side_rims(
        out, [speed_x, speed_y, viscous, gain], EARLY_DEPTHS, lambda side: side * EARLY_SIDE
    )
    levels, rows, width = water.shape
    for l in range(levels):
        for j in range(2):
            at = EARLY_ROWS + 2 * l + j
            out[at : at + 1] = water[l, rows - 1 - j : rows - j]
            out[at + 2 * levels : at + 2 * levels + 1] = water[l, j : j + 1]


def nearby(me, members, distance, arrays):
    at = me + distance
    inside = (at >= 0) & (at < members)
    found = 0.0
    for k in range(1, members):
        found = found + arrays[k].astype(F32) * flag(inside & ((me ^ k) == at))
    return found


def remap_forward(chunks, field_rows, side, depth):
    total = None
    for chunk, fields in zip(chunks, field_rows):
        down = chunk[0:side]
        right = chunk[side : side + depth]
        wide = jnp.concatenate(fields, axis=1) if len(fields) > 1 else fields[0]
        part = lax.dot_general(down, wide, (((0,), (0,)), ((), ())), preferred_element_type=F32)
        part = part.astype(BF16)
        width = fields[0].shape[1]
        if len(fields) > 1:
            part = jnp.concatenate(
                [part[:, c * width : (c + 1) * width] for c in range(len(fields))], axis=0
            )
        piece = lax.dot_general(part, right, (((1,), (1,)), ((), ())), preferred_element_type=F32)
        piece = piece.astype(BF16).astype(F32)
        total = piece if total is None else total + piece
    return total


def tails_of(chunks, others):
    at = min(c.shape[0] for c in chunks)
    return [c[at:] for c in chunks[:2]] + [other[...] for other in others]


def forcing_kernel(group, side, levels, subs, place, mass, drag, wind, early, *refs):
    hops, chunks = refs[: group - 2], refs[group - 2 : 2 * group - 2]
    out, current_o, push_o, store = refs[2 * group - 2 :]
    size = mass.shape[0]
    depth = chunks[0].shape[1]
    tails = tails_of(chunks, hops)
    fields = [[t[0:side], t[side : 2 * side]] for t in tails]
    total = remap_forward(chunks, fields, side, depth)
    pushes = []
    for c in range(2):
        current = total[c * size : (c + 1) * size]
        current_o[c] = current
        force = wind[pl.ds(c, size, stride=2), :]
        push = mass[...] * (force + drag[...] * current)
        push_o[c] = push
        pushes.append(push)
    store[0:EARLY_ROWS] = early[0:EARLY_ROWS]
    put_side_rims(store, pushes, LATE_DEPTHS, lambda side: EARLY_ROWS + side * LATE_SIDE)
    tail = [t[2 * side :].astype(F32) for t in tails]
    line = iota((1, size), 1)
    names = jnp.zeros((1, size), F32)
    for k in range(group):
        names = jnp.where(line // 8 == k, roll(tail[k][2 * levels : 2 * levels + 1], 8 * k, 1), names)
    me, step = place(), group // subs
    left, right = (nearby(me, group, d * step, tail) for d in (-1, 1))
    extra = [names]
    for l in range(levels):
        near = slice(2 * l, 2 * l + 1)
        extra.append(jnp.where(line < side, left[near], right[near]))
    extra.append(early[EARLY_ROWS:])
    used = BLOCK_ROWS + 1 + 5 * levels
    store[BLOCK_ROWS:] = jnp.concatenate(
        extra + [jnp.zeros((store.shape[0] - used, size), F32)], axis=0
    )
    out[...] = store[...].astype(BF16)


def ocean_halos(counts, tile_place, member_place, shape, messages, tails):
    tiles, subs, levs = counts
    levels, rows, width = shape
    my_tile, me = tile_place(), member_place()
    halo = {}
    extras = [m[BLOCK_ROWS:] for m in messages]
    ends = [t[2 * rows :] for t in tails]
    for dt in (-1, 1):
        extra = nearby(my_tile, tiles, dt, extras)
        corners, strips = extra[1 : 1 + levels], extra[1 + levels : 1 + 5 * levels]
        halo[dt, 0] = strips[: 2 * levels] if dt < 0 else strips[2 * levels :]
        at = rows - 1 if dt < 0 else 0
        for ds in (-1, 1):
            lane_at = at if ds < 0 else rows + at
            halo[dt, ds] = corners[:, lane_at : lane_at + 1]
    for ds in (-1, 1):
        beside = nearby(me, subs * levs, ds * levs, ends)[: 2 * levels]
        halo[0, ds] = roll(beside, -rows, 1) if ds > 0 else beside
    return halo


def biharmonic(x, top, bottom, left, right, corner):
    rows, width = x.shape
    row, lane = iota(x.shape, 0), iota(x.shape, 1)
    line = iota((1, width), 1)

    def laplacian(x, top, bottom, left, right):
        up = jnp.where(row == 0, top, roll(x, 1, 0))
        down = jnp.where(row == rows - 1, bottom, roll(x, -1, 0))
        west = jnp.where(lane == 0, left, roll(x, 1, 1))
        east = jnp.where(lane == width - 1, right, roll(x, -1, 1))
        return up + down + west + east - 4.0 * x

    def ring_row(mid, out_row, in_row, dt):
        west = jnp.where(line == 0, corner[dt, -1], roll(mid, 1, 1))
        east = jnp.where(line == width - 1, corner[dt, 1], roll(mid, -1, 1))
        return west + east + out_row + in_row - 4.0 * mid

    def ring_col(mid, out_col, in_col, ds):
        up = jnp.concatenate([corner[-1, ds], mid[:-1]], axis=0)
        down = jnp.concatenate([mid[1:], corner[1, ds]], axis=0)
        return up + down + out_col + in_col - 4.0 * mid

    return laplacian(
        laplacian(x, top[0], bottom[0], left[0], right[0]),
        ring_row(*top, x[0:1], -1),
        ring_row(*bottom, x[rows - 1 :], 1),
        ring_col(*left, x[:, 0:1], -1),
        ring_col(*right, x[:, width - 1 :], 1),
    )


def spread_out(count):
    return sorted(range(count), key=lambda k: (k == count // 2, k))


def split_refs(tiles, members, refs, outs):
    messages = [refs[spread_out(tiles).index(k)] for k in range(tiles)]
    chunks = refs[tiles : tiles + members]
    return messages, tails_of(chunks, refs[tiles + members : -outs]), refs[-outs:]


def relay_kernel(counts, tile_place, member_place, water, mixing, *refs):
    tiles, subs, levs = counts
    outs = 1 if levs == 1 else 2
    messages, tails, outs = split_refs(tiles, subs * levs, refs, outs)
    for k in range(tiles):
        outs[0][k * BLOCK_ROWS : (k + 1) * BLOCK_ROWS] = messages[k][0:BLOCK_ROWS]
    levels, rows, width = water.shape
    halo = ocean_halos(counts, tile_place, member_place, water.shape, messages, tails)

    def both(strip):
        near = sum(strip[2 * l : 2 * l + 1] for l in range(levels))
        far = sum(strip[2 * l + 1 : 2 * l + 2] for l in range(levels))
        return near, far

    def as_columns(strip):
        near, far = both(strip)
        across = jnp.concatenate([near, far] + [jnp.zeros_like(near)] * 6, axis=0).T
        return across[0:rows, 0:1], across[0:rows, 1:2]

    corner = {
        (dt, ds): jnp.sum(halo[dt, ds], axis=0, keepdims=True) for dt in (-1, 1) for ds in (-1, 1)
    }
    x = sum(water[l] for l in range(levels))
    twice = biharmonic(
        x, both(halo[-1, 0]), both(halo[1, 0]), as_columns(halo[0, -1]), as_columns(halo[0, 1]), corner
    )
    top = (x - mixing[...] * twice) / (levels * levs)
    if levs == 1:
        outs[0][tiles * BLOCK_ROWS :] = top.astype(BF16)
    else:
        outs[1][...] = top


def ocean_kernel(counts, tile_place, member_place, water, mixing, *refs):
    tiles, subs, levs = counts
    messages, tails, (warm_o,) = split_refs(tiles, subs * levs, refs, 1)
    levels, rows, width = water.shape
    halo = ocean_halos(counts, tile_place, member_place, water.shape, messages, tails)
    left, right = halo[0, -1].T, halo[0, 1].T
    for l in range(levels):
        x = water[l]
        pair = (2 * l, 2 * l + 1)
        twice = biharmonic(
            x,
            [halo[-1, 0][i : i + 1] for i in pair],
            [halo[1, 0][i : i + 1] for i in pair],
            [left[0:rows, i : i + 1] for i in pair],
            [right[0:rows, i : i + 1] for i in pair],
            {(dt, ds): halo[dt, ds][l : l + 1] for dt in (-1, 1) for ds in (-1, 1)},
        )
        warm_o[l] = x - mixing[...] * twice


def ice_kernel(
    tiles, members, side, table, viscous, gain, drag, conduct, current, speed, push, *refs
):
    chunks, relays = refs[:members], refs[members : 2 * members]
    out, own_o, beside_o, rims, names, named, field = refs[2 * members :]
    load_names = pltpu.make_async_copy(table, names, named)
    load_names.start()
    size = viscous.shape[0]
    depth = chunks[0].shape[1]
    for k in range(tiles):
        for m in range(members):
            block = relays[m][k * BLOCK_ROWS : (k + 1) * BLOCK_ROWS]
            rims[k * members + m, 0:BLOCK_ROWS] = block.astype(F32)
            rims[k * members + m, BLOCK_ROWS:] = jnp.zeros((2 * DEPTH, size), F32)
    half = DEPTH
    high = 2 * DEPTH
    sub = iota((high, size), 0)
    lane = iota((high, size), 1)
    edge = (sub & (half - 1)) == 0
    turn = jnp.where(sub < half, CORIOLIS_TURN, -CORIOLIS_TURN).astype(F32)
    first, last = lane == 0, lane == size - 1

    def load(device, side, mask, with_push=True):
        start = side * EARLY_SIDE
        velocity = rims[device, start : start + high] * mask
        if not with_push:
            return velocity
        both = rims[device, start + high : start + 2 * high]
        visc = jnp.where(sub < half, both, roll(both, half, 0))
        scale = jnp.where(sub < half, roll(both, 1 - half, 0), roll(both, 1, 0)) * mask
        start = EARLY_ROWS + side * LATE_SIDE
        late = rims[device, start : start + high]
        pushed = jnp.where(sub < half, late, roll(late, 1, 0))
        return [velocity, visc, scale, pushed]

    def follow(device, side):
        name = names[device, side]
        return jnp.where(name >= 0, name, 0), name >= 0

    def step(state, left, right, inner, outer):
        c, visc, scale, pushed = state
        spread = left + right + inner + outer - 4.0 * c
        return scale * (c + visc * spread + pushed + turn * roll(c, half, 0))

    base = high
    for c in range(2):
        field[0, c, base : base + size] = speed[c]
    load_names.wait()
    def along(cells, before, beyond):
        left = jnp.where(first, roll(before, 1, 1), roll(cells, 1, 1))
        return left, jnp.where(last, roll(beyond, -1, 1), roll(cells, -1, 1))

    def step_end(state, inside, across, away):
        cells = state[0]
        toward = jnp.where(first if away > 0 else last, roll(inside, away, 1), roll(cells, away, 1))
        inner = jnp.where(edge, across, roll(cells, 1, 0))
        return step(state, toward, roll(cells, -away, 1), inner, roll(cells, -1, 0))

    halos = [[] for _ in range(SUBCYCLES)]
    for q in range(4):
        x, has_x = follow(0, q)
        halo = load(x, OPPOSITE[q], flag(has_x))
        own = load(0, q, 1.0)
        ends = []
        for s in LATERAL[q]:
            y, has_y = follow(x, s)
            z, has_z = follow(y, OPPOSITE[q])
            w, has_w = follow(z, OPPOSITE[s])
            u, has_u = follow(0, s)
            v, has_v = follow(u, q)
            ends.append(
                [
                    load(y, OPPOSITE[q], flag(has_y)),
                    load(z, q, flag(has_z)),
                    load(w, q, flag(has_w), with_push=False),
                    load(u, q, flag(has_u)),
                    load(v, OPPOSITE[q], flag(has_v), with_push=False),
                ]
            )
        (y_hi, z_hi, w_hi, u_hi, v_hi), (y_lo, z_lo, w_lo, u_lo, v_lo) = ends
        for t in range(SUBCYCLES):
            halos[t].append(halo[0])
            if t == SUBCYCLES - 1:
                break
            c, o = halo[0], own[0]
            left, right = along(c, y_lo[0], y_hi[0])
            inner = jnp.where(edge, o, roll(c, 1, 0))
            new_halo = step(halo, left, right, inner, roll(c, -1, 0))
            if t < SUBCYCLES - 2:
                left, right = along(o, u_lo[0], u_hi[0])
                inner = jnp.where(edge, c, roll(o, 1, 0))
                new_own = step(own, left, right, inner, roll(o, -1, 0))
                new_y = step_end(y_hi, c, z_hi[0], 1), step_end(y_lo, c, z_lo[0], -1)
            if t < SUBCYCLES - 3:
                z_hi[0], z_lo[0] = (
                    step_end(z_hi, w_hi, y_hi[0], 1),
                    step_end(z_lo, w_lo, y_lo[0], -1),
                )
                u_hi[0], u_lo[0] = step_end(u_hi, o, v_hi, 1), step_end(u_lo, o, v_lo, -1)
            halo[0] = new_halo
            if t < SUBCYCLES - 2:
                own[0] = new_own
                y_hi[0], y_lo[0] = new_y
    columns = [jnp.where(edge, cells[2], roll(cells[3], 1, 0)).T for cells in halos]

    warm = remap_forward(chunks, [[r[r.shape[0] - side :]] for r in relays], side, depth)
    heat = (conduct[...] * warm).astype(BF16)

    for t in range(SUBCYCLES):
        cells, sides = halos[t], columns[t]
        now, later = t % 2, (t + 1) % 2
        for c in range(2):
            at = c * half
            field[now, c, base + size : base + size + 1] = cells[0][at : at + 1]
            field[now, c, base - 1 : base] = cells[1][at : at + 1]
        for i in range(size // high):
            rows = slice(i * high, (i + 1) * high)
            held = [field[now, c, base + i * high : base + (i + 1) * high] for c in range(2)]
            for c in range(2):
                v, at = held[c], base + i * high
                up = field[now, c, at + 1 : at + 1 + high]
                down = field[now, c, at - 1 : at - 1 + high]
                east = jnp.where(last, sides[rows, c * half : c * half + 1], roll(v, -1, 1))
                west = jnp.where(first, sides[rows, c * half + 1 : c * half + 2], roll(v, 1, 1))
                spread = up + down + east + west - 4.0 * v
                turned = (CORIOLIS_TURN if c == 0 else -CORIOLIS_TURN) * held[1 - c]
                new = gain[rows] * (v + viscous[rows] * spread + push[c, rows] + turned)
                if t == SUBCYCLES - 1:
                    out[c, rows] = new
                else:
                    field[later, c, at : at + high] = new
    stress = [(drag[...] * (out[c] - current[c])).astype(BF16) for c in range(2)]
    return_fluxes([heat, *stress], chunks, side, depth, own_o, beside_o)


def return_fluxes(fluxes, chunks, side, depth, own, beside):
    size = fluxes[0].shape[0]
    wide = jnp.concatenate(fluxes, axis=1)
    step = 3 * side
    down = jnp.concatenate([chunk[0:side] for chunk in chunks], axis=0)
    parts = jnp.dot(down, wide, preferred_element_type=F32).astype(BF16)
    for k, chunk in enumerate(chunks):
        part = parts[k * side : (k + 1) * side]
        part = jnp.concatenate([part[:, c * size : (c + 1) * size] for c in range(3)], axis=0)
        reply = jnp.dot(part, chunk[side : side + depth], preferred_element_type=F32)
        at = k // 2 * step
        if k % 2:
            beside[at : at + step] = reply.astype(BF16)
        else:
            own[at : at + step] = reply


def pair_kernel(own, beside, *outs):
    step = outs[0].shape[0]
    for k, out in enumerate(outs):
        at = (k + 1) * step
        out[...] = (own[at : at + step] + beside[at : at + step].astype(F32)).astype(BF16)


def settle_kernel(speed, own, beside, flat_o, total_o, flat, left):
    size = speed.shape[1]
    for c in range(2):
        flat[pl.ds(c, size, stride=2), :] = speed[c]
    copy = pltpu.make_async_copy(flat, flat_o, left)
    copy.start()
    rows = total_o.shape[0]
    total_o[...] = own[0:rows] + beside[0:rows].astype(F32)
    copy.wait()


def finish_kernel(warm, currents, total, *refs):
    replies, (heat_o, current_o, heat_v, current_v, left) = refs[:-5], refs[-5:]
    copies = [
        pltpu.make_async_copy(heat_v, heat_o, left.at[0]),
        pltpu.make_async_copy(current_v, current_o, left.at[1]),
    ]
    side = currents.shape[1]
    total = total[...]
    for reply in replies:
        total = total + reply[...].astype(F32)
    heat = THERMAL_DIFFUSE * total[0:side]
    for l in range(warm.shape[0]):
        heat_v[l] = warm[l] + heat
    copies[0].start()
    for c in range(2):
        current_v[c] = currents[c] + STRESS_MIXING * total[(c + 1) * side : (c + 2) * side]
    copies[1].start()
    for copy in copies:
        copy.wait()


def shards(
    water_heat_state,
    diffusion_coefficient,
    upper_current_vector,
    remap_blocks,
    remap_rows,
    remap_cols,
    neighbors,
    thickness,
    concentration,
    ice_velocity,
    wind_stress,
):
    tile_count, sub_count, lev_count = (lax.axis_size(a) for a in ("tile", "sub", "lev"))
    group = sub_count * lev_count
    devices = tile_count * group
    group_axes = ("sub", "lev")
    member_axes = ("tile", "sub", "lev")
    levels, side, width = water_heat_state.shape
    pairs, size = remap_rows.shape[1:3]
    categories = thickness.shape[2]

    def tile_place():
        return lax.axis_index("tile")

    def member_place():
        return lax.axis_index("sub") * lev_count + lax.axis_index("lev")

    def device_place():
        return lax.axis_index("tile") * group + member_place()

    def swap(value, axes, count):
        got = {0: value}
        for k in range(1, count):
            got[k] = lax.ppermute(value, axes, [(i, i ^ k) for i in range(count)])
        return [got[k] for k in range(count)]

    def swap_chips(value):
        return {0: value} | {
            k: lax.ppermute(value, group_axes, [(i, i ^ k) for i in range(group)])
            for k in range(2, group, 2)
        }

    def swap_cores(got):
        beside = [(i, i ^ 1) for i in range(group)]
        got = got | {k + 1: lax.ppermute(got[k], group_axes, beside) for k in got}
        return [got[k] for k in range(group)]

    def swap_each(values):
        got = {0: values[0]}
        for k in range(1, group):
            got[k] = lax.ppermute(values[k], group_axes, [(i, i ^ k) for i in range(group)])
        return [got[k] for k in range(group)]

    def shape(*dims, dtype=F32):
        return jax.ShapeDtypeStruct(dims, dtype)

    def interleaved(value):
        return value.reshape(2, size, size).transpose(1, 0, 2).reshape(2 * size, size)

    plane = shape(size, size)
    planes = shape(2, size, size)
    wind = interleaved(wind_stress)

    tail_rows = -(-(2 * levels + 1) // TILE_ROWS) * TILE_ROWS
    pair_rows = side + width
    chunk_rows = pair_rows + 2 * side + tail_rows
    *sent, fields = call(
        functools.partial(forward_kernel, (devices, group, member_place)),
        [shape(chunk_rows if k < 2 else pair_rows, width, dtype=BF16) for k in range(group)]
        + [shape(chunk_rows - pair_rows, width, dtype=BF16)],
        (
            neighbors,
            remap_blocks,
            remap_rows[0].swapaxes(1, 2),
            remap_cols[0],
            upper_current_vector,
            water_heat_state,
        ),
        scratch=[
            pltpu.SMEM(neighbors.shape, jnp.int32),
            pltpu.SMEM((1, pairs), jnp.int32),
            pltpu.VMEM((2, side, width), F32),
            pltpu.VMEM((pairs, pair_rows, width), BF16),
            pltpu.VMEM((levels, side, width), F32),
            pltpu.VMEM((chunk_rows - pair_rows, width), BF16),
            pltpu.VMEM((1 if pairs == group else group, pair_rows, width), BF16),
            pltpu.SemaphoreType.DMA((6,)),
            pltpu.SemaphoreType.DMA((2 * group + 1,)),
        ],
        hbm=(0, 1, 2, 3, 4, 5),
        grant=60 * 2**20,
        micros=10,
    )
    chunks = swap_each(sent)
    hops = []
    for k in range(2, group, 2):
        far = lax.ppermute(fields, group_axes, [(i, i ^ k) for i in range(group)])
        hops += [far, lax.ppermute(far, group_axes, [(i, i ^ 1) for i in range(group)])]

    early, viscous, gain, step_mass, drag, conduct, speed = call(
        rims_kernel,
        [shape(EARLY_ROWS + 4 * levels, size)] + [plane] * 5 + [planes],
        (
            thickness.reshape(categories, size, size),
            concentration.reshape(categories, size, size),
            interleaved(ice_velocity),
            water_heat_state,
        ),
    )
    extra_rows = -(-(1 + 5 * levels) // TILE_ROWS) * TILE_ROWS
    message, current_ice, push = call(
        functools.partial(forcing_kernel, group, side, levels, sub_count, member_place),
        [shape(BLOCK_ROWS + extra_rows, size, dtype=BF16), planes, planes],
        (step_mass, drag, wind, early, *hops, *chunks),
        scratch=[pltpu.VMEM((BLOCK_ROWS + extra_rows, size), F32)],
    )
    messages = swap(message, "tile", tile_count)

    counts = (tile_count, sub_count, lev_count)
    ocean = (*(messages[k] for k in spread_out(tile_count)), *chunks, *hops)
    relay_rows = tile_count * BLOCK_ROWS
    relay_shapes = [shape(relay_rows + (side if lev_count == 1 else 0), size, dtype=BF16)]
    if lev_count > 1:
        relay_shapes.append(shape(side, width))
    relay, *top = call(
        functools.partial(relay_kernel, counts, tile_place, member_place),
        relay_shapes,
        (water_heat_state, diffusion_coefficient, *ocean),
    )
    if lev_count > 1:
        relay = jnp.concatenate([relay, lax.psum(top[0], "lev").astype(BF16)], axis=0)
    relays = swap_chips(relay)

    mixing, _ = lax.optimization_barrier((diffusion_coefficient, relay))
    (warm,) = call(
        functools.partial(ocean_kernel, counts, tile_place, member_place),
        [shape(levels, side, width)],
        (water_heat_state, mixing, *ocean),
    )
    far = sorted(k for k in relays if k)
    relayed, _ = lax.optimization_barrier(([relays[k] for k in far], warm))
    relays = swap_cores({0: relay} | dict(zip(far, relayed)))

    names = jnp.stack([m[BLOCK_ROWS, : 8 * group] for m in messages])
    names = names.reshape(devices, 8).astype(jnp.int32)
    table = names[:, 0:4] * 128 + names[:, 4:8]
    table = jnp.where(table < 0, -1, table ^ device_place())
    step = 3 * side
    speed, own, beside = call(
        functools.partial(ice_kernel, tile_count, group, side),
        [
            planes,
            shape(group // 2 * step, width),
            shape(group // 2 * step, width, dtype=BF16),
        ],
        (table, viscous, gain, drag, conduct, current_ice, speed, push, *chunks, *relays),
        scratch=[
            pltpu.VMEM((devices, BLOCK_ROWS + 2 * DEPTH, size), F32),
            pltpu.SMEM((devices, 4), jnp.int32),
            pltpu.SemaphoreType.DMA,
            pltpu.VMEM((2, 2, size + 4 * DEPTH, size), F32),
        ],
        hbm=(0,),
    )
    beside = lax.ppermute(beside, group_axes, [(i, i ^ 1) for i in range(group)])
    paired = call(
        pair_kernel, [shape(step, width, dtype=BF16)] * (group // 2 - 1), (own, beside)
    )
    replies = [
        lax.ppermute(value, group_axes, [(i, i ^ (2 * k + 2)) for i in range(group)])
        for k, value in enumerate(paired)
    ]
    flat, total = call(
        settle_kernel,
        [shape(2 * size, size), shape(step, width)],
        (speed, own, beside),
        scratch=[pltpu.VMEM((2 * size, size), F32), pltpu.SemaphoreType.DMA],
        out_spaces=(pltpu.HBM, pltpu.VMEM),
    )
    if lev_count > 1:
        total = lax.psum(total + sum(r.astype(F32) for r in replies), "lev")
        replies = []
    heat, current = call(
        finish_kernel,
        [shape(levels, side, width), shape(2, side, width)],
        (warm, upper_current_vector, total, *replies),
        scratch=[
            pltpu.VMEM((levels, side, width), F32),
            pltpu.VMEM((2, side, width), F32),
            pltpu.SemaphoreType.DMA((2,)),
        ],
        out_space=pltpu.HBM,
    )
    velocity = flat.reshape(size, 2, size).transpose(1, 0, 2).reshape(1, 1, 2, size * size)
    return heat, current, velocity


def solution(mesh):
    member = ("tile", "sub", "lev")
    whole = ("copies",) + member
    ice = P(None, whole, None, None)
    water = P("lev", ("copies", "tile"), "sub")
    current = P(None, ("copies", "tile"), "sub")
    return jax.shard_map(
        shards,
        mesh=mesh,
        in_specs=(
            water,
            P("tile", "sub"),
            current,
            P(member, None),
            P(member, None, None, None),
            P(member, None, None, None),
            P(None, member, None),
            ice,
            ice,
            ice,
            ice,
        ),
        out_specs=(water, current, ice),
        check_vma=False,
    )
```

```python
import functools

import jax
import jax.numpy as jnp
from jax import lax
from jax.experimental import pallas as pl
from jax.experimental.pallas import tpu as pltpu
from jax.sharding import PartitionSpec as P

SUBCYCLES = 4
STRENGTH_DECAY = 5.0
VISCOUS_STEP = 0.24
SUBCYCLE_STEP = 0.5
CORIOLIS_TURN = 0.1
BASE_MASS = 0.5
HEAT_RATE = 0.2
THIN_ICE = 0.1
THERMAL_DIFFUSE = 0.5
STRESS_MIXING = 0.5

OPPOSITE = (1, 0, 3, 2)
LATERAL = ((2, 3), (2, 3), (0, 1), (0, 1))
DEPTH = SUBCYCLES
EARLY_DEPTHS = (DEPTH, DEPTH, DEPTH - 1, DEPTH - 1)
LATE_DEPTHS = (DEPTH - 1, DEPTH - 1)
EARLY_SIDE, LATE_SIDE = sum(EARLY_DEPTHS), sum(LATE_DEPTHS)
EARLY_ROWS = 4 * EARLY_SIDE
BLOCK_ROWS = EARLY_ROWS + 4 * LATE_SIDE
TILE_ROWS = 16
F32 = jnp.float32
BF16 = jnp.bfloat16
VMEM_LIMIT = 16 * 1024 * 1024
FLOPS_PER_MICRO = 1.15e9


def call(
    kernel, outs, args, scratch=(), smem=(), hbm=(), out_space=pltpu.VMEM, out_spaces=None,
    grant=VMEM_LIMIT, micros=0.01,
):
    def space(i):
        return pltpu.SMEM if i in smem else pltpu.HBM if i in hbm else pltpu.VMEM

    specs = [pl.BlockSpec(memory_space=space(i)) for i in range(len(args))]
    size = sum(a.size * a.dtype.itemsize for a in args)
    return pl.pallas_call(
        kernel,
        out_shape=outs,
        in_specs=specs,
        out_specs=(
            jax.tree.map(lambda _: pl.BlockSpec(memory_space=out_space), outs)
            if out_spaces is None
            else [pl.BlockSpec(memory_space=space) for space in out_spaces]
        ),
        scratch_shapes=list(scratch),
        compiler_params=pltpu.CompilerParams(vmem_limit_bytes=grant),
        cost_estimate=pl.CostEstimate(
            flops=int(micros * FLOPS_PER_MICRO), bytes_accessed=size, transcendentals=0
        ),
    )(*args)


def iota(shape, axis):
    return lax.broadcasted_iota(jnp.int32, shape, axis)


def roll(x, shift, axis):
    return pltpu.roll(x, shift % x.shape[axis], axis)


def flag(condition):
    return jnp.where(condition, 1.0, 0.0).astype(F32)


def ocean_columns(water):
    levels, rows, width = water.shape
    lane = iota((rows, width), 1)
    line = iota((1, width), 1)
    mixed = jnp.zeros((rows, width), F32)
    for l in range(levels):
        mixed = jnp.where(lane // 4 == l, roll(water[l], 2 + 4 * l, 1), mixed)
    across = jnp.concatenate([mixed, jnp.zeros((width - rows, width), F32)], axis=0).T
    beside = []
    for l in range(levels):
        for j in range(2):
            last = across[4 * l + 1 - j : 4 * l + 2 - j]
            lead = across[4 * l + 2 + j : 4 * l + 3 + j]
            beside.append(jnp.where(line < rows, last, roll(lead, rows, 1)))
    return beside


def forward_kernel(group, links_h, blocks_h, rows_h, cols_h, currents_h, water_h, *refs):
    devices, members, place = group
    outs, scratch = refs[:members], refs[members:]
    links, blocks, currents, weights, water, fields, kept, arrived, left = scratch
    pairs, side, width = rows_h.shape
    both = weights.shape[1]
    loads = [
        pltpu.make_async_copy(source, target, arrived.at[i])
        for i, (source, target) in enumerate(
            (
                (links_h, links),
                (blocks_h, blocks),
                (currents_h, currents),
                (rows_h, weights.at[:, pl.ds(0, side)]),
                (cols_h, weights.at[:, pl.ds(side, both - side)]),
                (water_h, water),
            )
        )
    ]
    for load in loads:
        load.start()
    for i in (1, 3, 4):
        loads[i].wait()
    me = place()
    owners = [lax.rem(lax.rem(blocks[0, m], devices), members) for m in range(pairs)]
    copies = []
    for k, out in enumerate(outs):
        partner = me ^ k
        pair = jnp.int32(0)
        for m in range(pairs):
            pair = jnp.where(owners[m] == partner, m, pair)
        source = weights.at[pair]
        if pairs < members:
            found = sum(flag(owners[m] == partner) for m in range(pairs))
            kept[k] = (weights[pair].astype(F32) * found).astype(BF16)
            source = kept.at[k]
        copies.append(pltpu.make_async_copy(source, out.at[pl.ds(0, both)], left.at[2 * k]))
        copies[-1].start()
    for i in (0, 2, 5):
        loads[i].wait()
    for c in range(2):
        fields[c * side : (c + 1) * side] = currents[c].astype(BF16)
    lane = iota((1, width), 1)
    numbers = jnp.zeros((1, width), F32)
    for q in range(4):
        numbers = jnp.where(lane == q, (links[0, 0, q] >> 7).astype(F32), numbers)
        numbers = jnp.where(lane == 4 + q, (links[0, 0, q] & 127).astype(F32), numbers)
    ends = ocean_columns(water) + [numbers]
    blank = jnp.zeros((fields.shape[0] - 2 * side - len(ends), width), F32)
    fields[2 * side :] = jnp.concatenate(ends + [blank], axis=0).astype(BF16)
    for k, out in enumerate(outs):
        if out.shape[0] > both:
            target = out.at[pl.ds(both, fields.shape[0])]
            copies.append(pltpu.make_async_copy(fields, target, left.at[2 * k + 1]))
            copies[-1].start()
    for copy in copies:
        copy.wait()


def put_side_rims(store, planes, depths, at):
    size = planes[0].shape[0]
    lane = iota((size, size), 1)
    mixed = jnp.zeros((size, size), F32)
    for i, plane in enumerate(planes):
        turned = roll(plane, DEPTH + 2 * DEPTH * i, 1)
        mixed = jnp.where(lane // (2 * DEPTH) == i, turned, mixed)
    across = mixed.T
    base = 0
    for i, plane in enumerate(planes):
        for k in range(depths[i]):
            east = 2 * DEPTH * i + DEPTH - 1 - k
            west = 2 * DEPTH * i + DEPTH + k
            store[at(0) + base : at(0) + base + 1] = plane[size - 1 - k : size - k]
            store[at(1) + base : at(1) + base + 1] = plane[k : k + 1]
            store[at(2) + base : at(2) + base + 1] = across[east : east + 1]
            store[at(3) + base : at(3) + base + 1] = across[west : west + 1]
            base += 1


def apart(pairs, wide):
    rows = pairs.shape[0]
    wide[0:rows] = pairs[...]
    return [wide[pl.ds(c, rows // 2, stride=2), :] for c in range(2)]


def rims_kernel(
    thick, conc, ice, water, out, viscous_o, gain_o, mass_o, drag_o, conduct_o,
    speed_o, wide,
):
    size = thick.shape[1]
    cover = jnp.zeros((size, size), F32)
    volume = jnp.zeros((size, size), F32)
    conduct = jnp.zeros((size, size), F32)
    for c in range(thick.shape[0]):
        h, a = thick[c], conc[c]
        cover = cover + a
        volume = volume + a * h
        conduct = conduct + a / (h + THIN_ICE)
    mass = volume + BASE_MASS
    viscous = VISCOUS_STEP * (volume * jnp.exp(-STRENGTH_DECAY * (1.0 - cover))) / mass
    step_mass = SUBCYCLE_STEP / mass
    gain = 1.0 / (1.0 + step_mass * cover)
    speed_x, speed_y = apart(ice, wide)
    viscous_o[...] = viscous
    gain_o[...] = gain
    mass_o[...] = step_mass
    drag_o[...] = cover
    conduct_o[...] = -HEAT_RATE * conduct
    speed_o[0] = speed_x
    speed_o[1] = speed_y
    put_side_rims(
        out, [speed_x, speed_y, viscous, gain], EARLY_DEPTHS, lambda side: side * EARLY_SIDE
    )
    levels, rows, width = water.shape
    for l in range(levels):
        for j in range(2):
            at = EARLY_ROWS + 2 * l + j
            out[at : at + 1] = water[l, rows - 1 - j : rows - j]
            out[at + 2 * levels : at + 2 * levels + 1] = water[l, j : j + 1]


def nearby(me, members, distance, arrays):
    at = me + distance
    inside = (at >= 0) & (at < members)
    found = 0.0
    for k in range(1, members):
        found = found + arrays[k].astype(F32) * flag(inside & ((me ^ k) == at))
    return found


def remap_forward(chunks, field_rows, side, depth):
    total = None
    for chunk, fields in zip(chunks, field_rows):
        down = chunk[0:side]
        right = chunk[side : side + depth]
        wide = jnp.concatenate(fields, axis=1) if len(fields) > 1 else fields[0]
        part = lax.dot_general(down, wide, (((0,), (0,)), ((), ())), preferred_element_type=F32)
        part = part.astype(BF16)
        width = fields[0].shape[1]
        if len(fields) > 1:
            part = jnp.concatenate(
                [part[:, c * width : (c + 1) * width] for c in range(len(fields))], axis=0
            )
        piece = lax.dot_general(part, right, (((1,), (1,)), ((), ())), preferred_element_type=F32)
        piece = piece.astype(BF16).astype(F32)
        total = piece if total is None else total + piece
    return total


def tails_of(chunks, hops):
    at = min(c.shape[0] for c in chunks)
    return [hops[k // 2 - 1][...] if k > 1 and k % 2 else c[at:] for k, c in enumerate(chunks)]


def forcing_kernel(group, side, levels, subs, place, mass, drag, wind, early, *refs):
    chunks = refs[:group][::-1]
    hops, (out, current_o, push_o, store, wide) = refs[group:-5], refs[-5:]
    forces = apart(wind, wide)
    size = mass.shape[0]
    depth = chunks[0].shape[1]
    tails = tails_of(chunks, hops)
    fields = [[t[0:side], t[side : 2 * side]] for t in tails]
    total = remap_forward(chunks, fields, side, depth)
    pushes = []
    for c in range(2):
        current = total[c * size : (c + 1) * size]
        current_o[c] = current
        push = mass[...] * (forces[c] + drag[...] * current)
        push_o[c] = push
        pushes.append(push)
    store[0:EARLY_ROWS] = early[0:EARLY_ROWS]
    put_side_rims(store, pushes, LATE_DEPTHS, lambda side: EARLY_ROWS + side * LATE_SIDE)
    tail = [t[2 * side :].astype(F32) for t in tails]
    line = iota((1, size), 1)
    names = jnp.zeros((1, size), F32)
    for k in range(group):
        names = jnp.where(line // 8 == k, roll(tail[k][2 * levels : 2 * levels + 1], 8 * k, 1), names)
    me, step = place(), group // subs
    left, right = (nearby(me, group, d * step, tail) for d in (-1, 1))
    extra = [names]
    for l in range(levels):
        near = slice(2 * l, 2 * l + 1)
        extra.append(jnp.where(line < side, left[near], right[near]))
    extra.append(early[EARLY_ROWS:])
    used = BLOCK_ROWS + 1 + 5 * levels
    store[BLOCK_ROWS:] = jnp.concatenate(
        extra + [jnp.zeros((store.shape[0] - used, size), F32)], axis=0
    )
    out[...] = store[...].astype(BF16)


def ocean_halos(counts, tile_place, member_place, shape, messages, tails):
    tiles, subs, levs = counts
    levels, rows, width = shape
    my_tile, me = tile_place(), member_place()
    halo = {}
    extras = [m[BLOCK_ROWS:] for m in messages]
    ends = [t[2 * rows :] for t in tails]
    for dt in (-1, 1):
        extra = nearby(my_tile, tiles, dt, extras)
        corners, strips = extra[1 : 1 + levels], extra[1 + levels : 1 + 5 * levels]
        halo[dt, 0] = strips[: 2 * levels] if dt < 0 else strips[2 * levels :]
        at = rows - 1 if dt < 0 else 0
        for ds in (-1, 1):
            lane_at = at if ds < 0 else rows + at
            halo[dt, ds] = corners[:, lane_at : lane_at + 1]
    for ds in (-1, 1):
        beside = nearby(me, subs * levs, ds * levs, ends)[: 2 * levels]
        halo[0, ds] = roll(beside, -rows, 1) if ds > 0 else beside
    return halo


def biharmonic(x, top, bottom, left, right, corner):
    rows, width = x.shape
    row, lane = iota(x.shape, 0), iota(x.shape, 1)
    line = iota((1, width), 1)

    def laplacian(x, top, bottom, left, right):
        up = jnp.where(row == 0, top, roll(x, 1, 0))
        down = jnp.where(row == rows - 1, bottom, roll(x, -1, 0))
        west = jnp.where(lane == 0, left, roll(x, 1, 1))
        east = jnp.where(lane == width - 1, right, roll(x, -1, 1))
        return up + down + west + east - 4.0 * x

    def ring_row(mid, out_row, in_row, dt):
        west = jnp.where(line == 0, corner[dt, -1], roll(mid, 1, 1))
        east = jnp.where(line == width - 1, corner[dt, 1], roll(mid, -1, 1))
        return west + east + out_row + in_row - 4.0 * mid

    def ring_col(mid, out_col, in_col, ds):
        up = jnp.concatenate([corner[-1, ds], mid[:-1]], axis=0)
        down = jnp.concatenate([mid[1:], corner[1, ds]], axis=0)
        return up + down + out_col + in_col - 4.0 * mid

    return laplacian(
        laplacian(x, top[0], bottom[0], left[0], right[0]),
        ring_row(*top, x[0:1], -1),
        ring_row(*bottom, x[rows - 1 :], 1),
        ring_col(*left, x[:, 0:1], -1),
        ring_col(*right, x[:, width - 1 :], 1),
    )


def spread_out(count):
    return sorted(range(count), key=lambda k: (k == count // 2, k))


def split_refs(tiles, members, refs, outs):
    messages = [refs[spread_out(tiles).index(k)] for k in range(tiles)]
    chunks = refs[tiles : tiles + members]
    return messages, tails_of(chunks, refs[tiles + members : -outs]), refs[-outs:]


def relay_kernel(counts, tile_place, member_place, water, mixing, *refs):
    tiles, subs, levs = counts
    outs = 1 if levs == 1 else 2
    messages, tails, outs = split_refs(tiles, subs * levs, refs, outs)
    for k in range(tiles):
        outs[0][k * BLOCK_ROWS : (k + 1) * BLOCK_ROWS] = messages[k][0:BLOCK_ROWS]
    levels, rows, width = water.shape
    halo = ocean_halos(counts, tile_place, member_place, water.shape, messages, tails)

    def both(strip):
        near = sum(strip[2 * l : 2 * l + 1] for l in range(levels))
        far = sum(strip[2 * l + 1 : 2 * l + 2] for l in range(levels))
        return near, far

    def as_columns(strip):
        near, far = both(strip)
        across = jnp.concatenate([near, far] + [jnp.zeros_like(near)] * 6, axis=0).T
        return across[0:rows, 0:1], across[0:rows, 1:2]

    corner = {
        (dt, ds): jnp.sum(halo[dt, ds], axis=0, keepdims=True) for dt in (-1, 1) for ds in (-1, 1)
    }
    x = sum(water[l] for l in range(levels))
    twice = biharmonic(
        x, both(halo[-1, 0]), both(halo[1, 0]), as_columns(halo[0, -1]), as_columns(halo[0, 1]), corner
    )
    top = (x - mixing[...] * twice) / (levels * levs)
    if levs == 1:
        outs[0][tiles * BLOCK_ROWS :] = top.astype(BF16)
    else:
        outs[1][...] = top


def ocean_kernel(counts, tile_place, member_place, water, mixing, *refs):
    tiles, subs, levs = counts
    messages, tails, (warm_o,) = split_refs(tiles, subs * levs, refs, 1)
    levels, rows, width = water.shape
    halo = ocean_halos(counts, tile_place, member_place, water.shape, messages, tails)
    left, right = halo[0, -1].T, halo[0, 1].T
    for l in range(levels):
        x = water[l]
        pair = (2 * l, 2 * l + 1)
        twice = biharmonic(
            x,
            [halo[-1, 0][i : i + 1] for i in pair],
            [halo[1, 0][i : i + 1] for i in pair],
            [left[0:rows, i : i + 1] for i in pair],
            [right[0:rows, i : i + 1] for i in pair],
            {(dt, ds): halo[dt, ds][l : l + 1] for dt in (-1, 1) for ds in (-1, 1)},
        )
        warm_o[l] = x - mixing[...] * twice


def ice_kernel(
    tiles, members, side, table, viscous, gain, drag, conduct, current, speed, push, *refs
):
    chunks, relays = refs[:members], refs[members : 2 * members]
    out, own_o, beside_o, rims, names, named, field = refs[2 * members :]
    load_names = pltpu.make_async_copy(table, names, named)
    load_names.start()
    size = viscous.shape[0]
    depth = chunks[0].shape[1]
    for k in range(tiles):
        for m in range(members):
            block = relays[m][k * BLOCK_ROWS : (k + 1) * BLOCK_ROWS]
            rims[k * members + m, 0:BLOCK_ROWS] = block.astype(F32)
            rims[k * members + m, BLOCK_ROWS:] = jnp.zeros((2 * DEPTH, size), F32)
    half = DEPTH
    high = 2 * DEPTH
    sub = iota((high, size), 0)
    lane = iota((high, size), 1)
    edge = (sub & (half - 1)) == 0
    turn = jnp.where(sub < half, CORIOLIS_TURN, -CORIOLIS_TURN).astype(F32)
    first, last = lane == 0, lane == size - 1

    def load(device, side, mask, with_push=True):
        start = side * EARLY_SIDE
        velocity = rims[device, start : start + high] * mask
        if not with_push:
            return velocity
        both = rims[device, start + high : start + 2 * high]
        visc = jnp.where(sub < half, both, roll(both, half, 0))
        scale = jnp.where(sub < half, roll(both, 1 - half, 0), roll(both, 1, 0)) * mask
        start = EARLY_ROWS + side * LATE_SIDE
        late = rims[device, start : start + high]
        pushed = jnp.where(sub < half, late, roll(late, 1, 0))
        return [velocity, visc, scale, pushed]

    def follow(device, side):
        name = names[device, side]
        return jnp.where(name >= 0, name, 0), name >= 0

    def step(state, left, right, inner, outer):
        c, visc, scale, pushed = state
        spread = left + right + inner + outer - 4.0 * c
        return scale * (c + visc * spread + pushed + turn * roll(c, half, 0))

    base = high
    for c in range(2):
        field[0, c, base : base + size] = speed[c]
    load_names.wait()
    def along(cells, before, beyond):
        left = jnp.where(first, roll(before, 1, 1), roll(cells, 1, 1))
        return left, jnp.where(last, roll(beyond, -1, 1), roll(cells, -1, 1))

    def step_end(state, inside, across, away):
        cells = state[0]
        toward = jnp.where(first if away > 0 else last, roll(inside, away, 1), roll(cells, away, 1))
        inner = jnp.where(edge, across, roll(cells, 1, 0))
        return step(state, toward, roll(cells, -away, 1), inner, roll(cells, -1, 0))

    halos = [[] for _ in range(SUBCYCLES)]
    for q in range(4):
        x, has_x = follow(0, q)
        halo = load(x, OPPOSITE[q], flag(has_x))
        own = load(0, q, 1.0)
        ends = []
        for s in LATERAL[q]:
            y, has_y = follow(x, s)
            z, has_z = follow(y, OPPOSITE[q])
            w, has_w = follow(z, OPPOSITE[s])
            u, has_u = follow(0, s)
            v, has_v = follow(u, q)
            ends.append(
                [
                    load(y, OPPOSITE[q], flag(has_y)),
                    load(z, q, flag(has_z)),
                    load(w, q, flag(has_w), with_push=False),
                    load(u, q, flag(has_u)),
                    load(v, OPPOSITE[q], flag(has_v), with_push=False),
                ]
            )
        (y_hi, z_hi, w_hi, u_hi, v_hi), (y_lo, z_lo, w_lo, u_lo, v_lo) = ends
        for t in range(SUBCYCLES):
            halos[t].append(halo[0])
            if t == SUBCYCLES - 1:
                break
            c, o = halo[0], own[0]
            left, right = along(c, y_lo[0], y_hi[0])
            inner = jnp.where(edge, o, roll(c, 1, 0))
            new_halo = step(halo, left, right, inner, roll(c, -1, 0))
            if t < SUBCYCLES - 2:
                left, right = along(o, u_lo[0], u_hi[0])
                inner = jnp.where(edge, c, roll(o, 1, 0))
                new_own = step(own, left, right, inner, roll(o, -1, 0))
                new_y = step_end(y_hi, c, z_hi[0], 1), step_end(y_lo, c, z_lo[0], -1)
            if t < SUBCYCLES - 3:
                z_hi[0], z_lo[0] = (
                    step_end(z_hi, w_hi, y_hi[0], 1),
                    step_end(z_lo, w_lo, y_lo[0], -1),
                )
                u_hi[0], u_lo[0] = step_end(u_hi, o, v_hi, 1), step_end(u_lo, o, v_lo, -1)
            halo[0] = new_halo
            if t < SUBCYCLES - 2:
                own[0] = new_own
                y_hi[0], y_lo[0] = new_y
    columns = [jnp.where(edge, cells[2], roll(cells[3], 1, 0)).T for cells in halos]

    warm = remap_forward(chunks, [[r[r.shape[0] - side :]] for r in relays], side, depth)
    heat = (conduct[...] * warm).astype(BF16)

    for t in range(SUBCYCLES):
        cells, sides = halos[t], columns[t]
        now, later = t % 2, (t + 1) % 2
        for c in range(2):
            at = c * half
            field[now, c, base + size : base + size + 1] = cells[0][at : at + 1]
            field[now, c, base - 1 : base] = cells[1][at : at + 1]
        for i in range(size // high):
            rows = slice(i * high, (i + 1) * high)
            held = [field[now, c, base + i * high : base + (i + 1) * high] for c in range(2)]
            for c in range(2):
                v, at = held[c], base + i * high
                up = field[now, c, at + 1 : at + 1 + high]
                down = field[now, c, at - 1 : at - 1 + high]
                east = jnp.where(last, sides[rows, c * half : c * half + 1], roll(v, -1, 1))
                west = jnp.where(first, sides[rows, c * half + 1 : c * half + 2], roll(v, 1, 1))
                spread = up + down + east + west - 4.0 * v
                turned = (CORIOLIS_TURN if c == 0 else -CORIOLIS_TURN) * held[1 - c]
                new = gain[rows] * (v + viscous[rows] * spread + push[c, rows] + turned)
                if t == SUBCYCLES - 1:
                    out[c, rows] = new
                else:
                    field[later, c, at : at + high] = new
    stress = [(drag[...] * (out[c] - current[c])).astype(BF16) for c in range(2)]
    return_fluxes([heat, *stress], chunks, side, depth, own_o, beside_o)


def return_fluxes(fluxes, chunks, side, depth, own, beside):
    size = fluxes[0].shape[0]
    wide = jnp.concatenate(fluxes, axis=1)
    step = 3 * side
    down = jnp.concatenate([chunk[0:side] for chunk in chunks], axis=0)
    parts = jnp.dot(down, wide, preferred_element_type=F32).astype(BF16)
    for k, chunk in enumerate(chunks):
        part = parts[k * side : (k + 1) * side]
        part = jnp.concatenate([part[:, c * size : (c + 1) * size] for c in range(3)], axis=0)
        reply = jnp.dot(part, chunk[side : side + depth], preferred_element_type=F32)
        at = k // 2 * step
        if k % 2:
            beside[at : at + step] = reply.astype(BF16)
        else:
            own[at : at + step] = reply


def pair_kernel(own, beside, *outs):
    step = outs[0].shape[0]
    for k, out in enumerate(outs):
        at = (k + 1) * step
        out[...] = (own[at : at + step] + beside[at : at + step].astype(F32)).astype(BF16)


def settle_kernel(speed, own, beside, flat_o, total_o, flat, left):
    size = speed.shape[1]
    for c in range(2):
        flat[pl.ds(c, size, stride=2), :] = speed[c]
    copy = pltpu.make_async_copy(flat.at[pl.ds(0, flat_o.shape[0])], flat_o, left)
    copy.start()
    rows = total_o.shape[0]
    total_o[...] = own[0:rows] + beside[0:rows].astype(F32)
    copy.wait()


def finish_kernel(warm, currents, total, *refs):
    replies, (heat_o, current_o, heat_v, current_v, left) = refs[:-5], refs[-5:]
    copies = [
        pltpu.make_async_copy(heat_v, heat_o, left.at[0]),
        pltpu.make_async_copy(current_v, current_o, left.at[1]),
    ]
    side = currents.shape[1]
    total = total[...]
    for reply in replies:
        total = total + reply[...].astype(F32)
    heat = THERMAL_DIFFUSE * total[0:side]
    for l in range(warm.shape[0]):
        heat_v[l] = warm[l] + heat
    copies[0].start()
    for c in range(2):
        current_v[c] = currents[c] + STRESS_MIXING * total[(c + 1) * side : (c + 2) * side]
    copies[1].start()
    for copy in copies:
        copy.wait()


def shards(
    water_heat_state,
    diffusion_coefficient,
    upper_current_vector,
    remap_blocks,
    remap_rows,
    remap_cols,
    neighbors,
    thickness,
    concentration,
    ice_velocity,
    wind_stress,
):
    tile_count, sub_count, lev_count = (lax.axis_size(a) for a in ("tile", "sub", "lev"))
    group = sub_count * lev_count
    devices = tile_count * group
    group_axes = ("sub", "lev")
    member_axes = ("tile", "sub", "lev")
    levels, side, width = water_heat_state.shape
    pairs, size = remap_rows.shape[1:3]
    categories = thickness.shape[2]

    def tile_place():
        return lax.axis_index("tile")

    def member_place():
        return lax.axis_index("sub") * lev_count + lax.axis_index("lev")

    def device_place():
        return lax.axis_index("tile") * group + member_place()

    def swap(value, axes, count):
        got = {0: value}
        for k in range(1, count):
            got[k] = lax.ppermute(value, axes, [(i, i ^ k) for i in range(count)])
        return [got[k] for k in range(count)]

    def swap_chips(value):
        return {0: value} | {
            k: lax.ppermute(value, group_axes, [(i, i ^ k) for i in range(group)])
            for k in range(2, group, 2)
        }

    def swap_cores(got):
        beside = [(i, i ^ 1) for i in range(group)]
        got = got | {k + 1: lax.ppermute(got[k], group_axes, beside) for k in got}
        return [got[k] for k in range(group)]

    def swap_each(values):
        got = {0: values[0]}
        for k in range(1, group):
            got[k] = lax.ppermute(values[k], group_axes, [(i, i ^ k) for i in range(group)])
        return [got[k] for k in range(group)]

    def shape(*dims, dtype=F32):
        return jax.ShapeDtypeStruct(dims, dtype)

    def interleaved(value):
        return value.reshape(2, size, size).transpose(1, 0, 2).reshape(2 * size, size)

    plane = shape(size, size)
    planes = shape(2, size, size)
    wind = interleaved(wind_stress)

    tail_rows = -(-(2 * levels + 1) // TILE_ROWS) * TILE_ROWS
    pair_rows = side + width
    chunk_rows = pair_rows + 2 * side + tail_rows
    sent = call(
        functools.partial(forward_kernel, (devices, group, member_place)),
        [
            shape(pair_rows if k > 1 and k % 2 else chunk_rows, width, dtype=BF16)
            for k in range(group)
        ],
        (
            neighbors,
            remap_blocks,
            remap_rows[0].swapaxes(1, 2),
            remap_cols[0],
            upper_current_vector,
            water_heat_state,
        ),
        scratch=[
            pltpu.SMEM(neighbors.shape, jnp.int32),
            pltpu.SMEM((1, pairs), jnp.int32),
            pltpu.VMEM((2, side, width), F32),
            pltpu.VMEM((pairs, pair_rows, width), BF16),
            pltpu.VMEM((levels, side, width), F32),
            pltpu.VMEM((chunk_rows - pair_rows, width), BF16),
            pltpu.VMEM((1 if pairs == group else group, pair_rows, width), BF16),
            pltpu.SemaphoreType.DMA((6,)),
            pltpu.SemaphoreType.DMA((2 * group,)),
        ],
        hbm=(0, 1, 2, 3, 4, 5),
        grant=60 * 2**20,
        micros=10,
    )
    chunks = swap_each(sent)
    hops = [
        lax.ppermute(chunks[k][pair_rows:], group_axes, [(i, i ^ 1) for i in range(group)])
        for k in range(2, group, 2)
    ]

    early, viscous, gain, step_mass, drag, conduct, speed = call(
        rims_kernel,
        [shape(EARLY_ROWS + 4 * levels, size)] + [plane] * 5 + [planes],
        (
            thickness.reshape(categories, size, size),
            concentration.reshape(categories, size, size),
            interleaved(ice_velocity),
            water_heat_state,
        ),
        scratch=[pltpu.VMEM((2 * size + 8, size), F32)],
    )
    extra_rows = -(-(1 + 5 * levels) // TILE_ROWS) * TILE_ROWS
    message, current_ice, push = call(
        functools.partial(forcing_kernel, group, side, levels, sub_count, member_place),
        [shape(BLOCK_ROWS + extra_rows, size, dtype=BF16), planes, planes],
        (step_mass, drag, wind, early, *chunks[::-1], *hops),
        scratch=[
            pltpu.VMEM((BLOCK_ROWS + extra_rows, size), F32),
            pltpu.VMEM((2 * size + 8, size), F32),
        ],
    )
    messages = swap(message, "tile", tile_count)

    counts = (tile_count, sub_count, lev_count)
    ocean = (*(messages[k] for k in spread_out(tile_count)), *chunks, *hops)
    relay_rows = tile_count * BLOCK_ROWS
    relay_shapes = [shape(relay_rows + (side if lev_count == 1 else 0), size, dtype=BF16)]
    if lev_count > 1:
        relay_shapes.append(shape(side, width))
    relay, *top = call(
        functools.partial(relay_kernel, counts, tile_place, member_place),
        relay_shapes,
        (water_heat_state, diffusion_coefficient, *ocean),
    )
    if lev_count > 1:
        relay = jnp.concatenate([relay, lax.psum(top[0], "lev").astype(BF16)], axis=0)
    relays = swap_chips(relay)

    mixing, _ = lax.optimization_barrier((diffusion_coefficient, relay))
    (warm,) = call(
        functools.partial(ocean_kernel, counts, tile_place, member_place),
        [shape(levels, side, width)],
        (water_heat_state, mixing, *ocean),
    )
    far = sorted(k for k in relays if k)
    relayed, _ = lax.optimization_barrier(([relays[k] for k in far], warm))
    relays = swap_cores({0: relay} | dict(zip(far, relayed)))

    names = jnp.stack([m[BLOCK_ROWS, : 8 * group] for m in messages])
    names = names.reshape(devices, 8).astype(jnp.int32)
    table = names[:, 0:4] * 128 + names[:, 4:8]
    table = jnp.where(table < 0, -1, table ^ device_place())
    step = 3 * side
    speed, own, beside = call(
        functools.partial(ice_kernel, tile_count, group, side),
        [
            planes,
            shape(group // 2 * step, width),
            shape(group // 2 * step, width, dtype=BF16),
        ],
        (table, viscous, gain, drag, conduct, current_ice, speed, push, *chunks, *relays),
        scratch=[
            pltpu.VMEM((devices, BLOCK_ROWS + 2 * DEPTH, size), F32),
            pltpu.SMEM((devices, 4), jnp.int32),
            pltpu.SemaphoreType.DMA,
            pltpu.VMEM((2, 2, size + 4 * DEPTH, size), F32),
        ],
        hbm=(0,),
    )
    beside = lax.ppermute(beside, group_axes, [(i, i ^ 1) for i in range(group)])
    paired = call(
        pair_kernel, [shape(step, width, dtype=BF16)] * (group // 2 - 1), (own, beside)
    )
    replies = [
        lax.ppermute(value, group_axes, [(i, i ^ (2 * k + 2)) for i in range(group)])
        for k, value in enumerate(paired)
    ]
    flat, total = call(
        settle_kernel,
        [shape(2 * size, size), shape(step, width)],
        (speed, own, beside),
        scratch=[pltpu.VMEM((2 * size + 8, size), F32), pltpu.SemaphoreType.DMA],
        out_spaces=(pltpu.HBM, pltpu.VMEM),
    )
    if lev_count > 1:
        total = lax.psum(total + sum(r.astype(F32) for r in replies), "lev")
        replies = []
    heat, current = call(
        finish_kernel,
        [shape(levels, side, width), shape(2, side, width)],
        (warm, upper_current_vector, total, *replies),
        scratch=[
            pltpu.VMEM((levels, side, width), F32),
            pltpu.VMEM((2, side, width), F32),
            pltpu.SemaphoreType.DMA((2,)),
        ],
        out_space=pltpu.HBM,
    )
    velocity = flat.reshape(size, 2, size).transpose(1, 0, 2).reshape(1, 1, 2, size * size)
    return heat, current, velocity


def solution(mesh):
    member = ("tile", "sub", "lev")
    whole = ("copies",) + member
    ice = P(None, whole, None, None)
    water = P("lev", ("copies", "tile"), "sub")
    current = P(None, ("copies", "tile"), "sub")
    return jax.shard_map(
        shards,
        mesh=mesh,
        in_specs=(
            water,
            P("tile", "sub"),
            current,
            P(member, None),
            P(member, None, None, None),
            P(member, None, None, None),
            P(None, member, None),
            ice,
            ice,
            ice,
            ice,
        ),
        out_specs=(water, current, ice),
        check_vma=False,
    )
```

```python
import functools

import jax
import jax.numpy as jnp
from jax import lax
from jax.experimental import pallas as pl
from jax.experimental.pallas import tpu as pltpu
from jax.sharding import PartitionSpec as P

SUBCYCLES = 4
STRENGTH_DECAY = 5.0
VISCOUS_STEP = 0.24
SUBCYCLE_STEP = 0.5
CORIOLIS_TURN = 0.1
BASE_MASS = 0.5
HEAT_RATE = 0.2
THIN_ICE = 0.1
THERMAL_DIFFUSE = 0.5
STRESS_MIXING = 0.5

OPPOSITE = (1, 0, 3, 2)
LATERAL = ((2, 3), (2, 3), (0, 1), (0, 1))
DEPTH = SUBCYCLES
EARLY_DEPTHS = (DEPTH, DEPTH, DEPTH - 1, DEPTH - 1)
LATE_DEPTHS = (DEPTH - 1, DEPTH - 1)
EARLY_SIDE, LATE_SIDE = sum(EARLY_DEPTHS), sum(LATE_DEPTHS)
EARLY_ROWS = 4 * EARLY_SIDE
BLOCK_ROWS = EARLY_ROWS + 4 * LATE_SIDE
TILE_ROWS = 16
F32 = jnp.float32
BF16 = jnp.bfloat16
VMEM_LIMIT = 16 * 1024 * 1024
FLOPS_PER_MICRO = 1.15e9


def call(
    kernel, outs, args, scratch=(), smem=(), hbm=(), out_space=pltpu.VMEM, out_spaces=None,
    grant=VMEM_LIMIT, micros=0.01,
):
    def space(i):
        return pltpu.SMEM if i in smem else pltpu.HBM if i in hbm else pltpu.VMEM

    specs = [pl.BlockSpec(memory_space=space(i)) for i in range(len(args))]
    size = sum(a.size * a.dtype.itemsize for a in args)
    return pl.pallas_call(
        kernel,
        out_shape=outs,
        in_specs=specs,
        out_specs=(
            jax.tree.map(lambda _: pl.BlockSpec(memory_space=out_space), outs)
            if out_spaces is None
            else [pl.BlockSpec(memory_space=space) for space in out_spaces]
        ),
        scratch_shapes=list(scratch),
        compiler_params=pltpu.CompilerParams(vmem_limit_bytes=grant),
        cost_estimate=pl.CostEstimate(
            flops=int(micros * FLOPS_PER_MICRO), bytes_accessed=size, transcendentals=0
        ),
    )(*args)


def iota(shape, axis):
    return lax.broadcasted_iota(jnp.int32, shape, axis)


def roll(x, shift, axis):
    return pltpu.roll(x, shift % x.shape[axis], axis)


def flag(condition):
    return jnp.where(condition, 1.0, 0.0).astype(F32)


def ocean_columns(water):
    levels, rows, width = water.shape
    lane = iota((rows, width), 1)
    line = iota((1, width), 1)
    mixed = jnp.zeros((rows, width), F32)
    for l in range(levels):
        mixed = jnp.where(lane // 4 == l, roll(water[l], 2 + 4 * l, 1), mixed)
    across = jnp.concatenate([mixed, jnp.zeros((width - rows, width), F32)], axis=0).T
    beside = []
    for l in range(levels):
        for j in range(2):
            last = across[4 * l + 1 - j : 4 * l + 2 - j]
            lead = across[4 * l + 2 + j : 4 * l + 3 + j]
            beside.append(jnp.where(line < rows, last, roll(lead, rows, 1)))
    return beside


def forward_kernel(group, links_h, blocks_h, rows_h, cols_h, currents_h, water_h, *refs):
    devices, members, place = group
    outs, scratch = refs[:members], refs[members:]
    links, blocks, currents, weights, water, fields, kept, arrived, left = scratch
    pairs, side, width = rows_h.shape
    both = weights.shape[1]
    loads = [
        pltpu.make_async_copy(source, target, arrived.at[i])
        for i, (source, target) in enumerate(
            (
                (links_h, links),
                (blocks_h, blocks),
                (currents_h, currents),
                (rows_h, weights.at[:, pl.ds(0, side)]),
                (cols_h, weights.at[:, pl.ds(side, both - side)]),
                (water_h, water),
            )
        )
    ]
    for i in (5, 2, 0, 1, 4, 3):
        loads[i].start()
    for i in (0, 2, 5):
        loads[i].wait()
    for c in range(2):
        fields[c * side : (c + 1) * side] = currents[c].astype(BF16)
    lane = iota((1, width), 1)
    numbers = jnp.zeros((1, width), F32)
    for q in range(4):
        numbers = jnp.where(lane == q, (links[0, 0, q] >> 7).astype(F32), numbers)
        numbers = jnp.where(lane == 4 + q, (links[0, 0, q] & 127).astype(F32), numbers)
    ends = ocean_columns(water) + [numbers]
    blank = jnp.zeros((fields.shape[0] - 2 * side - len(ends), width), F32)
    fields[2 * side :] = jnp.concatenate(ends + [blank], axis=0).astype(BF16)
    copies = []
    for k, out in enumerate(outs):
        if out.shape[0] > both:
            target = out.at[pl.ds(both, fields.shape[0])]
            copies.append(pltpu.make_async_copy(fields, target, left.at[2 * k + 1]))
            copies[-1].start()
    for i in (1, 3, 4):
        loads[i].wait()
    me = place()
    owners = [lax.rem(lax.rem(blocks[0, m], devices), members) for m in range(pairs)]
    for k, out in enumerate(outs):
        partner = me ^ k
        pair = jnp.int32(0)
        for m in range(pairs):
            pair = jnp.where(owners[m] == partner, m, pair)
        source = weights.at[pair]
        if pairs < members:
            found = sum(flag(owners[m] == partner) for m in range(pairs))
            kept[k] = (weights[pair].astype(F32) * found).astype(BF16)
            source = kept.at[k]
        copies.append(pltpu.make_async_copy(source, out.at[pl.ds(0, both)], left.at[2 * k]))
        copies[-1].start()
    for copy in copies:
        copy.wait()


def put_side_rims(store, planes, depths, at):
    size = planes[0].shape[0]
    lane = iota((size, size), 1)
    mixed = jnp.zeros((size, size), F32)
    for i, plane in enumerate(planes):
        turned = roll(plane, DEPTH + 2 * DEPTH * i, 1)
        mixed = jnp.where(lane // (2 * DEPTH) == i, turned, mixed)
    across = mixed.T
    base = 0
    for i, plane in enumerate(planes):
        for k in range(depths[i]):
            east = 2 * DEPTH * i + DEPTH - 1 - k
            west = 2 * DEPTH * i + DEPTH + k
            store[at(0) + base : at(0) + base + 1] = plane[size - 1 - k : size - k]
            store[at(1) + base : at(1) + base + 1] = plane[k : k + 1]
            store[at(2) + base : at(2) + base + 1] = across[east : east + 1]
            store[at(3) + base : at(3) + base + 1] = across[west : west + 1]
            base += 1


def apart(pairs, wide):
    rows = pairs.shape[0]
    wide[0:rows] = pairs[...]
    return [wide[pl.ds(c, rows // 2, stride=2), :] for c in range(2)]


def rims_kernel(
    thick, conc, ice, water, out, viscous_o, gain_o, mass_o, drag_o, conduct_o,
    speed_o, wide,
):
    size = thick.shape[1]
    cover = jnp.zeros((size, size), F32)
    volume = jnp.zeros((size, size), F32)
    conduct = jnp.zeros((size, size), F32)
    for c in range(thick.shape[0]):
        h, a = thick[c], conc[c]
        cover = cover + a
        volume = volume + a * h
        conduct = conduct + a / (h + THIN_ICE)
    mass = volume + BASE_MASS
    viscous = VISCOUS_STEP * (volume * jnp.exp(-STRENGTH_DECAY * (1.0 - cover))) / mass
    step_mass = SUBCYCLE_STEP / mass
    gain = 1.0 / (1.0 + step_mass * cover)
    speed_x, speed_y = apart(ice, wide)
    viscous_o[...] = viscous
    gain_o[...] = gain
    mass_o[...] = step_mass
    drag_o[...] = cover
    conduct_o[...] = -HEAT_RATE * conduct
    speed_o[0] = speed_x
    speed_o[1] = speed_y
    put_side_rims(
        out, [speed_x, speed_y, viscous, gain], EARLY_DEPTHS, lambda side: side * EARLY_SIDE
    )
    levels, rows, width = water.shape
    for l in range(levels):
        for j in range(2):
            at = EARLY_ROWS + 2 * l + j
            out[at : at + 1] = water[l, rows - 1 - j : rows - j]
            out[at + 2 * levels : at + 2 * levels + 1] = water[l, j : j + 1]


def nearby(me, members, distance, arrays):
    at = me + distance
    inside = (at >= 0) & (at < members)
    found = 0.0
    for k in range(1, members):
        found = found + arrays[k].astype(F32) * flag(inside & ((me ^ k) == at))
    return found


def remap_forward(chunks, field_rows, side, depth):
    total = None
    for chunk, fields in zip(chunks, field_rows):
        down = chunk[0:side]
        right = chunk[side : side + depth]
        wide = jnp.concatenate(fields, axis=1) if len(fields) > 1 else fields[0]
        part = lax.dot_general(down, wide, (((0,), (0,)), ((), ())), preferred_element_type=F32)
        part = part.astype(BF16)
        width = fields[0].shape[1]
        if len(fields) > 1:
            part = jnp.concatenate(
                [part[:, c * width : (c + 1) * width] for c in range(len(fields))], axis=0
            )
        piece = lax.dot_general(part, right, (((1,), (1,)), ((), ())), preferred_element_type=F32)
        piece = piece.astype(BF16).astype(F32)
        total = piece if total is None else total + piece
    return total


def tails_of(chunks, hops):
    at = min(c.shape[0] for c in chunks)
    return [hops[k // 2 - 1][...] if k > 1 and k % 2 else c[at:] for k, c in enumerate(chunks)]


def forcing_kernel(group, side, levels, subs, place, mass, drag, wind, early, *refs):
    chunks = refs[:group][::-1]
    hops, (out, current_o, push_o, store, wide) = refs[group:-5], refs[-5:]
    forces = apart(wind, wide)
    size = mass.shape[0]
    depth = chunks[0].shape[1]
    tails = tails_of(chunks, hops)
    fields = [[t[0:side], t[side : 2 * side]] for t in tails]
    total = remap_forward(chunks, fields, side, depth)
    pushes = []
    for c in range(2):
        current = total[c * size : (c + 1) * size]
        current_o[c] = current
        push = mass[...] * (forces[c] + drag[...] * current)
        push_o[c] = push
        pushes.append(push)
    store[0:EARLY_ROWS] = early[0:EARLY_ROWS]
    put_side_rims(store, pushes, LATE_DEPTHS, lambda side: EARLY_ROWS + side * LATE_SIDE)
    tail = [t[2 * side :].astype(F32) for t in tails]
    line = iota((1, size), 1)
    names = jnp.zeros((1, size), F32)
    for k in range(group):
        names = jnp.where(line // 8 == k, roll(tail[k][2 * levels : 2 * levels + 1], 8 * k, 1), names)
    me, step = place(), group // subs
    left, right = (nearby(me, group, d * step, tail) for d in (-1, 1))
    extra = [names]
    for l in range(levels):
        near = slice(2 * l, 2 * l + 1)
        extra.append(jnp.where(line < side, left[near], right[near]))
    extra.append(early[EARLY_ROWS:])
    used = BLOCK_ROWS + 1 + 5 * levels
    store[BLOCK_ROWS:] = jnp.concatenate(
        extra + [jnp.zeros((store.shape[0] - used, size), F32)], axis=0
    )
    out[...] = store[...].astype(BF16)


def ocean_halos(counts, tile_place, member_place, shape, messages, tails):
    tiles, subs, levs = counts
    levels, rows, width = shape
    my_tile, me = tile_place(), member_place()
    halo = {}
    extras = [m[BLOCK_ROWS:] for m in messages]
    ends = [t[2 * rows :] for t in tails]
    for dt in (-1, 1):
        extra = nearby(my_tile, tiles, dt, extras)
        corners, strips = extra[1 : 1 + levels], extra[1 + levels : 1 + 5 * levels]
        halo[dt, 0] = strips[: 2 * levels] if dt < 0 else strips[2 * levels :]
        at = rows - 1 if dt < 0 else 0
        for ds in (-1, 1):
            lane_at = at if ds < 0 else rows + at
            halo[dt, ds] = corners[:, lane_at : lane_at + 1]
    for ds in (-1, 1):
        beside = nearby(me, subs * levs, ds * levs, ends)[: 2 * levels]
        halo[0, ds] = roll(beside, -rows, 1) if ds > 0 else beside
    return halo


def biharmonic(x, top, bottom, left, right, corner):
    rows, width = x.shape
    row, lane = iota(x.shape, 0), iota(x.shape, 1)
    line = iota((1, width), 1)

    def laplacian(x, top, bottom, left, right):
        up = jnp.where(row == 0, top, roll(x, 1, 0))
        down = jnp.where(row == rows - 1, bottom, roll(x, -1, 0))
        west = jnp.where(lane == 0, left, roll(x, 1, 1))
        east = jnp.where(lane == width - 1, right, roll(x, -1, 1))
        return up + down + west + east - 4.0 * x

    def ring_row(mid, out_row, in_row, dt):
        west = jnp.where(line == 0, corner[dt, -1], roll(mid, 1, 1))
        east = jnp.where(line == width - 1, corner[dt, 1], roll(mid, -1, 1))
        return west + east + out_row + in_row - 4.0 * mid

    def ring_col(mid, out_col, in_col, ds):
        up = jnp.concatenate([corner[-1, ds], mid[:-1]], axis=0)
        down = jnp.concatenate([mid[1:], corner[1, ds]], axis=0)
        return up + down + out_col + in_col - 4.0 * mid

    return laplacian(
        laplacian(x, top[0], bottom[0], left[0], right[0]),
        ring_row(*top, x[0:1], -1),
        ring_row(*bottom, x[rows - 1 :], 1),
        ring_col(*left, x[:, 0:1], -1),
        ring_col(*right, x[:, width - 1 :], 1),
    )


def spread_out(count):
    return sorted(range(count), key=lambda k: (k == count // 2, k))


def split_refs(tiles, members, refs, outs):
    messages = [refs[spread_out(tiles).index(k)] for k in range(tiles)]
    chunks = refs[tiles : tiles + members]
    return messages, tails_of(chunks, refs[tiles + members : -outs]), refs[-outs:]


def relay_kernel(counts, tile_place, member_place, water, mixing, *refs):
    tiles, subs, levs = counts
    outs = 1 if levs == 1 else 2
    messages, tails, outs = split_refs(tiles, subs * levs, refs, outs)
    for k in range(tiles):
        outs[0][k * BLOCK_ROWS : (k + 1) * BLOCK_ROWS] = messages[k][0:BLOCK_ROWS]
    levels, rows, width = water.shape
    halo = ocean_halos(counts, tile_place, member_place, water.shape, messages, tails)

    def both(strip):
        near = sum(strip[2 * l : 2 * l + 1] for l in range(levels))
        far = sum(strip[2 * l + 1 : 2 * l + 2] for l in range(levels))
        return near, far

    def as_columns(strip):
        near, far = both(strip)
        across = jnp.concatenate([near, far] + [jnp.zeros_like(near)] * 6, axis=0).T
        return across[0:rows, 0:1], across[0:rows, 1:2]

    corner = {
        (dt, ds): jnp.sum(halo[dt, ds], axis=0, keepdims=True) for dt in (-1, 1) for ds in (-1, 1)
    }
    x = sum(water[l] for l in range(levels))
    twice = biharmonic(
        x, both(halo[-1, 0]), both(halo[1, 0]), as_columns(halo[0, -1]), as_columns(halo[0, 1]), corner
    )
    top = (x - mixing[...] * twice) / (levels * levs)
    if levs == 1:
        outs[0][tiles * BLOCK_ROWS :] = top.astype(BF16)
    else:
        outs[1][...] = top


def ocean_kernel(counts, tile_place, member_place, water, mixing, *refs):
    tiles, subs, levs = counts
    messages, tails, (warm_o,) = split_refs(tiles, subs * levs, refs, 1)
    levels, rows, width = water.shape
    halo = ocean_halos(counts, tile_place, member_place, water.shape, messages, tails)
    left, right = halo[0, -1].T, halo[0, 1].T
    for l in range(levels):
        x = water[l]
        pair = (2 * l, 2 * l + 1)
        twice = biharmonic(
            x,
            [halo[-1, 0][i : i + 1] for i in pair],
            [halo[1, 0][i : i + 1] for i in pair],
            [left[0:rows, i : i + 1] for i in pair],
            [right[0:rows, i : i + 1] for i in pair],
            {(dt, ds): halo[dt, ds][l : l + 1] for dt in (-1, 1) for ds in (-1, 1)},
        )
        warm_o[l] = x - mixing[...] * twice


def ice_kernel(
    tiles, members, side, table, viscous, gain, drag, conduct, current, speed, push, *refs
):
    chunks, relays = refs[:members], refs[members : 2 * members]
    out, own_o, beside_o, rims, names, named, field = refs[2 * members :]
    load_names = pltpu.make_async_copy(table, names, named)
    load_names.start()
    size = viscous.shape[0]
    depth = chunks[0].shape[1]
    for k in range(tiles):
        for m in range(members):
            block = relays[m][k * BLOCK_ROWS : (k + 1) * BLOCK_ROWS]
            rims[k * members + m, 0:BLOCK_ROWS] = block.astype(F32)
            rims[k * members + m, BLOCK_ROWS:] = jnp.zeros((2 * DEPTH, size), F32)
    half = DEPTH
    high = 2 * DEPTH
    sub = iota((high, size), 0)
    lane = iota((high, size), 1)
    edge = (sub & (half - 1)) == 0
    turn = jnp.where(sub < half, CORIOLIS_TURN, -CORIOLIS_TURN).astype(F32)
    first, last = lane == 0, lane == size - 1

    def load(device, side, mask, with_push=True):
        start = side * EARLY_SIDE
        velocity = rims[device, start : start + high] * mask
        if not with_push:
            return velocity
        both = rims[device, start + high : start + 2 * high]
        visc = jnp.where(sub < half, both, roll(both, half, 0))
        scale = jnp.where(sub < half, roll(both, 1 - half, 0), roll(both, 1, 0)) * mask
        start = EARLY_ROWS + side * LATE_SIDE
        late = rims[device, start : start + high]
        pushed = jnp.where(sub < half, late, roll(late, 1, 0))
        return [velocity, visc, scale, pushed]

    def follow(device, side):
        name = names[device, side]
        return jnp.where(name >= 0, name, 0), name >= 0

    def step(state, left, right, inner, outer):
        c, visc, scale, pushed = state
        spread = left + right + inner + outer - 4.0 * c
        return scale * (c + visc * spread + pushed + turn * roll(c, half, 0))

    base = high
    for c in range(2):
        field[0, c, base : base + size] = speed[c]
    load_names.wait()
    def along(cells, before, beyond):
        left = jnp.where(first, roll(before, 1, 1), roll(cells, 1, 1))
        return left, jnp.where(last, roll(beyond, -1, 1), roll(cells, -1, 1))

    def step_end(state, inside, across, away):
        cells = state[0]
        toward = jnp.where(first if away > 0 else last, roll(inside, away, 1), roll(cells, away, 1))
        inner = jnp.where(edge, across, roll(cells, 1, 0))
        return step(state, toward, roll(cells, -away, 1), inner, roll(cells, -1, 0))

    halos = [[] for _ in range(SUBCYCLES)]
    for q in range(4):
        x, has_x = follow(0, q)
        halo = load(x, OPPOSITE[q], flag(has_x))
        own = load(0, q, 1.0)
        ends = []
        for s in LATERAL[q]:
            y, has_y = follow(x, s)
            z, has_z = follow(y, OPPOSITE[q])
            w, has_w = follow(z, OPPOSITE[s])
            u, has_u = follow(0, s)
            v, has_v = follow(u, q)
            ends.append(
                [
                    load(y, OPPOSITE[q], flag(has_y)),
                    load(z, q, flag(has_z)),
                    load(w, q, flag(has_w), with_push=False),
                    load(u, q, flag(has_u)),
                    load(v, OPPOSITE[q], flag(has_v), with_push=False),
                ]
            )
        (y_hi, z_hi, w_hi, u_hi, v_hi), (y_lo, z_lo, w_lo, u_lo, v_lo) = ends
        for t in range(SUBCYCLES):
            halos[t].append(halo[0])
            if t == SUBCYCLES - 1:
                break
            c, o = halo[0], own[0]
            left, right = along(c, y_lo[0], y_hi[0])
            inner = jnp.where(edge, o, roll(c, 1, 0))
            new_halo = step(halo, left, right, inner, roll(c, -1, 0))
            if t < SUBCYCLES - 2:
                left, right = along(o, u_lo[0], u_hi[0])
                inner = jnp.where(edge, c, roll(o, 1, 0))
                new_own = step(own, left, right, inner, roll(o, -1, 0))
                new_y = step_end(y_hi, c, z_hi[0], 1), step_end(y_lo, c, z_lo[0], -1)
            if t < SUBCYCLES - 3:
                z_hi[0], z_lo[0] = (
                    step_end(z_hi, w_hi, y_hi[0], 1),
                    step_end(z_lo, w_lo, y_lo[0], -1),
                )
                u_hi[0], u_lo[0] = step_end(u_hi, o, v_hi, 1), step_end(u_lo, o, v_lo, -1)
            halo[0] = new_halo
            if t < SUBCYCLES - 2:
                own[0] = new_own
                y_hi[0], y_lo[0] = new_y
    columns = [jnp.where(edge, cells[2], roll(cells[3], 1, 0)).T for cells in halos]

    warm = remap_forward(chunks, [[r[r.shape[0] - side :]] for r in relays], side, depth)
    heat = (conduct[...] * warm).astype(BF16)

    for t in range(SUBCYCLES):
        cells, sides = halos[t], columns[t]
        now, later = t % 2, (t + 1) % 2
        for c in range(2):
            at = c * half
            field[now, c, base + size : base + size + 1] = cells[0][at : at + 1]
            field[now, c, base - 1 : base] = cells[1][at : at + 1]
        for i in range(size // high):
            rows = slice(i * high, (i + 1) * high)
            held = [field[now, c, base + i * high : base + (i + 1) * high] for c in range(2)]
            for c in range(2):
                v, at = held[c], base + i * high
                up = field[now, c, at + 1 : at + 1 + high]
                down = field[now, c, at - 1 : at - 1 + high]
                east = jnp.where(last, sides[rows, c * half : c * half + 1], roll(v, -1, 1))
                west = jnp.where(first, sides[rows, c * half + 1 : c * half + 2], roll(v, 1, 1))
                spread = up + down + east + west - 4.0 * v
                turned = (CORIOLIS_TURN if c == 0 else -CORIOLIS_TURN) * held[1 - c]
                new = gain[rows] * (v + viscous[rows] * spread + push[c, rows] + turned)
                if t == SUBCYCLES - 1:
                    out[c, rows] = new
                else:
                    field[later, c, at : at + high] = new
    stress = [(drag[...] * (out[c] - current[c])).astype(BF16) for c in range(2)]
    return_fluxes([heat, *stress], chunks, side, depth, own_o, beside_o)


def return_fluxes(fluxes, chunks, side, depth, own, beside):
    size = fluxes[0].shape[0]
    wide = jnp.concatenate(fluxes, axis=1)
    step = 3 * side
    down = jnp.concatenate([chunk[0:side] for chunk in chunks], axis=0)
    parts = jnp.dot(down, wide, preferred_element_type=F32).astype(BF16)
    for k, chunk in enumerate(chunks):
        part = parts[k * side : (k + 1) * side]
        part = jnp.concatenate([part[:, c * size : (c + 1) * size] for c in range(3)], axis=0)
        reply = jnp.dot(part, chunk[side : side + depth], preferred_element_type=F32)
        at = k // 2 * step
        if k % 2:
            beside[at : at + step] = reply.astype(BF16)
        else:
            own[at : at + step] = reply


def pair_kernel(own, beside, *outs):
    step = outs[0].shape[0]
    for k, out in enumerate(outs):
        at = (k + 1) * step
        out[...] = (own[at : at + step] + beside[at : at + step].astype(F32)).astype(BF16)


def settle_kernel(speed, own, beside, flat_o, total_o, flat, left):
    size = speed.shape[1]
    for c in range(2):
        flat[pl.ds(c, size, stride=2), :] = speed[c]
    copy = pltpu.make_async_copy(flat.at[pl.ds(0, flat_o.shape[0])], flat_o, left)
    copy.start()
    rows = total_o.shape[0]
    total_o[...] = own[0:rows] + beside[0:rows].astype(F32)
    copy.wait()


def finish_kernel(warm, currents, total, *refs):
    replies, (heat_o, current_o, heat_v, current_v, left) = refs[:-5], refs[-5:]
    copies = [
        pltpu.make_async_copy(heat_v, heat_o, left.at[0]),
        pltpu.make_async_copy(current_v, current_o, left.at[1]),
    ]
    side = currents.shape[1]
    total = total[...]
    for reply in replies:
        total = total + reply[...].astype(F32)
    heat = THERMAL_DIFFUSE * total[0:side]
    for l in range(warm.shape[0]):
        heat_v[l] = warm[l] + heat
    copies[0].start()
    for c in range(2):
        current_v[c] = currents[c] + STRESS_MIXING * total[(c + 1) * side : (c + 2) * side]
    copies[1].start()
    for copy in copies:
        copy.wait()


def shards(
    water_heat_state,
    diffusion_coefficient,
    upper_current_vector,
    remap_blocks,
    remap_rows,
    remap_cols,
    neighbors,
    thickness,
    concentration,
    ice_velocity,
    wind_stress,
):
    tile_count, sub_count, lev_count = (lax.axis_size(a) for a in ("tile", "sub", "lev"))
    group = sub_count * lev_count
    devices = tile_count * group
    group_axes = ("sub", "lev")
    member_axes = ("tile", "sub", "lev")
    levels, side, width = water_heat_state.shape
    pairs, size = remap_rows.shape[1:3]
    categories = thickness.shape[2]

    def tile_place():
        return lax.axis_index("tile")

    def member_place():
        return lax.axis_index("sub") * lev_count + lax.axis_index("lev")

    def device_place():
        return lax.axis_index("tile") * group + member_place()

    def swap(value, axes, count):
        got = {0: value}
        for k in range(1, count):
            got[k] = lax.ppermute(value, axes, [(i, i ^ k) for i in range(count)])
        return [got[k] for k in range(count)]

    def swap_chips(value):
        return {0: value} | {
            k: lax.ppermute(value, group_axes, [(i, i ^ k) for i in range(group)])
            for k in range(2, group, 2)
        }

    def swap_cores(got):
        beside = [(i, i ^ 1) for i in range(group)]
        got = got | {k + 1: lax.ppermute(got[k], group_axes, beside) for k in got}
        return [got[k] for k in range(group)]

    def swap_each(values):
        got = {0: values[0]}
        for k in range(1, group):
            got[k] = lax.ppermute(values[k], group_axes, [(i, i ^ k) for i in range(group)])
        return [got[k] for k in range(group)]

    def shape(*dims, dtype=F32):
        return jax.ShapeDtypeStruct(dims, dtype)

    def interleaved(value):
        return value.reshape(2, size, size).transpose(1, 0, 2).reshape(2 * size, size)

    plane = shape(size, size)
    planes = shape(2, size, size)
    wind = interleaved(wind_stress)

    tail_rows = -(-(2 * levels + 1) // TILE_ROWS) * TILE_ROWS
    pair_rows = side + width
    chunk_rows = pair_rows + 2 * side + tail_rows
    sent = call(
        functools.partial(forward_kernel, (devices, group, member_place)),
        [
            shape(pair_rows if k > 1 and k % 2 else chunk_rows, width, dtype=BF16)
            for k in range(group)
        ],
        (
            neighbors,
            remap_blocks,
            remap_rows[0].swapaxes(1, 2),
            remap_cols[0],
            upper_current_vector,
            water_heat_state,
        ),
        scratch=[
            pltpu.SMEM(neighbors.shape, jnp.int32),
            pltpu.SMEM((1, pairs), jnp.int32),
            pltpu.VMEM((2, side, width), F32),
            pltpu.VMEM((pairs, pair_rows, width), BF16),
            pltpu.VMEM((levels, side, width), F32),
            pltpu.VMEM((chunk_rows - pair_rows, width), BF16),
            pltpu.VMEM((1 if pairs == group else group, pair_rows, width), BF16),
            pltpu.SemaphoreType.DMA((6,)),
            pltpu.SemaphoreType.DMA((2 * group,)),
        ],
        hbm=(0, 1, 2, 3, 4, 5),
        grant=60 * 2**20,
        micros=10,
    )
    chunks = swap_each(sent)
    hops = [
        lax.ppermute(chunks[k][pair_rows:], group_axes, [(i, i ^ 1) for i in range(group)])
        for k in range(2, group, 2)
    ]

    early, viscous, gain, step_mass, drag, conduct, speed = call(
        rims_kernel,
        [shape(EARLY_ROWS + 4 * levels, size)] + [plane] * 5 + [planes],
        (
            thickness.reshape(categories, size, size),
            concentration.reshape(categories, size, size),
            interleaved(ice_velocity),
            water_heat_state,
        ),
        scratch=[pltpu.VMEM((2 * size + 8, size), F32)],
    )
    extra_rows = -(-(1 + 5 * levels) // TILE_ROWS) * TILE_ROWS
    message, current_ice, push = call(
        functools.partial(forcing_kernel, group, side, levels, sub_count, member_place),
        [shape(BLOCK_ROWS + extra_rows, size, dtype=BF16), planes, planes],
        (step_mass, drag, wind, early, *chunks[::-1], *hops),
        scratch=[
            pltpu.VMEM((BLOCK_ROWS + extra_rows, size), F32),
            pltpu.VMEM((2 * size + 8, size), F32),
        ],
    )
    messages = swap(message, "tile", tile_count)

    counts = (tile_count, sub_count, lev_count)
    ocean = (*(messages[k] for k in spread_out(tile_count)), *chunks, *hops)
    relay_rows = tile_count * BLOCK_ROWS
    relay_shapes = [shape(relay_rows + (side if lev_count == 1 else 0), size, dtype=BF16)]
    if lev_count > 1:
        relay_shapes.append(shape(side, width))
    relay, *top = call(
        functools.partial(relay_kernel, counts, tile_place, member_place),
        relay_shapes,
        (water_heat_state, diffusion_coefficient, *ocean),
    )
    if lev_count > 1:
        relay = jnp.concatenate([relay, lax.psum(top[0], "lev").astype(BF16)], axis=0)
    relays = swap_chips(relay)

    mixing, _ = lax.optimization_barrier((diffusion_coefficient, relay))
    (warm,) = call(
        functools.partial(ocean_kernel, counts, tile_place, member_place),
        [shape(levels, side, width)],
        (water_heat_state, mixing, *ocean),
    )
    far = sorted(k for k in relays if k)
    relayed, _ = lax.optimization_barrier(([relays[k] for k in far], warm))
    relays = swap_cores({0: relay} | dict(zip(far, relayed)))

    names = jnp.stack([m[BLOCK_ROWS, : 8 * group] for m in messages])
    names = names.reshape(devices, 8).astype(jnp.int32)
    table = names[:, 0:4] * 128 + names[:, 4:8]
    table = jnp.where(table < 0, -1, table ^ device_place())
    step = 3 * side
    speed, own, beside = call(
        functools.partial(ice_kernel, tile_count, group, side),
        [
            planes,
            shape(group // 2 * step, width),
            shape(group // 2 * step, width, dtype=BF16),
        ],
        (table, viscous, gain, drag, conduct, current_ice, speed, push, *chunks, *relays),
        scratch=[
            pltpu.VMEM((devices, BLOCK_ROWS + 2 * DEPTH, size), F32),
            pltpu.SMEM((devices, 4), jnp.int32),
            pltpu.SemaphoreType.DMA,
            pltpu.VMEM((2, 2, size + 4 * DEPTH, size), F32),
        ],
        hbm=(0,),
    )
    beside = lax.ppermute(beside, group_axes, [(i, i ^ 1) for i in range(group)])
    paired = call(
        pair_kernel, [shape(step, width, dtype=BF16)] * (group // 2 - 1), (own, beside)
    )
    replies = [
        lax.ppermute(value, group_axes, [(i, i ^ (2 * k + 2)) for i in range(group)])
        for k, value in enumerate(paired)
    ]
    flat, total = call(
        settle_kernel,
        [shape(2 * size, size), shape(step, width)],
        (speed, own, beside),
        scratch=[pltpu.VMEM((2 * size + 8, size), F32), pltpu.SemaphoreType.DMA],
        out_spaces=(pltpu.HBM, pltpu.VMEM),
    )
    if lev_count > 1:
        total = lax.psum(total + sum(r.astype(F32) for r in replies), "lev")
        replies = []
    heat, current = call(
        finish_kernel,
        [shape(levels, side, width), shape(2, side, width)],
        (warm, upper_current_vector, total, *replies),
        scratch=[
            pltpu.VMEM((levels, side, width), F32),
            pltpu.VMEM((2, side, width), F32),
            pltpu.SemaphoreType.DMA((2,)),
        ],
        out_space=pltpu.HBM,
    )
    velocity = flat.reshape(size, 2, size).transpose(1, 0, 2).reshape(1, 1, 2, size * size)
    return heat, current, velocity


def solution(mesh):
    member = ("tile", "sub", "lev")
    whole = ("copies",) + member
    ice = P(None, whole, None, None)
    water = P("lev", ("copies", "tile"), "sub")
    current = P(None, ("copies", "tile"), "sub")
    return jax.shard_map(
        shards,
        mesh=mesh,
        in_specs=(
            water,
            P("tile", "sub"),
            current,
            P(member, None),
            P(member, None, None, None),
            P(member, None, None, None),
            P(None, member, None),
            ice,
            ice,
            ice,
            ice,
        ),
        out_specs=(water, current, ice),
        check_vma=False,
    )
```
